32 devices in a mesh: grp: 4 (over x, core), seq: 8 (over z, y).
Axes of the slice: x: 2, y: 2, z: 4, core: 2. Of those that a mesh axis runs over, the one named last changes fastest.
Arguments:
- fields: bfloat16 [8, 2048, 1104], P('grp', 'seq'), may hold values from -6 to 6
- targets: bfloat16 [8, 2048, 1104], P('grp', 'seq'), may hold values from -6 to 6
- land_mask: int32 [8, 2048, 69], P('grp', 'seq'), may hold values from 0 to 1
- interval: int32 [8], P('grp'), may hold values from 0 to 2, as said below
- samples: int32 [8], P('grp'), may hold values from 4 to 13, as said below
- wide_weights: float32 [384, 7632], P('grp')
- wide_firsts: float32 [384, 7632], P('grp'), may hold values from -0.00036621094 to 0.00036621094
- wide_seconds: float32 [384, 7632], P('grp'), may hold values from 6.3374056e-10 to 2.5349622e-09
- tall_weights: float32 [2640, 384], P(None, 'grp')
- tall_firsts: float32 [2640, 384], P(None, 'grp'), may hold values from -0.00036621094 to 0.00036621094
- tall_seconds: float32 [2640, 384], P(None, 'grp'), may hold values from 6.3374056e-10 to 2.5349622e-09
- query_vector: float32 [384], P('grp'), may hold values from -4 to 4
- query_firsts: float32 [384], P('grp'), may hold values from -0.00036621094 to 0.00036621094
- query_seconds: float32 [384], P('grp'), may hold values from 6.3374056e-10 to 2.5349622e-09
Outputs:
- loss_sum: float32 [], replicated
- weight_sum: float32 [], replicated
- grad_norm: float32 [], replicated
- wide_master: float32 [384, 7632], P('grp')
- wide_momentum: float32 [384, 7632], P('grp')
- wide_variance: float32 [384, 7632], P('grp')
- wide_copy: bfloat16 [384, 7632], P('grp')
- tall_master: float32 [2640, 384], P(None, 'grp')
- tall_momentum: float32 [2640, 384], P(None, 'grp')
- tall_variance: float32 [2640, 384], P(None, 'grp')
- tall_copy: bfloat16 [2640, 384], P(None, 'grp')
- query_master: float32 [384], P('grp')
- query_momentum: float32 [384], P('grp')
- query_variance: float32 [384], P('grp')
- query_copy: bfloat16 [384], P('grp')
The draws below stay inside these ranges and needn't reach their ends.
Inputs may be any that keep to these rules, and one draw needn't show every extreme that they name: `samples`: the first forecast has the smallest count and the last the largest. The lead time is 6 * 2**interval hours; each of the three ids is used by some forecast, and the interval groups are of uneven sizes.
All inputs are finite; a program needn't handle non-finite values.
Results may differ from the reference program's by a relative error of at most 0.023.
Values may be sent and summed in bfloat16 or wider, within the bound.
No kernel may reach another device: no remote copies, remote signals or barrier semaphores. Data moves between devices by JAX's collectives and lax.ppermute only.
A program may use at most 384 MiB of HBM per device.

```python
import math
import jax
import jax.numpy as jnp
from jax import lax

D = 384
HEADS = 6
HEAD = 64
FF = 1536
VARS = 69
PIX = 16
COLS = 128
STEP = 5
TOK_DEV = 256
LENGTH = 2048
ITEMS = 8
NPARAM = 3944832


def draw_wide_weights(key, part):
    key = jax.random.fold_in(key, 11)
    columns = 13 * D + FF + VARS * PIX
    index = jnp.arange(columns)
    rising = (index % D).astype(jnp.float32) / D
    entries = jax.random.normal(key, (D, columns), jnp.float32)
    rising = 0.5 + rising
    factor = jnp.ones((columns,), jnp.float32)
    factor = jnp.where(index < D, 4.0, factor)
    factor = jnp.where((index >= 2 * D) & (index < 3 * D), rising, factor)
    factor = jnp.where((index >= 3 * D) & (index < 9 * D), 2.5, factor)
    factor = jnp.where((index >= 12 * D) & (index < 13 * D), float(max(1, LENGTH // 64)) ** 0.5, factor)
    return entries * factor[None, :] * D ** (-0.5)


def draw_tall_weights(key, part):
    key = jax.random.fold_in(key, 12)
    total_rows = VARS * PIX + FF
    entries = jax.random.normal(key, (total_rows, D), jnp.float32)
    index = jnp.arange(total_rows)
    factor = jnp.where(index < VARS * PIX, PIX ** (-0.5), FF ** (-0.5))
    return entries * factor[:, None]


def draw_land_mask(key, part):
    key = jax.random.fold_in(key, 13)
    tickets = jax.random.randint(key, (ITEMS, LENGTH, VARS), 0, 1000)
    position = jnp.arange(LENGTH)[None, :, None]
    limit = 300 + 600 * position // LENGTH
    present = (tickets < limit) | (jnp.arange(VARS)[None, None, :] == 0)
    return present.astype(jnp.int32)


def draw_samples(key, part):
    key = jax.random.fold_in(key, 14)
    extra = jax.random.randint(key, (ITEMS,), 0, 3)
    extra = extra.at[0].set(0).at[ITEMS - 1].set(2)
    return (ITEMS // 2 + jnp.arange(ITEMS) + extra).astype(jnp.int32)


def draw_interval(key, part):
    key = jax.random.fold_in(key, 15)
    order_key, id_key = jax.random.split(key)
    order = jax.random.permutation(order_key, ITEMS)
    ids = jax.random.randint(id_key, (ITEMS,), 0, 3)
    ids = ids.at[order[:3]].set(jnp.arange(3, dtype=jnp.int32))
    return ids.astype(jnp.int32)


def shard_levels(own_key, extent, cuts, low, high):
    def one(dim, blocks):
        heights = jax.random.uniform(jax.random.fold_in(jax.random.fold_in(own_key, 6), dim), (blocks,), jnp.float32, low / len(cuts), high / len(cuts))
        return jnp.repeat(jnp.exp(heights), extent[dim] // blocks).reshape((-1,) + (1,) * (len(extent) - dim - 1))

    loudness = one(*cuts[0])
    for cut in cuts[1:]:
        loudness = loudness * one(*cut)
    return loudness


def scatter_about(own_key, extent, spread, most, shards=(), kind=jnp.bfloat16):
    gain = shard_levels(own_key, extent, shards, -0.22, 0.18) if shards else 1.0
    result = jax.random.normal(own_key, extent, jnp.float32) * spread * gain
    return jnp.minimum(jnp.maximum(result, -most), most).astype(kind)


def setup_inputs(seed: int = 0) -> dict:
    arg_keys = jax.random.split(jax.random.key(seed), 15)
    fields = scatter_about(arg_keys[0], (ITEMS, LENGTH, VARS * PIX), 1.0, 6.0, ((0, 4), (1, 8)))
    targets = scatter_about(arg_keys[1], (ITEMS, LENGTH, VARS * PIX), 1.0, 6.0, ((0, 4), (1, 8)))
    land_mask = draw_land_mask(jax.random.fold_in(arg_keys[14], 71), 0)
    interval = draw_interval(jax.random.fold_in(arg_keys[14], 71), 0)
    samples = draw_samples(jax.random.fold_in(arg_keys[14], 71), 0)
    wide_weights = draw_wide_weights(jax.random.fold_in(arg_keys[14], 71), 0)
    wide_firsts = scatter_about(arg_keys[6], (D, 13 * D + FF + VARS * PIX), (0.05 / NPARAM ** 0.5), 0.00036621094, ((0, 4),), jnp.float32)
    wide_seconds = jnp.clip(jnp.exp(math.log(2.5349622401193983e-09) - 1.3862944 * jax.random.uniform(arg_keys[7], (D, 13 * D + FF + VARS * PIX), jnp.float32) ** shard_levels(arg_keys[7], (D, 13 * D + FF + VARS * PIX), ((0, 4),), -0.2, 0.2)), 6.337405600298496e-10, 2.5349622401193983e-09)
    tall_weights = draw_tall_weights(jax.random.fold_in(arg_keys[14], 71), 0)
    tall_firsts = scatter_about(arg_keys[9], (VARS * PIX + FF, D), (0.05 / NPARAM ** 0.5), 0.00036621094, ((1, 4),), jnp.float32)
    tall_seconds = jnp.clip(jnp.exp(math.log(2.5349622401193983e-09) - 1.3862944 * jax.random.uniform(arg_keys[10], (VARS * PIX + FF, D), jnp.float32) ** shard_levels(arg_keys[10], (VARS * PIX + FF, D), ((1, 4),), -0.2, 0.2)), 6.337405600298496e-10, 2.5349622401193983e-09)
    query_vector = scatter_about(arg_keys[11], (D,), 0.25, 4.0, ((0, 4),), jnp.float32)
    query_firsts = scatter_about(arg_keys[12], (D,), (0.05 / NPARAM ** 0.5), 0.00036621094, ((0, 4),), jnp.float32)
    query_seconds = jnp.clip(jnp.exp(math.log(2.5349622401193983e-09) - 1.3862944 * jax.random.uniform(arg_keys[13], (D,), jnp.float32) ** shard_levels(arg_keys[13], (D,), ((0, 4),), -0.2, 0.2)), 6.337405600298496e-10, 2.5349622401193983e-09)
    return {"fields": fields, "targets": targets, "land_mask": land_mask, "interval": interval, "samples": samples, "wide_weights": wide_weights, "wide_firsts": wide_firsts, "wide_seconds": wide_seconds, "tall_weights": tall_weights, "tall_firsts": tall_firsts, "tall_seconds": tall_seconds, "query_vector": query_vector, "query_firsts": query_firsts, "query_seconds": query_seconds}


@jax.custom_vjp
def low(v):
    return lax.optimization_barrier(v.astype(jnp.bfloat16)).astype(jnp.float32)

@jax.custom_vjp
def low_back(v):
    return v

def low_keep(v):
    return (low(v), None)

def low_pass(kept, grad):
    return (grad,)

def back_keep(v):
    return (v, None)

def back_low(kept, grad):
    return (low(grad),)
low.defvjp(low_keep, low_pass)
low_back.defvjp(back_keep, back_low)
beta_first = 0.5
beta_second = 0.5
learn_rate = 0.1
decay_rate = 0.01
adam_epsilon = 1e-08
clip_limit = 0.05
norm_epsilon = 1e-06
masked_score = -1e+30

def round_both(values):
    return low(low_back(values))

def contract(spec, left, right):
    return jnp.einsum(spec, left, right, precision=lax.Precision.HIGHEST)

def layer_norm(values):
    centered = values - lax.optimization_barrier(jnp.mean(values, axis=-1, keepdims=True))
    return centered * lax.rsqrt(lax.optimization_barrier(jnp.mean(centered * centered, axis=-1, keepdims=True)) + norm_epsilon)

def modulate(values, shift, scale):
    return layer_norm(values) * (1.0 + scale) + shift

def softmax_last(scores):
    top = lax.optimization_barrier(jnp.max(scores, axis=-1, keepdims=True))
    expo = jnp.exp(scores - top)
    return expo / lax.optimization_barrier(jnp.sum(expo, axis=-1, keepdims=True))

def lead_features(interval, width):
    hours = 6.0 * jnp.exp2(interval.astype(jnp.float32))
    half = width // 2
    freqs = jnp.exp(-jnp.log(1000.0) * jnp.arange(half, dtype=jnp.float32) / half)
    angles = hours[:, None] * freqs[None, :]
    return jax.nn.silu(jnp.concatenate([jnp.sin(angles), jnp.cos(angles)], axis=-1))

def adamw_update(param, first, second, grad):
    first = beta_first * first + (1.0 - beta_first) * grad
    second = beta_second * second + (1.0 - beta_second) * grad * grad
    mean_hat = first / (1.0 - beta_first ** STEP)
    var_hat = second / (1.0 - beta_second ** STEP)
    param = param - learn_rate * (mean_hat / (jnp.sqrt(var_hat) + adam_epsilon) + decay_rate * param)
    return (param, first, second, param.astype(jnp.bfloat16))

def item_loss(params, pixels, target_item, keep, lead, weight):
    wide, tall, query = params
    cuts = [0, D, 2 * D, 3 * D, 9 * D, 12 * D, 13 * D, 13 * D + FF, 13 * D + FF + VARS * PIX]
    agg_key, agg_value, agg_out, modulation, qkv_weight, attn_out, up_weight, head_weight = [wide[:, cuts[j]:cuts[j + 1]] for j in range(8)]
    embed = tall[:VARS * PIX].reshape(VARS, PIX, D)
    down_weight = tall[VARS * PIX:]
    scale = HEAD ** (-0.5)
    embedded = round_both(contract('pvk,vkd->pvd', pixels, embed))
    probe = low(contract('dhc,hc->hd', agg_key.reshape(D, HEADS, HEAD), query.reshape(HEADS, HEAD)))
    var_scores = jnp.where(keep[:, None, :], low_back(contract('pvd,hd->phv', embedded, probe) * scale), masked_score)
    var_probs = low(softmax_last(var_scores))
    pooled = round_both(contract('phv,pvd->phd', var_probs, embedded))
    gathered = round_both(contract('phd,dhc->phc', pooled, agg_value.reshape(D, HEADS, HEAD)).reshape(LENGTH, D))
    residual_a = low_back(contract('pd,de->pe', gathered, agg_out))
    modul = contract('d,de->e', low(lead), modulation).reshape(6, 1, D)
    normed_a = low(modulate(residual_a, modul[0], modul[1]))
    qkv = round_both(contract('pd,de->pe', normed_a, qkv_weight))
    queries = qkv[:, :D].reshape(LENGTH, HEADS, HEAD)
    keys = qkv[:, D:2 * D].reshape(LENGTH, HEADS, HEAD)
    values = qkv[:, 2 * D:].reshape(LENGTH, HEADS, HEAD)

    def attend(block):
        scores = low_back(contract('qhc,khc->hqk', block, keys) * scale)
        probs = low(softmax_last(scores))
        return contract('hqk,khc->qhc', probs, values)
    blocks = queries.reshape(LENGTH // TOK_DEV, TOK_DEV, HEADS, HEAD)
    attended = round_both(lax.map(jax.checkpoint(attend), blocks).reshape(LENGTH, D))
    residual_b = residual_a + modul[2] * low_back(contract('pd,de->pe', attended, attn_out))
    normed_b = low(modulate(residual_b, modul[3], modul[4]))
    expand = low_back(contract('pd,df->pf', normed_b, up_weight))
    activated = low(jax.nn.gelu(expand, approximate=True))
    residual_c = residual_b + modul[5] * low_back(contract('pf,fd->pd', activated, down_weight))
    final = low(layer_norm(residual_c))
    predicted = low_back(contract('pd,do->po', final, head_weight))
    diff = predicted.reshape(LENGTH, VARS, PIX) - target_item
    return jnp.sum(weight * lax.optimization_barrier(jnp.mean(diff * diff, axis=-1)))

def reference(fields, targets, land_mask, interval, samples, wide_weights, wide_firsts, wide_seconds, tall_weights, tall_firsts, tall_seconds, query_vector, query_firsts, query_seconds):
    params = (wide_weights.astype(jnp.bfloat16).astype(jnp.float32), tall_weights.astype(jnp.bfloat16).astype(jnp.float32), query_vector.astype(jnp.bfloat16).astype(jnp.float32))
    rows = (jnp.arange(LENGTH) // COLS).astype(jnp.float32)
    latitude = jnp.pi * ((rows + 0.5) / (LENGTH // COLS) - 0.5)
    weight = samples.astype(jnp.float32)[:, None, None] * jnp.cos(latitude)[None, :, None] * land_mask.astype(jnp.float32)
    weight_sum = jnp.sum(weight)
    inverse = 1.0 / weight_sum
    pixels = fields.astype(jnp.float32).reshape(ITEMS, LENGTH, VARS, PIX)
    target_all = targets.astype(jnp.float32).reshape(ITEMS, LENGTH, VARS, PIX)
    keep = land_mask > 0
    leads = lead_features(interval, D)

    def one_item(carry, item):
        loss_total, grads = carry
        pixel_item, target_item, keep_item, lead_item, weight_item = item
        loss_item, pull = jax.vjp(lambda ws: item_loss(ws, pixel_item, target_item, keep_item, lead_item, weight_item), params)
        item_grads, = pull(inverse)
        return ((loss_total + loss_item, jax.tree.map(jnp.add, grads, item_grads)), None)
    start = (jnp.zeros((), jnp.float32), jax.tree.map(jnp.zeros_like, params))
    (loss_sum, grads), _ = lax.scan(one_item, start, (pixels, target_all, keep, leads, weight))
    grad_norm = jnp.sqrt(sum((jnp.sum(grad * grad) for grad in grads)))
    factor = jnp.minimum(1.0, clip_limit / (grad_norm + 1e-06))
    wide_out = adamw_update(wide_weights, wide_firsts, wide_seconds, grads[0] * factor)
    tall_out = adamw_update(tall_weights, tall_firsts, tall_seconds, grads[1] * factor)
    query_out = adamw_update(query_vector, query_firsts, query_seconds, grads[2] * factor)
    return (loss_sum, weight_sum, grad_norm) + wide_out + tall_out + query_out
```

```python
import functools

import jax
import jax.numpy as jnp
from jax import lax
from jax.experimental import pallas as pl
from jax.experimental.pallas import tpu as pltpu
from jax.sharding import PartitionSpec as P

D = 384
HEADS = 6
HEAD = 64
FF = 1536
VARS = 69
PIX = 16
OUT = VARS * PIX
OUTP = 1152
COLS = 128
STEP = 5
CUTS = 4
SCALE = HEAD**-0.5
LOG2E = 1.4426950408889634

beta_first = 0.5
beta_second = 0.5
learn_rate = 0.1
decay_rate = 0.01
adam_epsilon = 1e-08
clip_limit = 0.05
norm_epsilon = 1e-06
masked_score = -1e30

F32 = jnp.float32
BF16 = jnp.bfloat16
LIMIT = 50 * 1024 * 1024


def dot(left, right, a, b):
    return lax.dot_general(left, right, (((a,), (b,)), ((), ())), preferred_element_type=F32)


def nn(left, right):
    return dot(left, right, 1, 0)


def nt(left, right):
    return dot(left, right, 1, 1)


def tn(left, right):
    return dot(left, right, 0, 0)


def iota(shape, dim):
    return lax.broadcasted_iota(jnp.int32, shape, dim)


def half_low(shape):
    return iota(shape, len(shape) - 1) < HEAD


def swap_halves(tile):
    return pltpu.roll(tile, HEAD, 1)


def spread():
    return iota((128, OUT), 1) // PIX == iota((128, OUT), 0)


def place():
    grp = lax.axis_index("grp")
    seq = lax.axis_index("seq")
    return grp, seq


def call(kernel, outs, grid=(), in_specs=None, out_specs=None, scratch=(), flops=0, limit=LIMIT):
    kw = {}
    if in_specs is not None:
        kw["in_specs"] = in_specs
    if out_specs is not None:
        kw["out_specs"] = out_specs
    return pl.pallas_call(
        kernel,
        out_shape=outs,
        grid=grid,
        scratch_shapes=list(scratch),
        compiler_params=pltpu.CompilerParams(vmem_limit_bytes=limit),
        **kw,
    )


def whole():
    return pl.BlockSpec(memory_space=pltpu.VMEM)


def smem():
    return pl.BlockSpec(memory_space=pltpu.SMEM)


def sds(shape, dtype):
    return jax.ShapeDtypeStruct(shape, dtype)


def standardize(x):
    centered = x - jnp.mean(x, axis=-1, keepdims=True)
    rstd = lax.rsqrt(jnp.mean(centered * centered, axis=-1, keepdims=True) + norm_epsilon)
    return centered * rstd, rstd


def standardize_back(grad, normed, rstd):
    return rstd * (
        grad
        - jnp.mean(grad, axis=-1, keepdims=True)
        - normed * jnp.mean(grad * normed, axis=-1, keepdims=True)
    )


def gelu_parts(x):
    k = 0.7978845608028654
    inner = k * (x + 0.044715 * x * x * x)
    t = jnp.tanh(inner)
    value = 0.5 * x * (1.0 + t)
    slope = 0.5 * (1.0 + t) + 0.5 * x * (1.0 - t * t) * k * (1.0 + 3 * 0.044715 * x * x)
    return value, slope


def pack_first(wide_ref, tall_ref, query_ref, out_ref):
    rows = wide_ref.shape[0]
    out_ref[:, : 3 * D] = wide_ref[...].astype(BF16)
    out_ref[:, 3 * D : 3 * D + OUT] = tall_ref[...].T.astype(BF16)
    eye = iota((rows, rows), 0) == iota((rows, rows), 1)
    column = jnp.sum(jnp.where(eye, query_ref[...], 0.0), axis=1, keepdims=True)
    tail = jnp.where(iota((rows, OUTP - OUT), 1) == 0, column, 0.0)
    out_ref[:, 3 * D + OUT :] = tail.astype(BF16)


def pack_rest(wide_ref, tall_ref, lead_ref, qkv_ref, late_ref, mod_ref):
    rows = wide_ref.shape[0]
    grp, _ = place()
    base = 3 * D
    low = half_low((rows, 128))
    for j in range(HEADS // 2):
        k = wide_ref[:, base + 6 * D + D + j * 128 : base + 6 * D + D + (j + 1) * 128]
        v = wide_ref[:, base + 6 * D + 2 * D + j * 128 : base + 6 * D + 2 * D + (j + 1) * 128]
        qkv_ref[:, (2 * j) * 128 : (2 * j + 1) * 128] = jnp.where(low, k, swap_halves(v)).astype(
            BF16
        )
        qkv_ref[:, (2 * j + 1) * 128 : (2 * j + 2) * 128] = jnp.where(
            low, swap_halves(k), v
        ).astype(BF16)
    qkv_ref[:, 2 * D :] = wide_ref[:, base + 6 * D : base + 7 * D].astype(BF16)
    start = 12 * D
    late_ref[:, : D + FF + OUT] = wide_ref[:, start:].astype(BF16)
    late_ref[:, D + FF + OUT : D + FF + OUTP] = jnp.zeros((rows, OUTP - OUT), BF16)
    late_ref[:, D + FF + OUTP :] = tall_ref[OUT:, :].T.astype(BF16)
    lead = lead_ref[pl.ds(pl.multiple_of(grp * rows, 16), rows), :].astype(F32)
    mod = wide_ref[:, base : base + 6 * D].astype(BF16).astype(F32)
    parts = [jnp.sum(lead[:, g : g + 1] * mod, axis=0, keepdims=True) for g in range(3)]
    mod_ref[...] = jnp.zeros_like(mod_ref)
    for g in range(3):
        mod_ref[g : g + 1, :] = parts[g]


def assemble(target, blocks, grp, lo, hi):
    for j, ref in enumerate(blocks):
        rows = ref.shape[0]
        at = pl.multiple_of(jnp.bitwise_xor(grp, j) * rows, 16)
        target[pl.ds(at, rows), :] = ref[:, lo:hi]


def prepare(*refs):
    blocks, (agg_ref, embed_ref, score_ref, fused_ref, probe_ref) = refs[:-5], refs[-5:]
    grp, _ = place()
    assemble(agg_ref, blocks, grp, 0, 3 * D)
    assemble(embed_ref, blocks, grp, 3 * D, 3 * D + OUTP)
    query = embed_ref[:, OUT : OUT + 1].astype(F32)
    picked = jnp.where(iota((D, 128), 1) == iota((D, 128), 0) // HEAD, query, 0.0).astype(BF16)
    probe = nn(agg_ref[:, :D], picked).astype(BF16)
    probe_ref[...] = probe
    embed = embed_ref[:, :OUT]
    rows = tn(probe, embed) * SCALE
    mine = spread()
    for h in range(HEADS):
        score_ref[h * 128 : (h + 1) * 128, :] = jnp.where(mine, rows[h : h + 1, :], 0.0).astype(
            BF16
        )
    fused_ref[...] = tn(agg_ref[:, D : 2 * D], embed).astype(BF16)


def widen_mask(mask_ref, scratch):
    scratch[...] = jnp.full(scratch.shape, -1, jnp.int32)
    scratch[:, :VARS] = mask_ref[0]
    value = scratch[...]
    return value > 0, value < 0


def aggregate(group, *refs):
    (interval, fields_ref, mask_ref, score_ref, fused_ref, agg_ref) = refs[:6]
    blocks = refs[6 : 6 + group]
    mods = refs[6 + group : 6 + 2 * group]
    outs = refs[6 + 2 * group :]
    (probs_ref, picked_ref, gathered_ref, x0_ref, n1_ref) = outs[:5]
    units = outs[5 : 5 + CUTS]
    qkv_w, mod_s, mask_s, unit_s = outs[5 + CUTS :]
    item = pl.program_id(0)
    grp, seq = place()
    tokens = fields_ref.shape[1]

    @pl.when(item == 0)
    def _():
        assemble(qkv_w, blocks, grp, 0, 3 * D)
        total = mods[0][...]
        for m in mods[1:]:
            total = total + m[...]
        mod_s[...] = total

    fields = fields_ref[0]
    wide_fields = fields.astype(F32)
    keep, pad = widen_mask(mask_ref, mask_s)
    scores = nt(fields, score_ref[...])
    expand = jnp.where(spread(), 1.0, 0.0).astype(BF16)
    low = half_low((tokens, 128))
    for j in range(HEADS // 2):
        pair = []
        for h in (2 * j, 2 * j + 1):
            s = jnp.where(
                keep, scores[:, h * 128 : (h + 1) * 128], jnp.where(pad, -3e38, masked_score)
            )
            e = jnp.exp(s - jnp.max(s, axis=-1, keepdims=True))
            a = e / jnp.sum(e, axis=-1, keepdims=True)
            probs_ref[0, :, h * 128 : (h + 1) * 128] = a
            picked = (nn(a.astype(BF16), expand) * wide_fields).astype(BF16)
            picked_ref[h] = picked
            pair.append(nt(picked, fused_ref[j * 128 : (j + 1) * 128, :]))
        gathered_ref[:, j * 128 : (j + 1) * 128] = jnp.where(low, pair[0], pair[1]).astype(BF16)
    x0 = nn(gathered_ref[...], agg_ref[:, 2 * D :])
    x0_ref[...] = x0
    mod = mod_s[pl.ds(interval[item], 1), :]
    normed, _ = standardize(x0)
    n1 = (normed * (1.0 + mod[:, D : 2 * D]) + mod[:, :D]).astype(BF16)
    n1_ref[...] = n1
    qkv = nn(n1, qkv_w[...])
    half = tokens // 2
    low = half_low((half, 128))
    for h in range(HEADS):
        unit_s[HEADS * item + h, :tokens, :] = qkv[:, h * 128 : (h + 1) * 128].astype(BF16)
    for j in range(HEADS // 2):
        pair = qkv[:, 2 * D + j * 128 : 2 * D + (j + 1) * 128]
        top, bottom = pair[:half], pair[half:]
        unit_s[HEADS * item + 2 * j, tokens:, :] = jnp.where(
            low, top, swap_halves(bottom)
        ).astype(BF16)
        unit_s[HEADS * item + 2 * j + 1, tokens:, :] = jnp.where(
            low, swap_halves(top), bottom
        ).astype(BF16)

    @pl.when(item == pl.num_programs(0) - 1)
    def _():
        deal(units, unit_s, seq)


def deal(targets, source, seq):
    a = seq // (lax.axis_size("seq") // CUTS)
    for m in range(CUTS):
        for r in range(targets[m].shape[0]):
            targets[m][r] = source[CUTS * r + jnp.bitwise_xor(a, m)]


def collect(target, sources, seq):
    a = seq // (lax.axis_size("seq") // CUTS)
    for m in range(CUTS):
        for r in range(sources[m].shape[0]):
            target[CUTS * r + jnp.bitwise_xor(a, m)] = sources[m][r]


def unpack(pack, at_low):
    wide = pack.astype(F32)
    low = half_low(wide.shape)
    if at_low:
        both = [jnp.where(low, wide, 0.0), jnp.where(low, swap_halves(wide), 0.0)]
    else:
        both = [jnp.where(low, 0.0, swap_halves(wide)), jnp.where(low, 0.0, wide)]
    return jnp.concatenate(both, axis=0).astype(BF16)


def pack_rows(tile, at_low):
    half = tile.shape[0] // 2
    top, bottom = tile[:half], tile[half:]
    low = half_low(top.shape)
    if at_low:
        return jnp.where(low, top, swap_halves(bottom))
    return jnp.where(low, swap_halves(top), bottom)


def attend(shares, *refs):
    own = refs[:CUTS]
    others = refs[CUTS : CUTS * shares]
    backs = refs[CUTS * shares : CUTS * shares + CUTS]
    kept_ref, lse_ref, keys_s, turned_s = refs[CUTS * shares + CUTS :]
    tokens = kept_ref.shape[2]
    for n, ref in enumerate(own + others):
        keys_s[n * tokens : (n + 1) * tokens, :] = ref[0, :tokens, :]
    keys = keys_s[...]
    turned_s[...] = keys.T
    for m in range(CUTS):
        queries = unpack(own[m][0, tokens:, :], True)
        scores = nt(keys, queries) * (SCALE * LOG2E)
        top = jnp.max(scores, axis=0, keepdims=True)
        probs = jnp.exp2(scores - top)
        total = jnp.sum(probs, axis=0, keepdims=True)
        out = nn(turned_s[...], probs.astype(BF16)) / total
        lse_ref[0, m] = jnp.broadcast_to(top + jnp.log2(total), (8, tokens))
        out = out.T
        kept_ref[0, m] = out
        backs[m][0] = pack_rows(out, False).astype(BF16)


def middle(group, *refs):
    (interval, wl, wg, x0_ref, fields_ref, mask_ref) = refs[:6]
    heads_in = refs[6 : 6 + CUTS]
    blocks = refs[6 + CUTS : 6 + CUTS + group]
    mods = refs[6 + CUTS + group : 6 + CUTS + 2 * group]
    outs = refs[6 + CUTS + 2 * group :]
    (dx1_ref, rows_ref, keep_ref, send_ref, loss_ref) = outs[:5]
    sends = outs[5 : 5 + CUTS]
    weights, mod_s, mask_s, head_s, grad_s, attended_s, acc = outs[5 + CUTS :]
    item = pl.program_id(0)
    grp, seq = place()
    tokens = x0_ref.shape[0]
    half = tokens // 2

    @pl.when(item == 0)
    def _():
        assemble(weights, blocks, grp, 0, D + FF + OUTP + FF)
        total = mods[0][...]
        for m in mods[1:]:
            total = total + m[...]
        mod_s[...] = total
        collect(head_s, heads_in, seq)
        acc[...] = jnp.zeros_like(acc)
        loss_ref[...] = jnp.zeros_like(loss_ref)

    low = half_low((half, 128))
    for j in range(HEADS // 2):
        one = head_s[HEADS * item + 2 * j].astype(F32)
        two = head_s[HEADS * item + 2 * j + 1].astype(F32)
        attended_s[:half, j * 128 : (j + 1) * 128] = jnp.where(low, one, swap_halves(two)).astype(
            BF16
        )
        attended_s[half:, j * 128 : (j + 1) * 128] = jnp.where(low, swap_halves(one), two).astype(
            BF16
        )
    out_w = slice(0, D)
    up_w = slice(D, D + FF)
    head_w = slice(D + FF, D + FF + OUT)
    down_w = slice(D + FF + OUTP, D + FF + OUTP + FF)
    mod = mod_s[pl.ds(interval[item], 1), :]
    gate_a, shift_b, scale_b, gate_b = [mod[:, k * D : (k + 1) * D] for k in range(2, 6)]
    attended = attended_s[...]
    branch_a = nn(attended, weights[:, out_w])
    x1 = x0_ref[...] + gate_a * branch_a
    normed_b, rstd_b = standardize(x1)
    n2 = (normed_b * (1.0 + scale_b) + shift_b).astype(BF16)
    value, slope = gelu_parts(nn(n2, weights[:, up_w]))
    active = value.astype(BF16)
    branch_b = nt(active, weights[:, down_w])
    x2 = x1 + gate_b * branch_b
    final, rstd_f = standardize(x2)
    nf = final.astype(BF16)
    diff = nn(nf, weights[:, head_w]) - fields_ref[0].astype(F32)
    keep, _ = widen_mask(mask_ref, mask_s)
    expand = jnp.where(spread(), 1.0, 0.0).astype(BF16)
    present = nn(jnp.where(keep, 1.0, 0.0).astype(BF16), expand)
    row = iota((tokens, 1), 0) // COLS
    weight = jnp.zeros((tokens, 1), F32)
    weight_grad = jnp.zeros((tokens, 1), F32)
    for r in range(tokens // COLS):
        weight = jnp.where(row == r, wl[item, r], weight)
        weight_grad = jnp.where(row == r, wg[item, r], weight_grad)
    masked = present * diff
    each = jnp.sum(masked * diff, axis=1, keepdims=True) * weight
    loss_ref[...] += jnp.broadcast_to(jnp.sum(each, axis=0, keepdims=True) / PIX, (8, 128))
    dpred = (masked * weight_grad).astype(BF16)

    acc[:, head_w] += tn(nf, dpred)
    dx2 = standardize_back(nt(dpred, weights[:, head_w]), final, rstd_f)
    db2 = (gate_b * dx2).astype(BF16)
    d_gate_b = jnp.sum(dx2 * branch_b, axis=0, keepdims=True)
    acc[:, down_w] += tn(db2, active)
    dh = (nn(db2, weights[:, down_w]) * slope).astype(BF16)
    acc[:, up_w] += tn(n2, dh)
    dn2 = nt(dh, weights[:, up_w])
    d_shift_b = jnp.sum(dn2, axis=0, keepdims=True)
    d_scale_b = jnp.sum(dn2 * normed_b, axis=0, keepdims=True)
    dx1 = dx2 + standardize_back(dn2 * (1.0 + scale_b), normed_b, rstd_b)
    dx1_ref[...] = dx1
    d_gate_a = jnp.sum(dx1 * branch_a, axis=0, keepdims=True)
    db1 = (gate_a * dx1).astype(BF16)
    acc[:, out_w] += tn(attended, db1)
    dout = nt(db1, weights[:, out_w])
    rows_ref[0] = jnp.concatenate(
        [d_gate_a, d_shift_b, d_scale_b, d_gate_b, jnp.zeros((4, D), F32)], axis=0
    )
    for j in range(HEADS // 2):
        pair = dout[:, j * 128 : (j + 1) * 128]
        top, bottom = pair[:half], pair[half:]
        grad_s[HEADS * item + 2 * j] = jnp.where(low, top, swap_halves(bottom)).astype(BF16)
        grad_s[HEADS * item + 2 * j + 1] = jnp.where(low, swap_halves(top), bottom).astype(BF16)

    @pl.when(item == pl.num_programs(0) - 1)
    def _():
        deal(sends, grad_s, seq)
        split_rows(acc, grp, keep_ref, send_ref)


def split_rows(acc, grp, keep_ref, send_ref):
    rows = keep_ref.shape[1]
    for j in range(keep_ref.shape[0]):
        for odd, ref in ((0, keep_ref), (1, send_ref)):
            at = pl.multiple_of(jnp.bitwise_xor(grp, 2 * j + odd) * rows, 16)
            ref[j] = acc[pl.ds(at, rows), :].astype(BF16)


def attend_back(shares, *refs):
    own = refs[:CUTS]
    others = refs[CUTS : CUTS * shares]
    grads = refs[CUTS * shares : CUTS * shares + CUTS]
    kept_ref, lse_ref = refs[CUTS * shares + CUTS : CUTS * shares + CUTS + 2]
    outs = refs[CUTS * shares + CUTS + 2 :]
    dq_ref, own_ref = outs[:2]
    far_refs = outs[2 : 2 + shares - 1]
    keys_s, turned_s, acc = outs[2 + shares - 1 :]
    tokens = kept_ref.shape[2]
    for n, ref in enumerate(own + others):
        keys_s[n * tokens : (n + 1) * tokens, :] = ref[0, :tokens, :]
    keys = keys_s[...]
    turned_s[...] = keys.T
    for m in range(CUTS):
        queries = unpack(own[m][0, tokens:, :], True)
        grad = unpack(grads[m][0], False)
        delta = jnp.sum((grad.astype(F32) * kept_ref[0, m]).T, axis=0, keepdims=True)
        scores = nt(keys, queries) * (SCALE * LOG2E)
        probs = jnp.exp2(scores - lse_ref[0, m, 0:1, :])
        dprobs = nt(keys, grad)
        dscores = (probs * (dprobs - delta)).astype(BF16)
        step = nn(probs.astype(BF16), grad) + nn(dscores, queries)
        if m == 0:
            acc[...] = step
        else:
            acc[...] += step
        dq = nn(turned_s[...], dscores).T * SCALE
        dq_ref[0, m] = pack_rows(dq, True).astype(BF16)
    factor = jnp.where(half_low((1, 128)), SCALE, 1.0)
    for m in range(CUTS):
        own_ref[0, m] = (acc[m * tokens : (m + 1) * tokens, :] * factor).astype(BF16)
        for n, ref in enumerate(far_refs):
            at = ((n + 1) * CUTS + m) * tokens
            ref[0, m] = (acc[at : at + tokens, :] * factor).astype(BF16)


def join_back(shares, *refs):
    dq_ref, own_ref = refs[:2]
    far = refs[2 : 2 + shares - 1]
    outs = refs[2 + shares - 1 :]
    tokens = own_ref.shape[2]
    for m in range(CUTS):
        for r in range(own_ref.shape[0]):
            total = own_ref[r, m].astype(F32)
            for ref in far:
                total = total + ref[r, m].astype(F32)
            outs[m][r, :tokens, :] = total.astype(BF16)
            outs[m][r, tokens:, :] = dq_ref[r, m]


def early_back(group, *refs):
    (interval, x0_ref, n1_ref, dx1_ref, rows_ref, gathered_ref, probs_ref, picked_ref) = refs[:8]
    (fields_ref, mask_ref, fused_ref, agg_ref, embed_ref, probe_ref) = refs[8:14]
    units = refs[14 : 14 + CUTS]
    blocks = refs[14 + CUTS : 14 + CUTS + group]
    mods = refs[14 + CUTS + group : 14 + CUTS + 2 * group]
    outs = refs[14 + CUTS + 2 * group :]
    (keep_ref, send_ref, dmod_ref) = outs[:3]
    qkv_w, mod_s, mask_s, unit_s, dqkv_s, acc, mix, dscore = outs[3:]
    item = pl.program_id(0)
    grp, seq = place()
    tokens = x0_ref.shape[0]
    half = tokens // 2
    qkv_at = 3 * D + OUTP

    @pl.when(item == 0)
    def _():
        assemble(qkv_w, blocks, grp, 0, 3 * D)
        total = mods[0][...]
        for m in mods[1:]:
            total = total + m[...]
        mod_s[...] = total
        collect(unit_s, units, seq)
        acc[...] = jnp.zeros_like(acc)
        mix[...] = jnp.zeros_like(mix)
        dscore[...] = jnp.zeros_like(dscore)
        dmod_ref[...] = jnp.zeros_like(dmod_ref)

    low = half_low((half, 128))
    for h in range(HEADS):
        dqkv_s[:, h * 128 : (h + 1) * 128] = unit_s[HEADS * item + h, :tokens, :]
    for j in range(HEADS // 2):
        one = unit_s[HEADS * item + 2 * j, tokens:, :].astype(F32)
        two = unit_s[HEADS * item + 2 * j + 1, tokens:, :].astype(F32)
        lanes = slice(2 * D + j * 128, 2 * D + (j + 1) * 128)
        dqkv_s[:half, lanes] = jnp.where(low, one, swap_halves(two)).astype(BF16)
        dqkv_s[half:, lanes] = jnp.where(low, swap_halves(one), two).astype(BF16)
    dqkv = dqkv_s[...]
    which = interval[item]
    mod = mod_s[pl.ds(which, 1), :]
    acc[:, qkv_at:] += tn(n1_ref[...], dqkv)
    dn1 = nt(dqkv, qkv_w[...])
    normed, rstd = standardize(x0_ref[...])
    d_shift = jnp.sum(dn1, axis=0, keepdims=True)
    d_scale = jnp.sum(dn1 * normed, axis=0, keepdims=True)
    dx0 = (
        dx1_ref[...] + standardize_back(dn1 * (1.0 + mod[:, D : 2 * D]), normed, rstd)
    ).astype(BF16)
    rows = rows_ref[0]
    for k, row in enumerate([d_shift, d_scale] + [rows[r : r + 1] for r in range(4)]):
        dmod_ref[pl.ds(which, 1), k * D : (k + 1) * D] += row

    acc[:, 2 * D : 3 * D] += tn(gathered_ref[...], dx0)
    dagg = nt(dx0, agg_ref[:, 2 * D :])
    fields = fields_ref[0]
    wide_fields = fields.astype(F32)
    keep, _ = widen_mask(mask_ref, mask_s)
    expand = jnp.where(spread(), 1.0, 0.0).astype(BF16)
    lower = half_low((tokens, 128))
    for j in range(HEADS // 2):
        pair = slice(j * 128, (j + 1) * 128)
        for h in (2 * j, 2 * j + 1):
            mine = lower if h % 2 == 0 else jnp.logical_not(lower)
            dpart = jnp.where(mine, dagg[:, pair], 0.0).astype(BF16)
            mix[pair, :] += tn(dpart, picked_ref[h])
            spreaded = (nn(dpart, fused_ref[pair, :]) * wide_fields).astype(BF16)
            dprobs = nt(spreaded, expand)
            probs = probs_ref[0, :, h * 128 : (h + 1) * 128]
            ds = probs * (dprobs - jnp.sum(probs * dprobs, axis=-1, keepdims=True))
            ds = jnp.where(keep, ds, 0.0).astype(BF16)
            dscore[h] += tn(ds, fields)

    @pl.when(item == pl.num_programs(0) - 1)
    def _():
        lines = iota((128, OUT), 0)
        owned = spread()
        drows = jnp.zeros((128, OUT), F32)
        for h in range(HEADS):
            line = jnp.sum(jnp.where(owned, dscore[h], 0.0), axis=0, keepdims=True) * SCALE
            drows = drows + jnp.where(lines == h, line, 0.0)
        drows = drows.astype(BF16)
        mixed = mix[...].astype(BF16)
        embed = embed_ref[:, :OUT]
        acc[:, 3 * D : 3 * D + OUT] = nn(agg_ref[:, D : 2 * D], mixed) + nn(probe_ref[...], drows)
        acc[:, D : 2 * D] = nt(embed, mixed)
        dprobe = nt(embed, drows)
        heads = jnp.where(iota((128, D), 1) // HEAD == iota((128, D), 0), 1.0, 0.0).astype(BF16)
        coarse = dprobe.astype(BF16)
        fine = (dprobe - coarse.astype(F32)).astype(BF16)
        by_column = nn(coarse, heads) + nn(fine, heads)
        eye = iota((D, D), 0) == iota((D, D), 1)
        query = embed_ref[:, OUT : OUT + 1].astype(F32)
        query_row = jnp.sum(jnp.where(eye, query, 0.0), axis=0, keepdims=True)
        acc[:, :D] = by_column * query_row
        dquery = jnp.sum(agg_ref[:, :D].astype(F32) * by_column, axis=0, keepdims=True)
        column = jnp.sum(jnp.where(eye, dquery, 0.0), axis=1, keepdims=True)
        acc[:, 3 * D + OUT : 3 * D + OUTP] = jnp.where(
            iota((D, OUTP - OUT), 1) == 0, column, 0.0
        )
        split_rows(acc, grp, keep_ref, send_ref)


def sum_cores(keep_ref, got_ref, *outs):
    for j, ref in enumerate(outs):
        ref[...] = (keep_ref[j].astype(F32) + got_ref[j].astype(F32)).astype(BF16)


def cut_granules(parts, *refs):
    sources, outs, table = refs[: -parts - 1], refs[-parts - 1 : -1], refs[-1]
    _, seq = place()
    total = sources[0][...].astype(F32)
    for ref in sources[1:]:
        total = total + ref[...].astype(F32)
    total = total.astype(BF16)
    rows, cols = total.shape
    per = rows // 16
    if table.shape[0] > per * (cols // 128):
        table[...] = jnp.zeros_like(table)
    for t in range(cols // 128):
        for g in range(per):
            table[t * per + g] = total[g * 16 : (g + 1) * 16, t * 128 : (t + 1) * 128]
    size = outs[0].shape[0]
    for j in range(parts):
        outs[j][...] = table[pl.ds(jnp.bitwise_xor(seq, j) * size, size)]


def sum_pieces(*refs):
    sources, (out_ref, square_ref) = refs[:-2], refs[-2:]
    total = sources[0][...].astype(F32)
    for ref in sources[1:]:
        total = total + ref[...].astype(F32)
    out_ref[...] = total.astype(BF16)
    square_ref[...] = jnp.sum(total * total, axis=0)


def all_squares(copies, early_ref, late_ref, loss_ref, lead_ref, dmod_ref, out_ref, dmod_out):
    grp, _ = place()
    rows = dmod_out.shape[0]
    lead = lead_ref[pl.ds(pl.multiple_of(grp * rows, 16), rows), :].astype(F32)
    grad = lead[:, 0:1] * dmod_ref[0:1, :]
    for g in (1, 2):
        grad = grad + lead[:, g : g + 1] * dmod_ref[g : g + 1, :]
    dmod_out[...] = grad
    squares = jnp.sum(early_ref[...] + late_ref[...]) + jnp.sum(grad * grad) / copies
    which = iota((8, 128), 0)
    out_ref[...] = jnp.where(which == 0, loss_ref[...], squares)


def step_values(param, first, second, grad):
    first = beta_first * first + (1.0 - beta_first) * grad
    second = beta_second * second + (1.0 - beta_second) * grad * grad
    mean_hat = first / (1.0 - beta_first**STEP)
    var_hat = second / (1.0 - beta_second**STEP)
    param = param - learn_rate * (
        mean_hat / (jnp.sqrt(var_hat) + adam_epsilon) + decay_rate * param
    )
    return param, first, second, param.astype(BF16)


def optimize(parts, *refs):
    reduced_ref = refs[0]
    early = refs[1 : 1 + parts]
    late = refs[1 + parts : 1 + 2 * parts]
    dmod_ref = refs[1 + 2 * parts]
    wide = refs[2 + 2 * parts : 5 + 2 * parts]
    tall = refs[5 + 2 * parts : 8 + 2 * parts]
    query = refs[8 + 2 * parts : 11 + 2 * parts]
    outs = refs[11 + 2 * parts :]
    norm_ref, wide_out, tall_out, query_out = outs[0], outs[1:5], outs[5:9], outs[9:13]
    early_s, late_s = outs[13:]
    _, seq = place()
    for table, pieces in ((early_s, early), (late_s, late)):
        size = pieces[0].shape[0]
        for j, ref in enumerate(pieces):
            table[pl.ds(jnp.bitwise_xor(seq, j) * size, size)] = ref[...]
    norm = jnp.sqrt(reduced_ref[1:2, 0:1])
    norm_ref[...] = jnp.broadcast_to(norm, norm_ref.shape)
    factor = jnp.minimum(1.0, clip_limit / (norm + 1e-06))
    rows = wide[0].shape[0]
    per = rows // 16

    def tile(table, t):
        return jnp.concatenate(
            [table[t * per + g] for g in range(per)], axis=0
        ).astype(F32)

    def put(ins, targets, at, grad):
        new = step_values(*[r[at] for r in ins], grad * factor)
        for ref, value in zip(targets, new):
            ref[at] = value

    def wide_at(t, width=128):
        return (slice(None), slice(t * 128, t * 128 + width))

    low = half_low((rows, 128))
    for t in range(9):
        put(wide, wide_out, wide_at(t), tile(late_s, t))
    for t in range(18):
        put(wide, wide_out, wide_at(9 + t), dmod_ref[:, t * 128 : (t + 1) * 128])
    qkv = 18
    for j in range(3):
        put(wide, wide_out, wide_at(27 + j), tile(late_s, qkv + 6 + j))
        one, two = tile(late_s, qkv + 2 * j), tile(late_s, qkv + 2 * j + 1)
        put(wide, wide_out, wide_at(30 + j), jnp.where(low, one, swap_halves(two)))
        put(wide, wide_out, wide_at(33 + j), jnp.where(low, swap_halves(one), two))
    for t in range(15 + 8):
        put(wide, wide_out, wide_at(36 + t), tile(early_s, t))
    rest = OUT - 8 * 128
    put(wide, wide_out, wide_at(59, rest), tile(early_s, 23)[:, :rest])
    for t in range(9):
        grad = tile(late_s, 9 + t).T
        if t < 8:
            put(tall, tall_out, (slice(t * 128, (t + 1) * 128), slice(None)), grad)
        else:
            put(tall, tall_out, (slice(t * 128, OUT), slice(None)), grad[:rest])
            put(query, query_out, (slice(None), slice(None)), grad[rest : rest + 1])
    for t in range(FF // 128):
        at = OUT + t * 128
        put(tall, tall_out, (slice(at, at + 128), slice(None)), tile(early_s, 24 + t).T)


def shift(value, axis, bit):
    size = lax.axis_size(axis)
    return lax.ppermute(value, axis, [(i, i ^ bit) for i in range(size)])


def gather_blocks(own, group):
    blocks = {0: own}
    for j in range(2, group, 2):
        blocks[j] = shift(own, "grp", j)
    for j in range(0, group, 2):
        blocks[j + 1] = shift(blocks[j], "grp", 1)
    return [blocks[j] for j in range(group)]


def reduce_granules(keep, send, group, parts):
    _, rows, cols = keep.shape
    got = shift(send, "grp", 1)
    halves = call(sum_cores, [sds((rows, cols), BF16)] * (group // 2))(keep, got)
    sums = [halves[0]] + [shift(halves[j], "grp", 2 * j) for j in range(1, group // 2)]
    count = (rows // 16) * (cols // 128)
    size = -(-count // parts)
    pieces = call(
        functools.partial(cut_granules, parts),
        [sds((size, 16, 128), BF16)] * parts,
        scratch=[pltpu.VMEM((size * parts, 16, 128), BF16)],
    )(*sums)
    pieces = [pieces[0]] + [shift(pieces[j], "seq", j) for j in range(1, parts)]
    return call(sum_pieces, [sds((size, 16, 128), BF16), sds((16, 128), F32)])(*pieces)


def gather_pieces(piece, parts):
    return [piece] + [shift(piece, "seq", j) for j in range(1, parts)]


def butterfly(value, axes):
    for axis in axes:
        bit = 1
        while bit < lax.axis_size(axis):
            value = value + shift(value, axis, bit)
            bit *= 2
    return value


def lead_features(interval, width):
    hours = 6.0 * jnp.exp2(interval.astype(F32))
    half = width // 2
    freqs = jnp.exp(-jnp.log(1000.0) * jnp.arange(half, dtype=F32) / half)
    angles = hours[:, None] * freqs[None, :]
    return jax.nn.silu(jnp.concatenate([jnp.sin(angles), jnp.cos(angles)], axis=-1))


def per_device(
    fields,
    targets,
    land_mask,
    interval,
    samples,
    wide_weights,
    wide_firsts,
    wide_seconds,
    tall_weights,
    tall_firsts,
    tall_seconds,
    query_vector,
    query_firsts,
    query_seconds,
):
    group = lax.axis_size("grp")
    parts = lax.axis_size("seq")
    shares = parts // CUTS
    rows, columns = wide_weights.shape
    items, tokens = fields.shape[:2]
    units = items * HEADS // CUTS
    every = items * tokens
    late_cols = D + FF + OUTP + FF

    query_row = query_vector.reshape(1, rows)
    lead = lead_features(jnp.arange(3, dtype=jnp.int32), D).astype(BF16)
    lead_columns = jnp.zeros((D, 128), BF16).at[:, :3].set(lead.T)

    first_own = call(
        pack_first,
        sds((rows, 3 * D + OUTP), BF16),
        grid=(1,),
        in_specs=[
            pl.BlockSpec((rows, 3 * D), lambda i: (0, 0)),
            pl.BlockSpec((OUT, rows), lambda i: (0, 0)),
            pl.BlockSpec((1, rows), lambda i: (0, 0)),
        ],
        out_specs=pl.BlockSpec((rows, 3 * D + OUTP), lambda i: (0, 0)),
    )(wide_weights, tall_weights, query_row)
    first = gather_blocks(first_own, group)
    qkv_own, late_own, mod_own = call(
        pack_rest,
        [
            sds((rows, 3 * D), BF16),
            sds((rows, late_cols), BF16),
            sds((8, 6 * D), F32),
        ],
    )(wide_weights, tall_weights, lead_columns)
    qkv_blocks = gather_blocks(qkv_own, group)
    mods = gather_blocks(mod_own, group)
    late_blocks = gather_blocks(late_own, group)

    lines = tokens // COLS
    line = lax.axis_index("seq") * lines + jnp.arange(lines)
    latitude = jnp.pi * ((line.astype(F32) + 0.5) / (lines * parts) - 0.5)
    weight_lines = samples.astype(F32)[:, None] * jnp.cos(latitude)[None, :]
    present = jnp.sum(land_mask.reshape(items, lines, COLS * VARS), axis=-1).astype(F32)
    weight_sum = butterfly(
        jnp.broadcast_to(jnp.sum(weight_lines * present), (8, 128)), ("grp", "seq")
    )[0, 0]
    weight_grads = weight_lines * (2.0 / PIX) / weight_sum

    agg_weights, embed, score_w, fused_w, probe = call(
        prepare,
        [
            sds((D, 3 * D), BF16),
            sds((D, OUTP), BF16),
            sds((HEADS * 128, OUT), BF16),
            sds((D, OUT), BF16),
            sds((D, 128), BF16),
        ],
    )(*first)

    by_item = pl.BlockSpec((tokens, D), lambda i: (i, 0))

    def item_block(width):
        return pl.BlockSpec((1, tokens, width), lambda i: (i, 0, 0))

    heads_spec = pl.BlockSpec((HEADS, tokens, OUT), lambda i: (0, i, 0))
    packed = tokens + tokens // 2

    results = call(
        functools.partial(aggregate, group),
        [
            sds((items, tokens, HEADS * 128), F32),
            sds((HEADS, every, OUT), BF16),
            sds((every, D), BF16),
            sds((every, D), F32),
            sds((every, D), BF16),
        ]
        + [sds((units, packed, 128), BF16)] * CUTS,
        grid=(items,),
        in_specs=[smem(), item_block(OUT), item_block(VARS)] + [whole()] * (3 + 2 * group),
        out_specs=[item_block(HEADS * 128), heads_spec, by_item, by_item, by_item]
        + [whole()] * CUTS,
        scratch=[
            pltpu.VMEM((D, 3 * D), BF16),
            pltpu.VMEM((8, 6 * D), F32),
            pltpu.VMEM((tokens, 128), jnp.int32),
            pltpu.VMEM((items * HEADS, packed, 128), BF16),
        ],
    )(interval, fields, land_mask, score_w, fused_w, agg_weights, *qkv_blocks, *mods)
    probs, picked, gathered, x0, n1 = results[:5]
    dealt = results[5:]

    own = [dealt[0]] + [shift(dealt[m], "seq", m * shares) for m in range(1, CUTS)]
    others = [shift(own[m], "seq", n) for n in range(1, shares) for m in range(CUTS)]
    keys_total = parts * tokens

    unit_in = pl.BlockSpec((1, packed, 128), lambda u: (u, 0, 0))
    half_in = pl.BlockSpec((1, tokens // 2, 128), lambda u: (u, 0, 0))
    kept_spec = pl.BlockSpec((1, CUTS, tokens, 128), lambda u: (u, 0, 0, 0))
    lse_spec = pl.BlockSpec((1, CUTS, 8, tokens), lambda u: (u, 0, 0, 0))
    pack_spec = pl.BlockSpec((1, CUTS, tokens // 2, 128), lambda u: (u, 0, 0, 0))
    half_out = sds((units, tokens // 2, 128), BF16)
    results = call(
        functools.partial(attend, shares),
        [half_out] * CUTS
        + [sds((units, CUTS, tokens, 128), F32), sds((units, CUTS, 8, tokens), F32)],
        grid=(units,),
        in_specs=[unit_in] * (CUTS * shares),
        out_specs=[half_in] * CUTS + [kept_spec, lse_spec],
        scratch=[pltpu.VMEM((keys_total, 128), BF16), pltpu.VMEM((128, keys_total), BF16)],
    )(*own, *others)
    backs, kept, lse = results[:CUTS], results[CUTS], results[CUTS + 1]
    heads_in = [backs[0]] + [shift(backs[m], "seq", m * shares) for m in range(1, CUTS)]

    results = call(
        functools.partial(middle, group),
        [
            sds((every, D), F32),
            sds((items, 8, D), F32),
            sds((group // 2, rows, late_cols), BF16),
            sds((group // 2, rows, late_cols), BF16),
            sds((8, 128), F32),
        ]
        + [half_out] * CUTS,
        grid=(items,),
        in_specs=[smem(), smem(), smem(), by_item, item_block(OUT), item_block(VARS)]
        + [whole()] * (CUTS + 2 * group),
        out_specs=[by_item, pl.BlockSpec((1, 8, D), lambda i: (i, 0, 0))] + [whole()] * (3 + CUTS),
        scratch=[
            pltpu.VMEM((D, late_cols), BF16),
            pltpu.VMEM((8, 6 * D), F32),
            pltpu.VMEM((tokens, 128), jnp.int32),
            pltpu.VMEM((items * HEADS, tokens // 2, 128), BF16),
            pltpu.VMEM((items * HEADS, tokens // 2, 128), BF16),
            pltpu.VMEM((tokens, D), BF16),
            pltpu.VMEM((D, late_cols), F32),
        ],
    )(
        interval,
        weight_lines,
        weight_grads,
        x0,
        targets,
        land_mask,
        *heads_in,
        *late_blocks,
        *mods,
    )
    dx1, mod_rows, early_keep, early_send, loss = results[:5]
    sends = results[5:]
    grads_in = [sends[0]] + [shift(sends[m], "seq", m * shares) for m in range(1, CUTS)]

    early_piece, early_squares = reduce_granules(early_keep, early_send, group, parts)

    results = call(
        functools.partial(attend_back, shares),
        [sds((units, CUTS, tokens // 2, 128), BF16)]
        + [sds((units, CUTS, tokens, 128), BF16)] * shares,
        grid=(units,),
        in_specs=[unit_in] * (CUTS * shares) + [half_in] * CUTS + [kept_spec, lse_spec],
        out_specs=[pack_spec] + [kept_spec] * shares,
        scratch=[
            pltpu.VMEM((keys_total, 128), BF16),
            pltpu.VMEM((128, keys_total), BF16),
            pltpu.VMEM((keys_total, 128), F32),
        ],
    )(*own, *others, *grads_in, kept, lse)
    dq, near, far = results[0], results[1], results[2:]
    far = [shift(far[n], "seq", n + 1) for n in range(shares - 1)]
    dealt = call(
        functools.partial(join_back, shares), [sds((units, packed, 128), BF16)] * CUTS
    )(dq, near, *far)
    units_in = [dealt[0]] + [shift(dealt[m], "seq", m * shares) for m in range(1, CUTS)]

    first_cols = 3 * D + OUTP + 3 * D
    late_keep, late_send, dmod = call(
        functools.partial(early_back, group),
        [
            sds((group // 2, rows, first_cols), BF16),
            sds((group // 2, rows, first_cols), BF16),
            sds((8, 6 * D), F32),
        ],
        grid=(items,),
        in_specs=[
            smem(),
            by_item,
            by_item,
            by_item,
            pl.BlockSpec((1, 8, D), lambda i: (i, 0, 0)),
            by_item,
            item_block(HEADS * 128),
            heads_spec,
            item_block(OUT),
            item_block(VARS),
        ]
        + [whole()] * (4 + CUTS + 2 * group),
        out_specs=[whole()] * 3,
        scratch=[
            pltpu.VMEM((D, 3 * D), BF16),
            pltpu.VMEM((8, 6 * D), F32),
            pltpu.VMEM((tokens, 128), jnp.int32),
            pltpu.VMEM((items * HEADS, packed, 128), BF16),
            pltpu.VMEM((tokens, 3 * D), BF16),
            pltpu.VMEM((D, first_cols), F32),
            pltpu.VMEM((D, OUT), F32),
            pltpu.VMEM((HEADS, 128, OUT), F32),
        ],
    )(
        interval,
        x0,
        n1,
        dx1,
        mod_rows,
        gathered,
        probs,
        picked,
        fields,
        land_mask,
        fused_w,
        agg_weights,
        embed,
        probe,
        *units_in,
        *qkv_blocks,
        *mods,
    )
    late_piece, late_squares = reduce_granules(late_keep, late_send, group, parts)
    dmod = butterfly(dmod, ("grp", "seq"))
    reduced, grad_modulation = call(
        functools.partial(all_squares, parts),
        [sds((8, 128), F32), sds((rows, 6 * D), F32)],
    )(early_squares, late_squares, loss, lead_columns, dmod)
    reduced = butterfly(reduced, ("grp", "seq"))
    early_all = gather_pieces(early_piece, parts)
    late_all = gather_pieces(late_piece, parts)

    def like(x, dtype=F32):
        return sds(x.shape, dtype)

    results = call(
        functools.partial(optimize, parts),
        [sds((8, 128), F32)]
        + [like(wide_weights)] * 3
        + [like(wide_weights, BF16)]
        + [like(tall_weights)] * 3
        + [like(tall_weights, BF16)]
        + [like(query_row)] * 3
        + [like(query_row, BF16)],
        scratch=[
            pltpu.VMEM((parts * early_piece.shape[0], 16, 128), BF16),
            pltpu.VMEM((parts * late_piece.shape[0], 16, 128), BF16),
        ],
    )(
        reduced,
        *early_all,
        *late_all,
        grad_modulation,
        wide_weights,
        wide_firsts,
        wide_seconds,
        tall_weights,
        tall_firsts,
        tall_seconds,
        query_row,
        query_firsts.reshape(1, rows),
        query_seconds.reshape(1, rows),
    )
    norm = results[0]
    query_out = tuple(r.reshape(rows) for r in results[9:13])
    return (reduced[0, 0], weight_sum, norm[0, 0]) + tuple(results[1:9]) + query_out


def solution(mesh):
    placed = (
        P("grp", "seq", None),
        P("grp", "seq", None),
        P("grp", "seq", None),
        P("grp"),
        P("grp"),
        P("grp", None),
        P("grp", None),
        P("grp", None),
        P(None, "grp"),
        P(None, "grp"),
        P(None, "grp"),
        P("grp"),
        P("grp"),
        P("grp"),
    )
    return jax.shard_map(
        per_device,
        mesh=mesh,
        in_specs=placed,
        out_specs=(
            P(),
            P(),
            P(),
            P("grp", None),
            P("grp", None),
            P("grp", None),
            P("grp", None),
            P(None, "grp"),
            P(None, "grp"),
            P(None, "grp"),
            P(None, "grp"),
            P("grp"),
            P("grp"),
            P("grp"),
            P("grp"),
        ),
        check_vma=False,
    )
```

```python
import functools

import jax
import numpy as np
import jax.numpy as jnp
from jax import lax
from jax.experimental import pallas as pl
from jax.experimental.pallas import tpu as pltpu
from jax.sharding import PartitionSpec as P

D = 384
HEADS = 6
HEAD = 64
FF = 1536
VARS = 69
PIX = 16
OUT = VARS * PIX
OUTP = 1152
COLS = 128
STEP = 5
CUTS = 4
SCALE = HEAD**-0.5
LOG2E = 1.4426950408889634

beta_first = 0.5
beta_second = 0.5
learn_rate = 0.1
decay_rate = 0.01
adam_epsilon = 1e-08
clip_limit = 0.05
norm_epsilon = 1e-06
masked_score = -1e30

F32 = jnp.float32
BF16 = jnp.bfloat16
LIMIT = 50 * 1024 * 1024


def dot(left, right, a, b):
    return lax.dot_general(left, right, (((a,), (b,)), ((), ())), preferred_element_type=F32)


def nn(left, right):
    return dot(left, right, 1, 0)


def nt(left, right):
    return dot(left, right, 1, 1)


def tn(left, right):
    return dot(left, right, 0, 0)


def iota(shape, dim):
    return lax.broadcasted_iota(jnp.int32, shape, dim)


def half_low(shape):
    return iota(shape, len(shape) - 1) < HEAD


def swap_halves(tile):
    return pltpu.roll(tile, HEAD, 1)


def spread():
    return iota((128, OUT), 1) // PIX == iota((128, OUT), 0)


def place():
    grp = lax.axis_index("grp")
    seq = lax.axis_index("seq")
    return grp, seq


def call(kernel, outs, grid=(), in_specs=None, out_specs=None, scratch=(), us=1, limit=LIMIT):
    kw = {}
    if in_specs is not None:
        kw["in_specs"] = in_specs
    if out_specs is not None:
        kw["out_specs"] = out_specs
    return pl.pallas_call(
        kernel,
        out_shape=outs,
        grid=grid,
        scratch_shapes=list(scratch),
        cost_estimate=pl.CostEstimate(
            flops=int(us * 1.15e9), transcendentals=0, bytes_accessed=1024
        ),
        compiler_params=pltpu.CompilerParams(vmem_limit_bytes=limit),
        **kw,
    )


def whole():
    return pl.BlockSpec(memory_space=pltpu.VMEM)


def anywhere():
    return pl.BlockSpec(memory_space=pl.ANY)


def smem():
    return pl.BlockSpec(memory_space=pltpu.SMEM)


def sds(shape, dtype):
    return jax.ShapeDtypeStruct(shape, dtype)


def standardize(x):
    centered = x - jnp.mean(x, axis=-1, keepdims=True)
    rstd = lax.rsqrt(jnp.mean(centered * centered, axis=-1, keepdims=True) + norm_epsilon)
    return centered * rstd, rstd


def standardize_back(grad, normed, rstd):
    return rstd * (
        grad
        - jnp.mean(grad, axis=-1, keepdims=True)
        - normed * jnp.mean(grad * normed, axis=-1, keepdims=True)
    )


def gelu_parts(x):
    k = 0.7978845608028654
    inner = k * (x + 0.044715 * x * x * x)
    t = jnp.tanh(inner)
    value = 0.5 * x * (1.0 + t)
    slope = 0.5 * (1.0 + t) + 0.5 * x * (1.0 - t * t) * k * (1.0 + 3 * 0.044715 * x * x)
    return value, slope


def pack_first(wide_ref, tall_ref, query_ref, out_ref):
    rows = wide_ref.shape[0]
    out_ref[:, : 3 * D] = wide_ref[...].astype(BF16)
    eye = iota((rows, rows), 0) == iota((rows, rows), 1)
    column = jnp.sum(jnp.where(eye, query_ref[...], 0.0), axis=1, keepdims=True)
    lane = iota((rows, OUTP), 1)
    embed = jnp.where(lane < OUT, tall_ref[...], jnp.where(lane == OUT, column, 0.0))
    out_ref[:, 3 * D :] = embed.astype(BF16)


def pack_qkv(wl, mod_a, mod_b, wide_ref, lead_ref, mask_ref, qkv_ref, mod_ref):
    rows = wide_ref.shape[0]
    grp, _ = place()
    low = half_low((rows, 128))
    for j in range(HEADS // 2):
        k = wide_ref[:, D + j * 128 : D + (j + 1) * 128]
        v = wide_ref[:, 2 * D + j * 128 : 2 * D + (j + 1) * 128]
        qkv_ref[:, (2 * j) * 128 : (2 * j + 1) * 128] = jnp.where(low, k, swap_halves(v)).astype(
            BF16
        )
        qkv_ref[:, (2 * j + 1) * 128 : (2 * j + 2) * 128] = jnp.where(
            low, swap_halves(k), v
        ).astype(BF16)
    qkv_ref[:, 2 * D :] = wide_ref[:, :D].astype(BF16)
    lead = lead_ref[pl.ds(pl.multiple_of(grp * rows, 16), rows), :].astype(F32)
    mod_ref[...] = jnp.zeros_like(mod_ref)
    for at, ref in ((0, mod_a), (3 * D, mod_b)):
        mod = ref[...].astype(BF16).astype(F32)
        for g in range(3):
            mod_ref[g : g + 1, at : at + 3 * D] = jnp.sum(
                lead[:, g : g + 1] * mod, axis=0, keepdims=True
            )
    items, tokens, _ = mask_ref.shape
    total = jnp.zeros((1, 1), F32)
    for i in range(items):
        for r in range(tokens // COLS):
            present = mask_ref[i, r * COLS : (r + 1) * COLS, :].astype(F32)
            total = total + wl[i, r] * jnp.sum(
                jnp.sum(present, axis=0, keepdims=True), axis=1, keepdims=True
            )
    mod_ref[3:4, :] = jnp.broadcast_to(total, (1, mod_ref.shape[1]))


def pack_late(wide_a, wide_b, wide_c, tall_ref, _, late_ref):
    rows = wide_a.shape[0]
    late_ref[:, : 3 * D] = wide_a[...].astype(BF16)
    late_ref[:, 3 * D : 6 * D] = wide_b[...].astype(BF16)
    rest = D + FF + OUT - 6 * D
    late_ref[:, 6 * D : D + FF + OUT] = wide_c[:, :rest].astype(BF16)
    late_ref[:, D + FF + OUT : D + FF + OUTP] = jnp.zeros((rows, OUTP - OUT), BF16)
    late_ref[:, D + FF + OUTP :] = tall_ref[:, OUT:].astype(BF16)


def assemble(target, blocks, grp, lo, hi):
    for j, ref in enumerate(blocks):
        rows = ref.shape[0]
        at = pl.multiple_of(jnp.bitwise_xor(grp, j) * rows, 16)
        target[pl.ds(at, rows), :] = ref[:, lo:hi]


def prepare(*refs):
    blocks, (agg_ref, embed_ref, score_ref, fused_ref, probe_ref) = refs[:-5], refs[-5:]
    grp, _ = place()
    assemble(agg_ref, blocks, grp, 0, 3 * D)
    assemble(embed_ref, blocks, grp, 3 * D, 3 * D + OUTP)
    query = embed_ref[:, OUT : OUT + 1].astype(F32)
    picked = jnp.where(iota((D, 128), 1) == iota((D, 128), 0) // HEAD, query, 0.0).astype(BF16)
    probe = nn(agg_ref[:, :D], picked).astype(BF16)
    probe_ref[...] = probe
    embed = embed_ref[:, :OUT]
    rows = tn(probe, embed) * SCALE
    mine = spread()
    for h in range(HEADS):
        score_ref[h * 128 : (h + 1) * 128, :] = jnp.where(mine, rows[h : h + 1, :], 0.0).astype(
            BF16
        )
    fused_ref[...] = tn(agg_ref[:, D : 2 * D], embed).astype(BF16)


def widen_mask(mask_ref, scratch):
    scratch[...] = jnp.full(scratch.shape, -1, jnp.int32)
    scratch[:, :VARS] = mask_ref[0]
    value = scratch[...]
    return value > 0, value < 0


def aggregate(group, *refs):
    (interval, fields_ref, mask_ref, score_ref, fused_ref, agg_ref) = refs[:6]
    blocks = refs[6 : 6 + group]
    mods = refs[6 + group : 6 + 2 * group]
    outs = refs[6 + 2 * group :]
    (probs_ref, picked_ref, gathered_ref, x0_ref, n1_ref) = outs[:5]
    units = outs[5 : 5 + CUTS]
    qkv_w, mod_s, mask_s, unit_s = outs[5 + CUTS :]
    item = pl.program_id(0)
    grp, seq = place()
    tokens = fields_ref.shape[1]

    @pl.when(item == 0)
    def _():
        assemble(qkv_w, blocks, grp, 0, 3 * D)
        total = mods[0][...]
        for m in mods[1:]:
            total = total + m[...]
        mod_s[...] = total

    fields = fields_ref[0]
    wide_fields = fields.astype(F32)
    keep, pad = widen_mask(mask_ref, mask_s)
    scores = nt(fields, score_ref[...])
    expand = jnp.where(spread(), 1.0, 0.0).astype(BF16)
    low = half_low((tokens, 128))
    for j in range(HEADS // 2):
        pair = []
        for h in (2 * j, 2 * j + 1):
            s = jnp.where(
                keep, scores[:, h * 128 : (h + 1) * 128], jnp.where(pad, -3e38, masked_score)
            )
            e = jnp.exp(s - jnp.max(s, axis=-1, keepdims=True))
            a = e / jnp.sum(e, axis=-1, keepdims=True)
            probs_ref[0, :, h * 128 : (h + 1) * 128] = a
            picked = (nn(a.astype(BF16), expand) * wide_fields).astype(BF16)
            picked_ref[h] = picked
            pair.append(nt(picked, fused_ref[j * 128 : (j + 1) * 128, :]))
        gathered_ref[:, j * 128 : (j + 1) * 128] = jnp.where(low, pair[0], pair[1]).astype(BF16)
    x0 = nn(gathered_ref[...], agg_ref[:, 2 * D :])
    x0_ref[...] = x0
    mod = mod_s[pl.ds(interval[item], 1), :]
    normed, _ = standardize(x0)
    n1 = (normed * (1.0 + mod[:, D : 2 * D]) + mod[:, :D]).astype(BF16)
    n1_ref[...] = n1
    qkv = nn(n1, qkv_w[...])
    half = tokens // 2
    low = half_low((half, 128))
    packed = tokens + half
    for h in range(HEADS):
        unit_s[HEADS * item + h, :tokens, :] = qkv[:, h * 128 : (h + 1) * 128].astype(BF16)
    for j in range(HEADS // 2):
        pair = qkv[:, 2 * D + j * 128 : 2 * D + (j + 1) * 128] * (SCALE * LOG2E)
        top, bottom = pair[:half], pair[half:]
        unit_s[HEADS * item + 2 * j, tokens:packed, :] = jnp.where(
            low, top, swap_halves(bottom)
        ).astype(BF16)
        unit_s[HEADS * item + 2 * j + 1, tokens:packed, :] = jnp.where(
            low, swap_halves(top), bottom
        ).astype(BF16)

    @pl.when(item == pl.num_programs(0) - 1)
    def _():
        value = jnp.broadcast_to(mod_s[3:4, :128], (16, 128))
        high = value.astype(BF16)
        value = value - high.astype(F32)
        middle_part = value.astype(BF16)
        low_part = (value - middle_part.astype(F32)).astype(BF16)
        lane = iota((16, 128), 1)
        zero = jnp.zeros((16, 128), BF16)
        rides = jnp.where(
            lane < 32,
            high.astype(F32),
            jnp.where(
                lane < 64,
                middle_part.astype(F32),
                jnp.where(lane < 96, low_part.astype(F32), 0.0),
            ),
        ).astype(BF16)
        for u in range(unit_s.shape[0]):
            unit_s[u, packed:, :] = rides if u < CUTS else zero
        deal(units, unit_s, seq)


def deal(targets, source, seq):
    a = seq // (lax.axis_size("seq") // CUTS)
    for m in range(CUTS):
        for r in range(targets[m].shape[0]):
            targets[m][r] = source[CUTS * r + jnp.bitwise_xor(a, m)]


def collect(target, sources, seq):
    a = seq // (lax.axis_size("seq") // CUTS)
    for m in range(CUTS):
        for r in range(sources[m].shape[0]):
            target[CUTS * r + jnp.bitwise_xor(a, m)] = sources[m][r]


def unpack(pack, at_low):
    wide = pack.astype(F32)
    low = half_low(wide.shape)
    if at_low:
        both = [jnp.where(low, wide, 0.0), jnp.where(low, swap_halves(wide), 0.0)]
    else:
        both = [jnp.where(low, 0.0, swap_halves(wide)), jnp.where(low, 0.0, wide)]
    return jnp.concatenate(both, axis=0).astype(BF16)


def pack_rows(tile, at_low):
    half = tile.shape[0] // 2
    top, bottom = tile[:half], tile[half:]
    low = half_low(top.shape)
    if at_low:
        return jnp.where(low, top, swap_halves(bottom))
    return jnp.where(low, swap_halves(top), bottom)


def attend(shares, *refs):
    own = refs[:CUTS]
    others = refs[CUTS : CUTS * shares]
    backs = refs[CUTS * shares : CUTS * shares + CUTS]
    kept_ref, lse_ref, weight_ref, keys_s, turned_s = refs[CUTS * shares + CUTS :]
    tokens = kept_ref.shape[2]
    packed = tokens + tokens // 2

    @pl.when(pl.program_id(0) == 0)
    def _():
        total = jnp.zeros((16, 128), F32)
        for ref in own + others:
            total = total + ref[0, packed:, :].astype(F32)
        total = jnp.sum(total[0:8], axis=1, keepdims=True) / 32.0
        weight_ref[...] = jnp.broadcast_to(total, (8, 128))

    for n, ref in enumerate(own + others):
        keys_s[n * tokens : (n + 1) * tokens, :] = ref[0, :tokens, :]
    keys = keys_s[...]
    turned = keys.T
    turned_s[...] = jnp.where(iota(turned.shape, 0) < HEAD, jnp.ones_like(turned), turned)
    for m in range(CUTS):
        queries = unpack(own[m][0, tokens:packed, :], True)
        scores = nt(keys, queries)
        top = jnp.max(scores, axis=0, keepdims=True)
        probs = jnp.exp2(scores - top).astype(BF16)
        out = nn(turned_s[...], probs)
        total = out[0:1, :]
        out = out / total
        lse_ref[0, m] = jnp.broadcast_to(top + jnp.log2(total), (8, tokens))
        out = out.T
        kept_ref[0, m] = out
        backs[m][0] = pack_rows(out, False).astype(BF16)


def middle(group, *refs):
    (interval, wl, sum_ref, x0_ref, fields_ref, mask_ref) = refs[:6]
    heads_in = refs[6 : 6 + CUTS]
    blocks = refs[6 + CUTS : 6 + CUTS + group]
    mods = refs[6 + CUTS + group : 6 + CUTS + 2 * group]
    outs = refs[6 + CUTS + 2 * group :]
    (dx1_ref, rows_ref, keep_ref, send_ref, loss_ref) = outs[:5]
    sends = outs[5 : 5 + CUTS]
    weights, mod_s, mask_s, head_s, grad_s, attended_s, acc = outs[5 + CUTS :]
    item = pl.program_id(0)
    grp, seq = place()
    tokens = x0_ref.shape[0]
    half = tokens // 2

    @pl.when(item == 0)
    def _():
        assemble(weights, blocks, grp, 0, D + FF + OUTP + FF)
        total = mods[0][...]
        for m in mods[1:]:
            total = total + m[...]
        mod_s[...] = total
        collect(head_s, heads_in, seq)
        acc[...] = jnp.zeros_like(acc)
        loss_ref[...] = jnp.zeros_like(loss_ref)

    low = half_low((half, 128))
    for j in range(HEADS // 2):
        one = head_s[HEADS * item + 2 * j].astype(F32)
        two = head_s[HEADS * item + 2 * j + 1].astype(F32)
        attended_s[:half, j * 128 : (j + 1) * 128] = jnp.where(low, one, swap_halves(two)).astype(
            BF16
        )
        attended_s[half:, j * 128 : (j + 1) * 128] = jnp.where(low, swap_halves(one), two).astype(
            BF16
        )
    out_w = slice(0, D)
    up_w = slice(D, D + FF)
    head_w = slice(D + FF, D + FF + OUT)
    down_w = slice(D + FF + OUTP, D + FF + OUTP + FF)
    mod = mod_s[pl.ds(interval[item], 1), :]
    gate_a, shift_b, scale_b, gate_b = [mod[:, k * D : (k + 1) * D] for k in range(2, 6)]
    attended = attended_s[...]
    branch_a = nn(attended, weights[:, out_w])
    x1 = x0_ref[...] + gate_a * branch_a
    normed_b, rstd_b = standardize(x1)
    n2 = (normed_b * (1.0 + scale_b) + shift_b).astype(BF16)
    value, slope = gelu_parts(nn(n2, weights[:, up_w]))
    active = value.astype(BF16)
    branch_b = nt(active, weights[:, down_w])
    x2 = x1 + gate_b * branch_b
    final, rstd_f = standardize(x2)
    nf = final.astype(BF16)
    diff = nn(nf, weights[:, head_w]) - fields_ref[0].astype(F32)
    keep, _ = widen_mask(mask_ref, mask_s)
    expand = jnp.where(spread(), 1.0, 0.0).astype(BF16)
    present = nn(jnp.where(keep, 1.0, 0.0).astype(BF16), expand)
    row = iota((tokens, 1), 0) // COLS
    weight = jnp.zeros((tokens, 1), F32)
    for r in range(tokens // COLS):
        weight = jnp.where(row == r, wl[item, r], weight)
    weight_grad = weight * (2.0 / PIX) / sum_ref[0:1, 0:1]
    masked = present * diff
    each = jnp.sum(masked * diff, axis=1, keepdims=True) * weight
    loss_ref[...] += jnp.broadcast_to(jnp.sum(each, axis=0, keepdims=True) / PIX, (8, 128))
    dpred = (masked * weight_grad).astype(BF16)

    acc[:, head_w] += tn(nf, dpred)
    dx2 = standardize_back(nt(dpred, weights[:, head_w]), final, rstd_f)
    db2 = (gate_b * dx2).astype(BF16)
    d_gate_b = jnp.sum(dx2 * branch_b, axis=0, keepdims=True)
    acc[:, down_w] += tn(db2, active)
    dh = (nn(db2, weights[:, down_w]) * slope).astype(BF16)
    acc[:, up_w] += tn(n2, dh)
    dn2 = nt(dh, weights[:, up_w])
    d_shift_b = jnp.sum(dn2, axis=0, keepdims=True)
    d_scale_b = jnp.sum(dn2 * normed_b, axis=0, keepdims=True)
    dx1 = dx2 + standardize_back(dn2 * (1.0 + scale_b), normed_b, rstd_b)
    dx1_ref[...] = dx1
    d_gate_a = jnp.sum(dx1 * branch_a, axis=0, keepdims=True)
    db1 = (gate_a * dx1).astype(BF16)
    acc[:, out_w] += tn(attended, db1)
    dout = nt(db1, weights[:, out_w])
    rows_ref[0] = jnp.concatenate(
        [d_gate_a, d_shift_b, d_scale_b, d_gate_b, jnp.zeros((4, D), F32)], axis=0
    )
    for j in range(HEADS // 2):
        pair = dout[:, j * 128 : (j + 1) * 128]
        top, bottom = pair[:half], pair[half:]
        grad_s[HEADS * item + 2 * j] = jnp.where(low, top, swap_halves(bottom)).astype(BF16)
        grad_s[HEADS * item + 2 * j + 1] = jnp.where(low, swap_halves(top), bottom).astype(BF16)

    @pl.when(item == pl.num_programs(0) - 1)
    def _():
        deal(sends, grad_s, seq)
        split_rows(acc, grp, keep_ref, send_ref)


def split_rows(acc, grp, keep_ref, send_ref):
    rows = keep_ref.shape[1]
    for j in range(keep_ref.shape[0]):
        for odd, ref in ((0, keep_ref), (1, send_ref)):
            at = pl.multiple_of(jnp.bitwise_xor(grp, 2 * j + odd) * rows, 16)
            ref[j, :, : acc.shape[1]] = acc[pl.ds(at, rows), :].astype(BF16)


def attend_back(shares, *refs):
    own = refs[:CUTS]
    others = refs[CUTS : CUTS * shares]
    grads = refs[CUTS * shares : CUTS * shares + CUTS]
    kept_ref, lse_ref = refs[CUTS * shares + CUTS : CUTS * shares + CUTS + 2]
    outs = refs[CUTS * shares + CUTS + 2 :]
    outs = outs[1:]
    dq_ref, own_ref = outs[:2]
    far_refs = outs[2 : 2 + shares - 1]
    keys_s, turned_s, acc = outs[2 + shares - 1 :]
    tokens = kept_ref.shape[2]
    for n, ref in enumerate(own + others):
        keys_s[n * tokens : (n + 1) * tokens, :] = ref[0, :tokens, :]
    keys = keys_s[...]
    turned_s[...] = keys.T
    for m in range(CUTS):
        queries = unpack(own[m][0, tokens : tokens + tokens // 2, :], True)
        grad = unpack(grads[m][0], False)
        delta = jnp.sum((grad.astype(F32) * kept_ref[0, m]).T, axis=0, keepdims=True)
        probs = jnp.exp2(nt(keys, queries) - lse_ref[0, m, 0:1, :])
        dprobs = nt(keys, grad)
        dscores = (probs * (dprobs - delta)).astype(BF16)
        step = nn(probs.astype(BF16), grad) + nn(dscores, queries)
        if m == 0:
            acc[...] = step
        else:
            acc[...] += step
        dq = nn(turned_s[...], dscores).T * SCALE
        dq_ref[0, m] = pack_rows(dq, True).astype(BF16)
    factor = jnp.where(half_low((1, 128)), 1.0 / LOG2E, 1.0)
    for m in range(CUTS):
        own_ref[0, m] = (acc[m * tokens : (m + 1) * tokens, :] * factor).astype(BF16)
        for n, ref in enumerate(far_refs):
            at = ((n + 1) * CUTS + m) * tokens
            ref[0, m] = (acc[at : at + tokens, :] * factor).astype(BF16)


def join_back(shares, *refs):
    dq_ref, own_ref = refs[:2]
    far = refs[2 : 2 + shares - 1]
    outs = refs[2 + shares - 1 :]
    tokens = own_ref.shape[2]
    for m in range(CUTS):
        for r in range(own_ref.shape[0]):
            total = own_ref[r, m].astype(F32)
            for ref in far:
                total = total + ref[r, m].astype(F32)
            outs[m][r, :tokens, :] = total.astype(BF16)
            outs[m][r, tokens:, :] = dq_ref[r, m]


def early_back(group, *refs):
    (interval, x0_ref, n1_ref, dx1_ref, rows_ref, gathered_ref, probs_ref, picked_ref) = refs[:8]
    (fields_ref, mask_ref, fused_ref, agg_ref, embed_ref, probe_ref) = refs[8:14]
    units = refs[14 : 14 + CUTS]
    blocks = refs[14 + CUTS : 14 + CUTS + group]
    mods = refs[14 + CUTS + group : 14 + CUTS + 2 * group]
    outs = refs[14 + CUTS + 2 * group + 1 :]
    (keep_ref, send_ref) = outs[:2]
    qkv_w, mod_s, mask_s, unit_s, dqkv_s, acc, mix, dscore, dmod_ref, lines_s = outs[2:]
    item = pl.program_id(0)
    grp, seq = place()
    tokens = x0_ref.shape[0]
    half = tokens // 2
    qkv_at = 3 * D + OUTP

    @pl.when(item == 0)
    def _():
        assemble(qkv_w, blocks, grp, 0, 3 * D)
        total = mods[0][...]
        for m in mods[1:]:
            total = total + m[...]
        mod_s[...] = total
        collect(unit_s, units, seq)
        acc[...] = jnp.zeros_like(acc)
        mix[...] = jnp.zeros_like(mix)
        dscore[...] = jnp.zeros_like(dscore)
        dmod_ref[...] = jnp.zeros_like(dmod_ref)

    low = half_low((half, 128))
    for h in range(HEADS):
        dqkv_s[:, h * 128 : (h + 1) * 128] = unit_s[HEADS * item + h, :tokens, :]
    for j in range(HEADS // 2):
        one = unit_s[HEADS * item + 2 * j, tokens:, :].astype(F32)
        two = unit_s[HEADS * item + 2 * j + 1, tokens:, :].astype(F32)
        lanes = slice(2 * D + j * 128, 2 * D + (j + 1) * 128)
        dqkv_s[:half, lanes] = jnp.where(low, one, swap_halves(two)).astype(BF16)
        dqkv_s[half:, lanes] = jnp.where(low, swap_halves(one), two).astype(BF16)
    dqkv = dqkv_s[...]
    which = interval[item]
    mod = mod_s[pl.ds(which, 1), :]
    acc[:, qkv_at:] += tn(n1_ref[...], dqkv)
    dn1 = nt(dqkv, qkv_w[...])
    normed, rstd = standardize(x0_ref[...])
    d_shift = jnp.sum(dn1, axis=0, keepdims=True)
    d_scale = jnp.sum(dn1 * normed, axis=0, keepdims=True)
    dx0 = (
        dx1_ref[...] + standardize_back(dn1 * (1.0 + mod[:, D : 2 * D]), normed, rstd)
    ).astype(BF16)
    rows = rows_ref[0]
    for k, row in enumerate([d_shift, d_scale] + [rows[r : r + 1] for r in range(4)]):
        dmod_ref[pl.ds(which, 1), k * D : (k + 1) * D] += row

    acc[:, 2 * D : 3 * D] += tn(gathered_ref[...], dx0)
    dagg = nt(dx0, agg_ref[:, 2 * D :])
    fields = fields_ref[0]
    wide_fields = fields.astype(F32)
    keep, _ = widen_mask(mask_ref, mask_s)
    expand = jnp.where(spread(), 1.0, 0.0).astype(BF16)
    lower = half_low((tokens, 128))
    for j in range(HEADS // 2):
        pair = slice(j * 128, (j + 1) * 128)
        for h in (2 * j, 2 * j + 1):
            mine = lower if h % 2 == 0 else jnp.logical_not(lower)
            dpart = jnp.where(mine, dagg[:, pair], 0.0).astype(BF16)
            mix[pair, :] += tn(dpart, picked_ref[h])
            spreaded = (nn(dpart, fused_ref[pair, :]) * wide_fields).astype(BF16)
            dprobs = nt(spreaded, expand)
            probs = probs_ref[0, :, h * 128 : (h + 1) * 128]
            ds = probs * (dprobs - jnp.sum(probs * dprobs, axis=-1, keepdims=True))
            ds = jnp.where(keep, ds, 0.0).astype(BF16)
            dscore[h] += tn(ds, fields)

    @pl.when(item == pl.num_programs(0) - 1)
    def _():
        lines = iota((128, OUT), 0)
        owned = spread()
        drows = jnp.zeros((128, OUT), F32)
        for h in range(HEADS):
            line = jnp.sum(jnp.where(owned, dscore[h], 0.0), axis=0, keepdims=True) * SCALE
            drows = drows + jnp.where(lines == h, line, 0.0)
        drows = drows.astype(BF16)
        mixed = mix[...].astype(BF16)
        embed = embed_ref[:, :OUT]
        acc[:, 3 * D : 3 * D + OUT] = nn(agg_ref[:, D : 2 * D], mixed) + nn(probe_ref[...], drows)
        acc[:, D : 2 * D] = nt(embed, mixed)
        dprobe = nt(embed, drows)
        heads = jnp.where(iota((128, D), 1) // HEAD == iota((128, D), 0), 1.0, 0.0).astype(BF16)
        coarse = dprobe.astype(BF16)
        fine = (dprobe - coarse.astype(F32)).astype(BF16)
        by_column = nn(coarse, heads) + nn(fine, heads)
        eye = iota((D, D), 0) == iota((D, D), 1)
        query = embed_ref[:, OUT : OUT + 1].astype(F32)
        query_row = jnp.sum(jnp.where(eye, query, 0.0), axis=0, keepdims=True)
        acc[:, :D] = by_column * query_row
        dquery = jnp.sum(agg_ref[:, :D].astype(F32) * by_column, axis=0, keepdims=True)
        column = jnp.sum(jnp.where(eye, dquery, 0.0), axis=1, keepdims=True)
        acc[:, 3 * D + OUT : 3 * D + OUTP] = jnp.where(
            iota((D, OUTP - OUT), 1) == 0, column, 0.0
        )
        split_rows(acc, grp, keep_ref, send_ref)
        lines_s[...] = jnp.zeros_like(lines_s)
        for t in range(6 * D // 128):
            lines_s[4 * t : 4 * t + 3, :] = dmod_ref[0:3, t * 128 : (t + 1) * 128]
        rows = keep_ref.shape[1]
        for t in range(mod_tiles(rows)):
            tile = lines_s[t * rows : (t + 1) * rows, :].astype(BF16)
            at = acc.shape[1] + t * 128
            for j in range(keep_ref.shape[0]):
                keep_ref[j, :, at : at + 128] = tile
                send_ref[j, :, at : at + 128] = tile


def mod_tiles(rows):
    return -(-4 * (6 * D // 128) // rows)


def sum_cores(keep_ref, got_ref, *outs):
    for j, ref in enumerate(outs):
        ref[...] = (keep_ref[j].astype(F32) + got_ref[j].astype(F32)).astype(BF16)


def cut_granules(parts, *refs):
    sources, outs, table = refs[: -parts - 1], refs[-parts - 1 : -1], refs[-1]
    _, seq = place()
    total = sources[0][...].astype(F32)
    for ref in sources[1:]:
        total = total + ref[...].astype(F32)
    total = total.astype(BF16)
    rows, cols = total.shape
    per = rows // 16
    if table.shape[0] > per * (cols // 128):
        table[...] = jnp.zeros_like(table)
    for t in range(cols // 128):
        for g in range(per):
            table[t * per + g] = total[g * 16 : (g + 1) * 16, t * 128 : (t + 1) * 128]
    size = outs[0].shape[0]
    for j in range(parts):
        outs[j][...] = table[pl.ds(jnp.bitwise_xor(seq, j) * size, size)]


def sum_pieces(*refs):
    sources, (out_ref, square_ref) = refs[:-2], refs[-2:]
    total = sources[0][...].astype(F32)
    for ref in sources[1:]:
        total = total + ref[...].astype(F32)
    out_ref[...] = total.astype(BF16)
    square_ref[...] = jnp.sum(total * total, axis=0)


def sum_late(start, stop, *refs):
    early_ref, loss_ref, lead_ref = refs[:3]
    sources, (out_ref, square_ref) = refs[3:-2], refs[-2:]
    grp, seq = place()
    rows = lead_ref.shape[0] // lax.axis_size("grp")
    lead = lead_ref[pl.ds(pl.multiple_of(grp * rows, 16), rows), :].astype(F32)
    cols = [lead[:, g : g + 1] for g in range(3)]

    def gram(f, g):
        return jnp.sum(cols[f] * cols[g], axis=0, keepdims=True)

    row = lax.rem(iota((16, 1), 0), 4)

    def pick(*values):
        out = jnp.zeros((16, 1), F32)
        for r, value in values:
            out = jnp.where(row == r, value, out)
        return out

    same = pick(*[(g, gram(g, g)) for g in range(3)])
    next_one = pick((1, 2 * gram(0, 1)), (2, 2 * gram(1, 2)))
    next_two = pick((2, 2 * gram(0, 2)))
    size = out_ref.shape[0]
    plain = jnp.zeros((16, 128), F32)
    for k in range(size):
        total = sources[0][k].astype(F32)
        for ref in sources[1:]:
            total = total + ref[k].astype(F32)
        out_ref[k] = total.astype(BF16)
        index = seq * size + k
        special = jnp.logical_and(index >= start, index < stop)
        square = total * total
        mixed = (
            square * same
            + total * pltpu.roll(total, 1, 0) * next_one
            + total * pltpu.roll(total, 2, 0) * next_two
        )
        plain = plain + jnp.where(special, mixed, square)
    squares = jnp.sum(jnp.sum(plain + early_ref[...], axis=0, keepdims=True), axis=1, keepdims=True)
    which = iota((8, 128), 0)
    square_ref[...] = jnp.where(which == 0, loss_ref[...], squares)


def step_values(param, first, second, grad):
    first = beta_first * first + (1.0 - beta_first) * grad
    second = beta_second * second + (1.0 - beta_second) * grad * grad
    mean_hat = first / (1.0 - beta_first**STEP)
    var_hat = second / (1.0 - beta_second**STEP)
    param = param - learn_rate * (
        mean_hat / (jnp.sqrt(var_hat) + adam_epsilon) + decay_rate * param
    )
    return param, first, second, param.astype(BF16)


def optimize(parts, *refs):
    reduced_ref, lead_ref = refs[:2]
    early = refs[2 : 2 + parts]
    late = refs[2 + parts : 2 + 2 * parts]
    wide = refs[2 + 2 * parts : 5 + 2 * parts]
    tall = refs[5 + 2 * parts : 8 + 2 * parts]
    query = refs[8 + 2 * parts : 11 + 2 * parts]
    outs = refs[11 + 2 * parts :]
    norm_ref, wide_out, tall_out, query_out = outs[0], outs[1:5], outs[5:9], outs[9:13]
    early_s, late_s = outs[13:]
    grp, seq = place()
    for table, pieces in ((early_s, early), (late_s, late)):
        size = pieces[0].shape[0]
        for j, ref in enumerate(pieces):
            table[pl.ds(jnp.bitwise_xor(seq, j) * size, size)] = ref[...]
    norm = jnp.sqrt(reduced_ref[1:2, 0:1])
    norm_ref[...] = jnp.broadcast_to(norm, norm_ref.shape)
    factor = jnp.minimum(1.0, clip_limit / (norm + 1e-06))
    rows = wide[0].shape[0]
    per = rows // 16

    def tile(table, t):
        return jnp.concatenate([table[t * per + g] for g in range(per)], axis=0).astype(F32)

    def put(ins, targets, at, grad):
        new = step_values(*[r[at] for r in ins], grad * factor)
        for ref, value in zip(targets, new):
            ref[at] = value

    def at(t, width=128):
        return (slice(None), slice(t * 128, t * 128 + width))

    low = half_low((rows, 128))
    for t in range(9):
        put(wide, wide_out, at(t), tile(late_s, t))
    lead = lead_ref[pl.ds(pl.multiple_of(grp * rows, 16), rows), :].astype(F32)
    lines = jnp.concatenate([tile(late_s, 27 + t) for t in range(mod_tiles(rows))], axis=0)
    for t in range(18):
        grad = lead[:, 0:1] * lines[4 * t : 4 * t + 1]
        for g in (1, 2):
            grad = grad + lead[:, g : g + 1] * lines[4 * t + g : 4 * t + g + 1]
        put(wide, wide_out, at(9 + t), grad)
    qkv = 18
    for j in range(3):
        put(wide, wide_out, at(27 + j), tile(late_s, qkv + 6 + j))
        one, two = tile(late_s, qkv + 2 * j), tile(late_s, qkv + 2 * j + 1)
        put(wide, wide_out, at(30 + j), jnp.where(low, one, swap_halves(two)))
        put(wide, wide_out, at(33 + j), jnp.where(low, swap_halves(one), two))
    for t in range(15 + 8):
        put(wide, wide_out, at(36 + t), tile(early_s, t))
    rest = OUT - 8 * 128
    put(wide, wide_out, at(59, rest), tile(early_s, 23)[:, :rest])
    for t in range(8):
        put(tall, tall_out, at(t), tile(late_s, 9 + t))
    last = tile(late_s, 17)
    lane = iota((rows, 128), 1)
    for t in range(FF // 128):
        turned = pltpu.roll(tile(early_s, 24 + t), rest, 1)
        put(tall, tall_out, at(8 + t), jnp.where(lane < rest, last, turned))
        if t == 0:
            eye = iota((rows, rows), 0) == iota((rows, rows), 1)
            grad = jnp.sum(jnp.where(eye, last[:, rest : rest + 1], 0.0), axis=0, keepdims=True)
            put(query, query_out, (slice(None), slice(None)), grad)
        last = turned
    put(tall, tall_out, at(8 + FF // 128, rest), last[:, :rest])


def shift(value, axis, bit):
    size = lax.axis_size(axis)
    return lax.ppermute(value, axis, [(i, i ^ bit) for i in range(size)])


def gather_blocks(own, group):
    blocks = {0: own}
    for j in range(2, group, 2):
        blocks[j] = shift(own, "grp", j)
    for j in range(0, group, 2):
        blocks[j + 1] = shift(blocks[j], "grp", 1)
    return [blocks[j] for j in range(group)]


def sum_over_cores(keep, send, group):
    _, rows, cols = keep.shape
    got = shift(send, "grp", 1)
    return call(sum_cores, [sds((rows, cols), BF16)] * (group // 2))(keep, got)


def scatter_pieces(halves, group, parts):
    rows, cols = halves[0].shape
    sums = [halves[0]] + [shift(halves[j], "grp", 2 * j) for j in range(1, group // 2)]
    count = (rows // 16) * (cols // 128)
    size = -(-count // parts)
    pieces = call(
        functools.partial(cut_granules, parts),
        [sds((size, 16, 128), BF16)] * parts,
        scratch=[pltpu.VMEM((size * parts, 16, 128), BF16)],
    )(*sums)
    return [pieces[0]] + [shift(pieces[j], "seq", j) for j in range(1, parts)]


def gather_pieces(piece, parts):
    return [piece] + [shift(piece, "seq", j) for j in range(1, parts)]


def butterfly(value, axes):
    for axis in axes:
        bit = 1
        while bit < lax.axis_size(axis):
            value = value + shift(value, axis, bit)
            bit *= 2
    return value


def lead_table():
    half = D // 2
    hours = 6.0 * np.exp2(np.arange(3, dtype=np.float32))
    freqs = np.exp(-np.log(np.float32(1000.0)) * np.arange(half, dtype=np.float32) / half)
    angles = hours[None, :] * freqs.astype(np.float32)[:, None]
    waves = np.concatenate([np.sin(angles), np.cos(angles)], axis=0)
    table = np.zeros((D, 128), np.float32)
    table[:, :3] = waves / (1.0 + np.exp(-waves))
    return jnp.asarray(table).astype(BF16)


def per_device(
    fields,
    targets,
    land_mask,
    interval,
    samples,
    wide_weights,
    wide_firsts,
    wide_seconds,
    tall_weights,
    tall_firsts,
    tall_seconds,
    query_vector,
    query_firsts,
    query_seconds,
):
    group = lax.axis_size("grp")
    parts = lax.axis_size("seq")
    shares = parts // CUTS
    rows, columns = wide_weights.shape
    items, tokens = fields.shape[:2]
    units = items * HEADS // CUTS
    every = items * tokens
    late_cols = D + FF + OUTP + FF

    query_row = query_vector.reshape(1, rows)
    tall = [x.T for x in (tall_weights, tall_firsts, tall_seconds)]
    lead = lead_table()
    lines = tokens // COLS
    line = lax.axis_index("seq") * lines + jnp.arange(lines)
    latitude = jnp.pi * ((line.astype(F32) + 0.5) / (lines * parts) - 0.5)
    weight_lines = samples.astype(F32)[:, None] * jnp.cos(latitude)[None, :]

    def columns_of(index):
        return pl.BlockSpec((rows, 3 * D), lambda i: (0, index))

    first_own = call(
        pack_first,
        sds((rows, 3 * D + OUTP), BF16),
        grid=(1,),
        in_specs=[columns_of(0), columns_of(0), pl.BlockSpec((1, rows), lambda i: (0, 0))],
        out_specs=pl.BlockSpec((rows, 3 * D + OUTP), lambda i: (0, 0)),
        us=2,
    )(wide_weights, tall[0], query_row)
    first = gather_blocks(first_own, group)
    qkv_own, mod_own = call(
        pack_qkv,
        [sds((rows, 3 * D), BF16), sds((8, 6 * D), F32)],
        grid=(1,),
        in_specs=[smem(), columns_of(1), columns_of(2), columns_of(3)] + [whole()] * 2,
        out_specs=[whole()] * 2,
        us=2,
    )(weight_lines, wide_weights, wide_weights, wide_weights, lead, land_mask)
    qkv_blocks = gather_blocks(qkv_own, group)
    mods = gather_blocks(mod_own, group)

    agg_weights, embed, score_w, fused_w, probe = call(
        prepare,
        [
            sds((D, 3 * D), BF16),
            sds((D, OUTP), BF16),
            sds((HEADS * 128, OUT), BF16),
            sds((D, OUT), BF16),
            sds((D, 128), BF16),
        ],
        us=4,
    )(*first)
    late_own = call(
        pack_late,
        sds((rows, late_cols), BF16),
        grid=(1,),
        in_specs=[columns_of(4), columns_of(5), columns_of(6), whole(), anywhere()],
        out_specs=whole(),
        us=2,
    )(wide_weights, wide_weights, wide_weights, tall[0], probe)
    late_blocks = gather_blocks(late_own, group)

    by_item = pl.BlockSpec((tokens, D), lambda i: (i, 0))

    def item_block(width):
        return pl.BlockSpec((1, tokens, width), lambda i: (i, 0, 0))

    heads_spec = pl.BlockSpec((HEADS, tokens, OUT), lambda i: (0, i, 0))
    packed = tokens + tokens // 2 + 16

    results = call(
        functools.partial(aggregate, group),
        [
            sds((items, tokens, HEADS * 128), F32),
            sds((HEADS, every, OUT), BF16),
            sds((every, D), BF16),
            sds((every, D), F32),
            sds((every, D), BF16),
        ]
        + [sds((units, packed, 128), BF16)] * CUTS,
        grid=(items,),
        in_specs=[smem(), item_block(OUT), item_block(VARS)] + [whole()] * (3 + 2 * group),
        out_specs=[item_block(HEADS * 128), heads_spec, by_item, by_item, by_item]
        + [whole()] * CUTS,
        scratch=[
            pltpu.VMEM((D, 3 * D), BF16),
            pltpu.VMEM((8, 6 * D), F32),
            pltpu.VMEM((tokens, 128), jnp.int32),
            pltpu.VMEM((items * HEADS, packed, 128), BF16),
        ],
        us=12,
    )(interval, fields, land_mask, score_w, fused_w, agg_weights, *qkv_blocks, *mods)
    probs, picked, gathered, x0, n1 = results[:5]
    dealt = results[5:]

    own = [dealt[0]] + [shift(dealt[m], "seq", m * shares) for m in range(1, CUTS)]
    others = [shift(own[m], "seq", n) for n in range(1, shares) for m in range(CUTS)]
    keys_total = parts * tokens

    unit_in = pl.BlockSpec((1, packed, 128), lambda u: (u, 0, 0))
    half_in = pl.BlockSpec((1, tokens // 2, 128), lambda u: (u, 0, 0))
    kept_spec = pl.BlockSpec((1, CUTS, tokens, 128), lambda u: (u, 0, 0, 0))
    lse_spec = pl.BlockSpec((1, CUTS, 8, tokens), lambda u: (u, 0, 0, 0))
    pack_spec = pl.BlockSpec((1, CUTS, tokens // 2, 128), lambda u: (u, 0, 0, 0))
    half_out = sds((units, tokens // 2, 128), BF16)
    results = call(
        functools.partial(attend, shares),
        [half_out] * CUTS
        + [
            sds((units, CUTS, tokens, 128), F32),
            sds((units, CUTS, 8, tokens), F32),
            sds((8, 128), F32),
        ],
        grid=(units,),
        in_specs=[unit_in] * (CUTS * shares),
        out_specs=[half_in] * CUTS + [kept_spec, lse_spec, whole()],
        scratch=[pltpu.VMEM((keys_total, 128), BF16), pltpu.VMEM((128, keys_total), BF16)],
        us=14,
    )(*own, *others)
    backs, (kept, lse, weight_sum) = results[:CUTS], results[CUTS:]
    heads_in = [backs[0]] + [shift(backs[m], "seq", m * shares) for m in range(1, CUTS)]

    results = call(
        functools.partial(middle, group),
        [
            sds((every, D), F32),
            sds((items, 8, D), F32),
            sds((group // 2, rows, late_cols), BF16),
            sds((group // 2, rows, late_cols), BF16),
            sds((8, 128), F32),
        ]
        + [half_out] * CUTS,
        grid=(items,),
        in_specs=[smem(), smem(), whole(), by_item, item_block(OUT), item_block(VARS)]
        + [whole()] * (CUTS + 2 * group),
        out_specs=[by_item, pl.BlockSpec((1, 8, D), lambda i: (i, 0, 0))] + [whole()] * (3 + CUTS),
        scratch=[
            pltpu.VMEM((D, late_cols), BF16),
            pltpu.VMEM((8, 6 * D), F32),
            pltpu.VMEM((tokens, 128), jnp.int32),
            pltpu.VMEM((items * HEADS, tokens // 2, 128), BF16),
            pltpu.VMEM((items * HEADS, tokens // 2, 128), BF16),
            pltpu.VMEM((tokens, D), BF16),
            pltpu.VMEM((D, late_cols), F32),
        ],
        us=16,
    )(
        interval,
        weight_lines,
        weight_sum,
        x0,
        targets,
        land_mask,
        *heads_in,
        *late_blocks,
        *mods,
    )
    dx1, mod_rows, early_keep, early_send, loss = results[:5]
    sends = results[5:]
    grads_in = [sends[0]] + [shift(sends[m], "seq", m * shares) for m in range(1, CUTS)]

    early_halves = sum_over_cores(early_keep, early_send, group)

    results = call(
        functools.partial(attend_back, shares),
        [sds((units, CUTS, tokens // 2, 128), BF16)]
        + [sds((units, CUTS, tokens, 128), BF16)] * shares,
        grid=(units,),
        in_specs=[unit_in] * (CUTS * shares)
        + [half_in] * CUTS
        + [kept_spec, lse_spec, anywhere()],
        out_specs=[pack_spec] + [kept_spec] * shares,
        scratch=[
            pltpu.VMEM((keys_total, 128), BF16),
            pltpu.VMEM((128, keys_total), BF16),
            pltpu.VMEM((keys_total, 128), F32),
        ],
        us=20,
    )(*own, *others, *grads_in, kept, lse, early_halves[0])
    early_pieces = scatter_pieces(early_halves, group, parts)
    dq, near, far = results[0], results[1], results[2:]
    far = [shift(far[n], "seq", n + 1) for n in range(shares - 1)]
    dealt = call(
        functools.partial(join_back, shares),
        [sds((units, tokens + tokens // 2, 128), BF16)] * CUTS,
    )(dq, near, *far)
    units_in = [dealt[0]] + [shift(dealt[m], "seq", m * shares) for m in range(1, CUTS)]

    size = early_pieces[0].shape[0]
    early_piece, early_squares = call(
        sum_pieces, [sds((size, 16, 128), BF16), sds((16, 128), F32)]
    )(*early_pieces)
    early_all = gather_pieces(early_piece, parts)

    first_cols = 3 * D + OUTP + 3 * D
    sent_cols = first_cols + mod_tiles(rows) * 128
    late_keep, late_send = call(
        functools.partial(early_back, group),
        [
            sds((group // 2, rows, sent_cols), BF16),
            sds((group // 2, rows, sent_cols), BF16),
        ],
        grid=(items,),
        in_specs=[
            smem(),
            by_item,
            by_item,
            by_item,
            pl.BlockSpec((1, 8, D), lambda i: (i, 0, 0)),
            by_item,
            item_block(HEADS * 128),
            heads_spec,
            item_block(OUT),
            item_block(VARS),
        ]
        + [whole()] * (4 + CUTS + 2 * group)
        + [anywhere()],
        out_specs=[whole()] * 2,
        scratch=[
            pltpu.VMEM((D, 3 * D), BF16),
            pltpu.VMEM((8, 6 * D), F32),
            pltpu.VMEM((tokens, 128), jnp.int32),
            pltpu.VMEM((items * HEADS, tokens + tokens // 2, 128), BF16),
            pltpu.VMEM((tokens, 3 * D), BF16),
            pltpu.VMEM((D, first_cols), F32),
            pltpu.VMEM((D, OUT), F32),
            pltpu.VMEM((HEADS, 128, OUT), F32),
            pltpu.VMEM((8, 6 * D), F32),
            pltpu.VMEM((mod_tiles(rows) * rows, 128), F32),
        ],
        us=20,
    )(
        interval,
        x0,
        n1,
        dx1,
        mod_rows,
        gathered,
        probs,
        picked,
        fields,
        land_mask,
        fused_w,
        agg_weights,
        embed,
        probe,
        *units_in,
        *qkv_blocks,
        *mods,
        early_piece,
    )
    late_halves = sum_over_cores(late_keep, late_send, group)
    late_pieces = scatter_pieces(late_halves, group, parts)
    size = late_pieces[0].shape[0]
    start = (rows // 16) * (first_cols // 128)
    stop = (rows // 16) * (sent_cols // 128)
    late_piece, reduced = call(
        functools.partial(sum_late, start, stop),
        [sds((size, 16, 128), BF16), sds((8, 128), F32)],
    )(early_squares, loss, lead, *late_pieces)
    reduced = butterfly(reduced, ("grp", "seq"))
    late_all = gather_pieces(late_piece, parts)

    def like(x, dtype=F32):
        return sds(x.shape, dtype)

    results = call(
        functools.partial(optimize, parts),
        [sds((8, 128), F32)]
        + [like(wide_weights)] * 3
        + [like(wide_weights, BF16)]
        + [like(tall[0])] * 3
        + [like(tall[0], BF16)]
        + [like(query_row)] * 3
        + [like(query_row, BF16)],
        scratch=[
            pltpu.VMEM((parts * early_piece.shape[0], 16, 128), BF16),
            pltpu.VMEM((parts * late_piece.shape[0], 16, 128), BF16),
        ],
        us=10,
        limit=36 * 1024 * 1024,
    )(
        reduced,
        lead,
        *early_all,
        *late_all,
        wide_weights,
        wide_firsts,
        wide_seconds,
        *tall,
        query_row,
        query_firsts.reshape(1, rows),
        query_seconds.reshape(1, rows),
    )
    norm = results[0]
    tall_out = tuple(r.T for r in results[5:9])
    query_out = tuple(r.reshape(rows) for r in results[9:13])
    return (
        (reduced[0, 0], weight_sum[0, 0], norm[0, 0])
        + tuple(results[1:5])
        + tall_out
        + query_out
    )


def solution(mesh):
    placed = (
        P("grp", "seq", None),
        P("grp", "seq", None),
        P("grp", "seq", None),
        P("grp"),
        P("grp"),
        P("grp", None),
        P("grp", None),
        P("grp", None),
        P(None, "grp"),
        P(None, "grp"),
        P(None, "grp"),
        P("grp"),
        P("grp"),
        P("grp"),
    )
    return jax.shard_map(
        per_device,
        mesh=mesh,
        in_specs=placed,
        out_specs=(
            P(),
            P(),
            P(),
            P("grp", None),
            P("grp", None),
            P("grp", None),
            P("grp", None),
            P(None, "grp"),
            P(None, "grp"),
            P(None, "grp"),
            P(None, "grp"),
            P("grp"),
            P("grp"),
            P("grp"),
            P("grp"),
        ),
        check_vma=False,
    )
```

```python
import functools

import jax
import numpy as np
import jax.numpy as jnp
from jax import lax
from jax.experimental import pallas as pl
from jax.experimental.pallas import tpu as pltpu
from jax.sharding import PartitionSpec as P

D = 384
HEADS = 6
HEAD = 64
FF = 1536
VARS = 69
PIX = 16
OUT = VARS * PIX
OUTP = 1152
VARP = 80
COLS = 128
STEP = 5
CUTS = 4
SCALE = HEAD**-0.5
LOG2E = 1.4426950408889634

beta_first = 0.5
beta_second = 0.5
learn_rate = 0.1
decay_rate = 0.01
adam_epsilon = 1e-08
clip_limit = 0.05
norm_epsilon = 1e-06
masked_score = -1e30

F32 = jnp.float32
BF16 = jnp.bfloat16
MIB = 1024 * 1024
RIDERS = 16


def dot(left, right, a, b):
    return lax.dot_general(left, right, (((a,), (b,)), ((), ())), preferred_element_type=F32)


def nn(left, right):
    return dot(left, right, 1, 0)


def nt(left, right):
    return dot(left, right, 1, 1)


def tn(left, right):
    return dot(left, right, 0, 0)


def iota(shape, dim):
    return lax.broadcasted_iota(jnp.int32, shape, dim)


def half_low(shape):
    return iota(shape, len(shape) - 1) < HEAD


def swap_halves(tile):
    return pltpu.roll(tile, HEAD, 1)


def spread():
    return iota((VARP, OUT), 1) // PIX == iota((VARP, OUT), 0)


def ones_where(mask):
    return jnp.where(mask, 1.0, 0.0).astype(BF16)


def place():
    grp = lax.axis_index("grp")
    seq = lax.axis_index("seq")
    return grp, seq


def call(kernel, outs, grid=(), in_specs=None, out_specs=None, scratch=(), us=1, limit=12):
    kw = {}
    if in_specs is not None:
        kw["in_specs"] = in_specs
    if out_specs is not None:
        kw["out_specs"] = out_specs
    return pl.pallas_call(
        kernel,
        out_shape=outs,
        grid=grid,
        scratch_shapes=list(scratch),
        cost_estimate=pl.CostEstimate(
            flops=int(us * 1.15e9), transcendentals=0, bytes_accessed=1024
        ),
        compiler_params=pltpu.CompilerParams(vmem_limit_bytes=limit * MIB),
        **kw,
    )


def whole():
    return pl.BlockSpec(memory_space=pltpu.VMEM)


def anywhere():
    return pl.BlockSpec(memory_space=pl.ANY)


def smem():
    return pl.BlockSpec(memory_space=pltpu.SMEM)


def sds(shape, dtype):
    return jax.ShapeDtypeStruct(shape, dtype)


def in_hbm(shape, dtype):
    return pltpu.HBM(shape, dtype)


def standardize(x):
    centered = x - jnp.mean(x, axis=-1, keepdims=True)
    rstd = lax.rsqrt(jnp.mean(centered * centered, axis=-1, keepdims=True) + norm_epsilon)
    return centered * rstd, rstd


def standardize_back(grad, normed, rstd):
    return rstd * (
        grad
        - jnp.mean(grad, axis=-1, keepdims=True)
        - normed * jnp.mean(grad * normed, axis=-1, keepdims=True)
    )


def gelu_parts(x):
    k = 0.7978845608028654
    inner = k * (x + 0.044715 * x * x * x)
    t = jnp.tanh(inner)
    value = 0.5 * x * (1.0 + t)
    slope = 0.5 * (1.0 + t) + 0.5 * x * (1.0 - t * t) * k * (1.0 + 3 * 0.044715 * x * x)
    return value, slope


def pack_first(*refs):
    samples, cosines, agg_ref, mod_a, mod_b, wide_ref, tall_ref, query_ref = refs[:8]
    lead_ref, mask_ref, out_ref, rider_s = refs[8:]
    rows = wide_ref.shape[0]
    grp, seq = place()
    out_ref[:rows, : 3 * D] = agg_ref[...].astype(BF16)
    eye = iota((rows, rows), 0) == iota((rows, rows), 1)
    column = jnp.sum(jnp.where(eye, query_ref[...], 0.0), axis=1, keepdims=True)
    lane = iota((rows, OUTP), 1)
    embed = jnp.where(lane < OUT, tall_ref[...], jnp.where(lane == OUT, column, 0.0))
    out_ref[:rows, 3 * D : 6 * D] = embed.astype(BF16)
    low = half_low((rows, 128))
    for j in range(HEADS // 2):
        k = wide_ref[:, D + j * 128 : D + (j + 1) * 128]
        v = wide_ref[:, 2 * D + j * 128 : 2 * D + (j + 1) * 128]
        at = 6 * D + 2 * j * 128
        out_ref[:rows, at : at + 128] = jnp.where(low, k, swap_halves(v)).astype(BF16)
        out_ref[:rows, at + 128 : at + 256] = jnp.where(low, swap_halves(k), v).astype(BF16)
    out_ref[:rows, 8 * D :] = wide_ref[:, :D].astype(BF16)
    rider_s[...] = jnp.zeros_like(rider_s)

    def ride(row, value):
        for part in range(3):
            piece = value.astype(BF16).astype(F32)
            at = part * 4 + row
            rider_s[at : at + 1, : 6 * D] = piece
            value = value - piece

    lead = lead_ref[pl.ds(pl.multiple_of(grp * rows, 16), rows), :].astype(F32)
    mod = jnp.concatenate([mod_a[...], mod_b[...]], axis=1).astype(BF16).astype(F32)
    for g in range(3):
        ride(g, jnp.sum(lead[:, g : g + 1] * mod, axis=0, keepdims=True))
    items, _, tokens = mask_ref.shape
    total = jnp.zeros((1, 1), F32)
    for i in range(items):
        present = jnp.maximum(mask_ref[i], 0).astype(F32)
        weighed = jnp.sum(present, axis=0, keepdims=True) * line_weights(
            samples[i], cosines, seq, iota((1, tokens), 1)
        )
        total = total + jnp.sum(weighed, axis=1, keepdims=True)
    ride(3, jnp.broadcast_to(total, (1, 6 * D)))
    out_ref[rows:, :] = rider_s[...].astype(BF16)


def line_weights(count, cosines, seq, position):
    lines = position.size // COLS
    value = jnp.zeros(position.shape, F32)
    for r in range(lines):
        value = jnp.where(position // COLS == r, cosines[seq * lines + r], value)
    return value * count.astype(F32)


def pack_late(wide_a, wide_b, wide_c, tall_ref, _, late_ref):
    rows = wide_a.shape[0]
    late_ref[:, : 3 * D] = wide_a[...].astype(BF16)
    late_ref[:, 3 * D : 6 * D] = wide_b[...].astype(BF16)
    rest = D + FF + OUT - 6 * D
    late_ref[:, 6 * D : D + FF + OUT] = wide_c[:, :rest].astype(BF16)
    late_ref[:, D + FF + OUT : D + FF + OUTP] = jnp.zeros((rows, OUTP - OUT), BF16)
    late_ref[:, D + FF + OUTP :] = tall_ref[:, OUT:].astype(BF16)


def assemble(target, blocks, grp, lo, hi):
    rows = target.shape[0] // len(blocks)
    for j, ref in enumerate(blocks):
        at = pl.multiple_of(jnp.bitwise_xor(grp, j) * rows, 16)
        target[pl.ds(at, rows), :] = ref[:rows, lo:hi]


def unride(target, blocks):
    for g in range(4):
        total = jnp.zeros((1, 6 * D), F32)
        for ref in blocks:
            for part in range(3):
                at = ref.shape[0] - RIDERS + part * 4 + g
                total = total + ref[at : at + 1, : 6 * D].astype(F32)
        target[g : g + 1, :] = total


def prepare(blocks, grp, outs, score_s, fused_s):
    (agg_ref, embed_ref, qkv_ref, fused_ref, probe_ref, mod_ref) = outs
    assemble(agg_ref, blocks, grp, 0, 3 * D)
    assemble(embed_ref, blocks, grp, 3 * D, 6 * D)
    assemble(qkv_ref, blocks, grp, 6 * D, 9 * D)
    mod_ref[...] = jnp.zeros_like(mod_ref)
    unride(mod_ref, blocks)
    query = embed_ref[:, OUT : OUT + 1].astype(F32)
    picked = jnp.where(iota((D, 128), 1) == iota((D, 128), 0) // HEAD, query, 0.0).astype(BF16)
    probe = nn(agg_ref[:, :D], picked).astype(BF16)
    probe_ref[...] = probe
    embed = embed_ref[:, :OUT]
    rows = tn(probe, embed) * SCALE
    mine = spread()
    for h in range(HEADS):
        score_s[h * VARP : (h + 1) * VARP, :] = jnp.where(mine, rows[h : h + 1, :], 0.0).astype(
            BF16
        )
    fused = tn(agg_ref[:, D : 2 * D], embed)
    fused_s[...] = fused.astype(BF16)
    fused_ref[...] = fused.T.astype(BF16)


def aggregate(group, *refs):
    (interval, fields_ref, mask_ref) = refs[:3]
    blocks, outs = refs[3 : 3 + group], refs[3 + group :]
    (probs_ref, picked_ref, gathered_ref, x0_ref, n1_ref) = outs[:5]
    kept, units = outs[5:11], outs[11 : 11 + CUTS]
    (agg_ref, _, qkv_w, _, _, mod_s) = kept
    score_s, fused_s, turned_s, unit_s = outs[11 + CUTS :]
    item = pl.program_id(0)
    grp, seq = place()
    tokens = fields_ref.shape[2]

    @pl.when(item == 0)
    def _():
        prepare(blocks, grp, kept, score_s, fused_s)

    fields = fields_ref[0]
    wide_fields = fields.astype(F32)
    mask = mask_ref[0]
    scores = nn(score_s[...], fields)
    expand = ones_where(iota((OUT, VARP), 0) // PIX == iota((OUT, VARP), 1))
    for h in range(HEADS):
        s = jnp.where(
            mask > 0,
            scores[h * VARP : (h + 1) * VARP],
            jnp.where(mask < 0, -3e38, masked_score),
        )
        e = jnp.exp(s - jnp.max(s, axis=0, keepdims=True))
        a = e / jnp.sum(e, axis=0, keepdims=True)
        probs_ref[0, h * VARP : (h + 1) * VARP, :] = a
        picked = (nn(expand, a.astype(BF16)) * wide_fields).astype(BF16)
        picked_ref[h, 0] = picked
        turned_s[h * HEAD : (h + 1) * HEAD, :] = nn(fused_s[h * HEAD : (h + 1) * HEAD, :], picked)
    gathered_ref[...] = turned_s[...].T.astype(BF16)
    x0 = nn(gathered_ref[...], agg_ref[:, 2 * D :])
    x0_ref[...] = x0
    mod = mod_s[pl.ds(interval[item], 1), :]
    normed, _ = standardize(x0)
    n1 = (normed * (1.0 + mod[:, D : 2 * D]) + mod[:, :D]).astype(BF16)
    n1_ref[...] = n1
    qkv = nn(n1, qkv_w[...])
    half = tokens // 2
    low = half_low((half, 128))
    packed = tokens + half
    for h in range(HEADS):
        unit_s[HEADS * item + h, :tokens, :] = qkv[:, h * 128 : (h + 1) * 128].astype(BF16)
    for j in range(HEADS // 2):
        pair = qkv[:, 2 * D + j * 128 : 2 * D + (j + 1) * 128] * (SCALE * LOG2E)
        top, bottom = pair[:half], pair[half:]
        unit_s[HEADS * item + 2 * j, tokens:packed, :] = jnp.where(
            low, top, swap_halves(bottom)
        ).astype(BF16)
        unit_s[HEADS * item + 2 * j + 1, tokens:packed, :] = jnp.where(
            low, swap_halves(top), bottom
        ).astype(BF16)

    @pl.when(item == pl.num_programs(0) - 1)
    def _():
        value = jnp.broadcast_to(mod_s[3:4, :128], (16, 128))
        high = value.astype(BF16)
        value = value - high.astype(F32)
        middle_part = value.astype(BF16)
        low_part = (value - middle_part.astype(F32)).astype(BF16)
        lane = iota((16, 128), 1)
        zero = jnp.zeros((16, 128), BF16)
        rides = jnp.where(
            lane < 32,
            high.astype(F32),
            jnp.where(
                lane < 64,
                middle_part.astype(F32),
                jnp.where(lane < 96, low_part.astype(F32), 0.0),
            ),
        ).astype(BF16)
        for u in range(unit_s.shape[0]):
            unit_s[u, packed:, :] = rides if u < CUTS else zero
        deal(units, unit_s, seq)


def deal(targets, source, seq):
    a = seq // (lax.axis_size("seq") // CUTS)
    for m in range(CUTS):
        for r in range(targets[m].shape[0]):
            targets[m][r] = source[CUTS * r + jnp.bitwise_xor(a, m)]


def collect(target, sources, seq):
    a = seq // (lax.axis_size("seq") // CUTS)
    for m in range(CUTS):
        for r in range(sources[m].shape[0]):
            target[CUTS * r + jnp.bitwise_xor(a, m)] = sources[m][r]


def unpack(pack, at_low):
    wide = pack.astype(F32)
    low = half_low(wide.shape)
    if at_low:
        both = [jnp.where(low, wide, 0.0), jnp.where(low, swap_halves(wide), 0.0)]
    else:
        both = [jnp.where(low, 0.0, swap_halves(wide)), jnp.where(low, 0.0, wide)]
    return jnp.concatenate(both, axis=0).astype(BF16)


def pack_rows(tile, at_low):
    half = tile.shape[0] // 2
    top, bottom = tile[:half], tile[half:]
    low = half_low(top.shape)
    if at_low:
        return jnp.where(low, top, swap_halves(bottom))
    return jnp.where(low, swap_halves(top), bottom)


def attend(shares, *refs):
    own = refs[:CUTS]
    others = refs[CUTS : CUTS * shares]
    backs = refs[CUTS * shares : CUTS * shares + CUTS]
    kept_ref, lse_ref, weight_ref, keys_s = refs[CUTS * shares + CUTS :]
    tokens = kept_ref.shape[2]
    packed = tokens + tokens // 2

    @pl.when(pl.program_id(0) == 0)
    def _():
        total = jnp.zeros((16, 128), F32)
        for ref in own + others:
            total = total + ref[0, packed:, :].astype(F32)
        total = jnp.sum(total[0:8], axis=1, keepdims=True) / 32.0
        weight_ref[...] = jnp.broadcast_to(total, (8, 128))

    for n, ref in enumerate(own + others):
        keys_s[n * tokens : (n + 1) * tokens, :] = ref[0, :tokens, :]
    keys = keys_s[...]
    values = jnp.where(half_low(keys.shape), jnp.ones_like(keys), keys)

    def scores_of(m):
        return nt(unpack(own[m][0, tokens:packed, :], True), keys)

    scores = scores_of(0)
    for m in range(CUTS):
        later = scores_of(m + 1) if m + 1 < CUTS else None
        top = jnp.max(scores, axis=1, keepdims=True)
        out = nn(jnp.exp2(scores - top).astype(BF16), values)
        total = out[:, 0:1]
        out = out / total
        lse = jnp.broadcast_to(top + jnp.log2(total), (tokens, 128)).T
        lse_ref[0, m] = lse[:8]
        kept_ref[0, m] = out
        backs[m][0] = pack_rows(out, False).astype(BF16)
        scores = later


def middle(group, *refs):
    (interval, samples, cosines, sum_ref, x0_ref, fields_ref, mask_ref) = refs[:7]
    heads_in = refs[7 : 7 + CUTS]
    blocks = refs[7 + CUTS : 7 + CUTS + group]
    mod_s = refs[7 + CUTS + group]
    outs = refs[7 + CUTS + group + 1 :]
    (dx1_ref, rows_ref, loss_ref) = outs[:3]
    sends = outs[3 : 3 + CUTS]
    attended_s, db1_ref, n2_ref, dh_ref, nf_ref, dpred_ref, db2_ref, active_ref = outs[
        3 + CUTS : 11 + CUTS
    ]
    weights, head_s, grad_s = outs[11 + CUTS :]
    item = pl.program_id(0)
    grp, seq = place()
    tokens = x0_ref.shape[0]
    half = tokens // 2

    @pl.when(item == 0)
    def _():
        assemble(weights, blocks, grp, 0, D + FF + OUTP + FF)
        collect(head_s, heads_in, seq)
        loss_ref[...] = jnp.zeros_like(loss_ref)

    low = half_low((half, 128))
    for j in range(HEADS // 2):
        one = head_s[HEADS * item + 2 * j].astype(F32)
        two = head_s[HEADS * item + 2 * j + 1].astype(F32)
        attended_s[:half, j * 128 : (j + 1) * 128] = jnp.where(low, one, swap_halves(two)).astype(
            BF16
        )
        attended_s[half:, j * 128 : (j + 1) * 128] = jnp.where(low, swap_halves(one), two).astype(
            BF16
        )
    out_w = slice(0, D)
    up_w = slice(D, D + FF)
    head_w = slice(D + FF, D + FF + OUT)
    down_w = slice(D + FF + OUTP, D + FF + OUTP + FF)
    mod = mod_s[pl.ds(interval[item], 1), :]
    gate_a, shift_b, scale_b, gate_b = [mod[:, k * D : (k + 1) * D] for k in range(2, 6)]
    attended = attended_s[...]
    branch_a = nn(attended, weights[:, out_w])
    x1 = x0_ref[...] + gate_a * branch_a
    normed_b, rstd_b = standardize(x1)
    n2 = (normed_b * (1.0 + scale_b) + shift_b).astype(BF16)
    n2_ref[...] = n2
    value, slope = gelu_parts(nn(n2, weights[:, up_w]))
    active = value.astype(BF16)
    active_ref[...] = active
    branch_b = nt(active, weights[:, down_w])
    x2 = x1 + gate_b * branch_b
    final, rstd_f = standardize(x2)
    nf = final.astype(BF16)
    nf_ref[...] = nf
    diff = nn(nf, weights[:, head_w]) - fields_ref[0].astype(F32)
    present = tn(ones_where(mask_ref[0] > 0), ones_where(spread()))
    weight = line_weights(samples[item], cosines, seq, iota((tokens, 1), 0))
    weight_grad = weight * (2.0 / PIX) / sum_ref[0:1, 0:1]
    masked = present * diff
    each = jnp.sum(masked * diff, axis=1, keepdims=True) * weight
    loss_ref[...] += jnp.broadcast_to(jnp.sum(each, axis=0, keepdims=True) / PIX, (8, 128))
    dpred = (masked * weight_grad).astype(BF16)
    dpred_ref[...] = dpred

    dx2 = standardize_back(nt(dpred, weights[:, head_w]), final, rstd_f)
    db2 = (gate_b * dx2).astype(BF16)
    db2_ref[...] = db2
    d_gate_b = jnp.sum(dx2 * branch_b, axis=0, keepdims=True)
    dh = (nn(db2, weights[:, down_w]) * slope).astype(BF16)
    dh_ref[...] = dh
    dn2 = nt(dh, weights[:, up_w])
    d_shift_b = jnp.sum(dn2, axis=0, keepdims=True)
    d_scale_b = jnp.sum(dn2 * normed_b, axis=0, keepdims=True)
    dx1 = dx2 + standardize_back(dn2 * (1.0 + scale_b), normed_b, rstd_b)
    dx1_ref[...] = dx1
    d_gate_a = jnp.sum(dx1 * branch_a, axis=0, keepdims=True)
    db1 = (gate_a * dx1).astype(BF16)
    db1_ref[...] = db1
    dout = nt(db1, weights[:, out_w])
    rows_ref[0] = jnp.concatenate(
        [d_gate_a, d_shift_b, d_scale_b, d_gate_b, jnp.zeros((4, D), F32)], axis=0
    )
    for j in range(HEADS // 2):
        pair = dout[:, j * 128 : (j + 1) * 128]
        top, bottom = pair[:half], pair[half:]
        grad_s[HEADS * item + 2 * j] = jnp.where(low, top, swap_halves(bottom)).astype(BF16)
        grad_s[HEADS * item + 2 * j + 1] = jnp.where(low, swap_halves(top), bottom).astype(BF16)

    @pl.when(item == pl.num_programs(0) - 1)
    def _():
        deal(sends, grad_s, seq)


def middle_weights(*refs):
    attended, db1, n2, dh, nf, dpred, db2, active = refs[:8]
    keep_ref, send_ref, acc = refs[8:]
    grp, _ = place()
    acc[:, :D] = tn(attended[...], db1[...])
    acc[:, D : D + FF] = tn(n2[...], dh[...])
    acc[:, D + FF : D + FF + OUT] = tn(nf[...], dpred[...])
    acc[:, D + FF + OUT : D + FF + OUTP] = jnp.zeros((D, OUTP - OUT), F32)
    acc[:, D + FF + OUTP :] = tn(db2[...], active[...])
    split_rows(acc, grp, keep_ref, send_ref)


def split_rows(acc, grp, keep_ref, send_ref):
    rows = keep_ref.shape[1]
    for j in range(keep_ref.shape[0]):
        for odd, ref in ((0, keep_ref), (1, send_ref)):
            at = pl.multiple_of(jnp.bitwise_xor(grp, 2 * j + odd) * rows, 16)
            ref[j, :, : acc.shape[1]] = acc[pl.ds(at, rows), :].astype(BF16)


def attend_back(shares, *refs):
    own = refs[:CUTS]
    others = refs[CUTS : CUTS * shares]
    grads = refs[CUTS * shares : CUTS * shares + CUTS]
    kept_ref, lse_ref = refs[CUTS * shares + CUTS : CUTS * shares + CUTS + 2]
    outs = refs[CUTS * shares + CUTS + 2 :]
    outs = outs[2:]
    dq_ref, own_ref = outs[:2]
    far_refs = outs[2 : 2 + shares - 1]
    keys_s, turned_s, acc = outs[2 + shares - 1 :]
    tokens = kept_ref.shape[2]
    for n, ref in enumerate(own + others):
        keys_s[n * tokens : (n + 1) * tokens, :] = ref[0, :tokens, :]
    turned_s[...] = keys_s[...].T
    every = range(CUTS)
    queries = jnp.concatenate(
        [unpack(own[m][0, tokens : tokens + tokens // 2, :], True) for m in every], axis=0
    )
    grads = [unpack(grads[m][0], False) for m in every]
    delta = jnp.concatenate(
        [
            jnp.sum((grads[m].astype(F32) * kept_ref[0, m]).T, axis=0, keepdims=True)
            for m in every
        ],
        axis=1,
    )
    grads = jnp.concatenate(grads, axis=0)
    lse = jnp.concatenate([lse_ref[0, m, 0:1, :] for m in every], axis=1)
    chunk = 2 * tokens
    count = keys_s.shape[0] // chunk

    def products_of(c):
        keys = keys_s[c * chunk : (c + 1) * chunk, :]
        return nt(keys, queries), nt(keys, grads)

    products, dq = products_of(0), None
    for c in range(count):
        scores, dprobs = products
        if c + 1 < count:
            products = products_of(c + 1)
        probs = jnp.exp2(scores - lse)
        dscores = (probs * (dprobs - delta)).astype(BF16)
        acc[c * chunk : (c + 1) * chunk, :] = nn(probs.astype(BF16), grads) + nn(dscores, queries)
        part = nn(turned_s[:, c * chunk : (c + 1) * chunk], dscores)
        dq = part if dq is None else dq + part
    for m in every:
        turned = dq[:, m * tokens : (m + 1) * tokens].T * SCALE
        dq_ref[0, m] = pack_rows(turned, True).astype(BF16)
    factor = jnp.where(half_low((1, 128)), 1.0 / LOG2E, 1.0)
    for m in range(CUTS):
        own_ref[0, m] = (acc[m * tokens : (m + 1) * tokens, :] * factor).astype(BF16)
        for n, ref in enumerate(far_refs):
            at = ((n + 1) * CUTS + m) * tokens
            ref[0, m] = (acc[at : at + tokens, :] * factor).astype(BF16)


def join_back(shares, *refs):
    dq_ref, own_ref = refs[:2]
    far = refs[2 : 2 + shares - 1]
    outs = refs[2 + shares - 1 :]
    tokens = own_ref.shape[2]
    for m in range(CUTS):
        total = own_ref[0, m].astype(F32)
        for ref in far:
            total = total + ref[0, m].astype(F32)
        outs[m][:tokens, :] = total.astype(BF16)
        outs[m][tokens:, :] = dq_ref[0, m]


def early_back(rounds, *refs):
    (interval, x0_ref, n1_ref, dx1_ref, rows_ref, gathered_ref, probs_ref, picked_ref) = refs[:8]
    (fields_ref, mask_ref, fused_ref, agg_ref, embed_ref, probe_ref, qkv_w, mod_s) = refs[8:16]
    units = refs[16 : 16 + CUTS * rounds]
    outs = refs[16 + CUTS * rounds + 2 :]
    (keep_ref, send_ref) = outs[:2]
    unit_s, dqkv_s, ds_s, acc, mix, dscore, dmod_ref, lines_s = outs[2:]
    item = pl.program_id(0)
    grp, seq = place()
    tokens = x0_ref.shape[0]
    half = tokens // 2
    qkv_at = 3 * D + OUTP

    @pl.when(item == 0)
    def _():
        a = seq // (lax.axis_size("seq") // CUTS)
        for r in range(rounds):
            for m in range(CUTS):
                unit_s[CUTS * r + jnp.bitwise_xor(a, m)] = units[CUTS * r + m][...]
        acc[...] = jnp.zeros_like(acc)
        mix[...] = jnp.zeros_like(mix)
        dscore[...] = jnp.zeros_like(dscore)
        dmod_ref[...] = jnp.zeros_like(dmod_ref)

    low = half_low((half, 128))
    for h in range(HEADS):
        dqkv_s[:, h * 128 : (h + 1) * 128] = unit_s[HEADS * item + h, :tokens, :]
    for j in range(HEADS // 2):
        one = unit_s[HEADS * item + 2 * j, tokens:, :].astype(F32)
        two = unit_s[HEADS * item + 2 * j + 1, tokens:, :].astype(F32)
        lanes = slice(2 * D + j * 128, 2 * D + (j + 1) * 128)
        dqkv_s[:half, lanes] = jnp.where(low, one, swap_halves(two)).astype(BF16)
        dqkv_s[half:, lanes] = jnp.where(low, swap_halves(one), two).astype(BF16)
    dqkv = dqkv_s[...]
    which = interval[item]
    mod = mod_s[pl.ds(which, 1), :]
    acc[:, qkv_at:] += tn(n1_ref[...], dqkv)
    dn1 = nt(dqkv, qkv_w[...])
    normed, rstd = standardize(x0_ref[...])
    d_shift = jnp.sum(dn1, axis=0, keepdims=True)
    d_scale = jnp.sum(dn1 * normed, axis=0, keepdims=True)
    dx0 = (
        dx1_ref[...] + standardize_back(dn1 * (1.0 + mod[:, D : 2 * D]), normed, rstd)
    ).astype(BF16)
    rows = rows_ref[0]
    for k, row in enumerate([d_shift, d_scale] + [rows[r : r + 1] for r in range(4)]):
        dmod_ref[pl.ds(which, 1), k * D : (k + 1) * D] += row

    acc[:, 2 * D : 3 * D] += tn(gathered_ref[...], dx0)
    dagg = nt(agg_ref[:, 2 * D :], dx0)
    fields = fields_ref[0]
    wide_fields = fields.astype(F32)
    keep = mask_ref[0] > 0
    expand = ones_where(spread())
    upper = iota((128, tokens), 0) < HEAD
    for j in range(HEADS // 2):
        pair = slice(j * 128, (j + 1) * 128)
        both = None
        for h in (2 * j, 2 * j + 1):
            mine = upper if h % 2 == 0 else jnp.logical_not(upper)
            dpart = jnp.where(mine, dagg[pair], 0.0).astype(BF16)
            part = nt(picked_ref[h, 0], dpart)
            both = part if both is None else both + part
            spreaded = (nn(fused_ref[:, pair], dpart) * wide_fields).astype(BF16)
            dprobs = nn(expand, spreaded)
            probs = probs_ref[0, h * VARP : (h + 1) * VARP, :]
            ds = probs * (dprobs - jnp.sum(probs * dprobs, axis=0, keepdims=True))
            ds_s[h * VARP : (h + 1) * VARP, :] = jnp.where(keep, ds, 0.0).astype(BF16)
        mix[:, pair] += both
    dscore[...] += nt(ds_s[...], fields)

    @pl.when(item == pl.num_programs(0) - 1)
    def _():
        lines = iota((128, OUT), 0)
        owned = spread()
        drows = jnp.zeros((128, OUT), F32)
        for h in range(HEADS):
            mine = dscore[h * VARP : (h + 1) * VARP, :]
            line = jnp.sum(jnp.where(owned, mine, 0.0), axis=0, keepdims=True) * SCALE
            drows = drows + jnp.where(lines == h, line, 0.0)
        drows = drows.astype(BF16)
        mixed = mix[...].astype(BF16)
        embed = embed_ref[:, :OUT]
        acc[:, 3 * D : 3 * D + OUT] = nt(agg_ref[:, D : 2 * D], mixed) + nn(probe_ref[...], drows)
        acc[:, D : 2 * D] = nn(embed, mixed)
        dprobe = nt(embed, drows)
        heads = jnp.where(iota((128, D), 1) // HEAD == iota((128, D), 0), 1.0, 0.0).astype(BF16)
        coarse = dprobe.astype(BF16)
        fine = (dprobe - coarse.astype(F32)).astype(BF16)
        by_column = nn(coarse, heads) + nn(fine, heads)
        eye = iota((D, D), 0) == iota((D, D), 1)
        query = embed_ref[:, OUT : OUT + 1].astype(F32)
        query_row = jnp.sum(jnp.where(eye, query, 0.0), axis=0, keepdims=True)
        acc[:, :D] = by_column * query_row
        dquery = jnp.sum(agg_ref[:, :D].astype(F32) * by_column, axis=0, keepdims=True)
        column = jnp.sum(jnp.where(eye, dquery, 0.0), axis=1, keepdims=True)
        acc[:, 3 * D + OUT : 3 * D + OUTP] = jnp.where(
            iota((D, OUTP - OUT), 1) == 0, column, 0.0
        )
        split_rows(acc, grp, keep_ref, send_ref)
        lines_s[...] = jnp.zeros_like(lines_s)
        for t in range(6 * D // 128):
            lines_s[4 * t : 4 * t + 3, :] = dmod_ref[0:3, t * 128 : (t + 1) * 128]
        rows = keep_ref.shape[1]
        for t in range(mod_tiles(rows)):
            tile = lines_s[t * rows : (t + 1) * rows, :].astype(BF16)
            at = acc.shape[1] + t * 128
            for j in range(keep_ref.shape[0]):
                keep_ref[j, :, at : at + 128] = tile
                send_ref[j, :, at : at + 128] = tile


def mod_tiles(rows):
    return -(-4 * (6 * D // 128) // rows)


def shares_of():
    shares = lax.axis_size("seq") // CUTS
    _, seq = place()
    return shares, seq // shares, lax.rem(seq, shares)


def added(refs, at=None):
    total = None
    for ref in refs:
        value = (ref[...] if at is None else ref[at]).astype(F32)
        total = value if total is None else total + value
    return total


def sum_cores(pairs, *refs):
    (keep_ref, got_ref), outs, table = refs[:2], refs[2:-1], refs[-1]
    shares, _, share = shares_of()
    first, second = outs[:pairs], outs[pairs:]
    half = table.shape[1] // 2
    size = half // shares
    rows, cols = keep_ref.shape[1:]
    per = rows // 16
    if 2 * half > per * (cols // 128):
        table[...] = jnp.zeros_like(table)
    for j in range(pairs):
        total = (keep_ref[j].astype(F32) + got_ref[j].astype(F32)).astype(BF16)
        for t in range(cols // 128):
            for g in range(per):
                table[j, t * per + g] = total[g * 16 : (g + 1) * 16, t * 128 : (t + 1) * 128]
        first[j][...] = table[j, :half]
        for n in range(shares):
            at = half + jnp.bitwise_xor(share, n) * size
            second[n][j * size : (j + 1) * size] = table[j, pl.ds(at, size)]


def sum_both(pairs, shares, *refs):
    by_grp, by_share = refs[:pairs], refs[pairs : pairs + shares]
    outs, (table,) = refs[pairs + shares : -1], refs[-1:]
    _, _, share = shares_of()
    table[...] = added(by_grp).astype(BF16)
    size = outs[0].shape[0]
    for n in range(shares):
        outs[n][...] = table[pl.ds(jnp.bitwise_xor(share, n) * size, size)]
    for j in range(pairs):
        at = slice(j * size, (j + 1) * size)
        outs[shares + j][...] = added(by_share, at).astype(BF16)


def sum_both_again(pairs, shares, *refs):
    refs = refs[1:]
    by_share, by_grp = refs[:shares], refs[shares : shares + pairs]
    outs, (table,) = refs[pairs + shares : -1], refs[-1:]
    _, cut, _ = shares_of()
    size = outs[0].shape[0] // 2
    table[0] = added(by_share).astype(BF16)
    table[1] = added(by_grp).astype(BF16)
    for m in range(CUTS):
        at = pl.ds(jnp.bitwise_xor(cut, m) * size, size)
        outs[m][:size] = table[0, at]
        outs[m][size:] = table[1, at]


def sum_pieces(*refs):
    sources, (out_ref, square_ref) = refs[1:-2], refs[-2:]
    total = added(sources)
    out_ref[...] = total.astype(BF16)
    square_ref[...] = jnp.sum(total * total, axis=0)


def sum_late(start, stop, *refs):
    early_ref, loss_ref, lead_ref = refs[:3]
    sources, (out_ref, square_ref) = refs[3:-2], refs[-2:]
    grp, _ = place()
    shares, cut, share = shares_of()
    rows = lead_ref.shape[0] // lax.axis_size("grp")
    lead = lead_ref[pl.ds(pl.multiple_of(grp * rows, 16), rows), :].astype(F32)
    cols = [lead[:, g : g + 1] for g in range(3)]

    def gram(f, g):
        return jnp.sum(cols[f] * cols[g], axis=0, keepdims=True)

    row = lax.rem(iota((16, 1), 0), 4)

    def pick(*values):
        out = jnp.zeros((16, 1), F32)
        for r, value in values:
            out = jnp.where(row == r, value, out)
        return out

    same = pick(*[(g, gram(g, g)) for g in range(3)])
    next_one = pick((1, 2 * gram(0, 1)), (2, 2 * gram(1, 2)))
    next_two = pick((2, 2 * gram(0, 2)))
    size = out_ref.shape[0] // 2
    plain = jnp.zeros((16, 128), F32)
    for half in range(2):
        for k in range(size):
            total = added(sources, half * size + k)
            out_ref[half * size + k] = total.astype(BF16)
            index = ((half * shares + share) * CUTS + cut) * size + k
            special = jnp.logical_and(index >= start, index < stop)
            square = total * total
            mixed = (
                square * same
                + total * pltpu.roll(total, 1, 0) * next_one
                + total * pltpu.roll(total, 2, 0) * next_two
            )
            plain = plain + jnp.where(special, mixed, square)
    squares = jnp.sum(jnp.sum(plain + early_ref[...], axis=0, keepdims=True), axis=1, keepdims=True)
    which = iota((8, 128), 0)
    square_ref[...] = jnp.where(which == 0, loss_ref[...], squares)


def stack(*refs):
    for m, ref in enumerate(refs[1:-1]):
        refs[-1][m] = ref[...]


def step_values(param, first, second, grad):
    first = beta_first * first + (1.0 - beta_first) * grad
    second = beta_second * second + (1.0 - beta_second) * grad * grad
    mean_hat = first / (1.0 - beta_first**STEP)
    var_hat = second / (1.0 - beta_second**STEP)
    param = param - learn_rate * (
        mean_hat / (jnp.sqrt(var_hat) + adam_epsilon) + decay_rate * param
    )
    return param, first, second, param.astype(BF16)


def optimize(shares, *refs):
    reduced_ref, lead_ref = refs[:2]
    early = refs[2 : 2 + shares]
    late = refs[2 + shares : 2 + 2 * shares]
    wide = refs[2 + 2 * shares : 5 + 2 * shares]
    tall = refs[5 + 2 * shares : 8 + 2 * shares]
    query = refs[8 + 2 * shares : 11 + 2 * shares]
    outs = refs[11 + 2 * shares :]
    norm_ref, wide_out, tall_out, query_out = outs[0], outs[1:5], outs[5:9], outs[9:13]
    early_s, late_s = outs[13:]
    grp, _ = place()
    _, cut, share = shares_of()
    for table, stacks in ((early_s, early), (late_s, late)):
        size = stacks[0].shape[1] // 2
        for n, ref in enumerate(stacks):
            for m in range(CUTS):
                for half in range(2):
                    at = (half * shares + jnp.bitwise_xor(share, n)) * CUTS
                    at = (at + jnp.bitwise_xor(cut, m)) * size
                    table[pl.ds(at, size)] = ref[m, half * size : (half + 1) * size]
    norm = jnp.sqrt(reduced_ref[1:2, 0:1])
    norm_ref[...] = jnp.broadcast_to(norm, norm_ref.shape)
    factor = jnp.minimum(1.0, clip_limit / (norm + 1e-06))
    rows = wide[0].shape[0]
    per = rows // 16

    def tile(table, t):
        return jnp.concatenate([table[t * per + g] for g in range(per)], axis=0).astype(F32)

    def put(ins, targets, at, grad):
        new = step_values(*[r[at] for r in ins], grad * factor)
        for ref, value in zip(targets, new):
            ref[at] = value

    def at(t, width=128):
        return (slice(None), slice(t * 128, t * 128 + width))

    low = half_low((rows, 128))
    for t in range(9):
        put(wide, wide_out, at(t), tile(late_s, t))
    lead = lead_ref[pl.ds(pl.multiple_of(grp * rows, 16), rows), :].astype(F32)
    lines = jnp.concatenate([tile(late_s, 27 + t) for t in range(mod_tiles(rows))], axis=0)
    for t in range(18):
        grad = lead[:, 0:1] * lines[4 * t : 4 * t + 1]
        for g in (1, 2):
            grad = grad + lead[:, g : g + 1] * lines[4 * t + g : 4 * t + g + 1]
        put(wide, wide_out, at(9 + t), grad)
    qkv = 18
    for j in range(3):
        put(wide, wide_out, at(27 + j), tile(late_s, qkv + 6 + j))
        one, two = tile(late_s, qkv + 2 * j), tile(late_s, qkv + 2 * j + 1)
        put(wide, wide_out, at(30 + j), jnp.where(low, one, swap_halves(two)))
        put(wide, wide_out, at(33 + j), jnp.where(low, swap_halves(one), two))
    for t in range(15 + 8):
        put(wide, wide_out, at(36 + t), tile(early_s, t))
    rest = OUT - 8 * 128
    put(wide, wide_out, at(59, rest), tile(early_s, 23)[:, :rest])
    for t in range(8):
        put(tall, tall_out, at(t), tile(late_s, 9 + t))
    last = tile(late_s, 17)
    lane = iota((rows, 128), 1)
    for t in range(FF // 128):
        turned = pltpu.roll(tile(early_s, 24 + t), rest, 1)
        put(tall, tall_out, at(8 + t), jnp.where(lane < rest, last, turned))
        if t == 0:
            eye = iota((rows, rows), 0) == iota((rows, rows), 1)
            grad = jnp.sum(jnp.where(eye, last[:, rest : rest + 1], 0.0), axis=0, keepdims=True)
            put(query, query_out, (slice(None), slice(None)), grad)
        last = turned
    put(tall, tall_out, at(8 + FF // 128, rest), last[:, :rest])


def shift(value, axis, bit):
    size = lax.axis_size(axis)
    return lax.ppermute(value, axis, [(i, i ^ bit) for i in range(size)])


def gather_blocks(own, group):
    blocks = {0: own}
    for j in range(2, group, 2):
        blocks[j] = shift(own, "grp", j)
    for j in range(0, group, 2):
        blocks[j + 1] = shift(blocks[j], "grp", 1)
    return [blocks[j] for j in range(group)]


def granules(rows, cols, shares):
    unit = 2 * shares * CUTS
    return -(-(rows // 16) * (cols // 128) // unit) * unit


def piece_shape(count):
    return sds((count, 16, 128), BF16)


def reduce_cores(keep, send):
    pairs, rows, cols = keep.shape
    shares = lax.axis_size("seq") // CUTS
    count = granules(rows, cols, shares)
    got = shift(send, "grp", 1)
    results = call(
        functools.partial(sum_cores, pairs),
        [piece_shape(count // 2)] * pairs + [piece_shape(count // 2 // shares * pairs)] * shares,
        scratch=[pltpu.VMEM((pairs, count, 16, 128), BF16)],
    )(keep, got)
    return results[:pairs], results[pairs:]


def reduce_once(by_grp, by_share):
    pairs, shares = len(by_grp), len(by_share)
    size = by_grp[0].shape[0] // shares
    results = call(
        functools.partial(sum_both, pairs, shares),
        [piece_shape(size)] * (pairs + shares),
        scratch=[pltpu.VMEM(by_grp[0].shape, BF16)],
    )(
        by_grp[0],
        *[shift(by_grp[j], "grp", 2 * j) for j in range(1, pairs)],
        by_share[0],
        *[shift(by_share[n], "seq", n) for n in range(1, shares)],
    )
    return results[:shares], results[shares:]


def exchange_again(by_share, by_grp):
    pairs, shares = len(by_grp), len(by_share)
    return [by_share[0]] + [shift(by_share[n], "seq", n) for n in range(1, shares)], [
        by_grp[0]
    ] + [shift(by_grp[j], "grp", 2 * j) for j in range(1, pairs)]


def reduce_twice(by_share, by_grp, token):
    pairs, shares = len(by_grp), len(by_share)
    size = by_grp[0].shape[0]
    return call(
        functools.partial(sum_both_again, pairs, shares),
        [piece_shape(2 * size // CUTS)] * CUTS,
        in_specs=[anywhere()] + [whole()] * (pairs + shares),
        scratch=[pltpu.VMEM((2, size, 16, 128), BF16)],
    )(token, *by_share, *by_grp)


def over_cuts(first, others=None):
    shares = lax.axis_size("seq") // CUTS
    sent = [first] * (CUTS - 1) if others is None else others
    return [first] + [shift(sent[m - 1], "seq", m * shares) for m in range(1, CUTS)]


def gather_pieces(piece, token):
    shares = lax.axis_size("seq") // CUTS
    column = call(
        stack, sds((CUTS,) + piece.shape, BF16), in_specs=[anywhere()] + [whole()] * CUTS
    )(token, *over_cuts(piece))
    return [column] + [shift(column, "seq", n) for n in range(1, shares)]


def butterfly(value, axis, bit, stop):
    while bit < stop:
        value = value + shift(value, axis, bit)
        bit *= 2
    return value


def lead_table():
    half = D // 2
    hours = 6.0 * np.exp2(np.arange(3, dtype=np.float32))
    freqs = np.exp(-np.log(np.float32(1000.0)) * np.arange(half, dtype=np.float32) / half)
    angles = hours[None, :] * freqs.astype(np.float32)[:, None]
    waves = np.concatenate([np.sin(angles), np.cos(angles)], axis=0)
    table = np.zeros((D, 128), np.float32)
    table[:, :3] = waves / (1.0 + np.exp(-waves))
    return jnp.asarray(table).astype(BF16)


def cosine_table(count):
    line = np.arange(count, dtype=np.float32)
    return jnp.asarray(np.cos(np.pi * ((line + 0.5) / count - 0.5)).astype(np.float32))


def per_device(
    fields,
    targets,
    land_mask,
    interval,
    samples,
    wide_weights,
    wide_firsts,
    wide_seconds,
    tall_weights,
    tall_firsts,
    tall_seconds,
    query_vector,
    query_firsts,
    query_seconds,
):
    group = lax.axis_size("grp")
    parts = lax.axis_size("seq")
    shares = parts // CUTS
    rows, columns = wide_weights.shape
    items, tokens = fields.shape[:2]
    units = items * HEADS // CUTS
    every = items * tokens
    late_cols = D + FF + OUTP + FF

    query_row = query_vector.reshape(1, rows)
    tall = [x.T for x in (tall_weights, tall_firsts, tall_seconds)]
    lead = lead_table()
    cosines = cosine_table(tokens // COLS * parts)
    fields = fields.transpose(0, 2, 1)
    mask = jnp.pad(
        land_mask.transpose(0, 2, 1), ((0, 0), (0, VARP - VARS), (0, 0)), constant_values=-1
    )

    def columns_of(index):
        return pl.BlockSpec((rows, 3 * D), lambda i: (0, index))

    first_own = call(
        pack_first,
        sds((rows + RIDERS, 9 * D), BF16),
        grid=(1,),
        in_specs=[smem(), smem()]
        + [columns_of(i) for i in (0, 1, 2, 3, 0)]
        + [pl.BlockSpec((1, rows), lambda i: (0, 0)), whole(), whole()],
        out_specs=whole(),
        scratch=[pltpu.VMEM((RIDERS, 9 * D), F32)],
        us=3,
        limit=62,
    )(samples, cosines, *[wide_weights] * 4, tall[0], query_row, lead, mask)
    first = gather_blocks(first_own, group)
    late_own = call(
        pack_late,
        sds((rows, late_cols), BF16),
        grid=(1,),
        in_specs=[columns_of(4), columns_of(5), columns_of(6), whole(), anywhere()],
        out_specs=whole(),
        us=2,
        limit=62,
    )(wide_weights, wide_weights, wide_weights, tall[0], first_own)
    late_blocks = gather_blocks(late_own, group)

    by_item = pl.BlockSpec((tokens, D), lambda i: (i, 0))

    def item_block(width):
        return pl.BlockSpec((1, tokens, width), lambda i: (i, 0, 0))

    def lane_block(height):
        return pl.BlockSpec((1, height, tokens), lambda i: (i, 0, 0))

    heads_spec = pl.BlockSpec((HEADS, 1, OUT, tokens), lambda i: (0, i, 0, 0))
    packed = tokens + tokens // 2 + 16

    results = call(
        functools.partial(aggregate, group),
        [
            in_hbm((items, HEADS * VARP, tokens), F32),
            in_hbm((HEADS, items, OUT, tokens), BF16),
            in_hbm((every, D), BF16),
            in_hbm((every, D), F32),
            in_hbm((every, D), BF16),
            in_hbm((D, 3 * D), BF16),
            in_hbm((D, OUTP), BF16),
            in_hbm((D, 3 * D), BF16),
            in_hbm((OUT, D), BF16),
            in_hbm((D, 128), BF16),
            in_hbm((8, 6 * D), F32),
        ]
        + [sds((units, packed, 128), BF16)] * CUTS,
        grid=(items,),
        in_specs=[smem(), lane_block(OUT), lane_block(VARP)] + [whole()] * group,
        out_specs=[lane_block(HEADS * VARP), heads_spec, by_item, by_item, by_item]
        + [whole()] * (6 + CUTS),
        scratch=[
            pltpu.VMEM((HEADS * VARP, OUT), BF16),
            pltpu.VMEM((D, OUT), BF16),
            pltpu.VMEM((D, tokens), F32),
            pltpu.VMEM((items * HEADS, packed, 128), BF16),
        ],
        us=12,
        limit=44,
    )(interval, fields, mask, *first)
    probs, picked, gathered, x0, n1 = results[:5]
    agg_weights, embed, qkv_weights, fused_w, probe, mods = results[5:11]
    dealt = results[11:]

    own = over_cuts(dealt[0], dealt[1:])
    others = [shift(own[m], "seq", n) for n in range(1, shares) for m in range(CUTS)]
    keys_total = parts * tokens

    unit_in = pl.BlockSpec((1, packed, 128), lambda u: (u, 0, 0))
    half_in = pl.BlockSpec((1, tokens // 2, 128), lambda u: (u, 0, 0))
    kept_spec = pl.BlockSpec((1, CUTS, tokens, 128), lambda u: (u, 0, 0, 0))
    lse_spec = pl.BlockSpec((1, CUTS, 8, tokens), lambda u: (u, 0, 0, 0))
    pack_spec = pl.BlockSpec((1, CUTS, tokens // 2, 128), lambda u: (u, 0, 0, 0))
    half_out = sds((units, tokens // 2, 128), BF16)
    results = call(
        functools.partial(attend, shares),
        [half_out] * CUTS
        + [
            in_hbm((units, CUTS, tokens, 128), F32),
            in_hbm((units, CUTS, 8, tokens), F32),
            in_hbm((8, 128), F32),
        ],
        grid=(units,),
        in_specs=[unit_in] * (CUTS * shares),
        out_specs=[half_in] * CUTS + [kept_spec, lse_spec, whole()],
        scratch=[pltpu.VMEM((keys_total, 128), BF16)],
        us=9,
        limit=32 if shares > 2 else 24,
    )(*own, *others)
    backs, (kept, lse, weight_sum) = results[:CUTS], results[CUTS:]
    heads_in = over_cuts(backs[0], backs[1:])

    saved = [D, D, D, FF, D, OUT, D, FF]
    results = call(
        functools.partial(middle, group),
        [in_hbm((every, D), F32), in_hbm((items, 8, D), F32), in_hbm((8, 128), F32)]
        + [half_out] * CUTS
        + [sds((every, width), BF16) for width in saved],
        grid=(items,),
        in_specs=[smem(), smem(), smem(), whole(), by_item, item_block(OUT), lane_block(VARP)]
        + [whole()] * (CUTS + group + 1),
        out_specs=[by_item, pl.BlockSpec((1, 8, D), lambda i: (i, 0, 0))]
        + [whole()] * (1 + CUTS)
        + [pl.BlockSpec((tokens, width), lambda i: (i, 0)) for width in saved],
        scratch=[
            pltpu.VMEM((D, late_cols), BF16),
            pltpu.VMEM((items * HEADS, tokens // 2, 128), BF16),
            pltpu.VMEM((items * HEADS, tokens // 2, 128), BF16),
        ],
        us=11,
        limit=40,
    )(
        interval,
        samples,
        cosines,
        weight_sum,
        x0,
        targets,
        mask,
        *heads_in,
        *late_blocks,
        mods,
    )
    dx1, mod_rows, loss = results[:3]
    sends, operands = results[3 : 3 + CUTS], results[3 + CUTS :]
    early_keep, early_send = call(
        middle_weights,
        [sds((group // 2, rows, late_cols), BF16)] * 2,
        scratch=[pltpu.VMEM((D, late_cols), F32)],
        us=6,
        limit=30,
    )(*operands)
    grads_in = over_cuts(sends[0], sends[1:])

    early_first = reduce_cores(early_keep, early_send)

    def of_unit(u, *shape):
        return pl.BlockSpec((1,) + shape, lambda i: (u,) + (0,) * len(shape))

    def back_of(u, *before):
        results = call(
            functools.partial(attend_back, shares),
            [sds((1, CUTS, tokens // 2, 128), BF16)]
            + [sds((1, CUTS, tokens, 128), BF16)] * shares,
            grid=(1,),
            in_specs=[of_unit(u, packed, 128)] * (CUTS * shares)
            + [of_unit(u, tokens // 2, 128)] * CUTS
            + [of_unit(u, CUTS, tokens, 128), of_unit(u, CUTS, 8, tokens)]
            + [anywhere()] * 2,
            out_specs=[whole()] * (1 + shares),
            scratch=[
                pltpu.VMEM((keys_total, 128), BF16),
                pltpu.VMEM((128, keys_total), BF16),
                pltpu.VMEM((keys_total, 128), F32),
            ],
            us=0.5,
            limit=26,
            )(*own, *others, *grads_in, kept, lse, *before)
        far = results[2:]
        return results[:2], [shift(far[n], "seq", n + 1) for n in range(shares - 1)]

    def joined(near, far):
        dealt = call(
            functools.partial(join_back, shares),
            [sds((tokens + tokens // 2, 128), BF16)] * CUTS,
        )(*near, *far)
        return over_cuts(dealt[0], dealt[1:])

    partial_sums, units_in = [], []
    for u in range(units):
        before = early_keep if u == 0 else partial_sums[u - 1][0][0]
        partial_sums.append(back_of(u, before, early_first[0][0] if u == 2 else early_keep))
        if u >= 1:
            units_in.append(joined(*partial_sums[u - 1]))
    units_in.append(joined(*partial_sums[-1]))
    early_second = reduce_once(*early_first)
    early_second = exchange_again(*early_second)

    first_cols = 3 * D + OUTP + 3 * D
    sent_cols = first_cols + mod_tiles(rows) * 128
    late_keep, late_send = call(
        functools.partial(early_back, units),
        [
            sds((group // 2, rows, sent_cols), BF16),
            sds((group // 2, rows, sent_cols), BF16),
        ],
        grid=(items,),
        in_specs=[
            smem(),
            by_item,
            by_item,
            by_item,
            pl.BlockSpec((1, 8, D), lambda i: (i, 0, 0)),
            by_item,
            lane_block(HEADS * VARP),
            heads_spec,
            lane_block(OUT),
            lane_block(VARP),
        ]
        + [whole()] * (6 + CUTS * units)
        + [anywhere()] * 2,
        out_specs=[whole()] * 2,
        scratch=[
            pltpu.VMEM((items * HEADS, tokens + tokens // 2, 128), BF16),
            pltpu.VMEM((tokens, 3 * D), BF16),
            pltpu.VMEM((HEADS * VARP, tokens), BF16),
            pltpu.VMEM((D, first_cols), F32),
            pltpu.VMEM((OUT, D), F32),
            pltpu.VMEM((HEADS * VARP, OUT), F32),
            pltpu.VMEM((8, 6 * D), F32),
            pltpu.VMEM((mod_tiles(rows) * rows, 128), F32),
        ],
        us=20,
        limit=44,
    )(
        interval,
        x0,
        n1,
        dx1,
        mod_rows,
        gathered,
        probs,
        picked,
        fields,
        mask,
        fused_w,
        agg_weights,
        embed,
        probe,
        qkv_weights,
        mods,
        *[x for unit in units_in for x in unit],
        early_second[0][1],
        early_second[1][1],
    )
    late_first = reduce_cores(late_keep, late_send)
    early_third = reduce_twice(*early_second, late_first[0][0])
    late_second = reduce_once(*late_first)
    early_pieces = over_cuts(early_third[0], early_third[1:])
    early_piece, early_squares = call(
        sum_pieces,
        [piece_shape(early_pieces[0].shape[0]), sds((16, 128), F32)],
        in_specs=[anywhere()] + [whole()] * CUTS,
    )(late_second[0][0], *early_pieces)
    late_third = reduce_twice(*exchange_again(*late_second), late_second[0][0])
    early_all = gather_pieces(early_piece, late_third[0])
    late_pieces = over_cuts(late_third[0], late_third[1:])
    start = (rows // 16) * (first_cols // 128)
    stop = (rows // 16) * (sent_cols // 128)
    late_piece, reduced = call(
        functools.partial(sum_late, start, stop),
        [piece_shape(late_pieces[0].shape[0]), sds((8, 128), F32)],
    )(early_squares, loss, lead, *late_pieces)
    reduced = butterfly(reduced, "seq", 1, shares)
    reduced = butterfly(reduced, "grp", 1, group)
    late_all = gather_pieces(late_piece, reduced)
    reduced = butterfly(reduced, "seq", shares, parts)

    def like(x, dtype=F32):
        return sds(x.shape, dtype)

    results = call(
        functools.partial(optimize, shares),
        [sds((8, 128), F32)]
        + [like(wide_weights)] * 3
        + [like(wide_weights, BF16)]
        + [like(tall[0])] * 3
        + [like(tall[0], BF16)]
        + [like(query_row)] * 3
        + [like(query_row, BF16)],
        scratch=[
            pltpu.VMEM((parts * early_piece.shape[0], 16, 128), BF16),
            pltpu.VMEM((parts * late_piece.shape[0], 16, 128), BF16),
        ],
        us=10,
        limit=34,
    )(
        reduced,
        lead,
        *early_all,
        *late_all,
        wide_weights,
        wide_firsts,
        wide_seconds,
        *tall,
        query_row,
        query_firsts.reshape(1, rows),
        query_seconds.reshape(1, rows),
    )
    norm = results[0]
    tall_out = tuple(r.T for r in results[5:9])
    query_out = tuple(r.reshape(rows) for r in results[9:13])
    return (
        (reduced[0, 0], weight_sum[0, 0], norm[0, 0])
        + tuple(results[1:5])
        + tall_out
        + query_out
    )


def solution(mesh):
    placed = (
        P("grp", "seq", None),
        P("grp", "seq", None),
        P("grp", "seq", None),
        P("grp"),
        P("grp"),
        P("grp", None),
        P("grp", None),
        P("grp", None),
        P(None, "grp"),
        P(None, "grp"),
        P(None, "grp"),
        P("grp"),
        P("grp"),
        P("grp"),
    )
    return jax.shard_map(
        per_device,
        mesh=mesh,
        in_specs=placed,
        out_specs=(
            P(),
            P(),
            P(),
            P("grp", None),
            P("grp", None),
            P("grp", None),
            P("grp", None),
            P(None, "grp"),
            P(None, "grp"),
            P(None, "grp"),
            P(None, "grp"),
            P("grp"),
            P("grp"),
            P("grp"),
            P("grp"),
        ),
        check_vma=False,
    )
```

```python
import functools

import jax
import numpy as np
import jax.numpy as jnp
from jax import lax
from jax.experimental import pallas as pl
from jax.experimental.pallas import tpu as pltpu
from jax.sharding import PartitionSpec as P

D = 384
HEADS = 6
HEAD = 64
FF = 1536
VARS = 69
PIX = 16
OUT = VARS * PIX
OUTP = 1152
VARP = 80
COLS = 128
STEP = 5
CUTS = 4
SCALE = HEAD**-0.5
LOG2E = 1.4426950408889634

beta_first = 0.5
beta_second = 0.5
learn_rate = 0.1
decay_rate = 0.01
adam_epsilon = 1e-08
clip_limit = 0.05
norm_epsilon = 1e-06
masked_score = -1e30

F32 = jnp.float32
BF16 = jnp.bfloat16
MIB = 1024 * 1024
RIDERS = 32


def dot(left, right, a, b):
    return lax.dot_general(left, right, (((a,), (b,)), ((), ())), preferred_element_type=F32)


def nn(left, right):
    return dot(left, right, 1, 0)


def nt(left, right):
    return dot(left, right, 1, 1)


def tn(left, right):
    return dot(left, right, 0, 0)


def iota(shape, dim):
    return lax.broadcasted_iota(jnp.int32, shape, dim)


def half_low(shape):
    return iota(shape, len(shape) - 1) < HEAD


def swap_halves(tile):
    return pltpu.roll(tile, HEAD, 1)


def spread():
    return iota((VARP, OUT), 1) // PIX == iota((VARP, OUT), 0)


def ones_where(mask):
    return jnp.where(mask, 1.0, 0.0).astype(BF16)


def place():
    grp = lax.axis_index("grp")
    seq = lax.axis_index("seq")
    return grp, seq


def call(
    kernel, outs, grid=(), in_specs=None, out_specs=None, scratch=(), us=1, limit=34, after=()
):
    def run(*args):
        count = len(args)

        def body(*refs):
            kernel(*refs[:count], *refs[count + len(after) :])

        kw = {} if out_specs is None else {"out_specs": out_specs}
        return pl.pallas_call(
            body,
            out_shape=outs,
            grid=grid,
            in_specs=(list(in_specs) if in_specs else [whole()] * count)
            + [pl.BlockSpec(memory_space=pl.ANY)] * len(after),
            scratch_shapes=list(scratch),
            cost_estimate=pl.CostEstimate(
                flops=int(us * 1.15e9), transcendentals=0, bytes_accessed=1024
            ),
            compiler_params=pltpu.CompilerParams(vmem_limit_bytes=limit * MIB),
            **kw,
        )(*args, *after)

    return run


def once_ready(value, after):
    space = pl.BlockSpec(memory_space=pl.ANY)
    return pl.pallas_call(
        lambda *refs: None,
        out_shape=jax.ShapeDtypeStruct(value.shape, value.dtype),
        in_specs=[space] * (1 + len(after)),
        out_specs=space,
        input_output_aliases={0: 0},
        cost_estimate=pl.CostEstimate(flops=1, transcendentals=0, bytes_accessed=1),
    )(value, *after)


def whole():
    return pl.BlockSpec(memory_space=pltpu.VMEM)


def smem():
    return pl.BlockSpec(memory_space=pltpu.SMEM)


def sds(shape, dtype):
    return jax.ShapeDtypeStruct(shape, dtype)


def in_hbm(shape, dtype):
    return pltpu.HBM(shape, dtype)


def standardize(x):
    centered = x - jnp.mean(x, axis=-1, keepdims=True)
    rstd = lax.rsqrt(jnp.mean(centered * centered, axis=-1, keepdims=True) + norm_epsilon)
    return centered * rstd, rstd


def standardize_back(grad, normed, rstd):
    return rstd * (
        grad
        - jnp.mean(grad, axis=-1, keepdims=True)
        - normed * jnp.mean(grad * normed, axis=-1, keepdims=True)
    )


def gelu_parts(x):
    k = 0.7978845608028654
    inner = k * (x + 0.044715 * x * x * x)
    t = jnp.tanh(inner)
    value = 0.5 * x * (1.0 + t)
    slope = 0.5 * (1.0 + t) + 0.5 * x * (1.0 - t * t) * k * (1.0 + 3 * 0.044715 * x * x)
    return value, slope


def pack_first(*refs):
    samples, cosines, agg_ref, mod_a, mod_b, wide_ref, tall_ref, query_ref = refs[:8]
    lead_ref, mask_ref, first_ref, second_ref, rider_s = refs[8:]
    rows = wide_ref.shape[0]
    grp, seq = place()
    first_ref[:, : 2 * D] = agg_ref[:, : 2 * D].astype(BF16)
    second_ref[:rows, :D] = agg_ref[:, 2 * D :].astype(BF16)
    eye = iota((rows, rows), 0) == iota((rows, rows), 1)
    column = jnp.sum(jnp.where(eye, query_ref[...], 0.0), axis=1, keepdims=True)
    lane = iota((rows, OUTP), 1)
    embed = jnp.where(lane < OUT, tall_ref[...], jnp.where(lane == OUT, column, 0.0))
    first_ref[:, 2 * D :] = embed.astype(BF16)
    low = half_low((rows, 128))
    for j in range(HEADS // 2):
        k = wide_ref[:, D + j * 128 : D + (j + 1) * 128]
        v = wide_ref[:, 2 * D + j * 128 : 2 * D + (j + 1) * 128]
        at = D + 2 * j * 128
        second_ref[:rows, at : at + 128] = jnp.where(low, k, swap_halves(v)).astype(BF16)
        second_ref[:rows, at + 128 : at + 256] = jnp.where(low, swap_halves(k), v).astype(BF16)
    second_ref[:rows, 3 * D :] = wide_ref[:, :D].astype(BF16)
    rider_s[...] = jnp.zeros_like(rider_s)

    def ride(row, value):
        for part in range(3):
            piece = value.astype(BF16).astype(F32)
            at = part * 8 + row
            rider_s[at : at + 1, : 3 * D] = piece
            value = value - piece

    lead = lead_ref[pl.ds(pl.multiple_of(grp * rows, 16), rows), :].astype(F32)
    for half, ref in ((0, mod_a), (1, mod_b)):
        mod = ref[...].astype(BF16).astype(F32)
        for g in range(3):
            ride(2 * g + half, jnp.sum(lead[:, g : g + 1] * mod, axis=0, keepdims=True))
    items, _, tokens = mask_ref.shape
    total = jnp.zeros((1, 1), F32)
    for i in range(items):
        present = jnp.maximum(mask_ref[i], 0).astype(F32)
        weighed = jnp.sum(present, axis=0, keepdims=True) * line_weights(
            samples[i], cosines, seq, iota((1, tokens), 1)
        )
        total = total + jnp.sum(weighed, axis=1, keepdims=True)
    ride(6, jnp.broadcast_to(total, (1, 3 * D)))
    second_ref[rows:, :] = rider_s[...].astype(BF16)


def line_weights(count, cosines, seq, position):
    lines = position.size // COLS
    value = jnp.zeros(position.shape, F32)
    for r in range(lines):
        value = jnp.where(position // COLS == r, cosines[seq * lines + r], value)
    return value * count.astype(F32)


def pack_late(wide_a, wide_b, wide_c, tall_ref, late_ref):
    rows = wide_a.shape[0]
    late_ref[:, : 3 * D] = wide_a[...].astype(BF16)
    late_ref[:, 3 * D : 6 * D] = wide_b[...].astype(BF16)
    rest = D + FF + OUT - 6 * D
    late_ref[:, 6 * D : D + FF + OUT] = wide_c[:, :rest].astype(BF16)
    late_ref[:, D + FF + OUT : D + FF + OUTP] = jnp.zeros((rows, OUTP - OUT), BF16)
    late_ref[:, D + FF + OUTP :] = tall_ref[:, OUT:].astype(BF16)


def assemble(target, blocks, grp, lo, hi):
    rows = target.shape[0] // len(blocks)
    for j, ref in enumerate(blocks):
        at = pl.multiple_of(jnp.bitwise_xor(grp, j) * rows, 16)
        target[pl.ds(at, rows), :] = ref[:rows, lo:hi]


def unride(target, blocks):
    target[...] = jnp.zeros_like(target)
    for g in range(4):
        for half in range(2):
            total = jnp.zeros((1, 3 * D), F32)
            for ref in blocks:
                for part in range(3):
                    at = ref.shape[0] - RIDERS + part * 8 + min(2 * g + half, 6)
                    total = total + ref[at : at + 1, : 3 * D].astype(F32)
            target[g : g + 1, half * 3 * D : (half + 1) * 3 * D] = total


def prepare(blocks, grp, outs, score_s, fused_s):
    (agg_ref, embed_ref, fused_ref, probe_ref) = outs
    assemble(agg_ref, blocks, grp, 0, 2 * D)
    assemble(embed_ref, blocks, grp, 2 * D, 2 * D + OUTP)
    query = embed_ref[:, OUT : OUT + 1].astype(F32)
    picked = jnp.where(iota((D, 128), 1) == iota((D, 128), 0) // HEAD, query, 0.0).astype(BF16)
    probe = nn(agg_ref[:, :D], picked).astype(BF16)
    probe_ref[...] = probe
    embed = embed_ref[:, :OUT]
    rows = tn(probe, embed) * SCALE
    mine = spread()
    for h in range(HEADS):
        score_s[h * VARP : (h + 1) * VARP, :] = jnp.where(mine, rows[h : h + 1, :], 0.0).astype(
            BF16
        )
    fused = tn(agg_ref[:, D:], embed)
    fused_s[...] = fused.astype(BF16)
    fused_ref[...] = fused.T.astype(BF16)


def aggregate(group, *refs):
    (fields_ref, mask_ref) = refs[:2]
    blocks, outs = refs[2 : 2 + group], refs[2 + group :]
    (probs_ref, picked_ref, gathered_ref), kept = outs[:3], outs[3:7]
    score_s, fused_s, turned_s = outs[7:]
    grp, _ = place()

    @pl.when(pl.program_id(0) == 0)
    def _():
        prepare(blocks, grp, kept, score_s, fused_s)

    fields = fields_ref[0]
    wide_fields = fields.astype(F32)
    mask = mask_ref[0]
    scores = nn(score_s[...], fields)
    expand = ones_where(iota((OUT, VARP), 0) // PIX == iota((OUT, VARP), 1))
    for h in range(HEADS):
        s = jnp.where(
            mask > 0,
            scores[h * VARP : (h + 1) * VARP],
            jnp.where(mask < 0, -3e38, masked_score),
        )
        e = jnp.exp(s - jnp.max(s, axis=0, keepdims=True))
        a = e / jnp.sum(e, axis=0, keepdims=True)
        probs_ref[0, h * VARP : (h + 1) * VARP, :] = a
        picked = (nn(expand, a.astype(BF16)) * wide_fields).astype(BF16)
        picked_ref[h, 0] = picked
        turned_s[h * HEAD : (h + 1) * HEAD, :] = nn(fused_s[h * HEAD : (h + 1) * HEAD, :], picked)
    gathered_ref[...] = turned_s[...].T.astype(BF16)


def project(group, *refs):
    (interval, gathered_ref), blocks, outs = refs[:2], refs[2 : 2 + group], refs[2 + group :]
    (x0_ref, n1_ref, weights, mod_s), units, (unit_s,) = outs[:4], outs[4:-1], outs[-1:]
    item = pl.program_id(0)
    grp, seq = place()
    tokens = gathered_ref.shape[0]

    @pl.when(item == 0)
    def _():
        assemble(weights, blocks, grp, 0, 4 * D)
        unride(mod_s, blocks)

    x0 = nn(gathered_ref[...], weights[:, :D])
    x0_ref[...] = x0
    mod = mod_s[pl.ds(interval[item], 1), :]
    normed, _ = standardize(x0)
    n1 = (normed * (1.0 + mod[:, D : 2 * D]) + mod[:, :D]).astype(BF16)
    n1_ref[...] = n1
    qkv = nn(n1, weights[:, D:])
    half = tokens // 2
    low = half_low((half, 128))
    packed = tokens + half
    for h in range(HEADS):
        unit_s[HEADS * item + h, :tokens, :] = qkv[:, h * 128 : (h + 1) * 128].astype(BF16)
    for j in range(HEADS // 2):
        pair = qkv[:, 2 * D + j * 128 : 2 * D + (j + 1) * 128] * (SCALE * LOG2E)
        top, bottom = pair[:half], pair[half:]
        unit_s[HEADS * item + 2 * j, tokens:packed, :] = jnp.where(
            low, top, swap_halves(bottom)
        ).astype(BF16)
        unit_s[HEADS * item + 2 * j + 1, tokens:packed, :] = jnp.where(
            low, swap_halves(top), bottom
        ).astype(BF16)

    @pl.when(item == pl.num_programs(0) - 1)
    def _():
        value = jnp.broadcast_to(mod_s[3:4, :128], (16, 128))
        high = value.astype(BF16)
        value = value - high.astype(F32)
        middle_part = value.astype(BF16)
        low_part = (value - middle_part.astype(F32)).astype(BF16)
        lane = iota((16, 128), 1)
        zero = jnp.zeros((16, 128), BF16)
        rides = jnp.where(
            lane < 32,
            high.astype(F32),
            jnp.where(
                lane < 64,
                middle_part.astype(F32),
                jnp.where(lane < 96, low_part.astype(F32), 0.0),
            ),
        ).astype(BF16)
        for u in range(unit_s.shape[0]):
            unit_s[u, packed:, :] = rides if u < CUTS else zero
        deal(units, unit_s, seq)


def deal(targets, source, seq):
    a = seq // (lax.axis_size("seq") // CUTS)
    for m in range(CUTS):
        for r in range(targets[m].shape[0]):
            targets[m][r] = source[CUTS * r + jnp.bitwise_xor(a, m)]


def collect(target, sources, seq):
    a = seq // (lax.axis_size("seq") // CUTS)
    for m in range(CUTS):
        for r in range(sources[m].shape[0]):
            target[CUTS * r + jnp.bitwise_xor(a, m)] = sources[m][r]


def unpack(pack, at_low):
    wide = pack.astype(F32)
    low = half_low(wide.shape)
    if at_low:
        both = [jnp.where(low, wide, 0.0), jnp.where(low, swap_halves(wide), 0.0)]
    else:
        both = [jnp.where(low, 0.0, swap_halves(wide)), jnp.where(low, 0.0, wide)]
    return jnp.concatenate(both, axis=0).astype(BF16)


def pack_rows(tile, at_low):
    half = tile.shape[0] // 2
    top, bottom = tile[:half], tile[half:]
    low = half_low(top.shape)
    if at_low:
        return jnp.where(low, top, swap_halves(bottom))
    return jnp.where(low, swap_halves(top), bottom)


def attend(shares, *refs):
    own = refs[:CUTS]
    others = refs[CUTS : CUTS * shares]
    backs = refs[CUTS * shares : CUTS * shares + CUTS]
    kept_ref, lse_ref, weight_ref, keys_s = refs[CUTS * shares + CUTS :]
    tokens = kept_ref.shape[2]
    packed = tokens + tokens // 2

    @pl.when(pl.program_id(0) == 0)
    def _():
        total = jnp.zeros((16, 128), F32)
        for ref in own + others:
            total = total + ref[0, packed:, :].astype(F32)
        total = jnp.sum(total[0:8], axis=1, keepdims=True) / 32.0
        weight_ref[...] = jnp.broadcast_to(total, (8, 128))

    for n, ref in enumerate(own + others):
        keys_s[n * tokens : (n + 1) * tokens, :] = ref[0, :tokens, :]
    keys = keys_s[...]
    values = jnp.where(half_low(keys.shape), jnp.ones_like(keys), keys)

    def scores_of(m):
        return nt(unpack(own[m][0, tokens:packed, :], True), keys)

    scores = scores_of(0)
    for m in range(CUTS):
        later = scores_of(m + 1) if m + 1 < CUTS else None
        top = jnp.max(scores, axis=1, keepdims=True)
        out = nn(jnp.exp2(scores - top).astype(BF16), values)
        total = out[:, 0:1]
        out = out / total
        lse = jnp.broadcast_to(top + jnp.log2(total), (tokens, 128)).T
        lse_ref[0, m] = lse[:8]
        kept_ref[0, m] = out
        backs[m][0] = pack_rows(out, False).astype(BF16)
        scores = later


def middle(group, *refs):
    (interval, samples, cosines, sum_ref, x0_ref, fields_ref, mask_ref) = refs[:7]
    heads_in = refs[7 : 7 + CUTS]
    blocks = refs[7 + CUTS : 7 + CUTS + group]
    mod_s = refs[7 + CUTS + group]
    outs = refs[7 + CUTS + group + 1 :]
    (dx1_ref, rows_ref, loss_ref) = outs[:3]
    sends = outs[3 : 3 + CUTS]
    attended_s, db1_ref, n2_ref, dh_ref, nf_ref, dpred_ref, db2_ref, active_ref = outs[
        3 + CUTS : 11 + CUTS
    ]
    weights, head_s, grad_s = outs[11 + CUTS :]
    item = pl.program_id(0)
    grp, seq = place()
    tokens = x0_ref.shape[0]
    half = tokens // 2

    @pl.when(item == 0)
    def _():
        assemble(weights, blocks, grp, 0, D + FF + OUTP + FF)
        collect(head_s, heads_in, seq)
        loss_ref[...] = jnp.zeros_like(loss_ref)

    low = half_low((half, 128))
    for j in range(HEADS // 2):
        one = head_s[HEADS * item + 2 * j].astype(F32)
        two = head_s[HEADS * item + 2 * j + 1].astype(F32)
        attended_s[:half, j * 128 : (j + 1) * 128] = jnp.where(low, one, swap_halves(two)).astype(
            BF16
        )
        attended_s[half:, j * 128 : (j + 1) * 128] = jnp.where(low, swap_halves(one), two).astype(
            BF16
        )
    out_w = slice(0, D)
    up_w = slice(D, D + FF)
    head_w = slice(D + FF, D + FF + OUT)
    down_w = slice(D + FF + OUTP, D + FF + OUTP + FF)
    mod = mod_s[pl.ds(interval[item], 1), :]
    gate_a, shift_b, scale_b, gate_b = [mod[:, k * D : (k + 1) * D] for k in range(2, 6)]
    attended = attended_s[...]
    branch_a = nn(attended, weights[:, out_w])
    x1 = x0_ref[...] + gate_a * branch_a
    normed_b, rstd_b = standardize(x1)
    n2 = (normed_b * (1.0 + scale_b) + shift_b).astype(BF16)
    n2_ref[...] = n2
    value, slope = gelu_parts(nn(n2, weights[:, up_w]))
    active = value.astype(BF16)
    active_ref[...] = active
    branch_b = nt(active, weights[:, down_w])
    x2 = x1 + gate_b * branch_b
    final, rstd_f = standardize(x2)
    nf = final.astype(BF16)
    nf_ref[...] = nf
    diff = nn(nf, weights[:, head_w]) - fields_ref[0].astype(F32).T
    present = tn(ones_where(mask_ref[0] > 0), ones_where(spread()))
    weight = line_weights(samples[item], cosines, seq, iota((tokens, 1), 0))
    weight_grad = weight * (2.0 / PIX) / sum_ref[0:1, 0:1]
    masked = present * diff
    each = jnp.sum(masked * diff, axis=1, keepdims=True) * weight
    loss_ref[...] += jnp.broadcast_to(jnp.sum(each, axis=0, keepdims=True) / PIX, (8, 128))
    dpred = (masked * weight_grad).astype(BF16)
    dpred_ref[...] = dpred

    dx2 = standardize_back(nt(dpred, weights[:, head_w]), final, rstd_f)
    db2 = (gate_b * dx2).astype(BF16)
    db2_ref[...] = db2
    d_gate_b = jnp.sum(dx2 * branch_b, axis=0, keepdims=True)
    dh = (nn(db2, weights[:, down_w]) * slope).astype(BF16)
    dh_ref[...] = dh
    dn2 = nt(dh, weights[:, up_w])
    d_shift_b = jnp.sum(dn2, axis=0, keepdims=True)
    d_scale_b = jnp.sum(dn2 * normed_b, axis=0, keepdims=True)
    dx1 = dx2 + standardize_back(dn2 * (1.0 + scale_b), normed_b, rstd_b)
    dx1_ref[...] = dx1
    d_gate_a = jnp.sum(dx1 * branch_a, axis=0, keepdims=True)
    db1 = (gate_a * dx1).astype(BF16)
    db1_ref[...] = db1
    dout = nt(db1, weights[:, out_w])
    rows_ref[0] = jnp.concatenate(
        [d_gate_a, d_shift_b, d_scale_b, d_gate_b, jnp.zeros((4, D), F32)], axis=0
    )
    for j in range(HEADS // 2):
        pair = dout[:, j * 128 : (j + 1) * 128]
        top, bottom = pair[:half], pair[half:]
        grad_s[HEADS * item + 2 * j] = jnp.where(low, top, swap_halves(bottom)).astype(BF16)
        grad_s[HEADS * item + 2 * j + 1] = jnp.where(low, swap_halves(top), bottom).astype(BF16)

    @pl.when(item == pl.num_programs(0) - 1)
    def _():
        deal(sends, grad_s, seq)


def middle_weights(*refs):
    attended, db1, n2, dh, nf, dpred, db2, active = refs[:8]
    keep_ref, send_ref, acc = refs[8:]
    grp, _ = place()
    acc[:, :D] = tn(attended[...], db1[...])
    acc[:, D : D + FF] = tn(n2[...], dh[...])
    acc[:, D + FF : D + FF + OUT] = tn(nf[...], dpred[...])
    acc[:, D + FF + OUT : D + FF + OUTP] = jnp.zeros((D, OUTP - OUT), F32)
    acc[:, D + FF + OUTP :] = tn(db2[...], active[...])
    split_rows(acc, grp, keep_ref, send_ref)


def split_rows(acc, grp, keep_ref, send_ref):
    rows = keep_ref.shape[1]
    for j in range(keep_ref.shape[0]):
        for odd, ref in ((0, keep_ref), (1, send_ref)):
            at = pl.multiple_of(jnp.bitwise_xor(grp, 2 * j + odd) * rows, 16)
            ref[j, :, : acc.shape[1]] = acc[pl.ds(at, rows), :].astype(BF16)


def attend_back(shares, *refs):
    own = refs[:CUTS]
    others = refs[CUTS : CUTS * shares]
    grads = refs[CUTS * shares : CUTS * shares + CUTS]
    kept_ref, lse_ref = refs[CUTS * shares + CUTS : CUTS * shares + CUTS + 2]
    outs = refs[CUTS * shares + CUTS + 2 :]
    dq_ref, own_ref = outs[:2]
    far_refs = outs[2 : 2 + shares - 1]
    keys_s, turned_s, acc = outs[2 + shares - 1 :]
    tokens = kept_ref.shape[2]
    for n, ref in enumerate(own + others):
        keys_s[n * tokens : (n + 1) * tokens, :] = ref[0, :tokens, :]
    turned_s[...] = keys_s[...].T
    every = range(CUTS)
    queries = jnp.concatenate(
        [unpack(own[m][0, tokens : tokens + tokens // 2, :], True) for m in every], axis=0
    )
    grads = [unpack(grads[m][0], False) for m in every]
    delta = jnp.concatenate(
        [
            jnp.sum((grads[m].astype(F32) * kept_ref[0, m]).T, axis=0, keepdims=True)
            for m in every
        ],
        axis=1,
    )
    grads = jnp.concatenate(grads, axis=0)
    lse = jnp.concatenate([lse_ref[0, m, 0:1, :] for m in every], axis=1)
    chunk = 2 * tokens
    count = keys_s.shape[0] // chunk

    def products_of(c):
        keys = keys_s[c * chunk : (c + 1) * chunk, :]
        return nt(keys, queries), nt(keys, grads)

    products, dq = products_of(0), None
    for c in range(count):
        scores, dprobs = products
        if c + 1 < count:
            products = products_of(c + 1)
        probs = jnp.exp2(scores - lse)
        dscores = (probs * (dprobs - delta)).astype(BF16)
        acc[c * chunk : (c + 1) * chunk, :] = nn(probs.astype(BF16), grads) + nn(dscores, queries)
        part = nn(turned_s[:, c * chunk : (c + 1) * chunk], dscores)
        dq = part if dq is None else dq + part
    for m in every:
        turned = dq[:, m * tokens : (m + 1) * tokens].T * SCALE
        dq_ref[0, m] = pack_rows(turned, True).astype(BF16)
    factor = jnp.where(half_low((1, 128)), 1.0 / LOG2E, 1.0)
    for m in range(CUTS):
        own_ref[0, m] = (acc[m * tokens : (m + 1) * tokens, :] * factor).astype(BF16)
        for n, ref in enumerate(far_refs):
            at = ((n + 1) * CUTS + m) * tokens
            ref[0, m] = (acc[at : at + tokens, :] * factor).astype(BF16)


def join_back(shares, *refs):
    dq_ref, own_ref = refs[:2]
    far = refs[2 : 2 + shares - 1]
    outs = refs[2 + shares - 1 :]
    tokens = own_ref.shape[2]
    for m in range(CUTS):
        total = own_ref[0, m].astype(F32)
        for ref in far:
            total = total + ref[0, m].astype(F32)
        outs[m][:tokens, :] = total.astype(BF16)
        outs[m][tokens:, :] = dq_ref[0, m]


def project_back(rounds, *refs):
    (interval, x0_ref, n1_ref, dx1_ref, rows_ref, gathered_ref, weights, mod_s) = refs[:8]
    units, outs = refs[8 : 8 + CUTS * rounds], refs[8 + CUTS * rounds :]
    (dagg_ref, keep_ref, send_ref) = outs[:3]
    unit_s, dqkv_s, acc, dmod_ref, lines_s = outs[3:]
    item = pl.program_id(0)
    grp, seq = place()
    tokens = x0_ref.shape[0]
    half = tokens // 2

    @pl.when(item == 0)
    def _():
        a = seq // (lax.axis_size("seq") // CUTS)
        for r in range(rounds):
            for m in range(CUTS):
                unit_s[CUTS * r + jnp.bitwise_xor(a, m)] = units[CUTS * r + m][...]
        acc[...] = jnp.zeros_like(acc)
        dmod_ref[...] = jnp.zeros_like(dmod_ref)

    low = half_low((half, 128))
    for h in range(HEADS):
        dqkv_s[:, h * 128 : (h + 1) * 128] = unit_s[HEADS * item + h, :tokens, :]
    for j in range(HEADS // 2):
        one = unit_s[HEADS * item + 2 * j, tokens:, :].astype(F32)
        two = unit_s[HEADS * item + 2 * j + 1, tokens:, :].astype(F32)
        lanes = slice(2 * D + j * 128, 2 * D + (j + 1) * 128)
        dqkv_s[:half, lanes] = jnp.where(low, one, swap_halves(two)).astype(BF16)
        dqkv_s[half:, lanes] = jnp.where(low, swap_halves(one), two).astype(BF16)
    dqkv = dqkv_s[...]
    which = interval[item]
    mod = mod_s[pl.ds(which, 1), :]
    acc[:, D:] += tn(n1_ref[...], dqkv)
    dn1 = nt(dqkv, weights[:, D:])
    normed, rstd = standardize(x0_ref[...])
    d_shift = jnp.sum(dn1, axis=0, keepdims=True)
    d_scale = jnp.sum(dn1 * normed, axis=0, keepdims=True)
    dx0 = (
        dx1_ref[...] + standardize_back(dn1 * (1.0 + mod[:, D : 2 * D]), normed, rstd)
    ).astype(BF16)
    rows = rows_ref[0]
    for k, row in enumerate([d_shift, d_scale] + [rows[r : r + 1] for r in range(4)]):
        dmod_ref[pl.ds(which, 1), k * D : (k + 1) * D] += row

    acc[:, :D] += tn(gathered_ref[...], dx0)
    dagg_ref[0] = nt(weights[:, :D], dx0).astype(BF16)

    @pl.when(item == pl.num_programs(0) - 1)
    def _():
        split_rows(acc, grp, keep_ref, send_ref)
        lines_s[...] = jnp.zeros_like(lines_s)
        for t in range(6 * D // 128):
            lines_s[4 * t : 4 * t + 3, :] = dmod_ref[0:3, t * 128 : (t + 1) * 128]
        rows = keep_ref.shape[1]
        for t in range(mod_tiles(rows)):
            tile = lines_s[t * rows : (t + 1) * rows, :].astype(BF16)
            at = acc.shape[1] + t * 128
            for j in range(keep_ref.shape[0]):
                keep_ref[j, :, at : at + 128] = tile
                send_ref[j, :, at : at + 128] = tile


def aggregate_back(*refs):
    (dagg_ref, probs_ref, picked_ref, fields_ref, mask_ref) = refs[:5]
    (fused_ref, agg_ref, embed_ref, probe_ref) = refs[5:9]
    keep_ref, send_ref, ds_s, acc, mix, dscore = refs[9:]
    item = pl.program_id(0)
    grp, _ = place()
    tokens = dagg_ref.shape[2]

    @pl.when(item == 0)
    def _():
        mix[...] = jnp.zeros_like(mix)
        dscore[...] = jnp.zeros_like(dscore)

    dagg = dagg_ref[0].astype(F32)
    fields = fields_ref[0]
    wide_fields = fields.astype(F32)
    keep = mask_ref[0] > 0
    expand = ones_where(spread())
    upper = iota((128, tokens), 0) < HEAD
    for j in range(HEADS // 2):
        pair = slice(j * 128, (j + 1) * 128)
        both = None
        for h in (2 * j, 2 * j + 1):
            mine = upper if h % 2 == 0 else jnp.logical_not(upper)
            dpart = jnp.where(mine, dagg[pair], 0.0).astype(BF16)
            part = nt(picked_ref[h, 0], dpart)
            both = part if both is None else both + part
            spreaded = (nn(fused_ref[:, pair], dpart) * wide_fields).astype(BF16)
            dprobs = nn(expand, spreaded)
            probs = probs_ref[0, h * VARP : (h + 1) * VARP, :]
            ds = probs * (dprobs - jnp.sum(probs * dprobs, axis=0, keepdims=True))
            ds_s[h * VARP : (h + 1) * VARP, :] = jnp.where(keep, ds, 0.0).astype(BF16)
        mix[:, pair] += both
    dscore[...] += nt(ds_s[...], fields)

    @pl.when(item == pl.num_programs(0) - 1)
    def _():
        lines = iota((128, OUT), 0)
        owned = spread()
        drows = jnp.zeros((128, OUT), F32)
        for h in range(HEADS):
            mine = dscore[h * VARP : (h + 1) * VARP, :]
            line = jnp.sum(jnp.where(owned, mine, 0.0), axis=0, keepdims=True) * SCALE
            drows = drows + jnp.where(lines == h, line, 0.0)
        drows = drows.astype(BF16)
        mixed = mix[...].astype(BF16)
        embed = embed_ref[:, :OUT]
        acc[:, 2 * D : 2 * D + OUT] = nt(agg_ref[:, D:], mixed) + nn(probe_ref[...], drows)
        acc[:, D : 2 * D] = nn(embed, mixed)
        dprobe = nt(embed, drows)
        heads = jnp.where(iota((128, D), 1) // HEAD == iota((128, D), 0), 1.0, 0.0).astype(BF16)
        coarse = dprobe.astype(BF16)
        fine = (dprobe - coarse.astype(F32)).astype(BF16)
        by_column = nn(coarse, heads) + nn(fine, heads)
        eye = iota((D, D), 0) == iota((D, D), 1)
        query = embed_ref[:, OUT : OUT + 1].astype(F32)
        query_row = jnp.sum(jnp.where(eye, query, 0.0), axis=0, keepdims=True)
        acc[:, :D] = by_column * query_row
        dquery = jnp.sum(agg_ref[:, :D].astype(F32) * by_column, axis=0, keepdims=True)
        column = jnp.sum(jnp.where(eye, dquery, 0.0), axis=1, keepdims=True)
        acc[:, 2 * D + OUT :] = jnp.where(iota((D, OUTP - OUT), 1) == 0, column, 0.0)
        split_rows(acc, grp, keep_ref, send_ref)


def mod_tiles(rows):
    return -(-4 * (6 * D // 128) // rows)


def shares_of():
    shares = lax.axis_size("seq") // CUTS
    _, seq = place()
    return shares, seq // shares, lax.rem(seq, shares)


def added(refs, at=None):
    total = None
    for ref in refs:
        value = (ref[...] if at is None else ref[at]).astype(F32)
        total = value if total is None else total + value
    return total


def sum_cores(pairs, sources, *refs):
    ins, outs, table = refs[: 2 * sources], refs[2 * sources : -1], refs[-1]
    shares, _, share = shares_of()
    first, second = outs[:pairs], outs[pairs:]
    half = table.shape[1] // 2
    size = half // shares
    per = ins[0].shape[1] // 16
    count = sum(ref.shape[2] for ref in ins[::2]) // 128 * per
    for j in range(pairs):
        at = 0
        for keep_ref, got_ref in zip(ins[::2], ins[1::2]):
            total = (keep_ref[j].astype(F32) + got_ref[j].astype(F32)).astype(BF16)
            for t in range(total.shape[1] // 128):
                for g in range(per):
                    table[j, at] = total[g * 16 : (g + 1) * 16, t * 128 : (t + 1) * 128]
                    at += 1
        for spare in range(count, 2 * half):
            table[j, spare] = jnp.zeros(table.shape[2:], BF16)
        first[j][...] = table[j, :half]
        for n in range(shares):
            at = half + jnp.bitwise_xor(share, n) * size
            second[n][j * size : (j + 1) * size] = table[j, pl.ds(at, size)]


def sum_cores_once(pairs, *refs):
    (keep_ref, got_ref), outs = refs[:2], refs[2:]
    per = keep_ref.shape[1] // 16
    count = keep_ref.shape[2] // 128 * per
    for j in range(pairs):
        total = (keep_ref[j].astype(F32) + got_ref[j].astype(F32)).astype(BF16)
        for t in range(keep_ref.shape[2] // 128):
            for g in range(per):
                outs[j][t * per + g] = total[g * 16 : (g + 1) * 16, t * 128 : (t + 1) * 128]
        for spare in range(count, outs[j].shape[0]):
            outs[j][spare] = jnp.zeros(outs[j].shape[1:], BF16)


def sum_and_deal(over_cuts, *refs):
    outs, table = refs[-1 - (CUTS if over_cuts else shares_of()[0]) : -1], refs[-1]
    _, cut, share = shares_of()
    table[...] = added(refs[: -1 - len(outs)]).astype(BF16)
    size = outs[0].shape[0]
    for n, ref in enumerate(outs):
        ref[...] = table[pl.ds(jnp.bitwise_xor(cut if over_cuts else share, n) * size, size)]


def sum_both(pairs, shares, *refs):
    by_grp, by_share = refs[:pairs], refs[pairs : pairs + shares]
    outs, (table,) = refs[pairs + shares : -1], refs[-1:]
    _, _, share = shares_of()
    table[...] = added(by_grp).astype(BF16)
    size = outs[0].shape[0]
    for n in range(shares):
        outs[n][...] = table[pl.ds(jnp.bitwise_xor(share, n) * size, size)]
    for j in range(pairs):
        at = slice(j * size, (j + 1) * size)
        outs[shares + j][...] = added(by_share, at).astype(BF16)


def sum_both_again(pairs, shares, *refs):
    by_share, by_grp = refs[:shares], refs[shares : shares + pairs]
    outs, (table,) = refs[pairs + shares : -1], refs[-1:]
    _, cut, _ = shares_of()
    size = outs[0].shape[0] // 2
    table[0] = added(by_share).astype(BF16)
    table[1] = added(by_grp).astype(BF16)
    for m in range(CUTS):
        at = pl.ds(jnp.bitwise_xor(cut, m) * size, size)
        outs[m][:size] = table[0, at]
        outs[m][size:] = table[1, at]


def sum_pieces(*refs):
    sources, (out_ref, square_ref) = refs[:-2], refs[-2:]
    total = added(sources)
    out_ref[...] = total.astype(BF16)
    square_ref[...] = jnp.sum(total * total, axis=0)


def sum_late(start, stop, *refs):
    early_ref, loss_ref, lead_ref = refs[:3]
    sources, out_ref = refs[3:-1], refs[-1]
    grp, _ = place()
    shares, cut, share = shares_of()
    rows = lead_ref.shape[0] // lax.axis_size("grp")
    lead = lead_ref[pl.ds(pl.multiple_of(grp * rows, 16), rows), :].astype(F32)
    cols = [lead[:, g : g + 1] for g in range(3)]

    def gram(f, g):
        return jnp.sum(cols[f] * cols[g], axis=0, keepdims=True)

    row = lax.rem(iota((16, 1), 0), 4)

    def pick(*values):
        out = jnp.zeros((16, 1), F32)
        for r, value in values:
            out = jnp.where(row == r, value, out)
        return out

    same = pick(*[(g, gram(g, g)) for g in range(3)])
    next_one = pick((1, 2 * gram(0, 1)), (2, 2 * gram(1, 2)))
    next_two = pick((2, 2 * gram(0, 2)))
    size = (out_ref.shape[0] - 1) // 2
    plain = jnp.zeros((16, 128), F32)
    for half in range(2):
        for k in range(size):
            total = added(sources, half * size + k)
            out_ref[half * size + k] = total.astype(BF16)
            index = ((half * shares + share) * CUTS + cut) * size + k
            special = jnp.logical_and(index >= start, index < stop)
            square = total * total
            mixed = (
                square * same
                + total * pltpu.roll(total, 1, 0) * next_one
                + total * pltpu.roll(total, 2, 0) * next_two
            )
            plain = plain + jnp.where(special, mixed, square)
    squares = jnp.sum(jnp.sum(plain + early_ref[...], axis=0, keepdims=True), axis=1, keepdims=True)
    rider = jnp.zeros((16, 128), F32)
    for at, value in ((0, loss_ref[0:1, :]), (3, jnp.broadcast_to(squares, (1, 128)))):
        for part in range(3):
            piece = value.astype(BF16).astype(F32)
            rider = jnp.where(iota((16, 128), 0) == at + part, piece, rider)
            value = value - piece
    out_ref[2 * size] = rider.astype(BF16)


def stack_late(*refs):
    pieces, (column_ref, reduced_ref) = refs[:-2], refs[-2:]
    count = column_ref.shape[1]
    rider = jnp.zeros((16, 128), F32)
    for m, ref in enumerate(pieces):
        column_ref[m] = ref[:count]
        rider = rider + ref[count].astype(F32)
    reduced_ref[...] = jnp.concatenate(
        [rider[0:1] + rider[1:2] + rider[2:3], rider[3:4] + rider[4:5] + rider[5:6]]
        + [jnp.zeros((6, 128), F32)],
        axis=0,
    )


def stack(*refs):
    for m, ref in enumerate(refs[:-1]):
        refs[-1][m] = ref[...]


def step_values(param, first, second, grad):
    first = beta_first * first + (1.0 - beta_first) * grad
    second = beta_second * second + (1.0 - beta_second) * grad * grad
    mean_hat = first * (1.0 / (1.0 - beta_first**STEP))
    var_hat = second * (1.0 / (1.0 - beta_second**STEP))
    param = param - learn_rate * (
        mean_hat / (jnp.sqrt(var_hat) + adam_epsilon) + decay_rate * param
    )
    return param, first, second, param.astype(BF16)


def optimize(shares, *refs):
    reduced_ref, sum_ref, lead_ref = refs[:3]
    early = refs[3 : 3 + shares]
    late = refs[3 + shares : 3 + 2 * shares]
    wide = refs[3 + 2 * shares : 6 + 2 * shares]
    tall = refs[6 + 2 * shares : 9 + 2 * shares]
    query = refs[9 + 2 * shares : 12 + 2 * shares]
    outs = refs[12 + 2 * shares :]
    scalars, wide_hbm, tall_hbm, query_out = outs[:3], outs[3:7], outs[7:11], outs[11:15]
    early_s, late_s, wide_out, tall_out, sems = outs[15], outs[16], outs[17:21], outs[21:25], outs[25]
    grp, _ = place()
    _, cut, share = shares_of()
    for table, stacks, halves in ((early_s, early, 1), (late_s, late, 2)):
        size = stacks[0].shape[1] // halves
        for n, ref in enumerate(stacks):
            for m in range(CUTS):
                for half in range(halves):
                    at = (half * shares + jnp.bitwise_xor(share, n)) * CUTS
                    at = (at + jnp.bitwise_xor(cut, m)) * size
                    table[pl.ds(at, size)] = ref[m, half * size : (half + 1) * size]
    norm = jnp.sqrt(reduced_ref[1:2, 0:1])
    for ref, value in zip(scalars, (reduced_ref[0:1, 0:1], sum_ref[0:1, 0:1], norm)):
        ref[...] = value
    factor = jnp.minimum(1.0, clip_limit / (norm + 1e-06))
    rows = wide[0].shape[0]
    per = rows // 16

    def tile(table, t):
        return jnp.concatenate([table[t * per + g] for g in range(per)], axis=0).astype(F32)

    def put(ins, targets, at, grad):
        new = step_values(*[r[at] for r in ins], grad * factor)
        for ref, value in zip(targets, new):
            ref[at] = value

    def at(t, width=128):
        return (slice(None), slice(t * 128, t * 128 + width))

    copies = []

    def flush(sources, targets, lo, hi):
        for source, target in zip(sources, targets):
            copy = pltpu.make_async_copy(
                source.at[:, lo:hi], target.at[:, lo:hi], sems.at[len(copies)]
            )
            copy.start()
            copies.append(copy)

    low = half_low((rows, 128))
    for t in range(6):
        put(wide, wide_out, at(t), tile(late_s, t))
    for t in range(3):
        put(wide, wide_out, at(6 + t), tile(late_s, 15 + t))
    flush(wide_out, wide_hbm, 0, 3 * D)
    lead = lead_ref[pl.ds(pl.multiple_of(grp * rows, 16), rows), :].astype(F32)
    lines = jnp.concatenate([tile(late_s, 27 + t) for t in range(mod_tiles(rows))], axis=0)
    for t in range(18):
        grad = lead[:, 0:1] * lines[4 * t : 4 * t + 1]
        for g in (1, 2):
            grad = grad + lead[:, g : g + 1] * lines[4 * t + g : 4 * t + g + 1]
        put(wide, wide_out, at(9 + t), grad)
    flush(wide_out, wide_hbm, 3 * D, 9 * D)
    qkv = 18
    for j in range(3):
        put(wide, wide_out, at(27 + j), tile(late_s, qkv + 6 + j))
        one, two = tile(late_s, qkv + 2 * j), tile(late_s, qkv + 2 * j + 1)
        put(wide, wide_out, at(30 + j), jnp.where(low, one, swap_halves(two)))
        put(wide, wide_out, at(33 + j), jnp.where(low, swap_halves(one), two))
    flush(wide_out, wide_hbm, 9 * D, 12 * D)
    for t in range(15 + 8):
        put(wide, wide_out, at(36 + t), tile(early_s, t))
    rest = OUT - 8 * 128
    put(wide, wide_out, at(59, rest), tile(early_s, 23)[:, :rest])
    flush(wide_out, wide_hbm, 12 * D, wide[0].shape[1])
    for t in range(8):
        put(tall, tall_out, at(t), tile(late_s, 6 + t))
    flush(tall_out, tall_hbm, 0, 8 * 128)
    last = tile(late_s, 14)
    lane = iota((rows, 128), 1)
    for t in range(FF // 128):
        turned = pltpu.roll(tile(early_s, 24 + t), rest, 1)
        put(tall, tall_out, at(8 + t), jnp.where(lane < rest, last, turned))
        if t == 0:
            eye = iota((rows, rows), 0) == iota((rows, rows), 1)
            grad = jnp.sum(jnp.where(eye, last[:, rest : rest + 1], 0.0), axis=0, keepdims=True)
            put(query, query_out, (slice(None), slice(None)), grad)
        last = turned
    put(tall, tall_out, at(8 + FF // 128, rest), last[:, :rest])
    flush(tall_out, tall_hbm, 8 * 128, tall[0].shape[1])
    for copy in copies:
        copy.wait()


def shift(value, axis, bit):
    size = lax.axis_size(axis)
    return lax.ppermute(value, axis, [(i, i ^ bit) for i in range(size)])


def gather_blocks(own, group):
    blocks = {0: own}
    for j in range(2, group, 2):
        blocks[j] = shift(own, "grp", j)
    for j in range(0, group, 2):
        blocks[j + 1] = shift(blocks[j], "grp", 1)
    return [blocks[j] for j in range(group)]


def granules(rows, cols, shares):
    unit = 2 * shares * CUTS
    return -(-(rows // 16) * (cols // 128) // unit) * unit


def piece_shape(count):
    return sds((count, 16, 128), BF16)


def reduce_cores(*sources, after=()):
    pairs, rows, _ = sources[0][0].shape
    shares = lax.axis_size("seq") // CUTS
    count = granules(rows, sum(keep.shape[2] for keep, _ in sources), shares)
    results = call(
        functools.partial(sum_cores, pairs, len(sources)),
        [piece_shape(count // 2)] * pairs + [piece_shape(count // 2 // shares * pairs)] * shares,
        scratch=[pltpu.VMEM((pairs, count, 16, 128), BF16)],
        after=after,
    )(*[x for source in sources for x in source])
    return results[:pairs], results[pairs:]


def reduce_cores_once(keep, got, after=()):
    pairs, rows, cols = keep.shape
    parts = lax.axis_size("seq")
    count = -(-(rows // 16) * (cols // 128) // parts) * parts
    halves = call(
        functools.partial(sum_cores_once, pairs), [piece_shape(count)] * pairs, after=after
    )(keep, got)
    return [halves[0]] + [shift(halves[j], "grp", 2 * j) for j in range(1, pairs)]


def reduce_and_deal(pieces, over, after=()):
    count = pieces[0].shape[0]
    number = CUTS if over else lax.axis_size("seq") // CUTS
    outs = call(
        functools.partial(sum_and_deal, over),
        [piece_shape(count // number)] * number,
        scratch=[pltpu.VMEM((count, 16, 128), BF16)],
        after=after,
    )(*pieces)
    if over:
        return over_cuts(outs[0], outs[1:])
    return [outs[0]] + [shift(outs[n], "seq", n) for n in range(1, number)]


def exchange_once(by_grp, by_share):
    return [by_grp[0]] + [shift(by_grp[j], "grp", 2 * j) for j in range(1, len(by_grp))], [
        by_share[0]
    ] + [shift(by_share[n], "seq", n) for n in range(1, len(by_share))]


def reduce_once(by_grp, by_share, after=()):
    pairs, shares = len(by_grp), len(by_share)
    size = by_grp[0].shape[0] // shares
    results = call(
        functools.partial(sum_both, pairs, shares),
        [piece_shape(size)] * (pairs + shares),
        scratch=[pltpu.VMEM(by_grp[0].shape, BF16)],
        after=after,
    )(*by_grp, *by_share)
    return results[:shares], results[shares:]


def exchange_again(by_share, by_grp):
    pairs, shares = len(by_grp), len(by_share)
    return [by_share[0]] + [shift(by_share[n], "seq", n) for n in range(1, shares)], [
        by_grp[0]
    ] + [shift(by_grp[j], "grp", 2 * j) for j in range(1, pairs)]


def reduce_twice(by_share, by_grp, after=()):
    pairs, shares = len(by_grp), len(by_share)
    size = by_grp[0].shape[0]
    return call(
        functools.partial(sum_both_again, pairs, shares),
        [piece_shape(2 * size // CUTS)] * CUTS,
        scratch=[pltpu.VMEM((2, size, 16, 128), BF16)],
        after=after,
    )(*by_share, *by_grp)


def over_cuts(first, others=None):
    shares = lax.axis_size("seq") // CUTS
    sent = [first] * (CUTS - 1) if others is None else others
    return [first] + [shift(sent[m - 1], "seq", m * shares) for m in range(1, CUTS)]


def gather_shares(pieces, after=()):
    shares = lax.axis_size("seq") // CUTS
    column = call(stack, sds((CUTS,) + pieces[0].shape, BF16), after=after)(*pieces)
    return [column] + [shift(column, "seq", n) for n in range(1, shares)]


def butterfly(value, axis, bit, stop):
    while bit < stop:
        value = value + shift(value, axis, bit)
        bit *= 2
    return value


def lead_table():
    half = D // 2
    hours = 6.0 * np.exp2(np.arange(3, dtype=np.float32))
    freqs = np.exp(-np.log(np.float32(1000.0)) * np.arange(half, dtype=np.float32) / half)
    angles = hours[None, :] * freqs.astype(np.float32)[:, None]
    waves = np.concatenate([np.sin(angles), np.cos(angles)], axis=0)
    table = np.zeros((D, 128), np.float32)
    table[:, :3] = waves / (1.0 + np.exp(-waves))
    return jnp.asarray(table).astype(BF16)


def cosine_table(count):
    line = np.arange(count, dtype=np.float32)
    return jnp.asarray(np.cos(np.pi * ((line + 0.5) / count - 0.5)).astype(np.float32))


def per_device(
    fields,
    targets,
    land_mask,
    interval,
    samples,
    wide_weights,
    wide_firsts,
    wide_seconds,
    tall_weights,
    tall_firsts,
    tall_seconds,
    query_vector,
    query_firsts,
    query_seconds,
):
    group = lax.axis_size("grp")
    parts = lax.axis_size("seq")
    shares = parts // CUTS
    rows, columns = wide_weights.shape
    items, tokens = fields.shape[:2]
    units = items * HEADS // CUTS
    every = items * tokens
    late_cols = D + FF + OUTP + FF

    query_row = query_vector.reshape(1, rows)
    tall = [x.T for x in (tall_weights, tall_firsts, tall_seconds)]
    lead = lead_table()
    cosines = cosine_table(tokens // COLS * parts)
    fields = fields.transpose(0, 2, 1)
    targets = targets.transpose(0, 2, 1)
    mask = jnp.pad(
        land_mask.transpose(0, 2, 1), ((0, 0), (0, VARP - VARS), (0, 0)), constant_values=-1
    )

    def columns_of(index):
        return pl.BlockSpec((rows, 3 * D), lambda i: (0, index))

    first_own, second_own = call(
        pack_first,
        [sds((rows, 2 * D + OUTP), BF16), sds((rows + RIDERS, 4 * D), BF16)],
        grid=(1,),
        in_specs=[smem(), smem()]
        + [columns_of(i) for i in (0, 1, 2, 3, 0)]
        + [pl.BlockSpec((1, rows), lambda i: (0, 0)), whole(), whole()],
        out_specs=[whole()] * 2,
        scratch=[pltpu.VMEM((RIDERS, 4 * D), F32)],
        us=3,
        limit=62,
    )(samples, cosines, *[wide_weights] * 4, tall[0], query_row, lead, mask)
    first = gather_blocks(first_own, group)
    second = gather_blocks(second_own, group)
    late_own = call(
        pack_late,
        sds((rows, late_cols), BF16),
        grid=(1,),
        in_specs=[columns_of(4), columns_of(5), columns_of(6), whole()],
        out_specs=whole(),
        us=2,
        limit=62,
        after=(first_own,),
    )(wide_weights, wide_weights, wide_weights, tall[0])
    late_blocks = gather_blocks(late_own, group)

    by_item = pl.BlockSpec((tokens, D), lambda i: (i, 0))

    def lane_block(height):
        return pl.BlockSpec((1, height, tokens), lambda i: (i, 0, 0))

    heads_spec = pl.BlockSpec((HEADS, 1, OUT, tokens), lambda i: (0, i, 0, 0))
    packed = tokens + tokens // 2 + 16

    probs, picked, gathered, agg_weights, embed, fused_w, probe = call(
        functools.partial(aggregate, group),
        [
            in_hbm((items, HEADS * VARP, tokens), F32),
            in_hbm((HEADS, items, OUT, tokens), BF16),
            sds((every, D), BF16),
            in_hbm((D, 2 * D), BF16),
            in_hbm((D, OUTP), BF16),
            in_hbm((OUT, D), BF16),
            in_hbm((D, 128), BF16),
        ],
        grid=(items,),
        in_specs=[lane_block(OUT), lane_block(VARP)] + [whole()] * group,
        out_specs=[lane_block(HEADS * VARP), heads_spec, by_item] + [whole()] * 4,
        scratch=[
            pltpu.VMEM((HEADS * VARP, OUT), BF16),
            pltpu.VMEM((D, OUT), BF16),
            pltpu.VMEM((D, tokens), F32),
        ],
        us=10,
        limit=34,
    )(fields, mask, *first)
    results = call(
        functools.partial(project, group),
        [
            in_hbm((every, D), F32),
            in_hbm((every, D), BF16),
            in_hbm((D, 4 * D), BF16),
            in_hbm((8, 6 * D), F32),
        ]
        + [sds((units, packed, 128), BF16)] * CUTS,
        grid=(items,),
        in_specs=[smem(), by_item] + [whole()] * group,
        out_specs=[by_item, by_item] + [whole()] * (2 + CUTS),
        scratch=[pltpu.VMEM((items * HEADS, packed, 128), BF16)],
        us=4,
        limit=34,
    )(interval, gathered, *second)
    x0, n1, second_weights, mods = results[:4]
    dealt = results[4:]

    own = over_cuts(dealt[0], dealt[1:])
    others = [shift(own[m], "seq", n) for n in range(1, shares) for m in range(CUTS)]
    keys_total = parts * tokens

    unit_in = pl.BlockSpec((1, packed, 128), lambda u: (u, 0, 0))
    half_in = pl.BlockSpec((1, tokens // 2, 128), lambda u: (u, 0, 0))
    kept_spec = pl.BlockSpec((1, CUTS, tokens, 128), lambda u: (u, 0, 0, 0))
    lse_spec = pl.BlockSpec((1, CUTS, 8, tokens), lambda u: (u, 0, 0, 0))
    pack_spec = pl.BlockSpec((1, CUTS, tokens // 2, 128), lambda u: (u, 0, 0, 0))
    half_out = sds((units, tokens // 2, 128), BF16)
    results = call(
        functools.partial(attend, shares),
        [half_out] * CUTS
        + [
            in_hbm((units, CUTS, tokens, 128), F32),
            in_hbm((units, CUTS, 8, tokens), F32),
            in_hbm((8, 128), F32),
        ],
        grid=(units,),
        in_specs=[unit_in] * (CUTS * shares),
        out_specs=[half_in] * CUTS + [kept_spec, lse_spec, whole()],
        scratch=[pltpu.VMEM((keys_total, 128), BF16)],
        us=9,
        limit=60 if shares > 2 else 34,
    )(*own, *others)
    backs, (kept, lse, weight_sum) = results[:CUTS], results[CUTS:]
    heads_in = over_cuts(backs[0], backs[1:])

    saved = [D, D, D, FF, D, OUT, D, FF]
    results = call(
        functools.partial(middle, group),
        [in_hbm((every, D), F32), in_hbm((items, 8, D), F32), in_hbm((8, 128), F32)]
        + [half_out] * CUTS
        + [sds((every, width), BF16) for width in saved],
        grid=(items,),
        in_specs=[smem(), smem(), smem(), whole(), by_item, lane_block(OUT), lane_block(VARP)]
        + [whole()] * (CUTS + group + 1),
        out_specs=[by_item, pl.BlockSpec((1, 8, D), lambda i: (i, 0, 0))]
        + [whole()] * (1 + CUTS)
        + [pl.BlockSpec((tokens, width), lambda i: (i, 0)) for width in saved],
        scratch=[
            pltpu.VMEM((D, late_cols), BF16),
            pltpu.VMEM((items * HEADS, tokens // 2, 128), BF16),
            pltpu.VMEM((items * HEADS, tokens // 2, 128), BF16),
        ],
        us=11,
        limit=34,
    )(
        interval,
        samples,
        cosines,
        weight_sum,
        x0,
        targets,
        mask,
        *heads_in,
        *late_blocks,
        mods,
    )
    dx1, mod_rows, loss = results[:3]
    sends, operands = results[3 : 3 + CUTS], results[3 + CUTS :]
    early_keep, early_send = call(
        middle_weights,
        [sds((group // 2, rows, late_cols), BF16)] * 2,
        scratch=[pltpu.VMEM((D, late_cols), F32)],
        us=6,
        limit=34,
    )(*operands)
    grads_in = over_cuts(sends[0], sends[1:])

    def of_unit(u, *shape):
        return pl.BlockSpec((1,) + shape, lambda i: (u,) + (0,) * len(shape))

    def back_of(u, after):
        results = call(
            functools.partial(attend_back, shares),
            [sds((1, CUTS, tokens // 2, 128), BF16)]
            + [sds((1, CUTS, tokens, 128), BF16)] * shares,
            grid=(1,),
            in_specs=[of_unit(u, packed, 128)] * (CUTS * shares)
            + [of_unit(u, tokens // 2, 128)] * CUTS
            + [of_unit(u, CUTS, tokens, 128), of_unit(u, CUTS, 8, tokens)],
            out_specs=[whole()] * (1 + shares),
            scratch=[
                pltpu.VMEM((keys_total, 128), BF16),
                pltpu.VMEM((128, keys_total), BF16),
                pltpu.VMEM((keys_total, 128), F32),
            ],
            us=6,
            limit=60 if shares > 2 else 34,
            after=after,
        )(*own, *others, *grads_in, kept, lse)
        far = results[2:]
        if u == 2:
            far = [once_ready(far[0], units_in[0][1:]), *far[1:]]
        return results[:2], [shift(far[n], "seq", n + 1) for n in range(shares - 1)]

    def joined(near, far):
        dealt = call(
            functools.partial(join_back, shares),
            [sds((tokens + tokens // 2, 128), BF16)] * CUTS,
        )(*near, *far)
        return over_cuts(dealt[0], dealt[1:])

    early_got = shift(early_send, "grp", 1)
    partial_sums, units_in = [], []
    for u in range(units):
        after = (early_keep,) if u == 0 else (partial_sums[u - 1][0][0],)
        if u == 2:
            early_once = reduce_cores_once(early_keep, early_got, after=after)
            after += (early_once[0],)
        if u >= 2:
            units_in.append(joined(*partial_sums[u - 2]))
        partial_sums.append(back_of(u, after))
    units_in.append(joined(*partial_sums[-2]))
    units_in.append(joined(*partial_sums[-1]))
    early_twice = reduce_and_deal(early_once, False, after=(units_in[1][1],))

    second_cols = 4 * D + mod_tiles(rows) * 128
    dagg, second_keep, second_send = call(
        functools.partial(project_back, units),
        [
            sds((items, D, tokens), BF16),
            sds((group // 2, rows, second_cols), BF16),
            sds((group // 2, rows, second_cols), BF16),
        ],
        grid=(items,),
        in_specs=[
            smem(),
            by_item,
            by_item,
            by_item,
            pl.BlockSpec((1, 8, D), lambda i: (i, 0, 0)),
            by_item,
        ]
        + [whole()] * (2 + CUTS * units),
        out_specs=[pl.BlockSpec((1, D, tokens), lambda i: (i, 0, 0))] + [whole()] * 2,
        scratch=[
            pltpu.VMEM((items * HEADS, tokens + tokens // 2, 128), BF16),
            pltpu.VMEM((tokens, 3 * D), BF16),
            pltpu.VMEM((D, 4 * D), F32),
            pltpu.VMEM((8, 6 * D), F32),
            pltpu.VMEM((mod_tiles(rows) * rows, 128), F32),
        ],
        us=4,
        limit=34,
    )(
        interval,
        x0,
        n1,
        dx1,
        mod_rows,
        gathered,
        second_weights,
        mods,
        *[x for unit in units_in for x in unit],
    )
    second_got = shift(second_send, "grp", 1)
    early_pieces = reduce_and_deal(early_twice, True, after=(dagg,))
    late_keep, late_send = call(
        aggregate_back,
        [sds((group // 2, rows, 2 * D + OUTP), BF16)] * 2,
        grid=(items,),
        in_specs=[
            pl.BlockSpec((1, D, tokens), lambda i: (i, 0, 0)),
            lane_block(HEADS * VARP),
            heads_spec,
            lane_block(OUT),
            lane_block(VARP),
        ]
        + [whole()] * 4,
        out_specs=[whole()] * 2,
        scratch=[
            pltpu.VMEM((HEADS * VARP, tokens), BF16),
            pltpu.VMEM((D, 2 * D + OUTP), F32),
            pltpu.VMEM((OUT, D), F32),
            pltpu.VMEM((HEADS * VARP, OUT), F32),
        ],
        us=13,
        limit=34,
        after=(early_pieces[0],),
    )(dagg, probs, picked, fields, mask, fused_w, agg_weights, embed, probe)
    early_piece, early_squares = call(
        sum_pieces,
        [piece_shape(early_pieces[0].shape[0]), sds((16, 128), F32)],
        after=(late_keep,),
    )(*early_pieces)
    early_column = over_cuts(early_piece)
    late_first = reduce_cores(
        (late_keep, shift(late_send, "grp", 1)),
        (second_keep, second_got),
    )
    late_second = reduce_once(*exchange_once(*late_first))
    early_all = gather_shares(early_column, after=(late_second[0][0],))
    late_third = reduce_twice(*exchange_again(*late_second))
    late_pieces = over_cuts(late_third[0], late_third[1:])
    start = (rows // 16) * 27
    stop = (rows // 16) * (27 + mod_tiles(rows))
    count = late_pieces[0].shape[0]
    late_piece = call(
        functools.partial(sum_late, start, stop), piece_shape(count + 1)
    )(early_squares, loss, lead, *late_pieces)
    late_column, reduced = call(
        stack_late, [sds((CUTS, count, 16, 128), BF16), sds((8, 128), F32)]
    )(*over_cuts(late_piece))
    late_all = [late_column] + [shift(late_column, "seq", n) for n in range(1, shares)]
    reduced = butterfly(reduced, "grp", 1, group)
    reduced = butterfly(reduced, "seq", 1, shares)

    def like(x, dtype=F32):
        return sds(x.shape, dtype)

    results = call(
        functools.partial(optimize, shares),
        [sds((1, 1), F32)] * 3
        + [like(wide_weights)] * 3
        + [like(wide_weights, BF16)]
        + [like(tall[0])] * 3
        + [like(tall[0], BF16)]
        + [like(query_row)] * 3
        + [like(query_row, BF16)],
        out_specs=[whole()] * 3 + [pl.BlockSpec(memory_space=pl.ANY)] * 8 + [whole()] * 4,
        scratch=[
            pltpu.VMEM((parts * early_piece.shape[0], 16, 128), BF16),
            pltpu.VMEM((parts * count, 16, 128), BF16),
        ]
        + [pltpu.VMEM(wide_weights.shape, dtype) for dtype in (F32, F32, F32, BF16)]
        + [pltpu.VMEM(tall[0].shape, dtype) for dtype in (F32, F32, F32, BF16)]
        + [pltpu.SemaphoreType.DMA((24,))],
        us=10,
        limit=34,
    )(
        reduced,
        weight_sum,
        lead,
        *early_all,
        *late_all,
        wide_weights,
        wide_firsts,
        wide_seconds,
        *tall,
        query_row,
        query_firsts.reshape(1, rows),
        query_seconds.reshape(1, rows),
    )
    tall_out = tuple(r.T for r in results[7:11])
    query_out = tuple(r.reshape(rows) for r in results[11:15])
    return tuple(r.reshape(()) for r in results[:3]) + tuple(results[3:7]) + tall_out + query_out


def solution(mesh):
    placed = (
        P("grp", "seq", None),
        P("grp", "seq", None),
        P("grp", "seq", None),
        P("grp"),
        P("grp"),
        P("grp", None),
        P("grp", None),
        P("grp", None),
        P(None, "grp"),
        P(None, "grp"),
        P(None, "grp"),
        P("grp"),
        P("grp"),
        P("grp"),
    )
    return jax.shard_map(
        per_device,
        mesh=mesh,
        in_specs=placed,
        out_specs=(
            P(),
            P(),
            P(),
            P("grp", None),
            P("grp", None),
            P("grp", None),
            P("grp", None),
            P(None, "grp"),
            P(None, "grp"),
            P(None, "grp"),
            P(None, "grp"),
            P("grp"),
            P("grp"),
            P("grp"),
            P("grp"),
        ),
        check_vma=False,
    )
```

```python
import functools

import jax
import numpy as np
import jax.numpy as jnp
from jax import lax
from jax.experimental import pallas as pl
from jax.experimental.pallas import tpu as pltpu
from jax.sharding import PartitionSpec as P

D = 384
HEADS = 6
HEAD = 64
FF = 1536
VARS = 69
PIX = 16
OUT = VARS * PIX
OUTP = 1152
VARP = 80
COLS = 128
STEP = 5
CUTS = 4
SCALE = HEAD**-0.5
LOG2E = 1.4426950408889634

beta_first = 0.5
beta_second = 0.5
learn_rate = 0.1
decay_rate = 0.01
adam_epsilon = 1e-08
clip_limit = 0.05
norm_epsilon = 1e-06
masked_score = -1e30

F32 = jnp.float32
BF16 = jnp.bfloat16
MIB = 1024 * 1024
RIDERS = 32


def dot(left, right, a, b):
    return lax.dot_general(left, right, (((a,), (b,)), ((), ())), preferred_element_type=F32)


def nn(left, right):
    return dot(left, right, 1, 0)


def nt(left, right):
    return dot(left, right, 1, 1)


def tn(left, right):
    return dot(left, right, 0, 0)


def iota(shape, dim):
    return lax.broadcasted_iota(jnp.int32, shape, dim)


def half_low(shape):
    return iota(shape, len(shape) - 1) < HEAD


def swap_halves(tile):
    return pltpu.roll(tile, HEAD, 1)


def spread():
    return iota((VARP, OUT), 1) // PIX == iota((VARP, OUT), 0)


def ones_where(mask):
    return jnp.where(mask, 1.0, 0.0).astype(BF16)


def place():
    grp = lax.axis_index("grp")
    seq = lax.axis_index("seq")
    return grp, seq


def call(
    kernel, outs, grid=(), in_specs=None, out_specs=None, scratch=(), us=1, limit=34, after=()
):
    def run(*args):
        count = len(args)

        def body(*refs):
            kernel(*refs[:count], *refs[count + len(after) :])

        kw = {} if out_specs is None else {"out_specs": out_specs}
        return pl.pallas_call(
            body,
            out_shape=outs,
            grid=grid,
            in_specs=(list(in_specs) if in_specs else [whole()] * count)
            + [pl.BlockSpec(memory_space=pl.ANY)] * len(after),
            scratch_shapes=list(scratch),
            cost_estimate=pl.CostEstimate(
                flops=int(us * 1.15e9), transcendentals=0, bytes_accessed=1024
            ),
            compiler_params=pltpu.CompilerParams(vmem_limit_bytes=limit * MIB),
            **kw,
        )(*args, *after)

    return run


def once_ready(value, after):
    space = pl.BlockSpec(memory_space=pl.ANY)
    return pl.pallas_call(
        lambda *refs: None,
        out_shape=jax.ShapeDtypeStruct(value.shape, value.dtype),
        in_specs=[space] * (1 + len(after)),
        out_specs=space,
        input_output_aliases={0: 0},
        cost_estimate=pl.CostEstimate(flops=1, transcendentals=0, bytes_accessed=1),
    )(value, *after)


def whole():
    return pl.BlockSpec(memory_space=pltpu.VMEM)


def smem():
    return pl.BlockSpec(memory_space=pltpu.SMEM)


def sds(shape, dtype):
    return jax.ShapeDtypeStruct(shape, dtype)


def in_hbm(shape, dtype):
    return pltpu.HBM(shape, dtype)


def standardize(x):
    centered = x - jnp.mean(x, axis=-1, keepdims=True)
    rstd = lax.rsqrt(jnp.mean(centered * centered, axis=-1, keepdims=True) + norm_epsilon)
    return centered * rstd, rstd


def standardize_back(grad, normed, rstd):
    return rstd * (
        grad
        - jnp.mean(grad, axis=-1, keepdims=True)
        - normed * jnp.mean(grad * normed, axis=-1, keepdims=True)
    )


def gelu_parts(x):
    k = 0.7978845608028654
    inner = k * (x + 0.044715 * x * x * x)
    t = jnp.tanh(inner)
    value = 0.5 * x * (1.0 + t)
    slope = 0.5 * (1.0 + t) + 0.5 * x * (1.0 - t * t) * k * (1.0 + 3 * 0.044715 * x * x)
    return value, slope


def pack_first(*refs):
    samples, cosines, agg_ref, mod_a, mod_b, wide_ref, tall_ref, query_ref = refs[:8]
    lead_ref, mask_ref, first_ref, second_ref, rider_s = refs[8:]
    rows = wide_ref.shape[0]
    grp, seq = place()
    first_ref[:, : 2 * D] = agg_ref[:, : 2 * D].astype(BF16)
    second_ref[:rows, :D] = agg_ref[:, 2 * D :].astype(BF16)
    eye = iota((rows, rows), 0) == iota((rows, rows), 1)
    column = jnp.sum(jnp.where(eye, query_ref[...], 0.0), axis=1, keepdims=True)
    lane = iota((rows, OUTP), 1)
    embed = jnp.where(lane < OUT, tall_ref[...], jnp.where(lane == OUT, column, 0.0))
    first_ref[:, 2 * D :] = embed.astype(BF16)
    low = half_low((rows, 128))
    for j in range(HEADS // 2):
        k = wide_ref[:, D + j * 128 : D + (j + 1) * 128]
        v = wide_ref[:, 2 * D + j * 128 : 2 * D + (j + 1) * 128]
        at = D + 2 * j * 128
        second_ref[:rows, at : at + 128] = jnp.where(low, k, swap_halves(v)).astype(BF16)
        second_ref[:rows, at + 128 : at + 256] = jnp.where(low, swap_halves(k), v).astype(BF16)
    second_ref[:rows, 3 * D :] = wide_ref[:, :D].astype(BF16)
    rider_s[...] = jnp.zeros_like(rider_s)

    def ride(row, value):
        for part in range(3):
            piece = value.astype(BF16).astype(F32)
            at = part * 8 + row
            rider_s[at : at + 1, : 3 * D] = piece
            value = value - piece

    lead = lead_ref[pl.ds(pl.multiple_of(grp * rows, 16), rows), :].astype(F32)
    for half, ref in ((0, mod_a), (1, mod_b)):
        mod = ref[...].astype(BF16).astype(F32)
        for g in range(3):
            ride(2 * g + half, jnp.sum(lead[:, g : g + 1] * mod, axis=0, keepdims=True))
    items, _, tokens = mask_ref.shape
    total = jnp.zeros((1, 1), F32)
    for i in range(items):
        present = jnp.maximum(mask_ref[i], 0).astype(F32)
        weighed = jnp.sum(present, axis=0, keepdims=True) * line_weights(
            samples[i], cosines, seq, iota((1, tokens), 1)
        )
        total = total + jnp.sum(weighed, axis=1, keepdims=True)
    ride(6, jnp.broadcast_to(total, (1, 3 * D)))
    second_ref[rows:, :] = rider_s[...].astype(BF16)


def line_weights(count, cosines, seq, position):
    lines = position.size // COLS
    value = jnp.zeros(position.shape, F32)
    for r in range(lines):
        value = jnp.where(position // COLS == r, cosines[seq * lines + r], value)
    return value * count.astype(F32)


def pack_late(wide_a, wide_b, wide_c, tall_ref, late_ref):
    rows = wide_a.shape[0]
    late_ref[:, : 3 * D] = wide_a[...].astype(BF16)
    late_ref[:, 3 * D : 6 * D] = wide_b[...].astype(BF16)
    rest = D + FF + OUT - 6 * D
    late_ref[:, 6 * D : D + FF + OUT] = wide_c[:, :rest].astype(BF16)
    late_ref[:, D + FF + OUT : D + FF + OUTP] = jnp.zeros((rows, OUTP - OUT), BF16)
    late_ref[:, D + FF + OUTP :] = tall_ref[:, OUT:].astype(BF16)


def assemble(target, blocks, grp, lo, hi):
    rows = target.shape[0] // len(blocks)
    for j, ref in enumerate(blocks):
        at = pl.multiple_of(jnp.bitwise_xor(grp, j) * rows, 16)
        target[pl.ds(at, rows), :] = ref[:rows, lo:hi]


def unride(target, blocks):
    target[...] = jnp.zeros_like(target)
    for g in range(4):
        for half in range(2):
            total = jnp.zeros((1, 3 * D), F32)
            for ref in blocks:
                for part in range(3):
                    at = ref.shape[0] - RIDERS + part * 8 + min(2 * g + half, 6)
                    total = total + ref[at : at + 1, : 3 * D].astype(F32)
            target[g : g + 1, half * 3 * D : (half + 1) * 3 * D] = total


def prepare(blocks, grp, outs, score_s, fused_s):
    (agg_ref, embed_ref, fused_ref, probe_ref) = outs
    assemble(agg_ref, blocks, grp, 0, 2 * D)
    assemble(embed_ref, blocks, grp, 2 * D, 2 * D + OUTP)
    query = embed_ref[:, OUT : OUT + 1].astype(F32)
    picked = jnp.where(iota((D, 128), 1) == iota((D, 128), 0) // HEAD, query, 0.0).astype(BF16)
    probe = nn(agg_ref[:, :D], picked).astype(BF16)
    probe_ref[...] = probe
    embed = embed_ref[:, :OUT]
    rows = tn(probe, embed) * SCALE
    mine = spread()
    for h in range(HEADS):
        score_s[h * VARP : (h + 1) * VARP, :] = jnp.where(mine, rows[h : h + 1, :], 0.0).astype(
            BF16
        )
    fused = tn(agg_ref[:, D:], embed)
    fused_s[...] = fused.astype(BF16)
    fused_ref[...] = fused.T.astype(BF16)


def aggregate(group, *refs):
    (fields_ref, mask_ref) = refs[:2]
    blocks, outs = refs[2 : 2 + group], refs[2 + group :]
    (probs_ref, picked_ref, gathered_ref), kept = outs[:3], outs[3:7]
    score_s, fused_s, turned_s = outs[7:]
    grp, _ = place()

    @pl.when(pl.program_id(0) == 0)
    def _():
        prepare(blocks, grp, kept, score_s, fused_s)

    fields = fields_ref[0]
    wide_fields = fields.astype(F32)
    mask = mask_ref[0]
    scores = nn(score_s[...], fields)
    expand = ones_where(iota((OUT, VARP), 0) // PIX == iota((OUT, VARP), 1))
    rounded = []
    for h in range(HEADS):
        s = jnp.where(
            mask > 0,
            scores[h * VARP : (h + 1) * VARP],
            jnp.where(mask < 0, -3e38, masked_score),
        )
        e = jnp.exp(s - jnp.max(s, axis=0, keepdims=True))
        a = e / jnp.sum(e, axis=0, keepdims=True)
        probs_ref[0, h * VARP : (h + 1) * VARP, :] = a
        rounded.append(a.astype(BF16))
    expanded = nn(expand, rounded[0])
    for h in range(HEADS):
        later = nn(expand, rounded[h + 1]) if h + 1 < HEADS else None
        picked = (expanded * wide_fields).astype(BF16)
        picked_ref[h, 0] = picked
        turned_s[h * HEAD : (h + 1) * HEAD, :] = nn(fused_s[h * HEAD : (h + 1) * HEAD, :], picked)
        expanded = later
    gathered_ref[...] = turned_s[...].T.astype(BF16)


def project(group, *refs):
    (interval, gathered_ref), blocks, outs = refs[:2], refs[2 : 2 + group], refs[2 + group :]
    (x0_ref, n1_ref, weights, mod_s), units, (unit_s,) = outs[:4], outs[4:-1], outs[-1:]
    item = pl.program_id(0)
    grp, seq = place()
    tokens = gathered_ref.shape[0]

    @pl.when(item == 0)
    def _():
        assemble(weights, blocks, grp, 0, 4 * D)
        unride(mod_s, blocks)

    x0 = nn(gathered_ref[...], weights[:, :D])
    x0_ref[...] = x0
    mod = mod_s[pl.ds(interval[item], 1), :]
    normed, _ = standardize(x0)
    n1 = (normed * (1.0 + mod[:, D : 2 * D]) + mod[:, :D]).astype(BF16)
    n1_ref[...] = n1
    qkv = nn(n1, weights[:, D:])
    half = tokens // 2
    low = half_low((half, 128))
    packed = tokens + half
    for h in range(HEADS):
        unit_s[HEADS * item + h, :tokens, :] = qkv[:, h * 128 : (h + 1) * 128].astype(BF16)
    for j in range(HEADS // 2):
        pair = qkv[:, 2 * D + j * 128 : 2 * D + (j + 1) * 128] * (SCALE * LOG2E)
        top, bottom = pair[:half], pair[half:]
        unit_s[HEADS * item + 2 * j, tokens:packed, :] = jnp.where(
            low, top, swap_halves(bottom)
        ).astype(BF16)
        unit_s[HEADS * item + 2 * j + 1, tokens:packed, :] = jnp.where(
            low, swap_halves(top), bottom
        ).astype(BF16)

    @pl.when(item == pl.num_programs(0) - 1)
    def _():
        value = jnp.broadcast_to(mod_s[3:4, :128], (16, 128))
        high = value.astype(BF16)
        value = value - high.astype(F32)
        middle_part = value.astype(BF16)
        low_part = (value - middle_part.astype(F32)).astype(BF16)
        lane = iota((16, 128), 1)
        rides = jnp.where(
            lane < 32,
            high.astype(F32),
            jnp.where(
                lane < 64,
                middle_part.astype(F32),
                jnp.where(lane < 96, low_part.astype(F32), 0.0),
            ),
        ).astype(BF16)
        a = seq // (lax.axis_size("seq") // CUTS)
        rounds = unit_s.shape[0] // CUTS
        queries = rounds * tokens + 16
        for m in range(CUTS):
            units[m][rounds * tokens : queries, :] = rides
            for r in range(rounds):
                unit = CUTS * r + jnp.bitwise_xor(a, m)
                units[m][r * tokens : (r + 1) * tokens, :] = unit_s[unit, :tokens, :]
                at = queries + r * half
                units[m][at : at + half, :] = unit_s[unit, tokens:packed, :]


def deal(targets, source, seq):
    a = seq // (lax.axis_size("seq") // CUTS)
    for m in range(CUTS):
        for r in range(targets[m].shape[0]):
            targets[m][r] = source[CUTS * r + jnp.bitwise_xor(a, m)]


def collect(target, sources, seq):
    a = seq // (lax.axis_size("seq") // CUTS)
    for m in range(CUTS):
        for r in range(sources[m].shape[0]):
            target[CUTS * r + jnp.bitwise_xor(a, m)] = sources[m][r]


def unpack(pack, at_low):
    wide = pack.astype(F32)
    low = half_low(wide.shape)
    if at_low:
        both = [jnp.where(low, wide, 0.0), jnp.where(low, swap_halves(wide), 0.0)]
    else:
        both = [jnp.where(low, 0.0, swap_halves(wide)), jnp.where(low, 0.0, wide)]
    return jnp.concatenate(both, axis=0).astype(BF16)


def pack_rows(tile, at_low):
    half = tile.shape[0] // 2
    top, bottom = tile[:half], tile[half:]
    low = half_low(top.shape)
    if at_low:
        return jnp.where(low, top, swap_halves(bottom))
    return jnp.where(low, swap_halves(top), bottom)


def attend(shares, *refs):
    own = refs[:CUTS]
    others = refs[CUTS : CUTS * shares]
    backs = refs[CUTS * shares : CUTS * shares + CUTS]
    kept_ref, lse_ref, weight_ref, keys_s = refs[CUTS * shares + CUTS :]
    tokens = kept_ref.shape[2]
    half = tokens // 2
    unit = pl.program_id(0)
    rows = own[0].shape[0] - 16
    rider = rows * tokens // (tokens + half)

    @pl.when(unit == 0)
    def _():
        total = jnp.zeros((16, 128), F32)
        for ref in own + others:
            total = total + ref[rider : rider + 16, :].astype(F32)
        total = jnp.sum(total[0:8], axis=1, keepdims=True) / 32.0
        weight_ref[...] = jnp.broadcast_to(total, (8, 128))

    for n, ref in enumerate(own + others):
        at = pl.ds(pl.multiple_of(unit * tokens, tokens), tokens)
        keys_s[n * tokens : (n + 1) * tokens, :] = ref[at, :]
    keys = keys_s[...]
    values = jnp.where(half_low(keys.shape), jnp.ones_like(keys), keys)

    def scores_of(m):
        at = pl.ds(pl.multiple_of(rider + 16 + unit * half, 16), half)
        return nt(unpack(own[m][at, :], True), keys)

    scores = scores_of(0)
    for m in range(CUTS):
        later = scores_of(m + 1) if m + 1 < CUTS else None
        top = jnp.max(scores, axis=1, keepdims=True)
        out = nn(jnp.exp2(scores - top).astype(BF16), values)
        total = out[:, 0:1]
        out = out / total
        lse = jnp.broadcast_to(top + jnp.log2(total), (tokens, 128)).T
        lse_ref[0, m] = lse[:8]
        kept_ref[0, m] = out
        backs[m][0] = pack_rows(out, False).astype(BF16)
        scores = later


def middle(group, *refs):
    (interval, samples, cosines, sum_ref, x0_ref, fields_ref, mask_ref) = refs[:7]
    heads_in = refs[7 : 7 + CUTS]
    blocks = refs[7 + CUTS : 7 + CUTS + group]
    mod_s = refs[7 + CUTS + group]
    outs = refs[7 + CUTS + group + 1 :]
    (dx1_ref, rows_ref, loss_ref) = outs[:3]
    sends = outs[3 : 3 + CUTS]
    attended_s, db1_ref, n2_ref, dh_ref, nf_ref, dpred_ref, db2_ref, active_ref = outs[
        3 + CUTS : 11 + CUTS
    ]
    weights, head_s, grad_s = outs[11 + CUTS :]
    item = pl.program_id(0)
    grp, seq = place()
    tokens = x0_ref.shape[0]
    half = tokens // 2

    @pl.when(item == 0)
    def _():
        assemble(weights, blocks, grp, 0, D + FF + OUTP + FF)
        collect(head_s, heads_in, seq)
        loss_ref[...] = jnp.zeros_like(loss_ref)

    low = half_low((half, 128))
    for j in range(HEADS // 2):
        one = head_s[HEADS * item + 2 * j].astype(F32)
        two = head_s[HEADS * item + 2 * j + 1].astype(F32)
        attended_s[:half, j * 128 : (j + 1) * 128] = jnp.where(low, one, swap_halves(two)).astype(
            BF16
        )
        attended_s[half:, j * 128 : (j + 1) * 128] = jnp.where(low, swap_halves(one), two).astype(
            BF16
        )
    out_w = slice(0, D)
    up_w = slice(D, D + FF)
    head_w = slice(D + FF, D + FF + OUT)
    down_w = slice(D + FF + OUTP, D + FF + OUTP + FF)
    mod = mod_s[pl.ds(interval[item], 1), :]
    gate_a, shift_b, scale_b, gate_b = [mod[:, k * D : (k + 1) * D] for k in range(2, 6)]
    attended = attended_s[...]
    branch_a = nn(attended, weights[:, out_w])
    x1 = x0_ref[...] + gate_a * branch_a
    normed_b, rstd_b = standardize(x1)
    n2 = (normed_b * (1.0 + scale_b) + shift_b).astype(BF16)
    n2_ref[...] = n2
    value, slope = gelu_parts(nn(n2, weights[:, up_w]))
    active = value.astype(BF16)
    active_ref[...] = active
    branch_b = nt(active, weights[:, down_w])
    x2 = x1 + gate_b * branch_b
    final, rstd_f = standardize(x2)
    nf = final.astype(BF16)
    nf_ref[...] = nf
    diff = nn(nf, weights[:, head_w]) - fields_ref[0].astype(F32).T
    present = tn(ones_where(mask_ref[0] > 0), ones_where(spread()))
    weight = line_weights(samples[item], cosines, seq, iota((tokens, 1), 0))
    weight_grad = weight * (2.0 / PIX) / sum_ref[0:1, 0:1]
    masked = present * diff
    each = jnp.sum(masked * diff, axis=1, keepdims=True) * weight
    loss_ref[...] += jnp.broadcast_to(jnp.sum(each, axis=0, keepdims=True) / PIX, (8, 128))
    dpred = (masked * weight_grad).astype(BF16)
    dpred_ref[...] = dpred

    dx2 = standardize_back(nt(dpred, weights[:, head_w]), final, rstd_f)
    db2 = (gate_b * dx2).astype(BF16)
    db2_ref[...] = db2
    d_gate_b = jnp.sum(dx2 * branch_b, axis=0, keepdims=True)
    dh = (nn(db2, weights[:, down_w]) * slope).astype(BF16)
    dh_ref[...] = dh
    dn2 = nt(dh, weights[:, up_w])
    d_shift_b = jnp.sum(dn2, axis=0, keepdims=True)
    d_scale_b = jnp.sum(dn2 * normed_b, axis=0, keepdims=True)
    dx1 = dx2 + standardize_back(dn2 * (1.0 + scale_b), normed_b, rstd_b)
    dx1_ref[...] = dx1
    d_gate_a = jnp.sum(dx1 * branch_a, axis=0, keepdims=True)
    db1 = (gate_a * dx1).astype(BF16)
    db1_ref[...] = db1
    dout = nt(db1, weights[:, out_w])
    rows_ref[0] = jnp.concatenate(
        [d_gate_a, d_shift_b, d_scale_b, d_gate_b, jnp.zeros((4, D), F32)], axis=0
    )
    for j in range(HEADS // 2):
        pair = dout[:, j * 128 : (j + 1) * 128]
        top, bottom = pair[:half], pair[half:]
        grad_s[HEADS * item + 2 * j] = jnp.where(low, top, swap_halves(bottom)).astype(BF16)
        grad_s[HEADS * item + 2 * j + 1] = jnp.where(low, swap_halves(top), bottom).astype(BF16)

    @pl.when(item == pl.num_programs(0) - 1)
    def _():
        deal(sends, grad_s, seq)


def middle_weights(*refs):
    attended, db1, n2, dh, nf, dpred, db2, active = refs[:8]
    keep_ref, send_ref, acc = refs[8:]
    grp, _ = place()
    acc[:, :D] = tn(attended[...], db1[...])
    acc[:, D : D + FF] = tn(n2[...], dh[...])
    acc[:, D + FF : D + FF + OUT] = tn(nf[...], dpred[...])
    acc[:, D + FF + OUT : D + FF + OUTP] = jnp.zeros((D, OUTP - OUT), F32)
    acc[:, D + FF + OUTP :] = tn(db2[...], active[...])
    split_rows(acc, grp, keep_ref, send_ref)


def split_rows(acc, grp, keep_ref, send_ref):
    rows = keep_ref.shape[1]
    for j in range(keep_ref.shape[0]):
        for odd, ref in ((0, keep_ref), (1, send_ref)):
            at = pl.multiple_of(jnp.bitwise_xor(grp, 2 * j + odd) * rows, 16)
            ref[j, :, : acc.shape[1]] = acc[pl.ds(at, rows), :].astype(BF16)


def attend_back(shares, unit, *refs):
    own = refs[:CUTS]
    others = refs[CUTS : CUTS * shares]
    grads = refs[CUTS * shares : CUTS * shares + CUTS]
    kept_ref, lse_ref = refs[CUTS * shares + CUTS : CUTS * shares + CUTS + 2]
    outs = refs[CUTS * shares + CUTS + 2 :]
    dq_ref, own_ref = outs[:2]
    far_refs = outs[2 : 2 + shares - 1]
    keys_s, turned_s, acc = outs[2 + shares - 1 :]
    tokens = kept_ref.shape[2]
    for n, ref in enumerate(own + others):
        keys_s[n * tokens : (n + 1) * tokens, :] = ref[unit * tokens : (unit + 1) * tokens, :]
    turned_s[...] = keys_s[...].T
    every = range(CUTS)
    half = tokens // 2
    at = (own[0].shape[0] - 16) * tokens // (tokens + half) + 16 + unit * half
    queries = jnp.concatenate(
        [unpack(own[m][at : at + half, :], True) for m in every], axis=0
    )
    grads = [unpack(grads[m][0], False) for m in every]
    delta = jnp.concatenate(
        [
            jnp.sum((grads[m].astype(F32) * kept_ref[0, m]).T, axis=0, keepdims=True)
            for m in every
        ],
        axis=1,
    )
    grads = jnp.concatenate(grads, axis=0)
    lse = jnp.concatenate([lse_ref[0, m, 0:1, :] for m in every], axis=1)
    chunk = 2 * tokens
    count = keys_s.shape[0] // chunk

    def products_of(c):
        keys = keys_s[c * chunk : (c + 1) * chunk, :]
        return nt(keys, queries), nt(keys, grads)

    products, dq = products_of(0), None
    for c in range(count):
        scores, dprobs = products
        if c + 1 < count:
            products = products_of(c + 1)
        probs = jnp.exp2(scores - lse)
        dscores = (probs * (dprobs - delta)).astype(BF16)
        acc[c * chunk : (c + 1) * chunk, :] = nn(probs.astype(BF16), grads) + nn(dscores, queries)
        part = nn(turned_s[:, c * chunk : (c + 1) * chunk], dscores)
        dq = part if dq is None else dq + part
    for m in every:
        turned = dq[:, m * tokens : (m + 1) * tokens].T * SCALE
        dq_ref[0, m] = pack_rows(turned, True).astype(BF16)
    factor = jnp.where(half_low((1, 128)), 1.0 / LOG2E, 1.0)
    for m in range(CUTS):
        own_ref[0, m] = (acc[m * tokens : (m + 1) * tokens, :] * factor).astype(BF16)
        for n, ref in enumerate(far_refs):
            at = ((n + 1) * CUTS + m) * tokens
            ref[0, m] = (acc[at : at + tokens, :] * factor).astype(BF16)


def join_back(shares, *refs):
    dq_ref, own_ref = refs[:2]
    far = refs[2 : 2 + shares - 1]
    outs = refs[2 + shares - 1 :]
    tokens = own_ref.shape[2]
    for m in range(CUTS):
        total = own_ref[0, m].astype(F32)
        for ref in far:
            total = total + ref[0, m].astype(F32)
        outs[m][:tokens, :] = total.astype(BF16)
        outs[m][tokens:, :] = dq_ref[0, m]


def project_back(rounds, *refs):
    (interval, x0_ref, n1_ref, dx1_ref, rows_ref, gathered_ref, weights, mod_s) = refs[:8]
    units, outs = refs[8 : 8 + CUTS * rounds], refs[8 + CUTS * rounds :]
    (dagg_ref, keep_ref, send_ref) = outs[:3]
    unit_s, dqkv_s, acc, dmod_ref, lines_s = outs[3:]
    item = pl.program_id(0)
    grp, seq = place()
    tokens = x0_ref.shape[0]
    half = tokens // 2

    @pl.when(item == 0)
    def _():
        a = seq // (lax.axis_size("seq") // CUTS)
        for r in range(rounds):
            for m in range(CUTS):
                unit_s[CUTS * r + jnp.bitwise_xor(a, m)] = units[CUTS * r + m][...]
        acc[...] = jnp.zeros_like(acc)
        dmod_ref[...] = jnp.zeros_like(dmod_ref)

    low = half_low((half, 128))
    for h in range(HEADS):
        dqkv_s[:, h * 128 : (h + 1) * 128] = unit_s[HEADS * item + h, :tokens, :]
    for j in range(HEADS // 2):
        one = unit_s[HEADS * item + 2 * j, tokens:, :].astype(F32)
        two = unit_s[HEADS * item + 2 * j + 1, tokens:, :].astype(F32)
        lanes = slice(2 * D + j * 128, 2 * D + (j + 1) * 128)
        dqkv_s[:half, lanes] = jnp.where(low, one, swap_halves(two)).astype(BF16)
        dqkv_s[half:, lanes] = jnp.where(low, swap_halves(one), two).astype(BF16)
    dqkv = dqkv_s[...]
    which = interval[item]
    mod = mod_s[pl.ds(which, 1), :]
    acc[:, D:] += tn(n1_ref[...], dqkv)
    dn1 = nt(dqkv, weights[:, D:])
    normed, rstd = standardize(x0_ref[...])
    d_shift = jnp.sum(dn1, axis=0, keepdims=True)
    d_scale = jnp.sum(dn1 * normed, axis=0, keepdims=True)
    dx0 = (
        dx1_ref[...] + standardize_back(dn1 * (1.0 + mod[:, D : 2 * D]), normed, rstd)
    ).astype(BF16)
    rows = rows_ref[0]
    for k, row in enumerate([d_shift, d_scale] + [rows[r : r + 1] for r in range(4)]):
        dmod_ref[pl.ds(which, 1), k * D : (k + 1) * D] += row

    acc[:, :D] += tn(gathered_ref[...], dx0)
    dagg_ref[0] = nt(weights[:, :D], dx0).astype(BF16)

    @pl.when(item == pl.num_programs(0) - 1)
    def _():
        split_rows(acc, grp, keep_ref, send_ref)
        lines_s[...] = jnp.zeros_like(lines_s)
        for t in range(6 * D // 128):
            lines_s[4 * t : 4 * t + 3, :] = dmod_ref[0:3, t * 128 : (t + 1) * 128]
        rows = keep_ref.shape[1]
        for t in range(mod_tiles(rows)):
            tile = lines_s[t * rows : (t + 1) * rows, :].astype(BF16)
            at = acc.shape[1] + t * 128
            for j in range(keep_ref.shape[0]):
                keep_ref[j, :, at : at + 128] = tile
                send_ref[j, :, at : at + 128] = tile


def aggregate_back(*refs):
    (dagg_ref, probs_ref, picked_ref, fields_ref, mask_ref) = refs[:5]
    (fused_ref, agg_ref, embed_ref, probe_ref) = refs[5:9]
    keep_ref, send_ref, ds_s, acc, mix, dscore = refs[9:]
    item = pl.program_id(0)
    grp, _ = place()
    tokens = dagg_ref.shape[2]

    @pl.when(item == 0)
    def _():
        mix[...] = jnp.zeros_like(mix)
        dscore[...] = jnp.zeros_like(dscore)

    dagg = dagg_ref[0].astype(F32)
    fields = fields_ref[0]
    wide_fields = fields.astype(F32)
    keep = mask_ref[0] > 0
    expand = ones_where(spread())
    upper = iota((128, tokens), 0) < HEAD
    dparts = []
    for h in range(HEADS):
        mine = upper if h % 2 == 0 else jnp.logical_not(upper)
        pair = slice(h // 2 * 128, (h // 2 + 1) * 128)
        dparts.append(jnp.where(mine, dagg[pair], 0.0).astype(BF16))

    def spread_out(h):
        return nn(fused_ref[:, h // 2 * 128 : (h // 2 + 1) * 128], dparts[h])

    spreaded = spread_out(0)
    for j in range(HEADS // 2):
        both = None
        for h in (2 * j, 2 * j + 1):
            later = spread_out(h + 1) if h + 1 < HEADS else None
            spreaded = (spreaded * wide_fields).astype(BF16)
            part = nt(picked_ref[h, 0], dparts[h])
            both = part if both is None else both + part
            dprobs = nn(expand, spreaded)
            probs = probs_ref[0, h * VARP : (h + 1) * VARP, :]
            ds = probs * (dprobs - jnp.sum(probs * dprobs, axis=0, keepdims=True))
            ds_s[h * VARP : (h + 1) * VARP, :] = jnp.where(keep, ds, 0.0).astype(BF16)
            spreaded = later
        mix[:, j * 128 : (j + 1) * 128] += both
    dscore[...] += nt(ds_s[...], fields)

    @pl.when(item == pl.num_programs(0) - 1)
    def _():
        lines = iota((128, OUT), 0)
        owned = spread()
        drows = jnp.zeros((128, OUT), F32)
        for h in range(HEADS):
            mine = dscore[h * VARP : (h + 1) * VARP, :]
            line = jnp.sum(jnp.where(owned, mine, 0.0), axis=0, keepdims=True) * SCALE
            drows = drows + jnp.where(lines == h, line, 0.0)
        drows = drows.astype(BF16)
        mixed = mix[...].astype(BF16)
        embed = embed_ref[:, :OUT]
        acc[:, 2 * D : 2 * D + OUT] = nt(agg_ref[:, D:], mixed) + nn(probe_ref[...], drows)
        acc[:, D : 2 * D] = nn(embed, mixed)
        dprobe = nt(embed, drows)
        heads = jnp.where(iota((128, D), 1) // HEAD == iota((128, D), 0), 1.0, 0.0).astype(BF16)
        coarse = dprobe.astype(BF16)
        fine = (dprobe - coarse.astype(F32)).astype(BF16)
        by_column = nn(coarse, heads) + nn(fine, heads)
        eye = iota((D, D), 0) == iota((D, D), 1)
        query = embed_ref[:, OUT : OUT + 1].astype(F32)
        query_row = jnp.sum(jnp.where(eye, query, 0.0), axis=0, keepdims=True)
        acc[:, :D] = by_column * query_row
        dquery = jnp.sum(agg_ref[:, :D].astype(F32) * by_column, axis=0, keepdims=True)
        column = jnp.sum(jnp.where(eye, dquery, 0.0), axis=1, keepdims=True)
        acc[:, 2 * D + OUT :] = jnp.where(iota((D, OUTP - OUT), 1) == 0, column, 0.0)
        split_rows(acc, grp, keep_ref, send_ref)


def mod_tiles(rows):
    return -(-4 * (6 * D // 128) // rows)


def shares_of():
    shares = lax.axis_size("seq") // CUTS
    _, seq = place()
    return shares, seq // shares, lax.rem(seq, shares)


def added(refs, at=None):
    total = None
    for ref in refs:
        value = (ref[...] if at is None else ref[at]).astype(F32)
        total = value if total is None else total + value
    return total


def sum_cores(pairs, sources, *refs):
    ins, outs, table = refs[: 2 * sources], refs[2 * sources : -1], refs[-1]
    shares, _, share = shares_of()
    first, second = outs[:pairs], outs[pairs:]
    half = table.shape[1] // 2
    size = half // shares
    per = ins[0].shape[1] // 16
    count = sum(ref.shape[2] for ref in ins[::2]) // 128 * per
    for j in range(pairs):
        at = 0
        for keep_ref, got_ref in zip(ins[::2], ins[1::2]):
            total = (keep_ref[j].astype(F32) + got_ref[j].astype(F32)).astype(BF16)
            for t in range(total.shape[1] // 128):
                for g in range(per):
                    table[j, at] = total[g * 16 : (g + 1) * 16, t * 128 : (t + 1) * 128]
                    at += 1
        for spare in range(count, 2 * half):
            table[j, spare] = jnp.zeros(table.shape[2:], BF16)
        first[j][...] = table[j, :half]
        for n in range(shares):
            at = half + jnp.bitwise_xor(share, n) * size
            second[n][j * size : (j + 1) * size] = table[j, pl.ds(at, size)]


def sum_cores_once(pairs, *refs):
    (keep_ref, got_ref), outs = refs[:2], refs[2:]
    per = keep_ref.shape[1] // 16
    count = keep_ref.shape[2] // 128 * per
    for j in range(pairs):
        total = (keep_ref[j].astype(F32) + got_ref[j].astype(F32)).astype(BF16)
        for t in range(keep_ref.shape[2] // 128):
            for g in range(per):
                outs[j][t * per + g] = total[g * 16 : (g + 1) * 16, t * 128 : (t + 1) * 128]
        for spare in range(count, outs[j].shape[0]):
            outs[j][spare] = jnp.zeros(outs[j].shape[1:], BF16)


def sum_and_deal(over_cuts, *refs):
    outs, table = refs[-1 - (CUTS if over_cuts else shares_of()[0]) : -1], refs[-1]
    _, cut, share = shares_of()
    table[...] = added(refs[: -1 - len(outs)]).astype(BF16)
    size = outs[0].shape[0]
    for n, ref in enumerate(outs):
        ref[...] = table[pl.ds(jnp.bitwise_xor(cut if over_cuts else share, n) * size, size)]


def sum_both(pairs, shares, *refs):
    by_grp, by_share = refs[:pairs], refs[pairs : pairs + shares]
    outs, (table,) = refs[pairs + shares : -1], refs[-1:]
    _, _, share = shares_of()
    table[...] = added(by_grp).astype(BF16)
    size = outs[0].shape[0]
    for n in range(shares):
        outs[n][...] = table[pl.ds(jnp.bitwise_xor(share, n) * size, size)]
    for j in range(pairs):
        at = slice(j * size, (j + 1) * size)
        outs[shares + j][...] = added(by_share, at).astype(BF16)


def sum_both_again(pairs, shares, *refs):
    by_share, by_grp = refs[:shares], refs[shares : shares + pairs]
    outs, (table,) = refs[pairs + shares : -1], refs[-1:]
    _, cut, _ = shares_of()
    size = outs[0].shape[0] // 2
    table[0] = added(by_share).astype(BF16)
    table[1] = added(by_grp).astype(BF16)
    for m in range(CUTS):
        at = pl.ds(jnp.bitwise_xor(cut, m) * size, size)
        outs[m][:size] = table[0, at]
        outs[m][size:] = table[1, at]


def sum_pieces(*refs):
    sources, (out_ref, square_ref) = refs[:-2], refs[-2:]
    total = added(sources)
    out_ref[...] = total.astype(BF16)
    square_ref[...] = jnp.sum(total * total, axis=0)


def sum_late(start, stop, *refs):
    early_ref, loss_ref, lead_ref = refs[:3]
    sources, out_ref = refs[3:-1], refs[-1]
    grp, _ = place()
    shares, cut, share = shares_of()
    rows = lead_ref.shape[0] // lax.axis_size("grp")
    lead = lead_ref[pl.ds(pl.multiple_of(grp * rows, 16), rows), :].astype(F32)
    cols = [lead[:, g : g + 1] for g in range(3)]

    def gram(f, g):
        return jnp.sum(cols[f] * cols[g], axis=0, keepdims=True)

    row = lax.rem(iota((16, 1), 0), 4)

    def pick(*values):
        out = jnp.zeros((16, 1), F32)
        for r, value in values:
            out = jnp.where(row == r, value, out)
        return out

    same = pick(*[(g, gram(g, g)) for g in range(3)])
    next_one = pick((1, 2 * gram(0, 1)), (2, 2 * gram(1, 2)))
    next_two = pick((2, 2 * gram(0, 2)))
    size = (out_ref.shape[0] - 1) // 2
    plain = jnp.zeros((16, 128), F32)
    for half in range(2):
        for k in range(size):
            total = added(sources, half * size + k)
            out_ref[half * size + k] = total.astype(BF16)
            index = ((half * shares + share) * CUTS + cut) * size + k
            special = jnp.logical_and(index >= start, index < stop)
            square = total * total
            mixed = (
                square * same
                + total * pltpu.roll(total, 1, 0) * next_one
                + total * pltpu.roll(total, 2, 0) * next_two
            )
            plain = plain + jnp.where(special, mixed, square)
    squares = jnp.sum(jnp.sum(plain + early_ref[...], axis=0, keepdims=True), axis=1, keepdims=True)
    rider = jnp.zeros((16, 128), F32)
    for at, value in ((0, loss_ref[0:1, :]), (3, jnp.broadcast_to(squares, (1, 128)))):
        for part in range(3):
            piece = value.astype(BF16).astype(F32)
            rider = jnp.where(iota((16, 128), 0) == at + part, piece, rider)
            value = value - piece
    out_ref[2 * size] = rider.astype(BF16)


def stack_late(*refs):
    pieces, (column_ref, reduced_ref) = refs[:-2], refs[-2:]
    count = column_ref.shape[1]
    rider = jnp.zeros((16, 128), F32)
    for m, ref in enumerate(pieces):
        column_ref[m] = ref[:count]
        rider = rider + ref[count].astype(F32)
    reduced_ref[...] = jnp.concatenate(
        [rider[0:1] + rider[1:2] + rider[2:3], rider[3:4] + rider[4:5] + rider[5:6]]
        + [jnp.zeros((6, 128), F32)],
        axis=0,
    )


def stack(*refs):
    for m, ref in enumerate(refs[:-1]):
        refs[-1][m] = ref[...]


def step_values(param, first, second, grad):
    first = beta_first * first + (1.0 - beta_first) * grad
    second = beta_second * second + (1.0 - beta_second) * grad * grad
    mean_hat = first * (1.0 / (1.0 - beta_first**STEP))
    var_hat = second * (1.0 / (1.0 - beta_second**STEP))
    param = param - learn_rate * (
        mean_hat / (jnp.sqrt(var_hat) + adam_epsilon) + decay_rate * param
    )
    return param, first, second, param.astype(BF16)


def optimize(shares, *refs):
    reduced_ref, sum_ref, lead_ref = refs[:3]
    early = refs[3 : 3 + shares]
    late = refs[3 + shares : 3 + 2 * shares]
    wide = refs[3 + 2 * shares : 6 + 2 * shares]
    tall = refs[6 + 2 * shares : 9 + 2 * shares]
    query = refs[9 + 2 * shares : 12 + 2 * shares]
    outs = refs[12 + 2 * shares :]
    scalars, wide_hbm, tall_hbm, query_out = outs[:3], outs[3:7], outs[7:11], outs[11:15]
    early_s, late_s, wide_out, tall_out, sems = outs[15], outs[16], outs[17:21], outs[21:25], outs[25]
    grp, _ = place()
    _, cut, share = shares_of()
    for table, stacks, halves in ((early_s, early, 1), (late_s, late, 2)):
        size = stacks[0].shape[1] // halves
        for n, ref in enumerate(stacks):
            for m in range(CUTS):
                for half in range(halves):
                    at = (half * shares + jnp.bitwise_xor(share, n)) * CUTS
                    at = (at + jnp.bitwise_xor(cut, m)) * size
                    table[pl.ds(at, size)] = ref[m, half * size : (half + 1) * size]
    norm = jnp.sqrt(reduced_ref[1:2, 0:1])
    for ref, value in zip(scalars, (reduced_ref[0:1, 0:1], sum_ref[0:1, 0:1], norm)):
        ref[...] = value
    factor = jnp.minimum(1.0, clip_limit / (norm + 1e-06))
    rows = wide[0].shape[0]
    per = rows // 16

    def tile(table, t):
        return jnp.concatenate([table[t * per + g] for g in range(per)], axis=0).astype(F32)

    def put(ins, targets, at, grad):
        new = step_values(*[r[at] for r in ins], grad * factor)
        for ref, value in zip(targets, new):
            ref[at] = value

    def at(t, width=128):
        return (slice(None), slice(t * 128, t * 128 + width))

    copies = []

    def flush(sources, targets, lo, hi):
        for source, target in zip(sources, targets):
            copy = pltpu.make_async_copy(
                source.at[:, lo:hi], target.at[:, lo:hi], sems.at[len(copies)]
            )
            copy.start()
            copies.append(copy)

    low = half_low((rows, 128))
    for t in range(6):
        put(wide, wide_out, at(t), tile(late_s, t))
    for t in range(3):
        put(wide, wide_out, at(6 + t), tile(late_s, 15 + t))
    flush(wide_out, wide_hbm, 0, 3 * D)
    lead = lead_ref[pl.ds(pl.multiple_of(grp * rows, 16), rows), :].astype(F32)
    lines = jnp.concatenate([tile(late_s, 27 + t) for t in range(mod_tiles(rows))], axis=0)
    for t in range(18):
        grad = lead[:, 0:1] * lines[4 * t : 4 * t + 1]
        for g in (1, 2):
            grad = grad + lead[:, g : g + 1] * lines[4 * t + g : 4 * t + g + 1]
        put(wide, wide_out, at(9 + t), grad)
    flush(wide_out, wide_hbm, 3 * D, 9 * D)
    qkv = 18
    for j in range(3):
        put(wide, wide_out, at(27 + j), tile(late_s, qkv + 6 + j))
        one, two = tile(late_s, qkv + 2 * j), tile(late_s, qkv + 2 * j + 1)
        put(wide, wide_out, at(30 + j), jnp.where(low, one, swap_halves(two)))
        put(wide, wide_out, at(33 + j), jnp.where(low, swap_halves(one), two))
    flush(wide_out, wide_hbm, 9 * D, 12 * D)
    for t in range(15 + 8):
        put(wide, wide_out, at(36 + t), tile(early_s, t))
    rest = OUT - 8 * 128
    put(wide, wide_out, at(59, rest), tile(early_s, 23)[:, :rest])
    flush(wide_out, wide_hbm, 12 * D, wide[0].shape[1])
    for t in range(8):
        put(tall, tall_out, at(t), tile(late_s, 6 + t))
    flush(tall_out, tall_hbm, 0, 8 * 128)
    last = tile(late_s, 14)
    lane = iota((rows, 128), 1)
    for t in range(FF // 128):
        turned = pltpu.roll(tile(early_s, 24 + t), rest, 1)
        put(tall, tall_out, at(8 + t), jnp.where(lane < rest, last, turned))
        if t == 0:
            eye = iota((rows, rows), 0) == iota((rows, rows), 1)
            grad = jnp.sum(jnp.where(eye, last[:, rest : rest + 1], 0.0), axis=0, keepdims=True)
            put(query, query_out, (slice(None), slice(None)), grad)
        last = turned
    put(tall, tall_out, at(8 + FF // 128, rest), last[:, :rest])
    flush(tall_out, tall_hbm, 8 * 128, tall[0].shape[1])
    for copy in copies:
        copy.wait()


def shift(value, axis, bit):
    size = lax.axis_size(axis)
    return lax.ppermute(value, axis, [(i, i ^ bit) for i in range(size)])


def gather_blocks(own, group):
    blocks = {0: own}
    for j in range(2, group, 2):
        blocks[j] = shift(own, "grp", j)
    for j in range(0, group, 2):
        blocks[j + 1] = shift(blocks[j], "grp", 1)
    return [blocks[j] for j in range(group)]


def granules(rows, cols, shares):
    unit = 2 * shares * CUTS
    return -(-(rows // 16) * (cols // 128) // unit) * unit


def piece_shape(count):
    return sds((count, 16, 128), BF16)


def reduce_cores(*sources, after=()):
    pairs, rows, _ = sources[0][0].shape
    shares = lax.axis_size("seq") // CUTS
    count = granules(rows, sum(keep.shape[2] for keep, _ in sources), shares)
    results = call(
        functools.partial(sum_cores, pairs, len(sources)),
        [piece_shape(count // 2)] * pairs + [piece_shape(count // 2 // shares * pairs)] * shares,
        scratch=[pltpu.VMEM((pairs, count, 16, 128), BF16)],
        after=after,
    )(*[x for source in sources for x in source])
    return results[:pairs], results[pairs:]


def reduce_cores_once(keep, got, after=()):
    pairs, rows, cols = keep.shape
    parts = lax.axis_size("seq")
    count = -(-(rows // 16) * (cols // 128) // parts) * parts
    halves = call(
        functools.partial(sum_cores_once, pairs), [piece_shape(count)] * pairs, after=after
    )(keep, got)
    return [halves[0]] + [shift(halves[j], "grp", 2 * j) for j in range(1, pairs)]


def reduce_and_deal(pieces, over, after=()):
    count = pieces[0].shape[0]
    number = CUTS if over else lax.axis_size("seq") // CUTS
    outs = call(
        functools.partial(sum_and_deal, over),
        [piece_shape(count // number)] * number,
        scratch=[pltpu.VMEM((count, 16, 128), BF16)],
        after=after,
    )(*pieces)
    if over:
        return over_cuts(outs[0], outs[1:])
    return [outs[0]] + [shift(outs[n], "seq", n) for n in range(1, number)]


def exchange_once(by_grp, by_share):
    return [by_grp[0]] + [shift(by_grp[j], "grp", 2 * j) for j in range(1, len(by_grp))], [
        by_share[0]
    ] + [shift(by_share[n], "seq", n) for n in range(1, len(by_share))]


def reduce_once(by_grp, by_share, after=()):
    pairs, shares = len(by_grp), len(by_share)
    size = by_grp[0].shape[0] // shares
    results = call(
        functools.partial(sum_both, pairs, shares),
        [piece_shape(size)] * (pairs + shares),
        scratch=[pltpu.VMEM(by_grp[0].shape, BF16)],
        after=after,
    )(*by_grp, *by_share)
    return results[:shares], results[shares:]


def exchange_again(by_share, by_grp):
    pairs, shares = len(by_grp), len(by_share)
    return [by_share[0]] + [shift(by_share[n], "seq", n) for n in range(1, shares)], [
        by_grp[0]
    ] + [shift(by_grp[j], "grp", 2 * j) for j in range(1, pairs)]


def reduce_twice(by_share, by_grp, after=()):
    pairs, shares = len(by_grp), len(by_share)
    size = by_grp[0].shape[0]
    return call(
        functools.partial(sum_both_again, pairs, shares),
        [piece_shape(2 * size // CUTS)] * CUTS,
        scratch=[pltpu.VMEM((2, size, 16, 128), BF16)],
        after=after,
    )(*by_share, *by_grp)


def over_cuts(first, others=None):
    shares = lax.axis_size("seq") // CUTS
    sent = [first] * (CUTS - 1) if others is None else others
    return [first] + [shift(sent[m - 1], "seq", m * shares) for m in range(1, CUTS)]


def gather_shares(pieces, after=()):
    shares = lax.axis_size("seq") // CUTS
    column = call(stack, sds((CUTS,) + pieces[0].shape, BF16), after=after)(*pieces)
    return [column] + [shift(column, "seq", n) for n in range(1, shares)]


def butterfly(value, axis, bit, stop):
    while bit < stop:
        value = value + shift(value, axis, bit)
        bit *= 2
    return value


def lead_table():
    half = D // 2
    hours = 6.0 * np.exp2(np.arange(3, dtype=np.float32))
    freqs = np.exp(-np.log(np.float32(1000.0)) * np.arange(half, dtype=np.float32) / half)
    angles = hours[None, :] * freqs.astype(np.float32)[:, None]
    waves = np.concatenate([np.sin(angles), np.cos(angles)], axis=0)
    table = np.zeros((D, 128), np.float32)
    table[:, :3] = waves / (1.0 + np.exp(-waves))
    return jnp.asarray(table).astype(BF16)


def cosine_table(count):
    line = np.arange(count, dtype=np.float32)
    return jnp.asarray(np.cos(np.pi * ((line + 0.5) / count - 0.5)).astype(np.float32))


def per_device(
    fields,
    targets,
    land_mask,
    interval,
    samples,
    wide_weights,
    wide_firsts,
    wide_seconds,
    tall_weights,
    tall_firsts,
    tall_seconds,
    query_vector,
    query_firsts,
    query_seconds,
):
    group = lax.axis_size("grp")
    parts = lax.axis_size("seq")
    shares = parts // CUTS
    rows, columns = wide_weights.shape
    items, tokens = fields.shape[:2]
    units = items * HEADS // CUTS
    every = items * tokens
    late_cols = D + FF + OUTP + FF

    query_row = query_vector.reshape(1, rows)
    tall = [x.T for x in (tall_weights, tall_firsts, tall_seconds)]
    lead = lead_table()
    cosines = cosine_table(tokens // COLS * parts)
    fields = fields.transpose(0, 2, 1)
    targets = targets.transpose(0, 2, 1)
    mask = jnp.pad(
        land_mask.transpose(0, 2, 1), ((0, 0), (0, VARP - VARS), (0, 0)), constant_values=-1
    )

    def columns_of(index):
        return pl.BlockSpec((rows, 3 * D), lambda i: (0, index))

    first_own, second_own = call(
        pack_first,
        [sds((rows, 2 * D + OUTP), BF16), sds((rows + RIDERS, 4 * D), BF16)],
        grid=(1,),
        in_specs=[smem(), smem()]
        + [columns_of(i) for i in (0, 1, 2, 3, 0)]
        + [pl.BlockSpec((1, rows), lambda i: (0, 0)), whole(), whole()],
        out_specs=[whole()] * 2,
        scratch=[pltpu.VMEM((RIDERS, 4 * D), F32)],
        us=3,
        limit=62,
    )(samples, cosines, *[wide_weights] * 4, tall[0], query_row, lead, mask)
    first = gather_blocks(first_own, group)
    second = gather_blocks(second_own, group)
    late_own = call(
        pack_late,
        sds((rows, late_cols), BF16),
        grid=(1,),
        in_specs=[columns_of(4), columns_of(5), columns_of(6), whole()],
        out_specs=whole(),
        us=2,
        limit=62,
        after=(first_own,),
    )(wide_weights, wide_weights, wide_weights, tall[0])
    late_blocks = gather_blocks(late_own, group)

    by_item = pl.BlockSpec((tokens, D), lambda i: (i, 0))

    def lane_block(height):
        return pl.BlockSpec((1, height, tokens), lambda i: (i, 0, 0))

    heads_spec = pl.BlockSpec((HEADS, 1, OUT, tokens), lambda i: (0, i, 0, 0))
    packed = units * (tokens + tokens // 2) + 16

    probs, picked, gathered, agg_weights, embed, fused_w, probe = call(
        functools.partial(aggregate, group),
        [
            in_hbm((items, HEADS * VARP, tokens), F32),
            in_hbm((HEADS, items, OUT, tokens), BF16),
            sds((every, D), BF16),
            in_hbm((D, 2 * D), BF16),
            in_hbm((D, OUTP), BF16),
            in_hbm((OUT, D), BF16),
            in_hbm((D, 128), BF16),
        ],
        grid=(items,),
        in_specs=[lane_block(OUT), lane_block(VARP)] + [whole()] * group,
        out_specs=[lane_block(HEADS * VARP), heads_spec, by_item] + [whole()] * 4,
        scratch=[
            pltpu.VMEM((HEADS * VARP, OUT), BF16),
            pltpu.VMEM((D, OUT), BF16),
            pltpu.VMEM((D, tokens), F32),
        ],
        us=10,
        limit=34,
    )(fields, mask, *first)
    results = call(
        functools.partial(project, group),
        [
            in_hbm((every, D), F32),
            in_hbm((every, D), BF16),
            in_hbm((D, 4 * D), BF16),
            in_hbm((8, 6 * D), F32),
        ]
        + [sds((packed, 128), BF16)] * CUTS,
        grid=(items,),
        in_specs=[smem(), by_item] + [whole()] * group,
        out_specs=[by_item, by_item] + [whole()] * (2 + CUTS),
        scratch=[pltpu.VMEM((items * HEADS, tokens + tokens // 2, 128), BF16)],
        us=4,
        limit=34,
    )(interval, gathered, *second)
    x0, n1, second_weights, mods = results[:4]
    dealt = results[4:]

    own = over_cuts(dealt[0], dealt[1:])
    keys_only = [x[: units * tokens + 16] for x in own]
    others = [shift(keys_only[m], "seq", n) for n in range(1, shares) for m in range(CUTS)]
    keys_total = parts * tokens

    half_in = pl.BlockSpec((1, tokens // 2, 128), lambda u: (u, 0, 0))
    kept_spec = pl.BlockSpec((1, CUTS, tokens, 128), lambda u: (u, 0, 0, 0))
    lse_spec = pl.BlockSpec((1, CUTS, 8, tokens), lambda u: (u, 0, 0, 0))
    pack_spec = pl.BlockSpec((1, CUTS, tokens // 2, 128), lambda u: (u, 0, 0, 0))
    half_out = sds((units, tokens // 2, 128), BF16)
    results = call(
        functools.partial(attend, shares),
        [half_out] * CUTS
        + [
            in_hbm((units, CUTS, tokens, 128), F32),
            in_hbm((units, CUTS, 8, tokens), F32),
            in_hbm((8, 128), F32),
        ],
        grid=(units,),
        in_specs=[whole()] * (CUTS * shares),
        out_specs=[half_in] * CUTS + [kept_spec, lse_spec, whole()],
        scratch=[pltpu.VMEM((keys_total, 128), BF16)],
        us=9,
        limit=60 if shares > 2 else 34,
    )(*own, *others)
    backs, (kept, lse, weight_sum) = results[:CUTS], results[CUTS:]
    heads_in = over_cuts(backs[0], backs[1:])

    saved = [D, D, D, FF, D, OUT, D, FF]
    results = call(
        functools.partial(middle, group),
        [in_hbm((every, D), F32), in_hbm((items, 8, D), F32), in_hbm((8, 128), F32)]
        + [half_out] * CUTS
        + [sds((every, width), BF16) for width in saved],
        grid=(items,),
        in_specs=[smem(), smem(), smem(), whole(), by_item, lane_block(OUT), lane_block(VARP)]
        + [whole()] * (CUTS + group + 1),
        out_specs=[by_item, pl.BlockSpec((1, 8, D), lambda i: (i, 0, 0))]
        + [whole()] * (1 + CUTS)
        + [pl.BlockSpec((tokens, width), lambda i: (i, 0)) for width in saved],
        scratch=[
            pltpu.VMEM((D, late_cols), BF16),
            pltpu.VMEM((items * HEADS, tokens // 2, 128), BF16),
            pltpu.VMEM((items * HEADS, tokens // 2, 128), BF16),
        ],
        us=11,
        limit=34,
    )(
        interval,
        samples,
        cosines,
        weight_sum,
        x0,
        targets,
        mask,
        *heads_in,
        *late_blocks,
        mods,
    )
    dx1, mod_rows, loss = results[:3]
    sends, operands = results[3 : 3 + CUTS], results[3 + CUTS :]
    early_keep, early_send = call(
        middle_weights,
        [sds((group // 2, rows, late_cols), BF16)] * 2,
        scratch=[pltpu.VMEM((D, late_cols), F32)],
        us=6,
        limit=34,
    )(*operands)
    grads_in = over_cuts(sends[0], sends[1:])

    def of_unit(u, *shape):
        return pl.BlockSpec((1,) + shape, lambda i: (u,) + (0,) * len(shape))

    def back_of(u, after):
        results = call(
            functools.partial(attend_back, shares, u),
            [sds((1, CUTS, tokens // 2, 128), BF16)]
            + [sds((1, CUTS, tokens, 128), BF16)] * shares,
            grid=(1,),
            in_specs=[whole()] * (CUTS * shares)
            + [of_unit(u, tokens // 2, 128)] * CUTS
            + [of_unit(u, CUTS, tokens, 128), of_unit(u, CUTS, 8, tokens)],
            out_specs=[whole()] * (1 + shares),
            scratch=[
                pltpu.VMEM((keys_total, 128), BF16),
                pltpu.VMEM((128, keys_total), BF16),
                pltpu.VMEM((keys_total, 128), F32),
            ],
            us=6,
            limit=60 if shares > 2 else 34,
            after=after,
        )(*own, *others, *grads_in, kept, lse)
        far = results[2:]
        if u == 2:
            far = [once_ready(far[0], units_in[0][1:]), *far[1:]]
        return results[:2], [shift(far[n], "seq", n + 1) for n in range(shares - 1)]

    def joined(near, far):
        dealt = call(
            functools.partial(join_back, shares),
            [sds((tokens + tokens // 2, 128), BF16)] * CUTS,
        )(*near, *far)
        return over_cuts(dealt[0], dealt[1:])

    early_got = shift(early_send, "grp", 1)
    partial_sums, units_in = [], []
    for u in range(units):
        after = (early_keep,) if u == 0 else (partial_sums[u - 1][0][0],)
        if u == 2:
            early_once = reduce_cores_once(early_keep, early_got, after=after)
            after += (early_once[0],)
        if u >= 2:
            units_in.append(joined(*partial_sums[u - 2]))
        partial_sums.append(back_of(u, after))
    units_in.append(joined(*partial_sums[-2]))
    units_in.append(joined(*partial_sums[-1]))
    early_twice = reduce_and_deal(early_once, False, after=(units_in[1][1],))

    second_cols = 4 * D + mod_tiles(rows) * 128
    dagg, second_keep, second_send = call(
        functools.partial(project_back, units),
        [
            sds((items, D, tokens), BF16),
            sds((group // 2, rows, second_cols), BF16),
            sds((group // 2, rows, second_cols), BF16),
        ],
        grid=(items,),
        in_specs=[
            smem(),
            by_item,
            by_item,
            by_item,
            pl.BlockSpec((1, 8, D), lambda i: (i, 0, 0)),
            by_item,
        ]
        + [whole()] * (2 + CUTS * units),
        out_specs=[pl.BlockSpec((1, D, tokens), lambda i: (i, 0, 0))] + [whole()] * 2,
        scratch=[
            pltpu.VMEM((items * HEADS, tokens + tokens // 2, 128), BF16),
            pltpu.VMEM((tokens, 3 * D), BF16),
            pltpu.VMEM((D, 4 * D), F32),
            pltpu.VMEM((8, 6 * D), F32),
            pltpu.VMEM((mod_tiles(rows) * rows, 128), F32),
        ],
        us=4,
        limit=34,
    )(
        interval,
        x0,
        n1,
        dx1,
        mod_rows,
        gathered,
        second_weights,
        mods,
        *[x for unit in units_in for x in unit],
    )
    second_got = shift(second_send, "grp", 1)
    early_pieces = reduce_and_deal(early_twice, True, after=(dagg,))
    late_keep, late_send = call(
        aggregate_back,
        [sds((group // 2, rows, 2 * D + OUTP), BF16)] * 2,
        grid=(items,),
        in_specs=[
            pl.BlockSpec((1, D, tokens), lambda i: (i, 0, 0)),
            lane_block(HEADS * VARP),
            heads_spec,
            lane_block(OUT),
            lane_block(VARP),
        ]
        + [whole()] * 4,
        out_specs=[whole()] * 2,
        scratch=[
            pltpu.VMEM((HEADS * VARP, tokens), BF16),
            pltpu.VMEM((D, 2 * D + OUTP), F32),
            pltpu.VMEM((OUT, D), F32),
            pltpu.VMEM((HEADS * VARP, OUT), F32),
        ],
        us=13,
        limit=34,
        after=(early_pieces[0],),
    )(dagg, probs, picked, fields, mask, fused_w, agg_weights, embed, probe)
    early_piece, early_squares = call(
        sum_pieces,
        [piece_shape(early_pieces[0].shape[0]), sds((16, 128), F32)],
        after=(late_keep,),
    )(*early_pieces)
    early_column = over_cuts(early_piece)
    late_first = reduce_cores(
        (late_keep, shift(late_send, "grp", 1)),
        (second_keep, second_got),
    )
    late_second = reduce_once(*exchange_once(*late_first))
    early_all = gather_shares(early_column, after=(late_second[0][0],))
    late_third = reduce_twice(*exchange_again(*late_second))
    late_pieces = over_cuts(late_third[0], late_third[1:])
    start = (rows // 16) * 27
    stop = (rows // 16) * (27 + mod_tiles(rows))
    count = late_pieces[0].shape[0]
    late_piece = call(
        functools.partial(sum_late, start, stop), piece_shape(count + 1)
    )(early_squares, loss, lead, *late_pieces)
    late_column, reduced = call(
        stack_late, [sds((CUTS, count, 16, 128), BF16), sds((8, 128), F32)]
    )(*over_cuts(late_piece))
    late_all = [late_column] + [shift(late_column, "seq", n) for n in range(1, shares)]
    reduced = butterfly(reduced, "grp", 1, group)
    reduced = butterfly(reduced, "seq", 1, shares)

    def like(x, dtype=F32):
        return sds(x.shape, dtype)

    results = call(
        functools.partial(optimize, shares),
        [sds((1, 1), F32)] * 3
        + [like(wide_weights)] * 3
        + [like(wide_weights, BF16)]
        + [like(tall[0])] * 3
        + [like(tall[0], BF16)]
        + [like(query_row)] * 3
        + [like(query_row, BF16)],
        out_specs=[whole()] * 3 + [pl.BlockSpec(memory_space=pl.ANY)] * 8 + [whole()] * 4,
        scratch=[
            pltpu.VMEM((parts * early_piece.shape[0], 16, 128), BF16),
            pltpu.VMEM((parts * count, 16, 128), BF16),
        ]
        + [pltpu.VMEM(wide_weights.shape, dtype) for dtype in (F32, F32, F32, BF16)]
        + [pltpu.VMEM(tall[0].shape, dtype) for dtype in (F32, F32, F32, BF16)]
        + [pltpu.SemaphoreType.DMA((24,))],
        us=10,
        limit=34,
    )(
        reduced,
        weight_sum,
        lead,
        *early_all,
        *late_all,
        wide_weights,
        wide_firsts,
        wide_seconds,
        *tall,
        query_row,
        query_firsts.reshape(1, rows),
        query_seconds.reshape(1, rows),
    )
    tall_out = tuple(r.T for r in results[7:11])
    query_out = tuple(r.reshape(rows) for r in results[11:15])
    return tuple(r.reshape(()) for r in results[:3]) + tuple(results[3:7]) + tall_out + query_out


def solution(mesh):
    placed = (
        P("grp", "seq", None),
        P("grp", "seq", None),
        P("grp", "seq", None),
        P("grp"),
        P("grp"),
        P("grp", None),
        P("grp", None),
        P("grp", None),
        P(None, "grp"),
        P(None, "grp"),
        P(None, "grp"),
        P("grp"),
        P("grp"),
        P("grp"),
    )
    return jax.shard_map(
        per_device,
        mesh=mesh,
        in_specs=placed,
        out_specs=(
            P(),
            P(),
            P(),
            P("grp", None),
            P("grp", None),
            P("grp", None),
            P("grp", None),
            P(None, "grp"),
            P(None, "grp"),
            P(None, "grp"),
            P(None, "grp"),
            P("grp"),
            P("grp"),
            P("grp"),
            P("grp"),
        ),
        check_vma=False,
    )
```

```python
import functools

import jax
import numpy as np
import jax.numpy as jnp
from jax import lax
from jax.experimental import pallas as pl
from jax.experimental.pallas import tpu as pltpu
from jax.sharding import PartitionSpec as P

D = 384
HEADS = 6
HEAD = 64
FF = 1536
VARS = 69
PIX = 16
OUT = VARS * PIX
OUTP = 1152
VARP = 80
COLS = 128
STEP = 5
CUTS = 4
SCALE = HEAD**-0.5
LOG2E = 1.4426950408889634

beta_first = 0.5
beta_second = 0.5
learn_rate = 0.1
decay_rate = 0.01
adam_epsilon = 1e-08
clip_limit = 0.05
norm_epsilon = 1e-06
masked_score = -1e30

F32 = jnp.float32
BF16 = jnp.bfloat16
MIB = 1024 * 1024
RIDERS = 32


def dot(left, right, a, b):
    return lax.dot_general(left, right, (((a,), (b,)), ((), ())), preferred_element_type=F32)


def nn(left, right):
    return dot(left, right, 1, 0)


def nt(left, right):
    return dot(left, right, 1, 1)


def tn(left, right):
    return dot(left, right, 0, 0)


def iota(shape, dim):
    return lax.broadcasted_iota(jnp.int32, shape, dim)


def half_low(shape):
    return iota(shape, len(shape) - 1) < HEAD


def swap_halves(tile):
    return pltpu.roll(tile, HEAD, 1)


def spread():
    return iota((VARP, OUT), 1) // PIX == iota((VARP, OUT), 0)


def ones_where(mask):
    return jnp.where(mask, 1.0, 0.0).astype(BF16)


def place():
    grp = lax.axis_index("grp")
    seq = lax.axis_index("seq")
    return grp, seq


def call(
    kernel, outs, grid=(), in_specs=None, out_specs=None, scratch=(), us=1, limit=34, after=()
):
    def run(*args):
        if after:
            args = (once_ready(args[0], after), *args[1:])
        kw = {} if out_specs is None else {"out_specs": out_specs}
        return pl.pallas_call(
            kernel,
            out_shape=outs,
            grid=grid,
            in_specs=list(in_specs) if in_specs else [whole()] * len(args),
            scratch_shapes=list(scratch),
            cost_estimate=pl.CostEstimate(
                flops=int(us * 1.15e9), transcendentals=0, bytes_accessed=1024
            ),
            compiler_params=pltpu.CompilerParams(vmem_limit_bytes=limit * MIB),
            **kw,
        )(*args)

    return run


def once_ready(value, after):
    return lax.optimization_barrier((value, *after))[0]


def whole():
    return pl.BlockSpec(memory_space=pltpu.VMEM)


def smem():
    return pl.BlockSpec(memory_space=pltpu.SMEM)


def sds(shape, dtype):
    return jax.ShapeDtypeStruct(shape, dtype)


def in_hbm(shape, dtype):
    return pltpu.HBM(shape, dtype)


def standardize(x):
    centered = x - jnp.mean(x, axis=-1, keepdims=True)
    rstd = lax.rsqrt(jnp.mean(centered * centered, axis=-1, keepdims=True) + norm_epsilon)
    return centered * rstd, rstd


def standardize_back(grad, normed, rstd):
    return rstd * (
        grad
        - jnp.mean(grad, axis=-1, keepdims=True)
        - normed * jnp.mean(grad * normed, axis=-1, keepdims=True)
    )


def gelu_parts(x):
    k = 0.7978845608028654
    inner = k * (x + 0.044715 * x * x * x)
    t = jnp.tanh(inner)
    value = 0.5 * x * (1.0 + t)
    slope = 0.5 * (1.0 + t) + 0.5 * x * (1.0 - t * t) * k * (1.0 + 3 * 0.044715 * x * x)
    return value, slope


def pack_first(*refs):
    samples, cosines, agg_ref, mod_a, mod_b, wide_ref, tall_ref, query_ref = refs[:8]
    lead_ref, mask_ref, first_ref, second_ref, rider_s = refs[8:]
    rows = wide_ref.shape[0]
    grp, seq = place()
    first_ref[:, : 2 * D] = agg_ref[:, : 2 * D].astype(BF16)
    second_ref[:rows, :D] = agg_ref[:, 2 * D :].astype(BF16)
    eye = iota((rows, rows), 0) == iota((rows, rows), 1)
    column = jnp.sum(jnp.where(eye, query_ref[...], 0.0), axis=1, keepdims=True)
    lane = iota((rows, OUTP), 1)
    embed = jnp.where(lane < OUT, tall_ref[...], jnp.where(lane == OUT, column, 0.0))
    first_ref[:, 2 * D :] = embed.astype(BF16)
    low = half_low((rows, 128))
    for j in range(HEADS // 2):
        k = wide_ref[:, D + j * 128 : D + (j + 1) * 128]
        v = wide_ref[:, 2 * D + j * 128 : 2 * D + (j + 1) * 128]
        at = D + 2 * j * 128
        second_ref[:rows, at : at + 128] = jnp.where(low, k, swap_halves(v)).astype(BF16)
        second_ref[:rows, at + 128 : at + 256] = jnp.where(low, swap_halves(k), v).astype(BF16)
    second_ref[:rows, 3 * D :] = wide_ref[:, :D].astype(BF16)
    rider_s[...] = jnp.zeros_like(rider_s)

    def ride(row, value):
        for part in range(3):
            piece = value.astype(BF16).astype(F32)
            at = part * 8 + row
            rider_s[at : at + 1, : 3 * D] = piece
            value = value - piece

    lead = lead_ref[pl.ds(pl.multiple_of(grp * rows, 16), rows), :].astype(F32)
    for half, ref in ((0, mod_a), (1, mod_b)):
        mod = ref[...].astype(BF16).astype(F32)
        for g in range(3):
            ride(2 * g + half, jnp.sum(lead[:, g : g + 1] * mod, axis=0, keepdims=True))
    items, _, tokens = mask_ref.shape
    total = jnp.zeros((1, 1), F32)
    for i in range(items):
        present = jnp.maximum(mask_ref[i], 0).astype(F32)
        weighed = jnp.sum(present, axis=0, keepdims=True) * line_weights(
            samples[i], cosines, seq, iota((1, tokens), 1)
        )
        total = total + jnp.sum(weighed, axis=1, keepdims=True)
    ride(6, jnp.broadcast_to(total, (1, 3 * D)))
    second_ref[rows:, :] = rider_s[...].astype(BF16)


def line_weights(count, cosines, seq, position):
    lines = position.size // COLS
    value = jnp.zeros(position.shape, F32)
    for r in range(lines):
        value = jnp.where(position // COLS == r, cosines[seq * lines + r], value)
    return value * count.astype(F32)


def pack_late(wide_a, wide_b, wide_c, tall_ref, late_ref):
    rows = wide_a.shape[0]
    late_ref[:, : 3 * D] = wide_a[...].astype(BF16)
    late_ref[:, 3 * D : 6 * D] = wide_b[...].astype(BF16)
    rest = D + FF + OUT - 6 * D
    late_ref[:, 6 * D : D + FF + OUT] = wide_c[:, :rest].astype(BF16)
    late_ref[:, D + FF + OUT : D + FF + OUTP] = jnp.zeros((rows, OUTP - OUT), BF16)
    late_ref[:, D + FF + OUTP :] = tall_ref[:, OUT:].astype(BF16)


def assemble(target, blocks, grp, lo, hi):
    rows = target.shape[0] // len(blocks)
    for j, ref in enumerate(blocks):
        at = pl.multiple_of(jnp.bitwise_xor(grp, j) * rows, 16)
        target[pl.ds(at, rows), :] = ref[:rows, lo:hi]


def unride(target, blocks):
    target[...] = jnp.zeros_like(target)
    for g in range(4):
        for half in range(2):
            total = jnp.zeros((1, 3 * D), F32)
            for ref in blocks:
                for part in range(3):
                    at = ref.shape[0] - RIDERS + part * 8 + min(2 * g + half, 6)
                    total = total + ref[at : at + 1, : 3 * D].astype(F32)
            target[g : g + 1, half * 3 * D : (half + 1) * 3 * D] = total


def prepare(blocks, grp, outs, score_s, fused_s):
    (agg_ref, embed_ref, fused_ref, probe_ref) = outs
    assemble(agg_ref, blocks, grp, 0, 2 * D)
    assemble(embed_ref, blocks, grp, 2 * D, 2 * D + OUTP)
    query = embed_ref[:, OUT : OUT + 1].astype(F32)
    picked = jnp.where(iota((D, 128), 1) == iota((D, 128), 0) // HEAD, query, 0.0).astype(BF16)
    probe = nn(agg_ref[:, :D], picked).astype(BF16)
    probe_ref[...] = probe
    embed = embed_ref[:, :OUT]
    rows = tn(probe, embed) * SCALE
    mine = spread()
    for h in range(HEADS):
        score_s[h * VARP : (h + 1) * VARP, :] = jnp.where(mine, rows[h : h + 1, :], 0.0).astype(
            BF16
        )
    fused = tn(agg_ref[:, D:], embed)
    fused_s[...] = fused.astype(BF16)
    fused_ref[...] = fused.T.astype(BF16)


def aggregate(group, *refs):
    (fields_ref, mask_ref) = refs[:2]
    blocks, outs = refs[2 : 2 + group], refs[2 + group :]
    (probs_ref, picked_ref, gathered_ref), kept = outs[:3], outs[3:7]
    score_s, fused_s, turned_s = outs[7:]
    grp, _ = place()

    @pl.when(pl.program_id(0) == 0)
    def _():
        prepare(blocks, grp, kept, score_s, fused_s)

    fields = fields_ref[0]
    wide_fields = fields.astype(F32)
    mask = mask_ref[0]
    scores = nn(score_s[...], fields)
    expand = ones_where(iota((OUT, VARP), 0) // PIX == iota((OUT, VARP), 1))
    rounded = []
    for h in range(HEADS):
        s = jnp.where(
            mask > 0,
            scores[h * VARP : (h + 1) * VARP],
            jnp.where(mask < 0, -3e38, masked_score),
        )
        e = jnp.exp(s - jnp.max(s, axis=0, keepdims=True))
        a = e / jnp.sum(e, axis=0, keepdims=True)
        probs_ref[0, h * VARP : (h + 1) * VARP, :] = a
        rounded.append(a.astype(BF16))
    expanded = nn(expand, rounded[0])
    for h in range(HEADS):
        later = nn(expand, rounded[h + 1]) if h + 1 < HEADS else None
        picked = (expanded * wide_fields).astype(BF16)
        picked_ref[h, 0] = picked
        turned_s[h * HEAD : (h + 1) * HEAD, :] = nn(fused_s[h * HEAD : (h + 1) * HEAD, :], picked)
        expanded = later
    gathered_ref[...] = turned_s[...].T.astype(BF16)


def project(group, *refs):
    (interval, gathered_ref), blocks, outs = refs[:2], refs[2 : 2 + group], refs[2 + group :]
    (x0_ref, n1_ref, weights, mod_s), units, (unit_s,) = outs[:4], outs[4:-1], outs[-1:]
    item = pl.program_id(0)
    grp, seq = place()
    tokens = gathered_ref.shape[0]

    @pl.when(item == 0)
    def _():
        assemble(weights, blocks, grp, 0, 4 * D)
        unride(mod_s, blocks)

    x0 = nn(gathered_ref[...], weights[:, :D])
    x0_ref[...] = x0
    mod = mod_s[pl.ds(interval[item], 1), :]
    normed, _ = standardize(x0)
    n1 = (normed * (1.0 + mod[:, D : 2 * D]) + mod[:, :D]).astype(BF16)
    n1_ref[...] = n1
    qkv = nn(n1, weights[:, D:])
    half = tokens // 2
    low = half_low((half, 128))
    packed = tokens + half
    for h in range(HEADS):
        unit_s[HEADS * item + h, :tokens, :] = qkv[:, h * 128 : (h + 1) * 128].astype(BF16)
    for j in range(HEADS // 2):
        pair = qkv[:, 2 * D + j * 128 : 2 * D + (j + 1) * 128] * (SCALE * LOG2E)
        top, bottom = pair[:half], pair[half:]
        unit_s[HEADS * item + 2 * j, tokens:packed, :] = jnp.where(
            low, top, swap_halves(bottom)
        ).astype(BF16)
        unit_s[HEADS * item + 2 * j + 1, tokens:packed, :] = jnp.where(
            low, swap_halves(top), bottom
        ).astype(BF16)

    @pl.when(item == pl.num_programs(0) - 1)
    def _():
        value = jnp.broadcast_to(mod_s[3:4, :128], (16, 128))
        high = value.astype(BF16)
        value = value - high.astype(F32)
        middle_part = value.astype(BF16)
        low_part = (value - middle_part.astype(F32)).astype(BF16)
        lane = iota((16, 128), 1)
        rides = jnp.where(
            lane < 32,
            high.astype(F32),
            jnp.where(
                lane < 64,
                middle_part.astype(F32),
                jnp.where(lane < 96, low_part.astype(F32), 0.0),
            ),
        ).astype(BF16)
        a = seq // (lax.axis_size("seq") // CUTS)
        rounds = unit_s.shape[0] // CUTS
        queries = rounds * tokens + 16
        for m in range(CUTS):
            units[m][rounds * tokens : queries, :] = rides
            for r in range(rounds):
                unit = CUTS * r + jnp.bitwise_xor(a, m)
                units[m][r * tokens : (r + 1) * tokens, :] = unit_s[unit, :tokens, :]
                at = queries + r * half
                units[m][at : at + half, :] = unit_s[unit, tokens:packed, :]


def deal(targets, source, seq):
    a = seq // (lax.axis_size("seq") // CUTS)
    for m in range(CUTS):
        for r in range(targets[m].shape[0]):
            targets[m][r] = source[CUTS * r + jnp.bitwise_xor(a, m)]


def collect(target, sources, seq):
    a = seq // (lax.axis_size("seq") // CUTS)
    for m in range(CUTS):
        for r in range(sources[m].shape[0]):
            target[CUTS * r + jnp.bitwise_xor(a, m)] = sources[m][r]


def unpack(pack, at_low):
    wide = pack.astype(F32)
    low = half_low(wide.shape)
    if at_low:
        both = [jnp.where(low, wide, 0.0), jnp.where(low, swap_halves(wide), 0.0)]
    else:
        both = [jnp.where(low, 0.0, swap_halves(wide)), jnp.where(low, 0.0, wide)]
    return jnp.concatenate(both, axis=0).astype(BF16)


def pack_rows(tile, at_low):
    half = tile.shape[0] // 2
    top, bottom = tile[:half], tile[half:]
    low = half_low(top.shape)
    if at_low:
        return jnp.where(low, top, swap_halves(bottom))
    return jnp.where(low, swap_halves(top), bottom)


def attend(shares, *refs):
    own = refs[:CUTS]
    others = refs[CUTS : CUTS * shares]
    backs = refs[CUTS * shares : CUTS * shares + CUTS]
    kept_ref, lse_ref, weight_ref, keys_s = refs[CUTS * shares + CUTS :]
    tokens = kept_ref.shape[2]
    half = tokens // 2
    unit = pl.program_id(0)
    rows = own[0].shape[0] - 16
    rider = rows * tokens // (tokens + half)

    @pl.when(unit == 0)
    def _():
        total = jnp.zeros((16, 128), F32)
        for ref in own + others:
            total = total + ref[rider : rider + 16, :].astype(F32)
        total = jnp.sum(total[0:8], axis=1, keepdims=True) / 32.0
        weight_ref[...] = jnp.broadcast_to(total, (8, 128))

    for n, ref in enumerate(own + others):
        at = pl.ds(pl.multiple_of(unit * tokens, tokens), tokens)
        keys_s[n * tokens : (n + 1) * tokens, :] = ref[at, :]
    keys = keys_s[...]
    values = jnp.where(half_low(keys.shape), jnp.ones_like(keys), keys)

    def scores_of(m):
        at = pl.ds(pl.multiple_of(rider + 16 + unit * half, 16), half)
        return nt(unpack(own[m][at, :], True), keys)

    scores = scores_of(0)
    for m in range(CUTS):
        later = scores_of(m + 1) if m + 1 < CUTS else None
        top = jnp.max(scores, axis=1, keepdims=True)
        out = nn(jnp.exp2(scores - top).astype(BF16), values)
        total = out[:, 0:1]
        out = out / total
        lse = jnp.broadcast_to(top + jnp.log2(total), (tokens, 128)).T
        lse_ref[0, m] = lse[:8]
        kept_ref[0, m] = out
        backs[m][0] = pack_rows(out, False).astype(BF16)
        scores = later


def middle(group, *refs):
    (interval, samples, cosines, sum_ref, x0_ref, fields_ref, mask_ref) = refs[:7]
    heads_in = refs[7 : 7 + CUTS]
    blocks = refs[7 + CUTS : 7 + CUTS + group]
    mod_s = refs[7 + CUTS + group]
    outs = refs[7 + CUTS + group + 1 :]
    (dx1_ref, rows_ref, loss_ref) = outs[:3]
    sends = outs[3 : 3 + CUTS]
    attended_s, db1_ref, n2_ref, dh_ref, nf_ref, dpred_ref, db2_ref, active_ref = outs[
        3 + CUTS : 11 + CUTS
    ]
    weights, head_s, grad_s = outs[11 + CUTS :]
    item = pl.program_id(0)
    grp, seq = place()
    tokens = x0_ref.shape[0]
    half = tokens // 2

    @pl.when(item == 0)
    def _():
        assemble(weights, blocks, grp, 0, D + FF + OUTP + FF)
        collect(head_s, heads_in, seq)
        loss_ref[...] = jnp.zeros_like(loss_ref)

    low = half_low((half, 128))
    for j in range(HEADS // 2):
        one = head_s[HEADS * item + 2 * j].astype(F32)
        two = head_s[HEADS * item + 2 * j + 1].astype(F32)
        attended_s[:half, j * 128 : (j + 1) * 128] = jnp.where(low, one, swap_halves(two)).astype(
            BF16
        )
        attended_s[half:, j * 128 : (j + 1) * 128] = jnp.where(low, swap_halves(one), two).astype(
            BF16
        )
    out_w = slice(0, D)
    up_w = slice(D, D + FF)
    head_w = slice(D + FF, D + FF + OUT)
    down_w = slice(D + FF + OUTP, D + FF + OUTP + FF)
    mod = mod_s[pl.ds(interval[item], 1), :]
    gate_a, shift_b, scale_b, gate_b = [mod[:, k * D : (k + 1) * D] for k in range(2, 6)]
    attended = attended_s[...]
    branch_a = nn(attended, weights[:, out_w])
    x1 = x0_ref[...] + gate_a * branch_a
    normed_b, rstd_b = standardize(x1)
    n2 = (normed_b * (1.0 + scale_b) + shift_b).astype(BF16)
    n2_ref[...] = n2
    value, slope = gelu_parts(nn(n2, weights[:, up_w]))
    active = value.astype(BF16)
    active_ref[...] = active
    branch_b = nt(active, weights[:, down_w])
    x2 = x1 + gate_b * branch_b
    final, rstd_f = standardize(x2)
    nf = final.astype(BF16)
    nf_ref[...] = nf
    diff = nn(nf, weights[:, head_w]) - fields_ref[0].astype(F32).T
    present = tn(ones_where(mask_ref[0] > 0), ones_where(spread()))
    weight = line_weights(samples[item], cosines, seq, iota((tokens, 1), 0))
    weight_grad = weight * (2.0 / PIX) / sum_ref[0:1, 0:1]
    masked = present * diff
    each = jnp.sum(masked * diff, axis=1, keepdims=True) * weight
    loss_ref[...] += jnp.broadcast_to(jnp.sum(each, axis=0, keepdims=True) / PIX, (8, 128))
    dpred = (masked * weight_grad).astype(BF16)
    dpred_ref[...] = dpred

    dx2 = standardize_back(nt(dpred, weights[:, head_w]), final, rstd_f)
    db2 = (gate_b * dx2).astype(BF16)
    db2_ref[...] = db2
    d_gate_b = jnp.sum(dx2 * branch_b, axis=0, keepdims=True)
    dh = (nn(db2, weights[:, down_w]) * slope).astype(BF16)
    dh_ref[...] = dh
    dn2 = nt(dh, weights[:, up_w])
    d_shift_b = jnp.sum(dn2, axis=0, keepdims=True)
    d_scale_b = jnp.sum(dn2 * normed_b, axis=0, keepdims=True)
    dx1 = dx2 + standardize_back(dn2 * (1.0 + scale_b), normed_b, rstd_b)
    dx1_ref[...] = dx1
    d_gate_a = jnp.sum(dx1 * branch_a, axis=0, keepdims=True)
    db1 = (gate_a * dx1).astype(BF16)
    db1_ref[...] = db1
    dout = nt(db1, weights[:, out_w])
    rows_ref[0] = jnp.concatenate(
        [d_gate_a, d_shift_b, d_scale_b, d_gate_b, jnp.zeros((4, D), F32)], axis=0
    )
    for j in range(HEADS // 2):
        pair = dout[:, j * 128 : (j + 1) * 128]
        top, bottom = pair[:half], pair[half:]
        grad_s[HEADS * item + 2 * j] = jnp.where(low, top, swap_halves(bottom)).astype(BF16)
        grad_s[HEADS * item + 2 * j + 1] = jnp.where(low, swap_halves(top), bottom).astype(BF16)

    @pl.when(item == pl.num_programs(0) - 1)
    def _():
        deal(sends, grad_s, seq)


def middle_weights(*refs):
    attended, db1, n2, dh, nf, dpred, db2, active = refs[:8]
    keep_ref, send_ref, acc = refs[8:]
    grp, _ = place()
    acc[:, :D] = tn(attended[...], db1[...])
    acc[:, D : D + FF] = tn(n2[...], dh[...])
    acc[:, D + FF : D + FF + OUT] = tn(nf[...], dpred[...])
    acc[:, D + FF + OUT : D + FF + OUTP] = jnp.zeros((D, OUTP - OUT), F32)
    acc[:, D + FF + OUTP :] = tn(db2[...], active[...])
    split_rows(acc, grp, keep_ref, send_ref)


def split_rows(acc, grp, keep_ref, send_ref):
    rows = keep_ref.shape[1]
    for j in range(keep_ref.shape[0]):
        for odd, ref in ((0, keep_ref), (1, send_ref)):
            at = pl.multiple_of(jnp.bitwise_xor(grp, 2 * j + odd) * rows, 16)
            ref[j, :, : acc.shape[1]] = acc[pl.ds(at, rows), :].astype(BF16)


def attend_back(shares, unit, *refs):
    own = refs[:CUTS]
    others = refs[CUTS : CUTS * shares]
    grads = refs[CUTS * shares : CUTS * shares + CUTS]
    kept_ref, lse_ref = refs[CUTS * shares + CUTS : CUTS * shares + CUTS + 2]
    outs = refs[CUTS * shares + CUTS + 2 :]
    dq_ref, own_ref = outs[:2]
    far_refs = outs[2 : 2 + shares - 1]
    keys_s, turned_s, acc = outs[2 + shares - 1 :]
    tokens = kept_ref.shape[2]
    for n, ref in enumerate(own + others):
        keys_s[n * tokens : (n + 1) * tokens, :] = ref[unit * tokens : (unit + 1) * tokens, :]
    turned_s[...] = keys_s[...].T
    every = range(CUTS)
    half = tokens // 2
    at = (own[0].shape[0] - 16) * tokens // (tokens + half) + 16 + unit * half
    queries = jnp.concatenate(
        [unpack(own[m][at : at + half, :], True) for m in every], axis=0
    )
    grads = [unpack(grads[m][0], False) for m in every]
    delta = jnp.concatenate(
        [
            jnp.sum((grads[m].astype(F32) * kept_ref[0, m]).T, axis=0, keepdims=True)
            for m in every
        ],
        axis=1,
    )
    grads = jnp.concatenate(grads, axis=0)
    lse = jnp.concatenate([lse_ref[0, m, 0:1, :] for m in every], axis=1)
    chunk = 2 * tokens
    count = keys_s.shape[0] // chunk

    def products_of(c):
        keys = keys_s[c * chunk : (c + 1) * chunk, :]
        return nt(keys, queries), nt(keys, grads)

    products, dq = products_of(0), None
    for c in range(count):
        scores, dprobs = products
        if c + 1 < count:
            products = products_of(c + 1)
        probs = jnp.exp2(scores - lse)
        dscores = (probs * (dprobs - delta)).astype(BF16)
        acc[c * chunk : (c + 1) * chunk, :] = nn(probs.astype(BF16), grads) + nn(dscores, queries)
        part = nn(turned_s[:, c * chunk : (c + 1) * chunk], dscores)
        dq = part if dq is None else dq + part
    for m in every:
        turned = dq[:, m * tokens : (m + 1) * tokens].T * SCALE
        dq_ref[0, m] = pack_rows(turned, True).astype(BF16)
    factor = jnp.where(half_low((1, 128)), 1.0 / LOG2E, 1.0)
    for m in range(CUTS):
        own_ref[0, m] = (acc[m * tokens : (m + 1) * tokens, :] * factor).astype(BF16)
        for n, ref in enumerate(far_refs):
            at = ((n + 1) * CUTS + m) * tokens
            ref[0, m] = (acc[at : at + tokens, :] * factor).astype(BF16)


def join_back(shares, *refs):
    dq_ref, own_ref = refs[:2]
    far = refs[2 : 2 + shares - 1]
    outs = refs[2 + shares - 1 :]
    tokens = own_ref.shape[2]
    for m in range(CUTS):
        total = own_ref[0, m].astype(F32)
        for ref in far:
            total = total + ref[0, m].astype(F32)
        outs[m][:tokens, :] = total.astype(BF16)
        outs[m][tokens:, :] = dq_ref[0, m]


def project_back(rounds, *refs):
    (interval, x0_ref, n1_ref, dx1_ref, rows_ref, gathered_ref, weights, mod_s) = refs[:8]
    units, outs = refs[8 : 8 + CUTS * rounds], refs[8 + CUTS * rounds :]
    (dagg_ref, keep_ref, send_ref) = outs[:3]
    unit_s, dqkv_s, acc, dmod_ref, lines_s = outs[3:]
    item = pl.program_id(0)
    grp, seq = place()
    tokens = x0_ref.shape[0]
    half = tokens // 2

    @pl.when(item == 0)
    def _():
        a = seq // (lax.axis_size("seq") // CUTS)
        for r in range(rounds):
            for m in range(CUTS):
                unit_s[CUTS * r + jnp.bitwise_xor(a, m)] = units[CUTS * r + m][...]
        acc[...] = jnp.zeros_like(acc)
        dmod_ref[...] = jnp.zeros_like(dmod_ref)

    low = half_low((half, 128))
    for h in range(HEADS):
        dqkv_s[:, h * 128 : (h + 1) * 128] = unit_s[HEADS * item + h, :tokens, :]
    for j in range(HEADS // 2):
        one = unit_s[HEADS * item + 2 * j, tokens:, :].astype(F32)
        two = unit_s[HEADS * item + 2 * j + 1, tokens:, :].astype(F32)
        lanes = slice(2 * D + j * 128, 2 * D + (j + 1) * 128)
        dqkv_s[:half, lanes] = jnp.where(low, one, swap_halves(two)).astype(BF16)
        dqkv_s[half:, lanes] = jnp.where(low, swap_halves(one), two).astype(BF16)
    dqkv = dqkv_s[...]
    which = interval[item]
    mod = mod_s[pl.ds(which, 1), :]
    acc[:, D:] += tn(n1_ref[...], dqkv)
    dn1 = nt(dqkv, weights[:, D:])
    normed, rstd = standardize(x0_ref[...])
    d_shift = jnp.sum(dn1, axis=0, keepdims=True)
    d_scale = jnp.sum(dn1 * normed, axis=0, keepdims=True)
    dx0 = (
        dx1_ref[...] + standardize_back(dn1 * (1.0 + mod[:, D : 2 * D]), normed, rstd)
    ).astype(BF16)
    rows = rows_ref[0]
    for k, row in enumerate([d_shift, d_scale] + [rows[r : r + 1] for r in range(4)]):
        dmod_ref[pl.ds(which, 1), k * D : (k + 1) * D] += row

    acc[:, :D] += tn(gathered_ref[...], dx0)
    dagg_ref[0] = nt(weights[:, :D], dx0).astype(BF16)

    @pl.when(item == pl.num_programs(0) - 1)
    def _():
        split_rows(acc, grp, keep_ref, send_ref)
        lines_s[...] = jnp.zeros_like(lines_s)
        for t in range(6 * D // 128):
            lines_s[4 * t : 4 * t + 3, :] = dmod_ref[0:3, t * 128 : (t + 1) * 128]
        rows = keep_ref.shape[1]
        for t in range(mod_tiles(rows)):
            tile = lines_s[t * rows : (t + 1) * rows, :].astype(BF16)
            at = acc.shape[1] + t * 128
            for j in range(keep_ref.shape[0]):
                keep_ref[j, :, at : at + 128] = tile
                send_ref[j, :, at : at + 128] = tile


def aggregate_back(*refs):
    (dagg_ref, probs_ref, picked_ref, fields_ref, mask_ref) = refs[:5]
    (fused_ref, agg_ref, embed_ref, probe_ref) = refs[5:9]
    keep_ref, send_ref, ds_s, acc, mix, dscore = refs[9:]
    item = pl.program_id(0)
    grp, _ = place()
    tokens = dagg_ref.shape[2]

    @pl.when(item == 0)
    def _():
        mix[...] = jnp.zeros_like(mix)
        dscore[...] = jnp.zeros_like(dscore)

    dagg = dagg_ref[0].astype(F32)
    fields = fields_ref[0]
    wide_fields = fields.astype(F32)
    keep = mask_ref[0] > 0
    expand = ones_where(spread())
    upper = iota((128, tokens), 0) < HEAD
    dparts = []
    for h in range(HEADS):
        mine = upper if h % 2 == 0 else jnp.logical_not(upper)
        pair = slice(h // 2 * 128, (h // 2 + 1) * 128)
        dparts.append(jnp.where(mine, dagg[pair], 0.0).astype(BF16))

    def spread_out(h):
        return nn(fused_ref[:, h // 2 * 128 : (h // 2 + 1) * 128], dparts[h])

    spreaded = spread_out(0)
    for j in range(HEADS // 2):
        both = None
        for h in (2 * j, 2 * j + 1):
            later = spread_out(h + 1) if h + 1 < HEADS else None
            spreaded = (spreaded * wide_fields).astype(BF16)
            part = nt(picked_ref[h, 0], dparts[h])
            both = part if both is None else both + part
            dprobs = nn(expand, spreaded)
            probs = probs_ref[0, h * VARP : (h + 1) * VARP, :]
            ds = probs * (dprobs - jnp.sum(probs * dprobs, axis=0, keepdims=True))
            ds_s[h * VARP : (h + 1) * VARP, :] = jnp.where(keep, ds, 0.0).astype(BF16)
            spreaded = later
        mix[:, j * 128 : (j + 1) * 128] += both
    dscore[...] += nt(ds_s[...], fields)

    @pl.when(item == pl.num_programs(0) - 1)
    def _():
        lines = iota((128, OUT), 0)
        owned = spread()
        drows = jnp.zeros((128, OUT), F32)
        for h in range(HEADS):
            mine = dscore[h * VARP : (h + 1) * VARP, :]
            line = jnp.sum(jnp.where(owned, mine, 0.0), axis=0, keepdims=True) * SCALE
            drows = drows + jnp.where(lines == h, line, 0.0)
        drows = drows.astype(BF16)
        mixed = mix[...].astype(BF16)
        embed = embed_ref[:, :OUT]
        acc[:, 2 * D : 2 * D + OUT] = nt(agg_ref[:, D:], mixed) + nn(probe_ref[...], drows)
        acc[:, D : 2 * D] = nn(embed, mixed)
        dprobe = nt(embed, drows)
        heads = jnp.where(iota((128, D), 1) // HEAD == iota((128, D), 0), 1.0, 0.0).astype(BF16)
        coarse = dprobe.astype(BF16)
        fine = (dprobe - coarse.astype(F32)).astype(BF16)
        by_column = nn(coarse, heads) + nn(fine, heads)
        eye = iota((D, D), 0) == iota((D, D), 1)
        query = embed_ref[:, OUT : OUT + 1].astype(F32)
        query_row = jnp.sum(jnp.where(eye, query, 0.0), axis=0, keepdims=True)
        acc[:, :D] = by_column * query_row
        dquery = jnp.sum(agg_ref[:, :D].astype(F32) * by_column, axis=0, keepdims=True)
        column = jnp.sum(jnp.where(eye, dquery, 0.0), axis=1, keepdims=True)
        acc[:, 2 * D + OUT :] = jnp.where(iota((D, OUTP - OUT), 1) == 0, column, 0.0)
        split_rows(acc, grp, keep_ref, send_ref)


def mod_tiles(rows):
    return -(-4 * (6 * D // 128) // rows)


def shares_of():
    shares = lax.axis_size("seq") // CUTS
    _, seq = place()
    return shares, seq // shares, lax.rem(seq, shares)


def added(refs, at=None):
    total = None
    for ref in refs:
        value = (ref[...] if at is None else ref[at]).astype(F32)
        total = value if total is None else total + value
    return total


def sum_cores(pairs, sources, *refs):
    ins, outs, table = refs[: 2 * sources], refs[2 * sources : -1], refs[-1]
    shares, _, share = shares_of()
    first, second = outs[:pairs], outs[pairs:]
    half = table.shape[1] // 2
    size = half // shares
    per = ins[0].shape[1] // 16
    count = sum(ref.shape[2] for ref in ins[::2]) // 128 * per
    for j in range(pairs):
        at = 0
        for keep_ref, got_ref in zip(ins[::2], ins[1::2]):
            total = (keep_ref[j].astype(F32) + got_ref[j].astype(F32)).astype(BF16)
            for t in range(total.shape[1] // 128):
                for g in range(per):
                    table[j, at] = total[g * 16 : (g + 1) * 16, t * 128 : (t + 1) * 128]
                    at += 1
        for spare in range(count, 2 * half):
            table[j, spare] = jnp.zeros(table.shape[2:], BF16)
        first[j][...] = table[j, :half]
        for n in range(shares):
            at = half + jnp.bitwise_xor(share, n) * size
            second[n][j * size : (j + 1) * size] = table[j, pl.ds(at, size)]


def sum_cores_once(pairs, *refs):
    (keep_ref, got_ref), outs = refs[:2], refs[2:]
    per = keep_ref.shape[1] // 16
    count = keep_ref.shape[2] // 128 * per
    for j in range(pairs):
        total = (keep_ref[j].astype(F32) + got_ref[j].astype(F32)).astype(BF16)
        for t in range(keep_ref.shape[2] // 128):
            for g in range(per):
                outs[j][t * per + g] = total[g * 16 : (g + 1) * 16, t * 128 : (t + 1) * 128]
        for spare in range(count, outs[j].shape[0]):
            outs[j][spare] = jnp.zeros(outs[j].shape[1:], BF16)


def sum_and_deal(over_cuts, *refs):
    outs, table = refs[-1 - (CUTS if over_cuts else shares_of()[0]) : -1], refs[-1]
    _, cut, share = shares_of()
    table[...] = added(refs[: -1 - len(outs)]).astype(BF16)
    size = outs[0].shape[0]
    for n, ref in enumerate(outs):
        ref[...] = table[pl.ds(jnp.bitwise_xor(cut if over_cuts else share, n) * size, size)]


def sum_both(pairs, shares, *refs):
    by_grp, by_share = refs[:pairs], refs[pairs : pairs + shares]
    outs, (table,) = refs[pairs + shares : -1], refs[-1:]
    _, _, share = shares_of()
    table[...] = added(by_grp).astype(BF16)
    size = outs[0].shape[0]
    for n in range(shares):
        outs[n][...] = table[pl.ds(jnp.bitwise_xor(share, n) * size, size)]
    for j in range(pairs):
        at = slice(j * size, (j + 1) * size)
        outs[shares + j][...] = added(by_share, at).astype(BF16)


def sum_both_again(pairs, shares, *refs):
    by_share, by_grp = refs[:shares], refs[shares : shares + pairs]
    outs, (table,) = refs[pairs + shares : -1], refs[-1:]
    _, cut, _ = shares_of()
    size = outs[0].shape[0] // 2
    table[0] = added(by_share).astype(BF16)
    table[1] = added(by_grp).astype(BF16)
    for m in range(CUTS):
        at = pl.ds(jnp.bitwise_xor(cut, m) * size, size)
        outs[m][:size] = table[0, at]
        outs[m][size:] = table[1, at]


def sum_pieces(*refs):
    sources, (out_ref, square_ref) = refs[:-2], refs[-2:]
    total = added(sources)
    out_ref[...] = total.astype(BF16)
    square_ref[...] = jnp.sum(total * total, axis=0)


def sum_late(start, stop, *refs):
    early_ref, loss_ref, lead_ref = refs[:3]
    sources, out_ref = refs[3:-1], refs[-1]
    grp, _ = place()
    shares, cut, share = shares_of()
    rows = lead_ref.shape[0] // lax.axis_size("grp")
    lead = lead_ref[pl.ds(pl.multiple_of(grp * rows, 16), rows), :].astype(F32)
    cols = [lead[:, g : g + 1] for g in range(3)]

    def gram(f, g):
        return jnp.sum(cols[f] * cols[g], axis=0, keepdims=True)

    row = lax.rem(iota((16, 1), 0), 4)

    def pick(*values):
        out = jnp.zeros((16, 1), F32)
        for r, value in values:
            out = jnp.where(row == r, value, out)
        return out

    same = pick(*[(g, gram(g, g)) for g in range(3)])
    next_one = pick((1, 2 * gram(0, 1)), (2, 2 * gram(1, 2)))
    next_two = pick((2, 2 * gram(0, 2)))
    size = (out_ref.shape[0] - 1) // 2
    plain = jnp.zeros((16, 128), F32)
    for half in range(2):
        for k in range(size):
            total = added(sources, half * size + k)
            out_ref[half * size + k] = total.astype(BF16)
            index = ((half * shares + share) * CUTS + cut) * size + k
            special = jnp.logical_and(index >= start, index < stop)
            square = total * total
            mixed = (
                square * same
                + total * pltpu.roll(total, 1, 0) * next_one
                + total * pltpu.roll(total, 2, 0) * next_two
            )
            plain = plain + jnp.where(special, mixed, square)
    squares = jnp.sum(jnp.sum(plain + early_ref[...], axis=0, keepdims=True), axis=1, keepdims=True)
    rider = jnp.zeros((16, 128), F32)
    for at, value in ((0, loss_ref[0:1, :]), (3, jnp.broadcast_to(squares, (1, 128)))):
        for part in range(3):
            piece = value.astype(BF16).astype(F32)
            rider = jnp.where(iota((16, 128), 0) == at + part, piece, rider)
            value = value - piece
    out_ref[2 * size] = rider.astype(BF16)


def stack_late(*refs):
    pieces, (column_ref, reduced_ref) = refs[:-2], refs[-2:]
    count = column_ref.shape[1]
    rider = jnp.zeros((16, 128), F32)
    for m, ref in enumerate(pieces):
        column_ref[m] = ref[:count]
        rider = rider + ref[count].astype(F32)
    reduced_ref[...] = jnp.concatenate(
        [rider[0:1] + rider[1:2] + rider[2:3], rider[3:4] + rider[4:5] + rider[5:6]]
        + [jnp.zeros((6, 128), F32)],
        axis=0,
    )


def stack(*refs):
    for m, ref in enumerate(refs[:-1]):
        refs[-1][m] = ref[...]


def step_values(param, first, second, grad):
    first = beta_first * first + (1.0 - beta_first) * grad
    second = beta_second * second + (1.0 - beta_second) * grad * grad
    mean_hat = first * (1.0 / (1.0 - beta_first**STEP))
    var_hat = second * (1.0 / (1.0 - beta_second**STEP))
    param = param - learn_rate * (
        mean_hat / (jnp.sqrt(var_hat) + adam_epsilon) + decay_rate * param
    )
    return param, first, second, param.astype(BF16)


def optimize(shares, *refs):
    reduced_ref, sum_ref, lead_ref = refs[:3]
    early = refs[3 : 3 + shares]
    late = refs[3 + shares : 3 + 2 * shares]
    wide = refs[3 + 2 * shares : 6 + 2 * shares]
    tall = refs[6 + 2 * shares : 9 + 2 * shares]
    query = refs[9 + 2 * shares : 12 + 2 * shares]
    outs = refs[12 + 2 * shares :]
    scalars, wide_hbm, tall_hbm, query_out = outs[:3], outs[3:7], outs[7:11], outs[11:15]
    early_s, late_s, wide_out, tall_out, sems = outs[15], outs[16], outs[17:21], outs[21:25], outs[25]
    grp, _ = place()
    _, cut, share = shares_of()
    for table, stacks, halves in ((early_s, early, 1), (late_s, late, 2)):
        size = stacks[0].shape[1] // halves
        for n, ref in enumerate(stacks):
            for m in range(CUTS):
                for half in range(halves):
                    at = (half * shares + jnp.bitwise_xor(share, n)) * CUTS
                    at = (at + jnp.bitwise_xor(cut, m)) * size
                    table[pl.ds(at, size)] = ref[m, half * size : (half + 1) * size]
    norm = jnp.sqrt(reduced_ref[1:2, 0:1])
    for ref, value in zip(scalars, (reduced_ref[0:1, 0:1], sum_ref[0:1, 0:1], norm)):
        ref[...] = value
    factor = jnp.minimum(1.0, clip_limit / (norm + 1e-06))
    rows = wide[0].shape[0]
    per = rows // 16

    def tile(table, t):
        return jnp.concatenate([table[t * per + g] for g in range(per)], axis=0).astype(F32)

    def put(ins, targets, at, grad):
        new = step_values(*[r[at] for r in ins], grad * factor)
        for ref, value in zip(targets, new):
            ref[at] = value

    def at(t, width=128):
        return (slice(None), slice(t * 128, t * 128 + width))

    copies = []

    def flush(sources, targets, lo, hi):
        for source, target in zip(sources, targets):
            copy = pltpu.make_async_copy(
                source.at[:, lo:hi], target.at[:, lo:hi], sems.at[len(copies)]
            )
            copy.start()
            copies.append(copy)

    low = half_low((rows, 128))
    for t in range(6):
        put(wide, wide_out, at(t), tile(late_s, t))
    for t in range(3):
        put(wide, wide_out, at(6 + t), tile(late_s, 15 + t))
    flush(wide_out, wide_hbm, 0, 3 * D)
    lead = lead_ref[pl.ds(pl.multiple_of(grp * rows, 16), rows), :].astype(F32)
    lines = jnp.concatenate([tile(late_s, 27 + t) for t in range(mod_tiles(rows))], axis=0)
    for t in range(18):
        grad = lead[:, 0:1] * lines[4 * t : 4 * t + 1]
        for g in (1, 2):
            grad = grad + lead[:, g : g + 1] * lines[4 * t + g : 4 * t + g + 1]
        put(wide, wide_out, at(9 + t), grad)
    flush(wide_out, wide_hbm, 3 * D, 9 * D)
    qkv = 18
    for j in range(3):
        put(wide, wide_out, at(27 + j), tile(late_s, qkv + 6 + j))
        one, two = tile(late_s, qkv + 2 * j), tile(late_s, qkv + 2 * j + 1)
        put(wide, wide_out, at(30 + j), jnp.where(low, one, swap_halves(two)))
        put(wide, wide_out, at(33 + j), jnp.where(low, swap_halves(one), two))
    flush(wide_out, wide_hbm, 9 * D, 12 * D)
    for t in range(15 + 8):
        put(wide, wide_out, at(36 + t), tile(early_s, t))
    rest = OUT - 8 * 128
    put(wide, wide_out, at(59, rest), tile(early_s, 23)[:, :rest])
    flush(wide_out, wide_hbm, 12 * D, wide[0].shape[1])
    for t in range(8):
        put(tall, tall_out, at(t), tile(late_s, 6 + t))
    flush(tall_out, tall_hbm, 0, 8 * 128)
    last = tile(late_s, 14)
    lane = iota((rows, 128), 1)
    for t in range(FF // 128):
        turned = pltpu.roll(tile(early_s, 24 + t), rest, 1)
        put(tall, tall_out, at(8 + t), jnp.where(lane < rest, last, turned))
        if t == 0:
            eye = iota((rows, rows), 0) == iota((rows, rows), 1)
            grad = jnp.sum(jnp.where(eye, last[:, rest : rest + 1], 0.0), axis=0, keepdims=True)
            put(query, query_out, (slice(None), slice(None)), grad)
        last = turned
    put(tall, tall_out, at(8 + FF // 128, rest), last[:, :rest])
    flush(tall_out, tall_hbm, 8 * 128, tall[0].shape[1])
    for copy in copies:
        copy.wait()


def shift(value, axis, bit):
    size = lax.axis_size(axis)
    return lax.ppermute(value, axis, [(i, i ^ bit) for i in range(size)])


def gather_blocks(own, group, behind=None):
    blocks = {0: own}
    for j in range(2, group, 2):
        blocks[j] = shift(own, "grp", j)
    if behind is not None:
        blocks = behind(blocks)
    for j in range(0, group, 2):
        blocks[j + 1] = shift(blocks[j], "grp", 1)
    return [blocks[j] for j in range(group)]


def granules(rows, cols, shares):
    unit = 2 * shares * CUTS
    return -(-(rows // 16) * (cols // 128) // unit) * unit


def piece_shape(count):
    return sds((count, 16, 128), BF16)


def reduce_cores(*sources, after=()):
    pairs, rows, _ = sources[0][0].shape
    shares = lax.axis_size("seq") // CUTS
    count = granules(rows, sum(keep.shape[2] for keep, _ in sources), shares)
    results = call(
        functools.partial(sum_cores, pairs, len(sources)),
        [piece_shape(count // 2)] * pairs + [piece_shape(count // 2 // shares * pairs)] * shares,
        scratch=[pltpu.VMEM((pairs, count, 16, 128), BF16)],
        after=after,
    )(*[x for source in sources for x in source])
    return results[:pairs], results[pairs:]


def reduce_cores_once(keep, got, after=()):
    pairs, rows, cols = keep.shape
    parts = lax.axis_size("seq")
    count = -(-(rows // 16) * (cols // 128) // parts) * parts
    halves = call(
        functools.partial(sum_cores_once, pairs), [piece_shape(count)] * pairs, after=after
    )(keep, got)
    return [halves[0]] + [shift(halves[j], "grp", 2 * j) for j in range(1, pairs)]


def reduce_and_deal(pieces, over, after=()):
    count = pieces[0].shape[0]
    number = CUTS if over else lax.axis_size("seq") // CUTS
    outs = call(
        functools.partial(sum_and_deal, over),
        [piece_shape(count // number)] * number,
        scratch=[pltpu.VMEM((count, 16, 128), BF16)],
        after=after,
    )(*pieces)
    if over:
        return over_cuts(outs[0], outs[1:])
    return [outs[0]] + [shift(outs[n], "seq", n) for n in range(1, number)]


def exchange_once(by_grp, by_share):
    return [by_grp[0]] + [shift(by_grp[j], "grp", 2 * j) for j in range(1, len(by_grp))], [
        by_share[0]
    ] + [shift(by_share[n], "seq", n) for n in range(1, len(by_share))]


def reduce_once(by_grp, by_share, after=()):
    pairs, shares = len(by_grp), len(by_share)
    size = by_grp[0].shape[0] // shares
    results = call(
        functools.partial(sum_both, pairs, shares),
        [piece_shape(size)] * (pairs + shares),
        scratch=[pltpu.VMEM(by_grp[0].shape, BF16)],
        after=after,
    )(*by_grp, *by_share)
    return results[:shares], results[shares:]


def exchange_again(by_share, by_grp):
    pairs, shares = len(by_grp), len(by_share)
    return [by_share[0]] + [shift(by_share[n], "seq", n) for n in range(1, shares)], [
        by_grp[0]
    ] + [shift(by_grp[j], "grp", 2 * j) for j in range(1, pairs)]


def reduce_twice(by_share, by_grp, after=()):
    pairs, shares = len(by_grp), len(by_share)
    size = by_grp[0].shape[0]
    return call(
        functools.partial(sum_both_again, pairs, shares),
        [piece_shape(2 * size // CUTS)] * CUTS,
        scratch=[pltpu.VMEM((2, size, 16, 128), BF16)],
        after=after,
    )(*by_share, *by_grp)


def over_cuts(first, others=None):
    shares = lax.axis_size("seq") // CUTS
    sent = [first] * (CUTS - 1) if others is None else others
    return [first] + [shift(sent[m - 1], "seq", m * shares) for m in range(1, CUTS)]


def gather_shares(pieces, after=()):
    shares = lax.axis_size("seq") // CUTS
    column = call(stack, sds((CUTS,) + pieces[0].shape, BF16), after=after)(*pieces)
    return [column] + [shift(column, "seq", n) for n in range(1, shares)]


def butterfly(value, axis, bit, stop):
    while bit < stop:
        value = value + shift(value, axis, bit)
        bit *= 2
    return value


def lead_table():
    half = D // 2
    hours = 6.0 * np.exp2(np.arange(3, dtype=np.float32))
    freqs = np.exp(-np.log(np.float32(1000.0)) * np.arange(half, dtype=np.float32) / half)
    angles = hours[None, :] * freqs.astype(np.float32)[:, None]
    waves = np.concatenate([np.sin(angles), np.cos(angles)], axis=0)
    table = np.zeros((D, 128), np.float32)
    table[:, :3] = waves / (1.0 + np.exp(-waves))
    return jnp.asarray(table).astype(BF16)


def cosine_table(count):
    line = np.arange(count, dtype=np.float32)
    return jnp.asarray(np.cos(np.pi * ((line + 0.5) / count - 0.5)).astype(np.float32))


def per_device(
    fields,
    targets,
    land_mask,
    interval,
    samples,
    wide_weights,
    wide_firsts,
    wide_seconds,
    tall_weights,
    tall_firsts,
    tall_seconds,
    query_vector,
    query_firsts,
    query_seconds,
):
    group = lax.axis_size("grp")
    parts = lax.axis_size("seq")
    shares = parts // CUTS
    rows, columns = wide_weights.shape
    items, tokens = fields.shape[:2]
    units = items * HEADS // CUTS
    every = items * tokens
    late_cols = D + FF + OUTP + FF

    query_row = query_vector.reshape(1, rows)
    tall = [x.T for x in (tall_weights, tall_firsts, tall_seconds)]
    lead = lead_table()
    cosines = cosine_table(tokens // COLS * parts)
    fields = fields.transpose(0, 2, 1)
    targets = targets.transpose(0, 2, 1)
    mask = jnp.pad(
        land_mask.transpose(0, 2, 1), ((0, 0), (0, VARP - VARS), (0, 0)), constant_values=-1
    )

    def columns_of(index):
        return pl.BlockSpec((rows, 3 * D), lambda i: (0, index))

    first_own, second_own = call(
        pack_first,
        [sds((rows, 2 * D + OUTP), BF16), sds((rows + RIDERS, 4 * D), BF16)],
        grid=(1,),
        in_specs=[smem(), smem()]
        + [columns_of(i) for i in (0, 1, 2, 3, 0)]
        + [pl.BlockSpec((1, rows), lambda i: (0, 0)), whole(), whole()],
        out_specs=[whole()] * 2,
        scratch=[pltpu.VMEM((RIDERS, 4 * D), F32)],
        us=3,
        limit=62,
    )(samples, cosines, *[wide_weights] * 4, tall[0], query_row, lead, mask)
    first = gather_blocks(first_own, group)
    by_item = pl.BlockSpec((tokens, D), lambda i: (i, 0))

    def lane_block(height):
        return pl.BlockSpec((1, height, tokens), lambda i: (i, 0, 0))

    heads_spec = pl.BlockSpec((HEADS, 1, OUT, tokens), lambda i: (0, i, 0, 0))
    packed = units * (tokens + tokens // 2) + 16

    probs, picked, gathered, agg_weights, embed, fused_w, probe = call(
        functools.partial(aggregate, group),
        [
            in_hbm((items, HEADS * VARP, tokens), F32),
            in_hbm((HEADS, items, OUT, tokens), BF16),
            sds((every, D), BF16),
            in_hbm((D, 2 * D), BF16),
            in_hbm((D, OUTP), BF16),
            in_hbm((OUT, D), BF16),
            in_hbm((D, 128), BF16),
        ],
        grid=(items,),
        in_specs=[lane_block(OUT), lane_block(VARP)] + [whole()] * group,
        out_specs=[lane_block(HEADS * VARP), heads_spec, by_item] + [whole()] * 4,
        scratch=[
            pltpu.VMEM((HEADS * VARP, OUT), BF16),
            pltpu.VMEM((D, OUT), BF16),
            pltpu.VMEM((D, tokens), F32),
        ],
        us=10,
        limit=34,
    )(fields, mask, *first)
    second = gather_blocks(
        second_own,
        group,
        lambda blocks: {j: once_ready(block, (gathered,)) for j, block in blocks.items()},
    )
    late_own = call(
        pack_late,
        sds((rows, late_cols), BF16),
        grid=(1,),
        in_specs=[columns_of(4), columns_of(5), columns_of(6), whole()],
        out_specs=whole(),
        us=2,
        limit=62,
        after=(gathered,),
    )(wide_weights, wide_weights, wide_weights, tall[0])
    late_blocks = gather_blocks(late_own, group)

    results = call(
        functools.partial(project, group),
        [
            in_hbm((every, D), F32),
            in_hbm((every, D), BF16),
            in_hbm((D, 4 * D), BF16),
            in_hbm((8, 6 * D), F32),
        ]
        + [sds((packed, 128), BF16)] * CUTS,
        grid=(items,),
        in_specs=[smem(), by_item] + [whole()] * group,
        out_specs=[by_item, by_item] + [whole()] * (2 + CUTS),
        scratch=[pltpu.VMEM((items * HEADS, tokens + tokens // 2, 128), BF16)],
        us=4,
        limit=34,
        after=(late_own,),
    )(interval, gathered, *second)
    x0, n1, second_weights, mods = results[:4]
    dealt = results[4:]

    own = over_cuts(dealt[0], dealt[1:])
    keys_only = [x[: units * tokens + 16] for x in own]
    others = [shift(keys_only[m], "seq", n) for n in range(1, shares) for m in range(CUTS)]
    keys_total = parts * tokens

    half_in = pl.BlockSpec((1, tokens // 2, 128), lambda u: (u, 0, 0))
    kept_spec = pl.BlockSpec((1, CUTS, tokens, 128), lambda u: (u, 0, 0, 0))
    lse_spec = pl.BlockSpec((1, CUTS, 8, tokens), lambda u: (u, 0, 0, 0))
    pack_spec = pl.BlockSpec((1, CUTS, tokens // 2, 128), lambda u: (u, 0, 0, 0))
    half_out = sds((units, tokens // 2, 128), BF16)
    results = call(
        functools.partial(attend, shares),
        [half_out] * CUTS
        + [
            in_hbm((units, CUTS, tokens, 128), F32),
            in_hbm((units, CUTS, 8, tokens), F32),
            in_hbm((8, 128), F32),
        ],
        grid=(units,),
        in_specs=[whole()] * (CUTS * shares),
        out_specs=[half_in] * CUTS + [kept_spec, lse_spec, whole()],
        scratch=[pltpu.VMEM((keys_total, 128), BF16)],
        us=9,
        limit=60 if shares > 2 else 34,
    )(*own, *others)
    backs, (kept, lse, weight_sum) = results[:CUTS], results[CUTS:]
    heads_in = over_cuts(backs[0], backs[1:])

    saved = [D, D, D, FF, D, OUT, D, FF]
    results = call(
        functools.partial(middle, group),
        [in_hbm((every, D), F32), in_hbm((items, 8, D), F32), in_hbm((8, 128), F32)]
        + [half_out] * CUTS
        + [sds((every, width), BF16) for width in saved],
        grid=(items,),
        in_specs=[smem(), smem(), smem(), whole(), by_item, lane_block(OUT), lane_block(VARP)]
        + [whole()] * (CUTS + group + 1),
        out_specs=[by_item, pl.BlockSpec((1, 8, D), lambda i: (i, 0, 0))]
        + [whole()] * (1 + CUTS)
        + [pl.BlockSpec((tokens, width), lambda i: (i, 0)) for width in saved],
        scratch=[
            pltpu.VMEM((D, late_cols), BF16),
            pltpu.VMEM((items * HEADS, tokens // 2, 128), BF16),
            pltpu.VMEM((items * HEADS, tokens // 2, 128), BF16),
        ],
        us=11,
        limit=34,
    )(
        interval,
        samples,
        cosines,
        weight_sum,
        x0,
        targets,
        mask,
        *heads_in,
        *late_blocks,
        mods,
    )
    dx1, mod_rows, loss = results[:3]
    sends, operands = results[3 : 3 + CUTS], results[3 + CUTS :]
    early_keep, early_send = call(
        middle_weights,
        [sds((group // 2, rows, late_cols), BF16)] * 2,
        scratch=[pltpu.VMEM((D, late_cols), F32)],
        us=6,
        limit=34,
    )(*operands)
    grads_in = over_cuts(sends[0], sends[1:])

    def of_unit(u, *shape):
        return pl.BlockSpec((1,) + shape, lambda i: (u,) + (0,) * len(shape))

    def back_of(u, after):
        results = call(
            functools.partial(attend_back, shares, u),
            [sds((1, CUTS, tokens // 2, 128), BF16)]
            + [sds((1, CUTS, tokens, 128), BF16)] * shares,
            grid=(1,),
            in_specs=[whole()] * (CUTS * shares)
            + [of_unit(u, tokens // 2, 128)] * CUTS
            + [of_unit(u, CUTS, tokens, 128), of_unit(u, CUTS, 8, tokens)],
            out_specs=[whole()] * (1 + shares),
            scratch=[
                pltpu.VMEM((keys_total, 128), BF16),
                pltpu.VMEM((128, keys_total), BF16),
                pltpu.VMEM((keys_total, 128), F32),
            ],
            us=6,
            limit=60 if shares > 2 else 34,
            after=after,
        )(*own, *others, *grads_in, kept, lse)
        far = results[2:]
        if u == 2:
            far = [once_ready(far[0], units_in[0][1:]), *far[1:]]
        return results[:2], [shift(far[n], "seq", n + 1) for n in range(shares - 1)]

    def joined(near, far):
        dealt = call(
            functools.partial(join_back, shares),
            [sds((tokens + tokens // 2, 128), BF16)] * CUTS,
        )(*near, *far)
        return over_cuts(dealt[0], dealt[1:])

    early_got = shift(early_send, "grp", 1)
    partial_sums, units_in = [], []
    for u in range(units):
        after = (early_keep,) if u == 0 else (partial_sums[u - 1][0][0],)
        if u == 2:
            early_once = reduce_cores_once(early_keep, early_got, after=after)
            after += (early_once[0],)
        if u >= 2:
            units_in.append(joined(*partial_sums[u - 2]))
        partial_sums.append(back_of(u, after))
    units_in.append(joined(*partial_sums[-2]))
    units_in.append(joined(*partial_sums[-1]))
    early_twice = reduce_and_deal(early_once, False, after=(units_in[1][1],))

    second_cols = 4 * D + mod_tiles(rows) * 128
    dagg, second_keep, second_send = call(
        functools.partial(project_back, units),
        [
            sds((items, D, tokens), BF16),
            sds((group // 2, rows, second_cols), BF16),
            sds((group // 2, rows, second_cols), BF16),
        ],
        grid=(items,),
        in_specs=[
            smem(),
            by_item,
            by_item,
            by_item,
            pl.BlockSpec((1, 8, D), lambda i: (i, 0, 0)),
            by_item,
        ]
        + [whole()] * (2 + CUTS * units),
        out_specs=[pl.BlockSpec((1, D, tokens), lambda i: (i, 0, 0))] + [whole()] * 2,
        scratch=[
            pltpu.VMEM((items * HEADS, tokens + tokens // 2, 128), BF16),
            pltpu.VMEM((tokens, 3 * D), BF16),
            pltpu.VMEM((D, 4 * D), F32),
            pltpu.VMEM((8, 6 * D), F32),
            pltpu.VMEM((mod_tiles(rows) * rows, 128), F32),
        ],
        us=4,
        limit=34,
    )(
        interval,
        x0,
        n1,
        dx1,
        mod_rows,
        gathered,
        second_weights,
        mods,
        *[x for unit in units_in for x in unit],
    )
    second_got = shift(second_send, "grp", 1)
    early_pieces = reduce_and_deal(early_twice, True, after=(dagg,))
    late_keep, late_send = call(
        aggregate_back,
        [sds((group // 2, rows, 2 * D + OUTP), BF16)] * 2,
        grid=(items,),
        in_specs=[
            pl.BlockSpec((1, D, tokens), lambda i: (i, 0, 0)),
            lane_block(HEADS * VARP),
            heads_spec,
            lane_block(OUT),
            lane_block(VARP),
        ]
        + [whole()] * 4,
        out_specs=[whole()] * 2,
        scratch=[
            pltpu.VMEM((HEADS * VARP, tokens), BF16),
            pltpu.VMEM((D, 2 * D + OUTP), F32),
            pltpu.VMEM((OUT, D), F32),
            pltpu.VMEM((HEADS * VARP, OUT), F32),
        ],
        us=13,
        limit=34,
        after=(early_pieces[0],),
    )(dagg, probs, picked, fields, mask, fused_w, agg_weights, embed, probe)
    early_piece, early_squares = call(
        sum_pieces,
        [piece_shape(early_pieces[0].shape[0]), sds((16, 128), F32)],
        after=(late_keep,),
    )(*early_pieces)
    early_column = over_cuts(early_piece)
    late_first = reduce_cores(
        (late_keep, shift(late_send, "grp", 1)),
        (second_keep, second_got),
    )
    late_second = reduce_once(*exchange_once(*late_first))
    early_all = gather_shares(early_column, after=(late_second[0][0],))
    late_third = reduce_twice(*exchange_again(*late_second))
    late_pieces = over_cuts(late_third[0], late_third[1:])
    start = (rows // 16) * 27
    stop = (rows // 16) * (27 + mod_tiles(rows))
    count = late_pieces[0].shape[0]
    late_piece = call(
        functools.partial(sum_late, start, stop), piece_shape(count + 1)
    )(early_squares, loss, lead, *late_pieces)
    late_column, reduced = call(
        stack_late, [sds((CUTS, count, 16, 128), BF16), sds((8, 128), F32)]
    )(*over_cuts(late_piece))
    late_all = [late_column] + [shift(late_column, "seq", n) for n in range(1, shares)]
    reduced = butterfly(reduced, "grp", 1, group)
    reduced = butterfly(reduced, "seq", 1, shares)

    def like(x, dtype=F32):
        return sds(x.shape, dtype)

    results = call(
        functools.partial(optimize, shares),
        [sds((1, 1), F32)] * 3
        + [like(wide_weights)] * 3
        + [like(wide_weights, BF16)]
        + [like(tall[0])] * 3
        + [like(tall[0], BF16)]
        + [like(query_row)] * 3
        + [like(query_row, BF16)],
        out_specs=[whole()] * 3 + [pl.BlockSpec(memory_space=pl.ANY)] * 8 + [whole()] * 4,
        scratch=[
            pltpu.VMEM((parts * early_piece.shape[0], 16, 128), BF16),
            pltpu.VMEM((parts * count, 16, 128), BF16),
        ]
        + [pltpu.VMEM(wide_weights.shape, dtype) for dtype in (F32, F32, F32, BF16)]
        + [pltpu.VMEM(tall[0].shape, dtype) for dtype in (F32, F32, F32, BF16)]
        + [pltpu.SemaphoreType.DMA((24,))],
        us=10,
        limit=34,
    )(
        reduced,
        weight_sum,
        lead,
        *early_all,
        *late_all,
        wide_weights,
        wide_firsts,
        wide_seconds,
        *tall,
        query_row,
        query_firsts.reshape(1, rows),
        query_seconds.reshape(1, rows),
    )
    tall_out = tuple(r.T for r in results[7:11])
    query_out = tuple(r.reshape(rows) for r in results[11:15])
    return tuple(r.reshape(()) for r in results[:3]) + tuple(results[3:7]) + tall_out + query_out


def solution(mesh):
    placed = (
        P("grp", "seq", None),
        P("grp", "seq", None),
        P("grp", "seq", None),
        P("grp"),
        P("grp"),
        P("grp", None),
        P("grp", None),
        P("grp", None),
        P(None, "grp"),
        P(None, "grp"),
        P(None, "grp"),
        P("grp"),
        P("grp"),
        P("grp"),
    )
    return jax.shard_map(
        per_device,
        mesh=mesh,
        in_specs=placed,
        out_specs=(
            P(),
            P(),
            P(),
            P("grp", None),
            P("grp", None),
            P("grp", None),
            P("grp", None),
            P(None, "grp"),
            P(None, "grp"),
            P(None, "grp"),
            P(None, "grp"),
            P("grp"),
            P("grp"),
            P("grp"),
            P("grp"),
        ),
        check_vma=False,
    )
```

```python
import functools

import jax
import numpy as np
import jax.numpy as jnp
from jax import lax
from jax.experimental import pallas as pl
from jax.experimental.pallas import tpu as pltpu
from jax.sharding import PartitionSpec as P

D = 384
HEADS = 6
HEAD = 64
FF = 1536
VARS = 69
PIX = 16
OUT = VARS * PIX
OUTP = 1152
VARP = 80
COLS = 128
STEP = 5
CUTS = 4
SCALE = HEAD**-0.5
LOG2E = 1.4426950408889634

beta_first = 0.5
beta_second = 0.5
learn_rate = 0.1
decay_rate = 0.01
adam_epsilon = 1e-08
clip_limit = 0.05
norm_epsilon = 1e-06
masked_score = -1e30

F32 = jnp.float32
BF16 = jnp.bfloat16
MIB = 1024 * 1024
RIDERS = 32


def dot(left, right, a, b):
    return lax.dot_general(left, right, (((a,), (b,)), ((), ())), preferred_element_type=F32)


def nn(left, right):
    return dot(left, right, 1, 0)


def nt(left, right):
    return dot(left, right, 1, 1)


def tn(left, right):
    return dot(left, right, 0, 0)


def iota(shape, dim):
    return lax.broadcasted_iota(jnp.int32, shape, dim)


def half_low(shape):
    return iota(shape, len(shape) - 1) < HEAD


def swap_halves(tile):
    return pltpu.roll(tile, HEAD, 1)


def spread():
    return iota((VARP, OUT), 1) // PIX == iota((VARP, OUT), 0)


def ones_where(mask):
    return jnp.where(mask, 1.0, 0.0).astype(BF16)


def place():
    grp = lax.axis_index("grp")
    seq = lax.axis_index("seq")
    return grp, seq


def call(
    kernel, outs, grid=(), in_specs=None, out_specs=None, scratch=(), us=1, limit=34, after=()
):
    def run(*args):
        if after:
            args = (once_ready(args[0], after), *args[1:])
        kw = {} if out_specs is None else {"out_specs": out_specs}
        return pl.pallas_call(
            kernel,
            out_shape=outs,
            grid=grid,
            in_specs=list(in_specs) if in_specs else [whole()] * len(args),
            scratch_shapes=list(scratch),
            cost_estimate=pl.CostEstimate(
                flops=int(us * 1.15e9), transcendentals=0, bytes_accessed=1024
            ),
            compiler_params=pltpu.CompilerParams(vmem_limit_bytes=limit * MIB),
            **kw,
        )(*args)

    return run


def once_ready(value, after):
    return lax.optimization_barrier((value, *after))[0]


def whole():
    return pl.BlockSpec(memory_space=pltpu.VMEM)


def smem():
    return pl.BlockSpec(memory_space=pltpu.SMEM)


def sds(shape, dtype):
    return jax.ShapeDtypeStruct(shape, dtype)


def in_hbm(shape, dtype):
    return pltpu.HBM(shape, dtype)


def standardize(x):
    centered = x - jnp.mean(x, axis=-1, keepdims=True)
    rstd = lax.rsqrt(jnp.mean(centered * centered, axis=-1, keepdims=True) + norm_epsilon)
    return centered * rstd, rstd


def standardize_back(grad, normed, rstd):
    return rstd * (
        grad
        - jnp.mean(grad, axis=-1, keepdims=True)
        - normed * jnp.mean(grad * normed, axis=-1, keepdims=True)
    )


def gelu_parts(x):
    k = 0.7978845608028654
    inner = k * (x + 0.044715 * x * x * x)
    t = jnp.tanh(inner)
    value = 0.5 * x * (1.0 + t)
    slope = 0.5 * (1.0 + t) + 0.5 * x * (1.0 - t * t) * k * (1.0 + 3 * 0.044715 * x * x)
    return value, slope


def pack_first(*refs):
    samples, cosines, agg_ref, mod_a, mod_b, wide_ref, tall_ref, query_ref = refs[:8]
    lead_ref, mask_ref, first_ref, second_ref, rider_s = refs[8:]
    rows = wide_ref.shape[0]
    grp, seq = place()
    first_ref[:, : 2 * D] = agg_ref[:, : 2 * D].astype(BF16)
    second_ref[:rows, :D] = agg_ref[:, 2 * D :].astype(BF16)
    eye = iota((rows, rows), 0) == iota((rows, rows), 1)
    column = jnp.sum(jnp.where(eye, query_ref[...], 0.0), axis=1, keepdims=True)
    lane = iota((rows, OUTP), 1)
    embed = jnp.where(lane < OUT, tall_ref[...], jnp.where(lane == OUT, column, 0.0))
    first_ref[:, 2 * D :] = embed.astype(BF16)
    low = half_low((rows, 128))
    for j in range(HEADS // 2):
        k = wide_ref[:, D + j * 128 : D + (j + 1) * 128]
        v = wide_ref[:, 2 * D + j * 128 : 2 * D + (j + 1) * 128]
        at = D + 2 * j * 128
        second_ref[:rows, at : at + 128] = jnp.where(low, k, swap_halves(v)).astype(BF16)
        second_ref[:rows, at + 128 : at + 256] = jnp.where(low, swap_halves(k), v).astype(BF16)
    second_ref[:rows, 3 * D :] = wide_ref[:, :D].astype(BF16)
    rider_s[...] = jnp.zeros_like(rider_s)

    def ride(row, value):
        for part in range(3):
            piece = value.astype(BF16).astype(F32)
            at = part * 8 + row
            rider_s[at : at + 1, : 3 * D] = piece
            value = value - piece

    lead = lead_ref[pl.ds(pl.multiple_of(grp * rows, 16), rows), :].astype(F32)
    for half, ref in ((0, mod_a), (1, mod_b)):
        mod = ref[...].astype(BF16).astype(F32)
        for g in range(3):
            ride(2 * g + half, jnp.sum(lead[:, g : g + 1] * mod, axis=0, keepdims=True))
    items, _, tokens = mask_ref.shape
    total = jnp.zeros((1, 1), F32)
    for i in range(items):
        present = jnp.maximum(mask_ref[i], 0).astype(F32)
        weighed = jnp.sum(present, axis=0, keepdims=True) * line_weights(
            samples[i], cosines, seq, iota((1, tokens), 1)
        )
        total = total + jnp.sum(weighed, axis=1, keepdims=True)
    ride(6, jnp.broadcast_to(total, (1, 3 * D)))
    second_ref[rows:, :] = rider_s[...].astype(BF16)


def line_weights(count, cosines, seq, position):
    lines = position.size // COLS
    value = jnp.zeros(position.shape, F32)
    for r in range(lines):
        value = jnp.where(position // COLS == r, cosines[seq * lines + r], value)
    return value * count.astype(F32)


def pack_late(wide_a, wide_b, wide_c, tall_ref, late_ref):
    rows = wide_a.shape[0]
    late_ref[:, : 3 * D] = wide_a[...].astype(BF16)
    late_ref[:, 3 * D : 6 * D] = wide_b[...].astype(BF16)
    rest = D + FF + OUT - 6 * D
    late_ref[:, 6 * D : D + FF + OUT] = wide_c[:, :rest].astype(BF16)
    late_ref[:, D + FF + OUT : D + FF + OUTP] = jnp.zeros((rows, OUTP - OUT), BF16)
    late_ref[:, D + FF + OUTP :] = tall_ref[:, OUT:].astype(BF16)


def assemble(target, blocks, grp, lo, hi):
    rows = target.shape[0] // len(blocks)
    for j, ref in enumerate(blocks):
        at = pl.multiple_of(jnp.bitwise_xor(grp, j) * rows, 16)
        target[pl.ds(at, rows), :] = ref[:rows, lo:hi]


def unride(target, blocks):
    target[...] = jnp.zeros_like(target)
    for g in range(4):
        for half in range(2):
            total = jnp.zeros((1, 3 * D), F32)
            for ref in blocks:
                for part in range(3):
                    at = ref.shape[0] - RIDERS + part * 8 + min(2 * g + half, 6)
                    total = total + ref[at : at + 1, : 3 * D].astype(F32)
            target[g : g + 1, half * 3 * D : (half + 1) * 3 * D] = total


def prepare(blocks, grp, outs, score_s, fused_s):
    (agg_ref, embed_ref, fused_ref, probe_ref) = outs
    assemble(agg_ref, blocks, grp, 0, 2 * D)
    assemble(embed_ref, blocks, grp, 2 * D, 2 * D + OUTP)
    query = embed_ref[:, OUT : OUT + 1].astype(F32)
    picked = jnp.where(iota((D, 128), 1) == iota((D, 128), 0) // HEAD, query, 0.0).astype(BF16)
    probe = nn(agg_ref[:, :D], picked).astype(BF16)
    probe_ref[...] = probe
    embed = embed_ref[:, :OUT]
    rows = tn(probe, embed) * SCALE
    mine = spread()
    for h in range(HEADS):
        score_s[h * VARP : (h + 1) * VARP, :] = jnp.where(mine, rows[h : h + 1, :], 0.0).astype(
            BF16
        )
    fused = tn(agg_ref[:, D:], embed)
    fused_s[...] = fused.astype(BF16)
    fused_ref[...] = fused.T.astype(BF16)


def aggregate(group, *refs):
    (fields_ref, mask_ref) = refs[:2]
    blocks, outs = refs[2 : 2 + group], refs[2 + group :]
    (probs_ref, picked_ref, gathered_ref), kept = outs[:3], outs[3:7]
    score_s, fused_s, turned_s = outs[7:]
    grp, _ = place()

    @pl.when(pl.program_id(0) == 0)
    def _():
        prepare(blocks, grp, kept, score_s, fused_s)

    fields = fields_ref[0]
    wide_fields = fields.astype(F32)
    mask = mask_ref[0]
    scores = nn(score_s[...], fields)
    expand = ones_where(iota((OUT, VARP), 0) // PIX == iota((OUT, VARP), 1))
    rounded = []
    for h in range(HEADS):
        s = jnp.where(
            mask > 0,
            scores[h * VARP : (h + 1) * VARP],
            jnp.where(mask < 0, -3e38, masked_score),
        )
        e = jnp.exp(s - jnp.max(s, axis=0, keepdims=True))
        a = e / jnp.sum(e, axis=0, keepdims=True)
        probs_ref[0, h * VARP : (h + 1) * VARP, :] = a
        rounded.append(a.astype(BF16))
    expanded = nn(expand, rounded[0])
    for h in range(HEADS):
        later = nn(expand, rounded[h + 1]) if h + 1 < HEADS else None
        picked = (expanded * wide_fields).astype(BF16)
        picked_ref[h, 0] = picked
        turned_s[h * HEAD : (h + 1) * HEAD, :] = nn(fused_s[h * HEAD : (h + 1) * HEAD, :], picked)
        expanded = later
    gathered_ref[...] = turned_s[...].T.astype(BF16)


def project(group, *refs):
    (interval, gathered_ref), blocks, outs = refs[:2], refs[2 : 2 + group], refs[2 + group :]
    (x0_ref, n1_ref, weights, mod_s), units, (unit_s,) = outs[:4], outs[4:-1], outs[-1:]
    item = pl.program_id(0)
    grp, seq = place()
    tokens = gathered_ref.shape[0]

    @pl.when(item == 0)
    def _():
        assemble(weights, blocks, grp, 0, 4 * D)
        unride(mod_s, blocks)

    x0 = nn(gathered_ref[...], weights[:, :D])
    x0_ref[...] = x0
    mod = mod_s[pl.ds(interval[item], 1), :]
    normed, _ = standardize(x0)
    n1 = (normed * (1.0 + mod[:, D : 2 * D]) + mod[:, :D]).astype(BF16)
    n1_ref[...] = n1
    qkv = nn(n1, weights[:, D:])
    half = tokens // 2
    low = half_low((half, 128))
    packed = tokens + half
    for h in range(HEADS):
        unit_s[HEADS * item + h, :tokens, :] = qkv[:, h * 128 : (h + 1) * 128].astype(BF16)
    for j in range(HEADS // 2):
        pair = qkv[:, 2 * D + j * 128 : 2 * D + (j + 1) * 128] * (SCALE * LOG2E)
        top, bottom = pair[:half], pair[half:]
        unit_s[HEADS * item + 2 * j, tokens:packed, :] = jnp.where(
            low, top, swap_halves(bottom)
        ).astype(BF16)
        unit_s[HEADS * item + 2 * j + 1, tokens:packed, :] = jnp.where(
            low, swap_halves(top), bottom
        ).astype(BF16)

    @pl.when(item == pl.num_programs(0) - 1)
    def _():
        value = jnp.broadcast_to(mod_s[3:4, :128], (16, 128))
        high = value.astype(BF16)
        value = value - high.astype(F32)
        middle_part = value.astype(BF16)
        low_part = (value - middle_part.astype(F32)).astype(BF16)
        lane = iota((16, 128), 1)
        rides = jnp.where(
            lane < 32,
            high.astype(F32),
            jnp.where(
                lane < 64,
                middle_part.astype(F32),
                jnp.where(lane < 96, low_part.astype(F32), 0.0),
            ),
        ).astype(BF16)
        a = seq // (lax.axis_size("seq") // CUTS)
        rounds = unit_s.shape[0] // CUTS
        queries = rounds * tokens + 16
        for m in range(CUTS):
            units[m][rounds * tokens : queries, :] = rides
            for r in range(rounds):
                unit = CUTS * r + jnp.bitwise_xor(a, m)
                units[m][r * tokens : (r + 1) * tokens, :] = unit_s[unit, :tokens, :]
                at = queries + r * half
                units[m][at : at + half, :] = unit_s[unit, tokens:packed, :]


def deal(targets, source, seq):
    a = seq // (lax.axis_size("seq") // CUTS)
    for m in range(CUTS):
        for r in range(targets[m].shape[0]):
            targets[m][r] = source[CUTS * r + jnp.bitwise_xor(a, m)]


def collect(target, sources, seq):
    a = seq // (lax.axis_size("seq") // CUTS)
    for m in range(CUTS):
        for r in range(sources[m].shape[0]):
            target[CUTS * r + jnp.bitwise_xor(a, m)] = sources[m][r]


def unpack(pack, at_low):
    wide = pack.astype(F32)
    low = half_low(wide.shape)
    if at_low:
        both = [jnp.where(low, wide, 0.0), jnp.where(low, swap_halves(wide), 0.0)]
    else:
        both = [jnp.where(low, 0.0, swap_halves(wide)), jnp.where(low, 0.0, wide)]
    return jnp.concatenate(both, axis=0).astype(BF16)


def pack_rows(tile, at_low):
    half = tile.shape[0] // 2
    top, bottom = tile[:half], tile[half:]
    low = half_low(top.shape)
    if at_low:
        return jnp.where(low, top, swap_halves(bottom))
    return jnp.where(low, swap_halves(top), bottom)


def attend(shares, *refs):
    own = refs[:CUTS]
    others = refs[CUTS : CUTS * shares]
    backs = refs[CUTS * shares : CUTS * shares + CUTS]
    kept_ref, lse_ref, weight_ref, keys_s = refs[CUTS * shares + CUTS :]
    tokens = kept_ref.shape[2]
    half = tokens // 2
    unit = pl.program_id(0)
    rows = own[0].shape[0] - 16
    rider = rows * tokens // (tokens + half)

    @pl.when(unit == 0)
    def _():
        total = jnp.zeros((16, 128), F32)
        for ref in own + others:
            total = total + ref[rider : rider + 16, :].astype(F32)
        total = jnp.sum(total[0:8], axis=1, keepdims=True) / 32.0
        weight_ref[...] = jnp.broadcast_to(total, (8, 128))

    for n, ref in enumerate(own + others):
        at = pl.ds(pl.multiple_of(unit * tokens, tokens), tokens)
        keys_s[n * tokens : (n + 1) * tokens, :] = ref[at, :]
    keys = keys_s[...]
    values = jnp.where(half_low(keys.shape), jnp.ones_like(keys), keys)

    def scores_of(m):
        at = pl.ds(pl.multiple_of(rider + 16 + unit * half, 16), half)
        return nt(unpack(own[m][at, :], True), keys)

    scores = scores_of(0)
    for m in range(CUTS):
        later = scores_of(m + 1) if m + 1 < CUTS else None
        top = jnp.max(scores, axis=1, keepdims=True)
        out = nn(jnp.exp2(scores - top).astype(BF16), values)
        total = out[:, 0:1]
        out = out / total
        lse = jnp.broadcast_to(top + jnp.log2(total), (tokens, 128)).T
        lse_ref[0, m] = lse[:8]
        kept_ref[0, m] = out
        backs[m][0] = pack_rows(out, False).astype(BF16)
        scores = later


def middle(group, *refs):
    (interval, samples, cosines, sum_ref, x0_ref, fields_ref, mask_ref) = refs[:7]
    heads_in = refs[7 : 7 + CUTS]
    blocks = refs[7 + CUTS : 7 + CUTS + group]
    mod_s = refs[7 + CUTS + group]
    outs = refs[7 + CUTS + group + 1 :]
    (dx1_ref, rows_ref, loss_ref) = outs[:3]
    sends = outs[3 : 3 + CUTS]
    attended_s, db1_ref, n2_ref, dh_ref, nf_ref, dpred_ref, db2_ref, active_ref = outs[
        3 + CUTS : 11 + CUTS
    ]
    weights, head_s, grad_s = outs[11 + CUTS :]
    item = pl.program_id(0)
    grp, seq = place()
    tokens = x0_ref.shape[0]
    half = tokens // 2

    @pl.when(item == 0)
    def _():
        assemble(weights, blocks, grp, 0, D + FF + OUTP + FF)
        collect(head_s, heads_in, seq)
        loss_ref[...] = jnp.zeros_like(loss_ref)

    low = half_low((half, 128))
    for j in range(HEADS // 2):
        one = head_s[HEADS * item + 2 * j].astype(F32)
        two = head_s[HEADS * item + 2 * j + 1].astype(F32)
        attended_s[:half, j * 128 : (j + 1) * 128] = jnp.where(low, one, swap_halves(two)).astype(
            BF16
        )
        attended_s[half:, j * 128 : (j + 1) * 128] = jnp.where(low, swap_halves(one), two).astype(
            BF16
        )
    out_w = slice(0, D)
    up_w = slice(D, D + FF)
    head_w = slice(D + FF, D + FF + OUT)
    down_w = slice(D + FF + OUTP, D + FF + OUTP + FF)
    mod = mod_s[pl.ds(interval[item], 1), :]
    gate_a, shift_b, scale_b, gate_b = [mod[:, k * D : (k + 1) * D] for k in range(2, 6)]
    attended = attended_s[...]
    branch_a = nn(attended, weights[:, out_w])
    x1 = x0_ref[...] + gate_a * branch_a
    normed_b, rstd_b = standardize(x1)
    n2 = (normed_b * (1.0 + scale_b) + shift_b).astype(BF16)
    n2_ref[...] = n2
    value, slope = gelu_parts(nn(n2, weights[:, up_w]))
    active = value.astype(BF16)
    active_ref[...] = active
    branch_b = nt(active, weights[:, down_w])
    x2 = x1 + gate_b * branch_b
    final, rstd_f = standardize(x2)
    nf = final.astype(BF16)
    nf_ref[...] = nf
    diff = nn(nf, weights[:, head_w]) - fields_ref[0].astype(F32).T
    present = tn(ones_where(mask_ref[0] > 0), ones_where(spread()))
    weight = line_weights(samples[item], cosines, seq, iota((tokens, 1), 0))
    weight_grad = weight * (2.0 / PIX) / sum_ref[0:1, 0:1]
    masked = present * diff
    each = jnp.sum(masked * diff, axis=1, keepdims=True) * weight
    loss_ref[...] += jnp.broadcast_to(jnp.sum(each, axis=0, keepdims=True) / PIX, (8, 128))
    dpred = (masked * weight_grad).astype(BF16)
    dpred_ref[...] = dpred

    dx2 = standardize_back(nt(dpred, weights[:, head_w]), final, rstd_f)
    db2 = (gate_b * dx2).astype(BF16)
    db2_ref[...] = db2
    d_gate_b = jnp.sum(dx2 * branch_b, axis=0, keepdims=True)
    dh = (nn(db2, weights[:, down_w]) * slope).astype(BF16)
    dh_ref[...] = dh
    dn2 = nt(dh, weights[:, up_w])
    d_shift_b = jnp.sum(dn2, axis=0, keepdims=True)
    d_scale_b = jnp.sum(dn2 * normed_b, axis=0, keepdims=True)
    dx1 = dx2 + standardize_back(dn2 * (1.0 + scale_b), normed_b, rstd_b)
    dx1_ref[...] = dx1
    d_gate_a = jnp.sum(dx1 * branch_a, axis=0, keepdims=True)
    db1 = (gate_a * dx1).astype(BF16)
    db1_ref[...] = db1
    dout = nt(db1, weights[:, out_w])
    rows_ref[0] = jnp.concatenate(
        [d_gate_a, d_shift_b, d_scale_b, d_gate_b, jnp.zeros((4, D), F32)], axis=0
    )
    for j in range(HEADS // 2):
        pair = dout[:, j * 128 : (j + 1) * 128]
        top, bottom = pair[:half], pair[half:]
        grad_s[HEADS * item + 2 * j] = jnp.where(low, top, swap_halves(bottom)).astype(BF16)
        grad_s[HEADS * item + 2 * j + 1] = jnp.where(low, swap_halves(top), bottom).astype(BF16)

    @pl.when(item == pl.num_programs(0) - 1)
    def _():
        deal(sends, grad_s, seq)


def middle_weights(*refs):
    attended, db1, n2, dh, nf, dpred, db2, active = refs[:8]
    keep_ref, send_ref, acc = refs[8:]
    grp, _ = place()
    acc[:, :D] = tn(attended[...], db1[...])
    acc[:, D : D + FF] = tn(n2[...], dh[...])
    acc[:, D + FF : D + FF + OUT] = tn(nf[...], dpred[...])
    acc[:, D + FF + OUT : D + FF + OUTP] = jnp.zeros((D, OUTP - OUT), F32)
    acc[:, D + FF + OUTP :] = tn(db2[...], active[...])
    split_rows(acc, grp, keep_ref, send_ref)


def split_rows(acc, grp, keep_ref, send_ref):
    rows = keep_ref.shape[1]
    for j in range(keep_ref.shape[0]):
        for odd, ref in ((0, keep_ref), (1, send_ref)):
            at = pl.multiple_of(jnp.bitwise_xor(grp, 2 * j + odd) * rows, 16)
            ref[j, :, : acc.shape[1]] = acc[pl.ds(at, rows), :].astype(BF16)


def attend_back(shares, unit, *refs):
    own = refs[:CUTS]
    others = refs[CUTS : CUTS * shares]
    grads = refs[CUTS * shares : CUTS * shares + CUTS]
    kept_ref, lse_ref = refs[CUTS * shares + CUTS : CUTS * shares + CUTS + 2]
    outs = refs[CUTS * shares + CUTS + 2 :]
    dq_ref, own_ref = outs[:2]
    far_refs = outs[2 : 2 + shares - 1]
    keys_s, turned_s, acc = outs[2 + shares - 1 :]
    tokens = kept_ref.shape[2]
    for n, ref in enumerate(own + others):
        keys_s[n * tokens : (n + 1) * tokens, :] = ref[unit * tokens : (unit + 1) * tokens, :]
    turned_s[...] = keys_s[...].T
    every = range(CUTS)
    half = tokens // 2
    at = (own[0].shape[0] - 16) * tokens // (tokens + half) + 16 + unit * half
    queries = jnp.concatenate(
        [unpack(own[m][at : at + half, :], True) for m in every], axis=0
    )
    grads = [unpack(grads[m][0], False) for m in every]
    delta = jnp.concatenate(
        [
            jnp.sum((grads[m].astype(F32) * kept_ref[0, m]).T, axis=0, keepdims=True)
            for m in every
        ],
        axis=1,
    )
    grads = jnp.concatenate(grads, axis=0)
    lse = jnp.concatenate([lse_ref[0, m, 0:1, :] for m in every], axis=1)
    chunk = 2 * tokens
    count = keys_s.shape[0] // chunk

    def products_of(c):
        keys = keys_s[c * chunk : (c + 1) * chunk, :]
        return nt(keys, queries), nt(keys, grads)

    products, dq = products_of(0), None
    for c in range(count):
        scores, dprobs = products
        if c + 1 < count:
            products = products_of(c + 1)
        probs = jnp.exp2(scores - lse)
        dscores = (probs * (dprobs - delta)).astype(BF16)
        acc[c * chunk : (c + 1) * chunk, :] = nn(probs.astype(BF16), grads) + nn(dscores, queries)
        part = nn(turned_s[:, c * chunk : (c + 1) * chunk], dscores)
        dq = part if dq is None else dq + part
    for m in every:
        turned = dq[:, m * tokens : (m + 1) * tokens].T * SCALE
        dq_ref[0, m] = pack_rows(turned, True).astype(BF16)
    factor = jnp.where(half_low((1, 128)), 1.0 / LOG2E, 1.0)
    for m in range(CUTS):
        own_ref[0, m] = (acc[m * tokens : (m + 1) * tokens, :] * factor).astype(BF16)
        for n, ref in enumerate(far_refs):
            at = ((n + 1) * CUTS + m) * tokens
            ref[0, m] = (acc[at : at + tokens, :] * factor).astype(BF16)


def join_back(shares, *refs):
    dq_ref, own_ref = refs[:2]
    far = refs[2 : 2 + shares - 1]
    outs = refs[2 + shares - 1 :]
    tokens = own_ref.shape[2]
    for m in range(CUTS):
        total = own_ref[0, m].astype(F32)
        for ref in far:
            total = total + ref[0, m].astype(F32)
        outs[m][:tokens, :] = total.astype(BF16)
        outs[m][tokens:, :] = dq_ref[0, m]


def project_back(rounds, *refs):
    (interval, x0_ref, n1_ref, dx1_ref, rows_ref, gathered_ref, weights, mod_s) = refs[:8]
    units, outs = refs[8 : 8 + CUTS * rounds], refs[8 + CUTS * rounds :]
    (dagg_ref, keep_ref, send_ref) = outs[:3]
    unit_s, dqkv_s, acc, dmod_ref, lines_s = outs[3:]
    item = pl.program_id(0)
    grp, seq = place()
    tokens = x0_ref.shape[0]
    half = tokens // 2

    @pl.when(item == 0)
    def _():
        a = seq // (lax.axis_size("seq") // CUTS)
        for r in range(rounds):
            for m in range(CUTS):
                unit_s[CUTS * r + jnp.bitwise_xor(a, m)] = units[CUTS * r + m][...]
        acc[...] = jnp.zeros_like(acc)
        dmod_ref[...] = jnp.zeros_like(dmod_ref)

    low = half_low((half, 128))
    for h in range(HEADS):
        dqkv_s[:, h * 128 : (h + 1) * 128] = unit_s[HEADS * item + h, :tokens, :]
    for j in range(HEADS // 2):
        one = unit_s[HEADS * item + 2 * j, tokens:, :].astype(F32)
        two = unit_s[HEADS * item + 2 * j + 1, tokens:, :].astype(F32)
        lanes = slice(2 * D + j * 128, 2 * D + (j + 1) * 128)
        dqkv_s[:half, lanes] = jnp.where(low, one, swap_halves(two)).astype(BF16)
        dqkv_s[half:, lanes] = jnp.where(low, swap_halves(one), two).astype(BF16)
    dqkv = dqkv_s[...]
    which = interval[item]
    mod = mod_s[pl.ds(which, 1), :]
    acc[:, D:] += tn(n1_ref[...], dqkv)
    dn1 = nt(dqkv, weights[:, D:])
    normed, rstd = standardize(x0_ref[...])
    d_shift = jnp.sum(dn1, axis=0, keepdims=True)
    d_scale = jnp.sum(dn1 * normed, axis=0, keepdims=True)
    dx0 = (
        dx1_ref[...] + standardize_back(dn1 * (1.0 + mod[:, D : 2 * D]), normed, rstd)
    ).astype(BF16)
    rows = rows_ref[0]
    for k, row in enumerate([d_shift, d_scale] + [rows[r : r + 1] for r in range(4)]):
        dmod_ref[pl.ds(which, 1), k * D : (k + 1) * D] += row

    acc[:, :D] += tn(gathered_ref[...], dx0)
    dagg_ref[0] = nt(weights[:, :D], dx0).astype(BF16)

    @pl.when(item == pl.num_programs(0) - 1)
    def _():
        split_rows(acc, grp, keep_ref, send_ref)
        lines_s[...] = jnp.zeros_like(lines_s)
        for t in range(6 * D // 128):
            lines_s[4 * t : 4 * t + 3, :] = dmod_ref[0:3, t * 128 : (t + 1) * 128]
        rows = keep_ref.shape[1]
        for t in range(mod_tiles(rows)):
            tile = lines_s[t * rows : (t + 1) * rows, :].astype(BF16)
            at = acc.shape[1] + t * 128
            for j in range(keep_ref.shape[0]):
                keep_ref[j, :, at : at + 128] = tile
                send_ref[j, :, at : at + 128] = tile


def aggregate_back(*refs):
    (dagg_ref, probs_ref, picked_ref, fields_ref, mask_ref) = refs[:5]
    (fused_ref, agg_ref, embed_ref, probe_ref) = refs[5:9]
    keep_ref, send_ref, ds_s, acc, mix, dscore = refs[9:]
    item = pl.program_id(0)
    grp, _ = place()
    tokens = dagg_ref.shape[2]

    @pl.when(item == 0)
    def _():
        mix[...] = jnp.zeros_like(mix)
        dscore[...] = jnp.zeros_like(dscore)

    dagg = dagg_ref[0].astype(F32)
    fields = fields_ref[0]
    wide_fields = fields.astype(F32)
    keep = mask_ref[0] > 0
    expand = ones_where(spread())
    upper = iota((128, tokens), 0) < HEAD
    dparts = []
    for h in range(HEADS):
        mine = upper if h % 2 == 0 else jnp.logical_not(upper)
        pair = slice(h // 2 * 128, (h // 2 + 1) * 128)
        dparts.append(jnp.where(mine, dagg[pair], 0.0).astype(BF16))

    def spread_out(h):
        return nn(fused_ref[:, h // 2 * 128 : (h // 2 + 1) * 128], dparts[h])

    spreaded = spread_out(0)
    for j in range(HEADS // 2):
        both = None
        for h in (2 * j, 2 * j + 1):
            later = spread_out(h + 1) if h + 1 < HEADS else None
            spreaded = (spreaded * wide_fields).astype(BF16)
            part = nt(picked_ref[h, 0], dparts[h])
            both = part if both is None else both + part
            dprobs = nn(expand, spreaded)
            probs = probs_ref[0, h * VARP : (h + 1) * VARP, :]
            ds = probs * (dprobs - jnp.sum(probs * dprobs, axis=0, keepdims=True))
            ds_s[h * VARP : (h + 1) * VARP, :] = jnp.where(keep, ds, 0.0).astype(BF16)
            spreaded = later
        mix[:, j * 128 : (j + 1) * 128] += both
    dscore[...] += nt(ds_s[...], fields)

    @pl.when(item == pl.num_programs(0) - 1)
    def _():
        lines = iota((128, OUT), 0)
        owned = spread()
        drows = jnp.zeros((128, OUT), F32)
        for h in range(HEADS):
            mine = dscore[h * VARP : (h + 1) * VARP, :]
            line = jnp.sum(jnp.where(owned, mine, 0.0), axis=0, keepdims=True) * SCALE
            drows = drows + jnp.where(lines == h, line, 0.0)
        drows = drows.astype(BF16)
        mixed = mix[...].astype(BF16)
        embed = embed_ref[:, :OUT]
        acc[:, 2 * D : 2 * D + OUT] = nt(agg_ref[:, D:], mixed) + nn(probe_ref[...], drows)
        acc[:, D : 2 * D] = nn(embed, mixed)
        dprobe = nt(embed, drows)
        heads = jnp.where(iota((128, D), 1) // HEAD == iota((128, D), 0), 1.0, 0.0).astype(BF16)
        coarse = dprobe.astype(BF16)
        fine = (dprobe - coarse.astype(F32)).astype(BF16)
        by_column = nn(coarse, heads) + nn(fine, heads)
        eye = iota((D, D), 0) == iota((D, D), 1)
        query = embed_ref[:, OUT : OUT + 1].astype(F32)
        query_row = jnp.sum(jnp.where(eye, query, 0.0), axis=0, keepdims=True)
        acc[:, :D] = by_column * query_row
        dquery = jnp.sum(agg_ref[:, :D].astype(F32) * by_column, axis=0, keepdims=True)
        column = jnp.sum(jnp.where(eye, dquery, 0.0), axis=1, keepdims=True)
        acc[:, 2 * D + OUT :] = jnp.where(iota((D, OUTP - OUT), 1) == 0, column, 0.0)
        split_rows(acc, grp, keep_ref, send_ref)


def mod_tiles(rows):
    return -(-4 * (6 * D // 128) // rows)


def shares_of():
    shares = lax.axis_size("seq") // CUTS
    _, seq = place()
    return shares, seq // shares, lax.rem(seq, shares)


def added(refs, at=None):
    total = None
    for ref in refs:
        value = (ref[...] if at is None else ref[at]).astype(F32)
        total = value if total is None else total + value
    return total


def sum_cores(pairs, sources, *refs):
    ins, outs, table = refs[: 2 * sources], refs[2 * sources : -1], refs[-1]
    shares, _, share = shares_of()
    first, second = outs[:pairs], outs[pairs:]
    half = table.shape[1] // 2
    size = half // shares
    per = ins[0].shape[1] // 16
    count = sum(ref.shape[2] for ref in ins[::2]) // 128 * per
    for j in range(pairs):
        at = 0
        for keep_ref, got_ref in zip(ins[::2], ins[1::2]):
            total = (keep_ref[j].astype(F32) + got_ref[j].astype(F32)).astype(BF16)
            for t in range(total.shape[1] // 128):
                for g in range(per):
                    table[j, at] = total[g * 16 : (g + 1) * 16, t * 128 : (t + 1) * 128]
                    at += 1
        for spare in range(count, 2 * half):
            table[j, spare] = jnp.zeros(table.shape[2:], BF16)
        first[j][...] = table[j, :half]
        for n in range(shares):
            at = half + jnp.bitwise_xor(share, n) * size
            second[n][j * size : (j + 1) * size] = table[j, pl.ds(at, size)]


def sum_cores_once(pairs, *refs):
    (keep_ref, got_ref), outs = refs[:2], refs[2:]
    per = keep_ref.shape[1] // 16
    count = keep_ref.shape[2] // 128 * per
    for j in range(pairs):
        total = (keep_ref[j].astype(F32) + got_ref[j].astype(F32)).astype(BF16)
        for t in range(keep_ref.shape[2] // 128):
            for g in range(per):
                outs[j][t * per + g] = total[g * 16 : (g + 1) * 16, t * 128 : (t + 1) * 128]
        for spare in range(count, outs[j].shape[0]):
            outs[j][spare] = jnp.zeros(outs[j].shape[1:], BF16)


def sum_and_deal(over_cuts, *refs):
    outs, table = refs[-1 - (CUTS if over_cuts else shares_of()[0]) : -1], refs[-1]
    _, cut, share = shares_of()
    table[...] = added(refs[: -1 - len(outs)]).astype(BF16)
    size = outs[0].shape[0]
    for n, ref in enumerate(outs):
        ref[...] = table[pl.ds(jnp.bitwise_xor(cut if over_cuts else share, n) * size, size)]


def sum_both(pairs, shares, *refs):
    by_grp, by_share = refs[:pairs], refs[pairs : pairs + shares]
    outs, (table,) = refs[pairs + shares : -1], refs[-1:]
    _, _, share = shares_of()
    table[...] = added(by_grp).astype(BF16)
    size = outs[0].shape[0]
    for n in range(shares):
        outs[n][...] = table[pl.ds(jnp.bitwise_xor(share, n) * size, size)]
    for j in range(pairs):
        at = slice(j * size, (j + 1) * size)
        outs[shares + j][...] = added(by_share, at).astype(BF16)


def sum_both_again(pairs, shares, *refs):
    by_share, by_grp = refs[:shares], refs[shares : shares + pairs]
    outs, (table,) = refs[pairs + shares : -1], refs[-1:]
    _, cut, _ = shares_of()
    size = outs[0].shape[0] // 2
    table[0] = added(by_share).astype(BF16)
    table[1] = added(by_grp).astype(BF16)
    for m in range(CUTS):
        at = pl.ds(jnp.bitwise_xor(cut, m) * size, size)
        outs[m][:size] = table[0, at]
        outs[m][size:] = table[1, at]


def sum_pieces(*refs):
    sources, (out_ref, square_ref) = refs[:-2], refs[-2:]
    total = added(sources)
    out_ref[...] = total.astype(BF16)
    square_ref[...] = jnp.sum(total * total, axis=0)


def sum_late(start, stop, *refs):
    early_ref, loss_ref, lead_ref = refs[:3]
    sources, out_ref = refs[3:-1], refs[-1]
    grp, _ = place()
    shares, cut, share = shares_of()
    rows = lead_ref.shape[0] // lax.axis_size("grp")
    lead = lead_ref[pl.ds(pl.multiple_of(grp * rows, 16), rows), :].astype(F32)
    cols = [lead[:, g : g + 1] for g in range(3)]

    def gram(f, g):
        return jnp.sum(cols[f] * cols[g], axis=0, keepdims=True)

    row = lax.rem(iota((16, 1), 0), 4)

    def pick(*values):
        out = jnp.zeros((16, 1), F32)
        for r, value in values:
            out = jnp.where(row == r, value, out)
        return out

    same = pick(*[(g, gram(g, g)) for g in range(3)])
    next_one = pick((1, 2 * gram(0, 1)), (2, 2 * gram(1, 2)))
    next_two = pick((2, 2 * gram(0, 2)))
    size = (out_ref.shape[0] - 1) // 2
    plain = jnp.zeros((16, 128), F32)
    for half in range(2):
        for k in range(size):
            total = added(sources, half * size + k)
            out_ref[half * size + k] = total.astype(BF16)
            index = ((half * shares + share) * CUTS + cut) * size + k
            special = jnp.logical_and(index >= start, index < stop)
            square = total * total
            mixed = (
                square * same
                + total * pltpu.roll(total, 1, 0) * next_one
                + total * pltpu.roll(total, 2, 0) * next_two
            )
            plain = plain + jnp.where(special, mixed, square)
    squares = jnp.sum(jnp.sum(plain + early_ref[...], axis=0, keepdims=True), axis=1, keepdims=True)
    rider = jnp.zeros((16, 128), F32)
    for at, value in ((0, loss_ref[0:1, :]), (3, jnp.broadcast_to(squares, (1, 128)))):
        for part in range(3):
            piece = value.astype(BF16).astype(F32)
            rider = jnp.where(iota((16, 128), 0) == at + part, piece, rider)
            value = value - piece
    out_ref[2 * size] = rider.astype(BF16)


def stack_late(*refs):
    pieces, (column_ref, reduced_ref) = refs[:-2], refs[-2:]
    count = column_ref.shape[1]
    rider = jnp.zeros((16, 128), F32)
    for m, ref in enumerate(pieces):
        column_ref[m] = ref[:count]
        rider = rider + ref[count].astype(F32)
    reduced_ref[...] = jnp.concatenate(
        [rider[0:1] + rider[1:2] + rider[2:3], rider[3:4] + rider[4:5] + rider[5:6]]
        + [jnp.zeros((6, 128), F32)],
        axis=0,
    )


def stack(*refs):
    for m, ref in enumerate(refs[:-1]):
        refs[-1][m] = ref[...]


def step_values(param, first, second, grad):
    first = beta_first * first + (1.0 - beta_first) * grad
    second = beta_second * second + (1.0 - beta_second) * grad * grad
    mean_hat = first * (1.0 / (1.0 - beta_first**STEP))
    var_hat = second * (1.0 / (1.0 - beta_second**STEP))
    param = param - learn_rate * (
        mean_hat / (jnp.sqrt(var_hat) + adam_epsilon) + decay_rate * param
    )
    return param, first, second, param.astype(BF16)


def optimize(shares, *refs):
    reduced_ref, sum_ref, lead_ref = refs[:3]
    early = refs[3 : 3 + shares]
    late = refs[3 + shares : 3 + 2 * shares]
    wide = refs[3 + 2 * shares : 6 + 2 * shares]
    tall = refs[6 + 2 * shares : 9 + 2 * shares]
    query = refs[9 + 2 * shares : 12 + 2 * shares]
    outs = refs[12 + 2 * shares :]
    scalars, wide_hbm, tall_hbm, query_out = outs[:3], outs[3:7], outs[7:11], outs[11:15]
    early_s, late_s, wide_out, tall_out, sems = outs[15], outs[16], outs[17:21], outs[21:25], outs[25]
    grp, _ = place()
    _, cut, share = shares_of()
    for table, stacks, halves in ((early_s, early, 1), (late_s, late, 2)):
        size = stacks[0].shape[1] // halves
        for n, ref in enumerate(stacks):
            for m in range(CUTS):
                for half in range(halves):
                    at = (half * shares + jnp.bitwise_xor(share, n)) * CUTS
                    at = (at + jnp.bitwise_xor(cut, m)) * size
                    table[pl.ds(at, size)] = ref[m, half * size : (half + 1) * size]
    norm = jnp.sqrt(reduced_ref[1:2, 0:1])
    for ref, value in zip(scalars, (reduced_ref[0:1, 0:1], sum_ref[0:1, 0:1], norm)):
        ref[...] = value
    factor = jnp.minimum(1.0, clip_limit / (norm + 1e-06))
    rows = wide[0].shape[0]
    per = rows // 16

    def tile(table, t):
        return jnp.concatenate([table[t * per + g] for g in range(per)], axis=0).astype(F32)

    def put(ins, targets, at, grad):
        new = step_values(*[r[at] for r in ins], grad * factor)
        for ref, value in zip(targets, new):
            ref[at] = value

    def at(t, width=128):
        return (slice(None), slice(t * 128, t * 128 + width))

    copies = []

    def flush(sources, targets, lo, hi):
        for source, target in zip(sources, targets):
            copy = pltpu.make_async_copy(
                source.at[:, lo:hi], target.at[:, lo:hi], sems.at[len(copies)]
            )
            copy.start()
            copies.append(copy)

    low = half_low((rows, 128))
    for t in range(6):
        put(wide, wide_out, at(t), tile(late_s, t))
    for t in range(3):
        put(wide, wide_out, at(6 + t), tile(late_s, 15 + t))
    flush(wide_out, wide_hbm, 0, 3 * D)
    lead = lead_ref[pl.ds(pl.multiple_of(grp * rows, 16), rows), :].astype(F32)
    lines = jnp.concatenate([tile(late_s, 27 + t) for t in range(mod_tiles(rows))], axis=0)
    for t in range(18):
        grad = lead[:, 0:1] * lines[4 * t : 4 * t + 1]
        for g in (1, 2):
            grad = grad + lead[:, g : g + 1] * lines[4 * t + g : 4 * t + g + 1]
        put(wide, wide_out, at(9 + t), grad)
    flush(wide_out, wide_hbm, 3 * D, 9 * D)
    qkv = 18
    for j in range(3):
        put(wide, wide_out, at(27 + j), tile(late_s, qkv + 6 + j))
        one, two = tile(late_s, qkv + 2 * j), tile(late_s, qkv + 2 * j + 1)
        put(wide, wide_out, at(30 + j), jnp.where(low, one, swap_halves(two)))
        put(wide, wide_out, at(33 + j), jnp.where(low, swap_halves(one), two))
    flush(wide_out, wide_hbm, 9 * D, 12 * D)
    for t in range(15 + 8):
        put(wide, wide_out, at(36 + t), tile(early_s, t))
    rest = OUT - 8 * 128
    put(wide, wide_out, at(59, rest), tile(early_s, 23)[:, :rest])
    flush(wide_out, wide_hbm, 12 * D, wide[0].shape[1])
    for t in range(8):
        put(tall, tall_out, at(t), tile(late_s, 6 + t))
    flush(tall_out, tall_hbm, 0, 8 * 128)
    last = tile(late_s, 14)
    lane = iota((rows, 128), 1)
    for t in range(FF // 128):
        turned = pltpu.roll(tile(early_s, 24 + t), rest, 1)
        put(tall, tall_out, at(8 + t), jnp.where(lane < rest, last, turned))
        if t == 0:
            eye = iota((rows, rows), 0) == iota((rows, rows), 1)
            grad = jnp.sum(jnp.where(eye, last[:, rest : rest + 1], 0.0), axis=0, keepdims=True)
            put(query, query_out, (slice(None), slice(None)), grad)
        last = turned
    put(tall, tall_out, at(8 + FF // 128, rest), last[:, :rest])
    flush(tall_out, tall_hbm, 8 * 128, tall[0].shape[1])
    for copy in copies:
        copy.wait()


def shift(value, axis, bit):
    size = lax.axis_size(axis)
    return lax.ppermute(value, axis, [(i, i ^ bit) for i in range(size)])


def gather_blocks(own, group, behind=None):
    blocks = {0: own}
    for j in range(2, group, 2):
        blocks[j] = shift(own, "grp", j)
    if behind is not None:
        blocks = behind(blocks)
    for j in range(0, group, 2):
        blocks[j + 1] = shift(blocks[j], "grp", 1)
    return [blocks[j] for j in range(group)]


def granules(rows, cols, shares):
    unit = 2 * shares * CUTS
    return -(-(rows // 16) * (cols // 128) // unit) * unit


def piece_shape(count):
    return sds((count, 16, 128), BF16)


def reduce_cores(*sources, after=()):
    pairs, rows, _ = sources[0][0].shape
    shares = lax.axis_size("seq") // CUTS
    count = granules(rows, sum(keep.shape[2] for keep, _ in sources), shares)
    results = call(
        functools.partial(sum_cores, pairs, len(sources)),
        [piece_shape(count // 2)] * pairs + [piece_shape(count // 2 // shares * pairs)] * shares,
        scratch=[pltpu.VMEM((pairs, count, 16, 128), BF16)],
        after=after,
    )(*[x for source in sources for x in source])
    return results[:pairs], results[pairs:]


def reduce_cores_once(keep, got, after=()):
    pairs, rows, cols = keep.shape
    parts = lax.axis_size("seq")
    count = -(-(rows // 16) * (cols // 128) // parts) * parts
    halves = call(
        functools.partial(sum_cores_once, pairs), [piece_shape(count)] * pairs, after=after
    )(keep, got)
    return [halves[0]] + [shift(halves[j], "grp", 2 * j) for j in range(1, pairs)]


def reduce_and_deal(pieces, over, after=()):
    count = pieces[0].shape[0]
    number = CUTS if over else lax.axis_size("seq") // CUTS
    outs = call(
        functools.partial(sum_and_deal, over),
        [piece_shape(count // number)] * number,
        scratch=[pltpu.VMEM((count, 16, 128), BF16)],
        after=after,
    )(*pieces)
    if over:
        return over_cuts(outs[0], outs[1:])
    return [outs[0]] + [shift(outs[n], "seq", n) for n in range(1, number)]


def exchange_once(by_grp, by_share):
    return [by_grp[0]] + [shift(by_grp[j], "grp", 2 * j) for j in range(1, len(by_grp))], [
        by_share[0]
    ] + [shift(by_share[n], "seq", n) for n in range(1, len(by_share))]


def reduce_once(by_grp, by_share, after=()):
    pairs, shares = len(by_grp), len(by_share)
    size = by_grp[0].shape[0] // shares
    results = call(
        functools.partial(sum_both, pairs, shares),
        [piece_shape(size)] * (pairs + shares),
        scratch=[pltpu.VMEM(by_grp[0].shape, BF16)],
        after=after,
    )(*by_grp, *by_share)
    return results[:shares], results[shares:]


def exchange_again(by_share, by_grp):
    pairs, shares = len(by_grp), len(by_share)
    return [by_share[0]] + [shift(by_share[n], "seq", n) for n in range(1, shares)], [
        by_grp[0]
    ] + [shift(by_grp[j], "grp", 2 * j) for j in range(1, pairs)]


def reduce_twice(by_share, by_grp, after=()):
    pairs, shares = len(by_grp), len(by_share)
    size = by_grp[0].shape[0]
    return call(
        functools.partial(sum_both_again, pairs, shares),
        [piece_shape(2 * size // CUTS)] * CUTS,
        scratch=[pltpu.VMEM((2, size, 16, 128), BF16)],
        after=after,
    )(*by_share, *by_grp)


def over_cuts(first, others=None):
    shares = lax.axis_size("seq") // CUTS
    sent = [first] * (CUTS - 1) if others is None else others
    return [first] + [shift(sent[m - 1], "seq", m * shares) for m in range(1, CUTS)]


def stacked(pieces):
    return call(stack, sds((CUTS,) + pieces[0].shape, BF16))(*pieces)


def over_shares(column):
    shares = lax.axis_size("seq") // CUTS
    return [column] + [shift(column, "seq", n) for n in range(1, shares)]


def butterfly(value, axis, bit, stop):
    while bit < stop:
        value = value + shift(value, axis, bit)
        bit *= 2
    return value


def lead_table():
    half = D // 2
    hours = 6.0 * np.exp2(np.arange(3, dtype=np.float32))
    freqs = np.exp(-np.log(np.float32(1000.0)) * np.arange(half, dtype=np.float32) / half)
    angles = hours[None, :] * freqs.astype(np.float32)[:, None]
    waves = np.concatenate([np.sin(angles), np.cos(angles)], axis=0)
    table = np.zeros((D, 128), np.float32)
    table[:, :3] = waves / (1.0 + np.exp(-waves))
    return jnp.asarray(table).astype(BF16)


def cosine_table(count):
    line = np.arange(count, dtype=np.float32)
    return jnp.asarray(np.cos(np.pi * ((line + 0.5) / count - 0.5)).astype(np.float32))


def per_device(
    fields,
    targets,
    land_mask,
    interval,
    samples,
    wide_weights,
    wide_firsts,
    wide_seconds,
    tall_weights,
    tall_firsts,
    tall_seconds,
    query_vector,
    query_firsts,
    query_seconds,
):
    group = lax.axis_size("grp")
    parts = lax.axis_size("seq")
    shares = parts // CUTS
    rows, columns = wide_weights.shape
    items, tokens = fields.shape[:2]
    units = items * HEADS // CUTS
    every = items * tokens
    late_cols = D + FF + OUTP + FF

    query_row = query_vector.reshape(1, rows)
    tall = [x.T for x in (tall_weights, tall_firsts, tall_seconds)]
    lead = lead_table()
    cosines = cosine_table(tokens // COLS * parts)
    fields = fields.transpose(0, 2, 1)
    targets = targets.transpose(0, 2, 1)
    mask = jnp.pad(
        land_mask.transpose(0, 2, 1), ((0, 0), (0, VARP - VARS), (0, 0)), constant_values=-1
    )

    def columns_of(index):
        return pl.BlockSpec((rows, 3 * D), lambda i: (0, index))

    first_own, second_own = call(
        pack_first,
        [sds((rows, 2 * D + OUTP), BF16), sds((rows + RIDERS, 4 * D), BF16)],
        grid=(1,),
        in_specs=[smem(), smem()]
        + [columns_of(i) for i in (0, 1, 2, 3, 0)]
        + [pl.BlockSpec((1, rows), lambda i: (0, 0)), whole(), whole()],
        out_specs=[whole()] * 2,
        scratch=[pltpu.VMEM((RIDERS, 4 * D), F32)],
        us=3,
        limit=62,
    )(samples, cosines, *[wide_weights] * 4, tall[0], query_row, lead, mask)
    first = gather_blocks(first_own, group)
    by_item = pl.BlockSpec((tokens, D), lambda i: (i, 0))

    def lane_block(height):
        return pl.BlockSpec((1, height, tokens), lambda i: (i, 0, 0))

    heads_spec = pl.BlockSpec((HEADS, 1, OUT, tokens), lambda i: (0, i, 0, 0))
    packed = units * (tokens + tokens // 2) + 16

    probs, picked, gathered, agg_weights, embed, fused_w, probe = call(
        functools.partial(aggregate, group),
        [
            in_hbm((items, HEADS * VARP, tokens), F32),
            in_hbm((HEADS, items, OUT, tokens), BF16),
            sds((every, D), BF16),
            in_hbm((D, 2 * D), BF16),
            in_hbm((D, OUTP), BF16),
            in_hbm((OUT, D), BF16),
            in_hbm((D, 128), BF16),
        ],
        grid=(items,),
        in_specs=[lane_block(OUT), lane_block(VARP)] + [whole()] * group,
        out_specs=[lane_block(HEADS * VARP), heads_spec, by_item] + [whole()] * 4,
        scratch=[
            pltpu.VMEM((HEADS * VARP, OUT), BF16),
            pltpu.VMEM((D, OUT), BF16),
            pltpu.VMEM((D, tokens), F32),
        ],
        us=10,
        limit=34,
    )(fields, mask, *first)
    second = gather_blocks(
        second_own,
        group,
        lambda blocks: {j: once_ready(block, (gathered,)) for j, block in blocks.items()},
    )
    late_own = call(
        pack_late,
        sds((rows, late_cols), BF16),
        grid=(1,),
        in_specs=[columns_of(4), columns_of(5), columns_of(6), whole()],
        out_specs=whole(),
        us=2,
        limit=62,
        after=(gathered,),
    )(wide_weights, wide_weights, wide_weights, tall[0])
    late_blocks = gather_blocks(late_own, group)

    results = call(
        functools.partial(project, group),
        [
            in_hbm((every, D), F32),
            in_hbm((every, D), BF16),
            in_hbm((D, 4 * D), BF16),
            in_hbm((8, 6 * D), F32),
        ]
        + [sds((packed, 128), BF16)] * CUTS,
        grid=(items,),
        in_specs=[smem(), by_item] + [whole()] * group,
        out_specs=[by_item, by_item] + [whole()] * (2 + CUTS),
        scratch=[pltpu.VMEM((items * HEADS, tokens + tokens // 2, 128), BF16)],
        us=4,
        limit=34,
        after=(late_own,),
    )(interval, gathered, *second)
    x0, n1, second_weights, mods = results[:4]
    dealt = results[4:]

    own = over_cuts(dealt[0], dealt[1:])
    keys_only = [x[: units * tokens + 16] for x in own]
    others = [shift(keys_only[m], "seq", n) for n in range(1, shares) for m in range(CUTS)]
    keys_total = parts * tokens

    half_in = pl.BlockSpec((1, tokens // 2, 128), lambda u: (u, 0, 0))
    kept_spec = pl.BlockSpec((1, CUTS, tokens, 128), lambda u: (u, 0, 0, 0))
    lse_spec = pl.BlockSpec((1, CUTS, 8, tokens), lambda u: (u, 0, 0, 0))
    pack_spec = pl.BlockSpec((1, CUTS, tokens // 2, 128), lambda u: (u, 0, 0, 0))
    half_out = sds((units, tokens // 2, 128), BF16)
    results = call(
        functools.partial(attend, shares),
        [half_out] * CUTS
        + [
            in_hbm((units, CUTS, tokens, 128), F32),
            in_hbm((units, CUTS, 8, tokens), F32),
            in_hbm((8, 128), F32),
        ],
        grid=(units,),
        in_specs=[whole()] * (CUTS * shares),
        out_specs=[half_in] * CUTS + [kept_spec, lse_spec, whole()],
        scratch=[pltpu.VMEM((keys_total, 128), BF16)],
        us=9,
        limit=60 if shares > 2 else 34,
    )(*own, *others)
    backs, (kept, lse, weight_sum) = results[:CUTS], results[CUTS:]
    heads_in = over_cuts(backs[0], backs[1:])

    saved = [D, D, D, FF, D, OUT, D, FF]
    results = call(
        functools.partial(middle, group),
        [in_hbm((every, D), F32), in_hbm((items, 8, D), F32), in_hbm((8, 128), F32)]
        + [half_out] * CUTS
        + [sds((every, width), BF16) for width in saved],
        grid=(items,),
        in_specs=[smem(), smem(), smem(), whole(), by_item, lane_block(OUT), lane_block(VARP)]
        + [whole()] * (CUTS + group + 1),
        out_specs=[by_item, pl.BlockSpec((1, 8, D), lambda i: (i, 0, 0))]
        + [whole()] * (1 + CUTS)
        + [pl.BlockSpec((tokens, width), lambda i: (i, 0)) for width in saved],
        scratch=[
            pltpu.VMEM((D, late_cols), BF16),
            pltpu.VMEM((items * HEADS, tokens // 2, 128), BF16),
            pltpu.VMEM((items * HEADS, tokens // 2, 128), BF16),
        ],
        us=11,
        limit=34,
    )(
        interval,
        samples,
        cosines,
        weight_sum,
        x0,
        targets,
        mask,
        *heads_in,
        *late_blocks,
        mods,
    )
    dx1, mod_rows, loss = results[:3]
    sends, operands = results[3 : 3 + CUTS], results[3 + CUTS :]
    early_keep, early_send = call(
        middle_weights,
        [sds((group // 2, rows, late_cols), BF16)] * 2,
        scratch=[pltpu.VMEM((D, late_cols), F32)],
        us=6,
        limit=34,
    )(*operands)
    grads_in = over_cuts(sends[0], sends[1:])

    def of_unit(u, *shape):
        return pl.BlockSpec((1,) + shape, lambda i: (u,) + (0,) * len(shape))

    def back_of(u, after):
        results = call(
            functools.partial(attend_back, shares, u),
            [sds((1, CUTS, tokens // 2, 128), BF16)]
            + [sds((1, CUTS, tokens, 128), BF16)] * shares,
            grid=(1,),
            in_specs=[whole()] * (CUTS * shares)
            + [of_unit(u, tokens // 2, 128)] * CUTS
            + [of_unit(u, CUTS, tokens, 128), of_unit(u, CUTS, 8, tokens)],
            out_specs=[whole()] * (1 + shares),
            scratch=[
                pltpu.VMEM((keys_total, 128), BF16),
                pltpu.VMEM((128, keys_total), BF16),
                pltpu.VMEM((keys_total, 128), F32),
            ],
            us=6,
            limit=60 if shares > 2 else 34,
            after=after,
        )(*own, *others, *grads_in, kept, lse)
        far = results[2:]
        if u == 2:
            far = [once_ready(far[0], units_in[0][1:]), *far[1:]]
        return results[:2], [shift(far[n], "seq", n + 1) for n in range(shares - 1)]

    def joined(near, far):
        dealt = call(
            functools.partial(join_back, shares),
            [sds((tokens + tokens // 2, 128), BF16)] * CUTS,
        )(*near, *far)
        return over_cuts(dealt[0], dealt[1:])

    early_got = shift(early_send, "grp", 1)
    partial_sums, units_in = [], []
    for u in range(units):
        after = (early_keep,) if u == 0 else (partial_sums[u - 1][0][0],)
        if u == 2:
            early_once = reduce_cores_once(early_keep, early_got, after=after)
            after += (early_once[0],)
        if u >= 2:
            units_in.append(joined(*partial_sums[u - 2]))
        partial_sums.append(back_of(u, after))
    units_in.append(joined(*partial_sums[-2]))
    units_in.append(joined(*partial_sums[-1]))
    early_twice = reduce_and_deal(early_once, False, after=(units_in[1][1],))

    second_cols = 4 * D + mod_tiles(rows) * 128
    dagg, second_keep, second_send = call(
        functools.partial(project_back, units),
        [
            sds((items, D, tokens), BF16),
            sds((group // 2, rows, second_cols), BF16),
            sds((group // 2, rows, second_cols), BF16),
        ],
        grid=(items,),
        in_specs=[
            smem(),
            by_item,
            by_item,
            by_item,
            pl.BlockSpec((1, 8, D), lambda i: (i, 0, 0)),
            by_item,
        ]
        + [whole()] * (2 + CUTS * units),
        out_specs=[pl.BlockSpec((1, D, tokens), lambda i: (i, 0, 0))] + [whole()] * 2,
        scratch=[
            pltpu.VMEM((items * HEADS, tokens + tokens // 2, 128), BF16),
            pltpu.VMEM((tokens, 3 * D), BF16),
            pltpu.VMEM((D, 4 * D), F32),
            pltpu.VMEM((8, 6 * D), F32),
            pltpu.VMEM((mod_tiles(rows) * rows, 128), F32),
        ],
        us=4,
        limit=34,
    )(
        interval,
        x0,
        n1,
        dx1,
        mod_rows,
        gathered,
        second_weights,
        mods,
        *[x for unit in units_in for x in unit],
    )
    second_got = shift(second_send, "grp", 1)
    early_pieces = reduce_and_deal(early_twice, True, after=(dagg,))
    late_keep, late_send = call(
        aggregate_back,
        [sds((group // 2, rows, 2 * D + OUTP), BF16)] * 2,
        grid=(items,),
        in_specs=[
            pl.BlockSpec((1, D, tokens), lambda i: (i, 0, 0)),
            lane_block(HEADS * VARP),
            heads_spec,
            lane_block(OUT),
            lane_block(VARP),
        ]
        + [whole()] * 4,
        out_specs=[whole()] * 2,
        scratch=[
            pltpu.VMEM((HEADS * VARP, tokens), BF16),
            pltpu.VMEM((D, 2 * D + OUTP), F32),
            pltpu.VMEM((OUT, D), F32),
            pltpu.VMEM((HEADS * VARP, OUT), F32),
        ],
        us=13,
        limit=34,
        after=(early_pieces[0],),
    )(dagg, probs, picked, fields, mask, fused_w, agg_weights, embed, probe)
    early_piece, early_squares = call(
        sum_pieces,
        [piece_shape(early_pieces[0].shape[0]), sds((16, 128), F32)],
        after=(late_keep,),
    )(*early_pieces)
    early_column = over_cuts(early_piece)
    late_first = reduce_cores(
        (late_keep, shift(once_ready(late_send, (early_piece,)), "grp", 1)),
        (second_keep, second_got),
    )
    late_second = reduce_once(*exchange_once(*late_first))
    early_column = stacked(early_column)
    late_second = [[once_ready(x, (early_column,)) for x in side] for side in late_second]
    late_twice = exchange_again(*late_second)
    early_all = over_shares(once_ready(early_column, (late_twice[0][1], late_twice[1][1])))
    late_third = reduce_twice(*late_twice)
    late_pieces = over_cuts(late_third[0], late_third[1:])
    start = (rows // 16) * 27
    stop = (rows // 16) * (27 + mod_tiles(rows))
    count = late_pieces[0].shape[0]
    late_piece = call(
        functools.partial(sum_late, start, stop), piece_shape(count + 1), after=early_all[1:]
    )(early_squares, loss, lead, *late_pieces)
    late_column, reduced = call(
        stack_late, [sds((CUTS, count, 16, 128), BF16), sds((8, 128), F32)]
    )(*over_cuts(late_piece))
    late_all = over_shares(late_column)
    reduced = butterfly(reduced, "grp", 1, group)
    reduced = butterfly(reduced, "seq", 1, shares)

    def like(x, dtype=F32):
        return sds(x.shape, dtype)

    results = call(
        functools.partial(optimize, shares),
        [sds((1, 1), F32)] * 3
        + [like(wide_weights)] * 3
        + [like(wide_weights, BF16)]
        + [like(tall[0])] * 3
        + [like(tall[0], BF16)]
        + [like(query_row)] * 3
        + [like(query_row, BF16)],
        out_specs=[whole()] * 3 + [pl.BlockSpec(memory_space=pl.ANY)] * 8 + [whole()] * 4,
        scratch=[
            pltpu.VMEM((parts * early_piece.shape[0], 16, 128), BF16),
            pltpu.VMEM((parts * count, 16, 128), BF16),
        ]
        + [pltpu.VMEM(wide_weights.shape, dtype) for dtype in (F32, F32, F32, BF16)]
        + [pltpu.VMEM(tall[0].shape, dtype) for dtype in (F32, F32, F32, BF16)]
        + [pltpu.SemaphoreType.DMA((24,))],
        us=10,
        limit=34,
    )(
        reduced,
        weight_sum,
        lead,
        *early_all,
        *late_all,
        wide_weights,
        wide_firsts,
        wide_seconds,
        *tall,
        query_row,
        query_firsts.reshape(1, rows),
        query_seconds.reshape(1, rows),
    )
    tall_out = tuple(r.T for r in results[7:11])
    query_out = tuple(r.reshape(rows) for r in results[11:15])
    return tuple(r.reshape(()) for r in results[:3]) + tuple(results[3:7]) + tall_out + query_out


def solution(mesh):
    placed = (
        P("grp", "seq", None),
        P("grp", "seq", None),
        P("grp", "seq", None),
        P("grp"),
        P("grp"),
        P("grp", None),
        P("grp", None),
        P("grp", None),
        P(None, "grp"),
        P(None, "grp"),
        P(None, "grp"),
        P("grp"),
        P("grp"),
        P("grp"),
    )
    return jax.shard_map(
        per_device,
        mesh=mesh,
        in_specs=placed,
        out_specs=(
            P(),
            P(),
            P(),
            P("grp", None),
            P("grp", None),
            P("grp", None),
            P("grp", None),
            P(None, "grp"),
            P(None, "grp"),
            P(None, "grp"),
            P(None, "grp"),
            P("grp"),
            P("grp"),
            P("grp"),
            P("grp"),
        ),
        check_vma=False,
    )
```

```python
import functools

import jax
import numpy as np
import jax.numpy as jnp
from jax import lax
from jax.experimental import pallas as pl
from jax.experimental.pallas import tpu as pltpu
from jax.sharding import PartitionSpec as P

D = 384
HEADS = 6
HEAD = 64
FF = 1536
VARS = 69
PIX = 16
OUT = VARS * PIX
OUTP = 1152
VARP = 80
COLS = 128
STEP = 5
CUTS = 4
SCALE = HEAD**-0.5
LOG2E = 1.4426950408889634

beta_first = 0.5
beta_second = 0.5
learn_rate = 0.1
decay_rate = 0.01
adam_epsilon = 1e-08
clip_limit = 0.05
norm_epsilon = 1e-06
masked_score = -1e30

F32 = jnp.float32
BF16 = jnp.bfloat16
MIB = 1024 * 1024
RIDERS = 32


def dot(left, right, a, b):
    return lax.dot_general(left, right, (((a,), (b,)), ((), ())), preferred_element_type=F32)


def nn(left, right):
    return dot(left, right, 1, 0)


def nt(left, right):
    return dot(left, right, 1, 1)


def tn(left, right):
    return dot(left, right, 0, 0)


def iota(shape, dim):
    return lax.broadcasted_iota(jnp.int32, shape, dim)


def half_low(shape):
    return iota(shape, len(shape) - 1) < HEAD


def swap_halves(tile):
    return pltpu.roll(tile, HEAD, 1)


def spread():
    return iota((VARP, OUT), 1) // PIX == iota((VARP, OUT), 0)


def ones_where(mask):
    return jnp.where(mask, 1.0, 0.0).astype(BF16)


def place():
    grp = lax.axis_index("grp")
    seq = lax.axis_index("seq")
    return grp, seq


def call(
    kernel, outs, grid=(), in_specs=None, out_specs=None, scratch=(), us=1, limit=34, after=()
):
    def run(*args):
        if after:
            args = (once_ready(args[0], after), *args[1:])
        kw = {} if out_specs is None else {"out_specs": out_specs}
        return pl.pallas_call(
            kernel,
            out_shape=outs,
            grid=grid,
            in_specs=list(in_specs) if in_specs else [whole()] * len(args),
            scratch_shapes=list(scratch),
            cost_estimate=pl.CostEstimate(
                flops=int(us * 1.15e9), transcendentals=0, bytes_accessed=1024
            ),
            compiler_params=pltpu.CompilerParams(vmem_limit_bytes=limit * MIB),
            **kw,
        )(*args)

    return run


def once_ready(value, after):
    return lax.optimization_barrier((value, *after))[0]


def whole():
    return pl.BlockSpec(memory_space=pltpu.VMEM)


def smem():
    return pl.BlockSpec(memory_space=pltpu.SMEM)


def sds(shape, dtype):
    return jax.ShapeDtypeStruct(shape, dtype)


def in_hbm(shape, dtype):
    return pltpu.HBM(shape, dtype)


def standardize(x):
    centered = x - jnp.mean(x, axis=-1, keepdims=True)
    rstd = lax.rsqrt(jnp.mean(centered * centered, axis=-1, keepdims=True) + norm_epsilon)
    return centered * rstd, rstd


def standardize_back(grad, normed, rstd):
    return rstd * (
        grad
        - jnp.mean(grad, axis=-1, keepdims=True)
        - normed * jnp.mean(grad * normed, axis=-1, keepdims=True)
    )


def gelu_parts(x):
    k = 0.7978845608028654
    inner = k * (x + 0.044715 * x * x * x)
    t = jnp.tanh(inner)
    value = 0.5 * x * (1.0 + t)
    slope = 0.5 * (1.0 + t) + 0.5 * x * (1.0 - t * t) * k * (1.0 + 3 * 0.044715 * x * x)
    return value, slope


def pack_first(agg_ref, tall_ref, query_ref, first_ref):
    rows = agg_ref.shape[0]
    first_ref[:, : 2 * D] = agg_ref[:, : 2 * D].astype(BF16)
    eye = iota((rows, rows), 0) == iota((rows, rows), 1)
    column = jnp.sum(jnp.where(eye, query_ref[...], 0.0), axis=1, keepdims=True)
    lane = iota((rows, OUTP), 1)
    embed = jnp.where(lane < OUT, tall_ref[...], jnp.where(lane == OUT, column, 0.0))
    first_ref[:, 2 * D :] = embed.astype(BF16)


def pack_second(*refs):
    samples, cosines, agg_ref, mod_a, mod_b, wide_ref, lead_ref, mask_ref = refs[:8]
    second_ref, rider_s = refs[8:]
    rows = wide_ref.shape[0]
    grp, seq = place()
    second_ref[:rows, :D] = agg_ref[:, 2 * D :].astype(BF16)
    low = half_low((rows, 128))
    for j in range(HEADS // 2):
        k = wide_ref[:, D + j * 128 : D + (j + 1) * 128]
        v = wide_ref[:, 2 * D + j * 128 : 2 * D + (j + 1) * 128]
        at = D + 2 * j * 128
        second_ref[:rows, at : at + 128] = jnp.where(low, k, swap_halves(v)).astype(BF16)
        second_ref[:rows, at + 128 : at + 256] = jnp.where(low, swap_halves(k), v).astype(BF16)
    second_ref[:rows, 3 * D :] = wide_ref[:, :D].astype(BF16)
    rider_s[...] = jnp.zeros_like(rider_s)

    def ride(row, value):
        for part in range(3):
            piece = value.astype(BF16).astype(F32)
            at = part * 8 + row
            rider_s[at : at + 1, : 3 * D] = piece
            value = value - piece

    lead = lead_ref[pl.ds(pl.multiple_of(grp * rows, 16), rows), :].astype(F32)
    for half, ref in ((0, mod_a), (1, mod_b)):
        mod = ref[...].astype(BF16).astype(F32)
        for g in range(3):
            ride(2 * g + half, jnp.sum(lead[:, g : g + 1] * mod, axis=0, keepdims=True))
    items, _, tokens = mask_ref.shape
    total = jnp.zeros((1, 1), F32)
    for i in range(items):
        present = jnp.maximum(mask_ref[i], 0).astype(F32)
        weighed = jnp.sum(present, axis=0, keepdims=True) * line_weights(
            samples[i], cosines, seq, iota((1, tokens), 1)
        )
        total = total + jnp.sum(weighed, axis=1, keepdims=True)
    ride(6, jnp.broadcast_to(total, (1, 3 * D)))
    second_ref[rows:, :] = rider_s[...].astype(BF16)


def line_weights(count, cosines, seq, position):
    lines = position.size // COLS
    value = jnp.zeros(position.shape, F32)
    for r in range(lines):
        value = jnp.where(position // COLS == r, cosines[seq * lines + r], value)
    return value * count.astype(F32)


def pack_late(wide_a, wide_b, wide_c, tall_ref, late_ref):
    rows = wide_a.shape[0]
    late_ref[:, : 3 * D] = wide_a[...].astype(BF16)
    late_ref[:, 3 * D : 6 * D] = wide_b[...].astype(BF16)
    rest = D + FF + OUT - 6 * D
    late_ref[:, 6 * D : D + FF + OUT] = wide_c[:, :rest].astype(BF16)
    late_ref[:, D + FF + OUT : D + FF + OUTP] = jnp.zeros((rows, OUTP - OUT), BF16)
    late_ref[:, D + FF + OUTP :] = tall_ref[:, OUT:].astype(BF16)


def assemble(target, blocks, grp, lo, hi):
    rows = target.shape[0] // len(blocks)
    for j, ref in enumerate(blocks):
        at = pl.multiple_of(jnp.bitwise_xor(grp, j) * rows, 16)
        target[pl.ds(at, rows), :] = ref[:rows, lo:hi]


def unride(target, blocks):
    target[...] = jnp.zeros_like(target)
    for g in range(4):
        for half in range(2):
            total = jnp.zeros((1, 3 * D), F32)
            for ref in blocks:
                for part in range(3):
                    at = ref.shape[0] - RIDERS + part * 8 + min(2 * g + half, 6)
                    total = total + ref[at : at + 1, : 3 * D].astype(F32)
            target[g : g + 1, half * 3 * D : (half + 1) * 3 * D] = total


def prepare(blocks, grp, outs, score_s, fused_s):
    (agg_ref, embed_ref, fused_ref, probe_ref) = outs
    assemble(agg_ref, blocks, grp, 0, 2 * D)
    assemble(embed_ref, blocks, grp, 2 * D, 2 * D + OUTP)
    query = embed_ref[:, OUT : OUT + 1].astype(F32)
    picked = jnp.where(iota((D, 128), 1) == iota((D, 128), 0) // HEAD, query, 0.0).astype(BF16)
    probe = nn(agg_ref[:, :D], picked).astype(BF16)
    probe_ref[...] = probe
    embed = embed_ref[:, :OUT]
    rows = tn(probe, embed) * SCALE
    mine = spread()
    for h in range(HEADS):
        score_s[h * VARP : (h + 1) * VARP, :] = jnp.where(mine, rows[h : h + 1, :], 0.0).astype(
            BF16
        )
    fused = tn(agg_ref[:, D:], embed)
    fused_s[...] = fused.astype(BF16)
    fused_ref[...] = fused.T.astype(BF16)


def aggregate(group, *refs):
    (fields_ref, mask_ref) = refs[:2]
    blocks, outs = refs[2 : 2 + group], refs[2 + group :]
    (probs_ref, picked_ref, gathered_ref), kept = outs[:3], outs[3:7]
    score_s, fused_s, turned_s = outs[7:]
    grp, _ = place()

    @pl.when(pl.program_id(0) == 0)
    def _():
        prepare(blocks, grp, kept, score_s, fused_s)

    fields = fields_ref[0]
    wide_fields = fields.astype(F32)
    mask = mask_ref[0]
    scores = nn(score_s[...], fields)
    expand = ones_where(iota((OUT, VARP), 0) // PIX == iota((OUT, VARP), 1))
    rounded = []
    for h in range(HEADS):
        s = jnp.where(
            mask > 0,
            scores[h * VARP : (h + 1) * VARP],
            jnp.where(mask < 0, -3e38, masked_score),
        )
        e = jnp.exp(s - jnp.max(s, axis=0, keepdims=True))
        a = e / jnp.sum(e, axis=0, keepdims=True)
        probs_ref[0, h * VARP : (h + 1) * VARP, :] = a
        rounded.append(a.astype(BF16))
    expanded = nn(expand, rounded[0])
    for h in range(HEADS):
        later = nn(expand, rounded[h + 1]) if h + 1 < HEADS else None
        picked = (expanded * wide_fields).astype(BF16)
        picked_ref[h, 0] = picked
        turned_s[h * HEAD : (h + 1) * HEAD, :] = nn(fused_s[h * HEAD : (h + 1) * HEAD, :], picked)
        expanded = later
    gathered_ref[...] = turned_s[...].T.astype(BF16)


def project(group, *refs):
    (interval, gathered_ref), blocks, outs = refs[:2], refs[2 : 2 + group], refs[2 + group :]
    (x0_ref, n1_ref, weights, mod_s), units, (unit_s,) = outs[:4], outs[4:-1], outs[-1:]
    item = pl.program_id(0)
    grp, seq = place()
    tokens = gathered_ref.shape[0]

    @pl.when(item == 0)
    def _():
        assemble(weights, blocks, grp, 0, 4 * D)
        unride(mod_s, blocks)

    x0 = nn(gathered_ref[...], weights[:, :D])
    x0_ref[...] = x0
    mod = mod_s[pl.ds(interval[item], 1), :]
    normed, _ = standardize(x0)
    n1 = (normed * (1.0 + mod[:, D : 2 * D]) + mod[:, :D]).astype(BF16)
    n1_ref[...] = n1
    qkv = nn(n1, weights[:, D:])
    half = tokens // 2
    low = half_low((half, 128))
    packed = tokens + half
    for h in range(HEADS):
        unit_s[HEADS * item + h, :tokens, :] = qkv[:, h * 128 : (h + 1) * 128].astype(BF16)
    for j in range(HEADS // 2):
        pair = qkv[:, 2 * D + j * 128 : 2 * D + (j + 1) * 128] * (SCALE * LOG2E)
        top, bottom = pair[:half], pair[half:]
        unit_s[HEADS * item + 2 * j, tokens:packed, :] = jnp.where(
            low, top, swap_halves(bottom)
        ).astype(BF16)
        unit_s[HEADS * item + 2 * j + 1, tokens:packed, :] = jnp.where(
            low, swap_halves(top), bottom
        ).astype(BF16)

    @pl.when(item == pl.num_programs(0) - 1)
    def _():
        value = jnp.broadcast_to(mod_s[3:4, :128], (16, 128))
        high = value.astype(BF16)
        value = value - high.astype(F32)
        middle_part = value.astype(BF16)
        low_part = (value - middle_part.astype(F32)).astype(BF16)
        lane = iota((16, 128), 1)
        rides = jnp.where(
            lane < 32,
            high.astype(F32),
            jnp.where(
                lane < 64,
                middle_part.astype(F32),
                jnp.where(lane < 96, low_part.astype(F32), 0.0),
            ),
        ).astype(BF16)
        a = seq // (lax.axis_size("seq") // CUTS)
        rounds = unit_s.shape[0] // CUTS
        queries = rounds * tokens + 16
        for m in range(CUTS):
            units[m][rounds * tokens : queries, :] = rides
            for r in range(rounds):
                unit = CUTS * r + jnp.bitwise_xor(a, m)
                units[m][r * tokens : (r + 1) * tokens, :] = unit_s[unit, :tokens, :]
                at = queries + r * half
                units[m][at : at + half, :] = unit_s[unit, tokens:packed, :]


def deal(targets, source, seq):
    a = seq // (lax.axis_size("seq") // CUTS)
    for m in range(CUTS):
        for r in range(targets[m].shape[0]):
            targets[m][r] = source[CUTS * r + jnp.bitwise_xor(a, m)]


def collect(target, sources, seq):
    a = seq // (lax.axis_size("seq") // CUTS)
    for m in range(CUTS):
        for r in range(sources[m].shape[0]):
            target[CUTS * r + jnp.bitwise_xor(a, m)] = sources[m][r]


def unpack(pack, at_low):
    wide = pack.astype(F32)
    low = half_low(wide.shape)
    if at_low:
        both = [jnp.where(low, wide, 0.0), jnp.where(low, swap_halves(wide), 0.0)]
    else:
        both = [jnp.where(low, 0.0, swap_halves(wide)), jnp.where(low, 0.0, wide)]
    return jnp.concatenate(both, axis=0).astype(BF16)


def pack_rows(tile, at_low):
    half = tile.shape[0] // 2
    top, bottom = tile[:half], tile[half:]
    low = half_low(top.shape)
    if at_low:
        return jnp.where(low, top, swap_halves(bottom))
    return jnp.where(low, swap_halves(top), bottom)


def attend(shares, *refs):
    own = refs[:CUTS]
    others = refs[CUTS : CUTS * shares]
    backs = refs[CUTS * shares : CUTS * shares + CUTS]
    kept_ref, lse_ref, weight_ref, keys_s = refs[CUTS * shares + CUTS :]
    tokens = kept_ref.shape[2]
    half = tokens // 2
    unit = pl.program_id(0)
    rows = own[0].shape[0] - 16
    rider = rows * tokens // (tokens + half)

    @pl.when(unit == 0)
    def _():
        total = jnp.zeros((16, 128), F32)
        for ref in own + others:
            total = total + ref[rider : rider + 16, :].astype(F32)
        total = jnp.sum(total[0:8], axis=1, keepdims=True) / 32.0
        weight_ref[...] = jnp.broadcast_to(total, (8, 128))

    for n, ref in enumerate(own + others):
        at = pl.ds(pl.multiple_of(unit * tokens, tokens), tokens)
        keys_s[n * tokens : (n + 1) * tokens, :] = ref[at, :]
    keys = keys_s[...]
    values = jnp.where(half_low(keys.shape), jnp.ones_like(keys), keys)

    def scores_of(m):
        at = pl.ds(pl.multiple_of(rider + 16 + unit * half, 16), half)
        return nt(unpack(own[m][at, :], True), keys)

    scores = scores_of(0)
    for m in range(CUTS):
        later = scores_of(m + 1) if m + 1 < CUTS else None
        top = jnp.max(scores, axis=1, keepdims=True)
        out = nn(jnp.exp2(scores - top).astype(BF16), values)
        total = out[:, 0:1]
        out = out / total
        lse = jnp.broadcast_to(top + jnp.log2(total), (tokens, 128)).T
        lse_ref[0, m] = lse[:8]
        kept_ref[0, m] = out
        backs[m][0] = pack_rows(out, False).astype(BF16)
        scores = later


def middle(group, *refs):
    (interval, samples, cosines, sum_ref, x0_ref, fields_ref, mask_ref) = refs[:7]
    heads_in = refs[7 : 7 + CUTS]
    blocks = refs[7 + CUTS : 7 + CUTS + group]
    mod_s = refs[7 + CUTS + group]
    outs = refs[7 + CUTS + group + 1 :]
    (dx1_ref, rows_ref, loss_ref) = outs[:3]
    sends = outs[3 : 3 + CUTS]
    attended_s, db1_ref, n2_ref, dh_ref, nf_ref, dpred_ref, db2_ref, active_ref = outs[
        3 + CUTS : 11 + CUTS
    ]
    weights, head_s, grad_s = outs[11 + CUTS :]
    item = pl.program_id(0)
    grp, seq = place()
    tokens = x0_ref.shape[0]
    half = tokens // 2

    @pl.when(item == 0)
    def _():
        assemble(weights, blocks, grp, 0, D + FF + OUTP + FF)
        collect(head_s, heads_in, seq)
        loss_ref[...] = jnp.zeros_like(loss_ref)

    low = half_low((half, 128))
    for j in range(HEADS // 2):
        one = head_s[HEADS * item + 2 * j].astype(F32)
        two = head_s[HEADS * item + 2 * j + 1].astype(F32)
        attended_s[:half, j * 128 : (j + 1) * 128] = jnp.where(low, one, swap_halves(two)).astype(
            BF16
        )
        attended_s[half:, j * 128 : (j + 1) * 128] = jnp.where(low, swap_halves(one), two).astype(
            BF16
        )
    out_w = slice(0, D)
    up_w = slice(D, D + FF)
    head_w = slice(D + FF, D + FF + OUT)
    down_w = slice(D + FF + OUTP, D + FF + OUTP + FF)
    mod = mod_s[pl.ds(interval[item], 1), :]
    gate_a, shift_b, scale_b, gate_b = [mod[:, k * D : (k + 1) * D] for k in range(2, 6)]
    attended = attended_s[...]
    branch_a = nn(attended, weights[:, out_w])
    x1 = x0_ref[...] + gate_a * branch_a
    normed_b, rstd_b = standardize(x1)
    n2 = (normed_b * (1.0 + scale_b) + shift_b).astype(BF16)
    n2_ref[...] = n2
    value, slope = gelu_parts(nn(n2, weights[:, up_w]))
    active = value.astype(BF16)
    active_ref[...] = active
    branch_b = nt(active, weights[:, down_w])
    x2 = x1 + gate_b * branch_b
    final, rstd_f = standardize(x2)
    nf = final.astype(BF16)
    nf_ref[...] = nf
    diff = nn(nf, weights[:, head_w]) - fields_ref[0].astype(F32).T
    present = tn(ones_where(mask_ref[0] > 0), ones_where(spread()))
    weight = line_weights(samples[item], cosines, seq, iota((tokens, 1), 0))
    weight_grad = weight * (2.0 / PIX) / sum_ref[0:1, 0:1]
    masked = present * diff
    each = jnp.sum(masked * diff, axis=1, keepdims=True) * weight
    loss_ref[...] += jnp.broadcast_to(jnp.sum(each, axis=0, keepdims=True) / PIX, (8, 128))
    dpred = (masked * weight_grad).astype(BF16)
    dpred_ref[...] = dpred

    dx2 = standardize_back(nt(dpred, weights[:, head_w]), final, rstd_f)
    db2 = (gate_b * dx2).astype(BF16)
    db2_ref[...] = db2
    d_gate_b = jnp.sum(dx2 * branch_b, axis=0, keepdims=True)
    dh = (nn(db2, weights[:, down_w]) * slope).astype(BF16)
    dh_ref[...] = dh
    dn2 = nt(dh, weights[:, up_w])
    d_shift_b = jnp.sum(dn2, axis=0, keepdims=True)
    d_scale_b = jnp.sum(dn2 * normed_b, axis=0, keepdims=True)
    dx1 = dx2 + standardize_back(dn2 * (1.0 + scale_b), normed_b, rstd_b)
    dx1_ref[...] = dx1
    d_gate_a = jnp.sum(dx1 * branch_a, axis=0, keepdims=True)
    db1 = (gate_a * dx1).astype(BF16)
    db1_ref[...] = db1
    dout = nt(db1, weights[:, out_w])
    rows_ref[0] = jnp.concatenate(
        [d_gate_a, d_shift_b, d_scale_b, d_gate_b, jnp.zeros((4, D), F32)], axis=0
    )
    for j in range(HEADS // 2):
        pair = dout[:, j * 128 : (j + 1) * 128]
        top, bottom = pair[:half], pair[half:]
        grad_s[HEADS * item + 2 * j] = jnp.where(low, top, swap_halves(bottom)).astype(BF16)
        grad_s[HEADS * item + 2 * j + 1] = jnp.where(low, swap_halves(top), bottom).astype(BF16)

    @pl.when(item == pl.num_programs(0) - 1)
    def _():
        deal(sends, grad_s, seq)


def middle_weights(*refs):
    attended, db1, n2, dh, nf, dpred, db2, active = refs[:8]
    keep_ref, send_ref, acc = refs[8:]
    grp, _ = place()
    acc[:, :D] = tn(attended[...], db1[...])
    acc[:, D : D + FF] = tn(n2[...], dh[...])
    acc[:, D + FF : D + FF + OUT] = tn(nf[...], dpred[...])
    acc[:, D + FF + OUT : D + FF + OUTP] = jnp.zeros((D, OUTP - OUT), F32)
    acc[:, D + FF + OUTP :] = tn(db2[...], active[...])
    split_rows(acc, grp, keep_ref, send_ref)


def split_rows(acc, grp, keep_ref, send_ref):
    rows = keep_ref.shape[1]
    for j in range(keep_ref.shape[0]):
        for odd, ref in ((0, keep_ref), (1, send_ref)):
            at = pl.multiple_of(jnp.bitwise_xor(grp, 2 * j + odd) * rows, 16)
            ref[j, :, : acc.shape[1]] = acc[pl.ds(at, rows), :].astype(BF16)


def attend_back(shares, unit, *refs):
    own = refs[:CUTS]
    others = refs[CUTS : CUTS * shares]
    grads = refs[CUTS * shares : CUTS * shares + CUTS]
    kept_ref, lse_ref = refs[CUTS * shares + CUTS : CUTS * shares + CUTS + 2]
    outs = refs[CUTS * shares + CUTS + 2 :]
    dq_ref, own_ref = outs[:2]
    far_refs = outs[2 : 2 + shares - 1]
    keys_s, turned_s, acc = outs[2 + shares - 1 :]
    tokens = kept_ref.shape[2]
    for n, ref in enumerate(own + others):
        keys_s[n * tokens : (n + 1) * tokens, :] = ref[unit * tokens : (unit + 1) * tokens, :]
    turned_s[...] = keys_s[...].T
    every = range(CUTS)
    half = tokens // 2
    at = (own[0].shape[0] - 16) * tokens // (tokens + half) + 16 + unit * half
    queries = jnp.concatenate(
        [unpack(own[m][at : at + half, :], True) for m in every], axis=0
    )
    grads = [unpack(grads[m][0], False) for m in every]
    delta = jnp.concatenate(
        [
            jnp.sum((grads[m].astype(F32) * kept_ref[0, m]).T, axis=0, keepdims=True)
            for m in every
        ],
        axis=1,
    )
    grads = jnp.concatenate(grads, axis=0)
    lse = jnp.concatenate([lse_ref[0, m, 0:1, :] for m in every], axis=1)
    chunk = 2 * tokens
    count = keys_s.shape[0] // chunk

    def products_of(c):
        keys = keys_s[c * chunk : (c + 1) * chunk, :]
        return nt(keys, queries), nt(keys, grads)

    products, dq = products_of(0), None
    for c in range(count):
        scores, dprobs = products
        if c + 1 < count:
            products = products_of(c + 1)
        probs = jnp.exp2(scores - lse)
        dscores = (probs * (dprobs - delta)).astype(BF16)
        acc[c * chunk : (c + 1) * chunk, :] = nn(probs.astype(BF16), grads) + nn(dscores, queries)
        part = nn(turned_s[:, c * chunk : (c + 1) * chunk], dscores)
        dq = part if dq is None else dq + part
    for m in every:
        turned = dq[:, m * tokens : (m + 1) * tokens].T * SCALE
        dq_ref[0, m] = pack_rows(turned, True).astype(BF16)
    factor = jnp.where(half_low((1, 128)), 1.0 / LOG2E, 1.0)
    for m in range(CUTS):
        own_ref[0, m] = (acc[m * tokens : (m + 1) * tokens, :] * factor).astype(BF16)
        for n, ref in enumerate(far_refs):
            at = ((n + 1) * CUTS + m) * tokens
            ref[0, m] = (acc[at : at + tokens, :] * factor).astype(BF16)


def join_back(shares, *refs):
    dq_ref, own_ref = refs[:2]
    far = refs[2 : 2 + shares - 1]
    outs = refs[2 + shares - 1 :]
    tokens = own_ref.shape[2]
    for m in range(CUTS):
        total = own_ref[0, m].astype(F32)
        for ref in far:
            total = total + ref[0, m].astype(F32)
        outs[m][:tokens, :] = total.astype(BF16)
        outs[m][tokens:, :] = dq_ref[0, m]


def project_back(rounds, *refs):
    (interval, x0_ref, n1_ref, dx1_ref, rows_ref, gathered_ref, weights, mod_s) = refs[:8]
    units, outs = refs[8 : 8 + CUTS * rounds], refs[8 + CUTS * rounds :]
    (dagg_ref, keep_ref, send_ref) = outs[:3]
    unit_s, dqkv_s, acc, dmod_ref, lines_s = outs[3:]
    item = pl.program_id(0)
    grp, seq = place()
    tokens = x0_ref.shape[0]
    half = tokens // 2

    @pl.when(item == 0)
    def _():
        a = seq // (lax.axis_size("seq") // CUTS)
        for r in range(rounds):
            for m in range(CUTS):
                unit_s[CUTS * r + jnp.bitwise_xor(a, m)] = units[CUTS * r + m][...]
        acc[...] = jnp.zeros_like(acc)
        dmod_ref[...] = jnp.zeros_like(dmod_ref)

    low = half_low((half, 128))
    for h in range(HEADS):
        dqkv_s[:, h * 128 : (h + 1) * 128] = unit_s[HEADS * item + h, :tokens, :]
    for j in range(HEADS // 2):
        one = unit_s[HEADS * item + 2 * j, tokens:, :].astype(F32)
        two = unit_s[HEADS * item + 2 * j + 1, tokens:, :].astype(F32)
        lanes = slice(2 * D + j * 128, 2 * D + (j + 1) * 128)
        dqkv_s[:half, lanes] = jnp.where(low, one, swap_halves(two)).astype(BF16)
        dqkv_s[half:, lanes] = jnp.where(low, swap_halves(one), two).astype(BF16)
    dqkv = dqkv_s[...]
    which = interval[item]
    mod = mod_s[pl.ds(which, 1), :]
    acc[:, D:] += tn(n1_ref[...], dqkv)
    dn1 = nt(dqkv, weights[:, D:])
    normed, rstd = standardize(x0_ref[...])
    d_shift = jnp.sum(dn1, axis=0, keepdims=True)
    d_scale = jnp.sum(dn1 * normed, axis=0, keepdims=True)
    dx0 = (
        dx1_ref[...] + standardize_back(dn1 * (1.0 + mod[:, D : 2 * D]), normed, rstd)
    ).astype(BF16)
    rows = rows_ref[0]
    for k, row in enumerate([d_shift, d_scale] + [rows[r : r + 1] for r in range(4)]):
        dmod_ref[pl.ds(which, 1), k * D : (k + 1) * D] += row

    acc[:, :D] += tn(gathered_ref[...], dx0)
    dagg_ref[0] = nt(weights[:, :D], dx0).astype(BF16)

    @pl.when(item == pl.num_programs(0) - 1)
    def _():
        split_rows(acc, grp, keep_ref, send_ref)
        lines_s[...] = jnp.zeros_like(lines_s)
        for t in range(6 * D // 128):
            lines_s[4 * t : 4 * t + 3, :] = dmod_ref[0:3, t * 128 : (t + 1) * 128]
        rows = keep_ref.shape[1]
        for t in range(mod_tiles(rows)):
            tile = lines_s[t * rows : (t + 1) * rows, :].astype(BF16)
            at = acc.shape[1] + t * 128
            for j in range(keep_ref.shape[0]):
                keep_ref[j, :, at : at + 128] = tile
                send_ref[j, :, at : at + 128] = tile


def aggregate_back(*refs):
    (dagg_ref, probs_ref, picked_ref, fields_ref, mask_ref) = refs[:5]
    (fused_ref, agg_ref, embed_ref, probe_ref) = refs[5:9]
    keep_ref, send_ref, ds_s, acc, mix, dscore = refs[9:]
    item = pl.program_id(0)
    grp, _ = place()
    tokens = dagg_ref.shape[2]

    @pl.when(item == 0)
    def _():
        mix[...] = jnp.zeros_like(mix)
        dscore[...] = jnp.zeros_like(dscore)

    dagg = dagg_ref[0].astype(F32)
    fields = fields_ref[0]
    wide_fields = fields.astype(F32)
    keep = mask_ref[0] > 0
    expand = ones_where(spread())
    upper = iota((128, tokens), 0) < HEAD
    dparts = []
    for h in range(HEADS):
        mine = upper if h % 2 == 0 else jnp.logical_not(upper)
        pair = slice(h // 2 * 128, (h // 2 + 1) * 128)
        dparts.append(jnp.where(mine, dagg[pair], 0.0).astype(BF16))

    def spread_out(h):
        return nn(fused_ref[:, h // 2 * 128 : (h // 2 + 1) * 128], dparts[h])

    spreaded = spread_out(0)
    for j in range(HEADS // 2):
        both = None
        for h in (2 * j, 2 * j + 1):
            later = spread_out(h + 1) if h + 1 < HEADS else None
            spreaded = (spreaded * wide_fields).astype(BF16)
            part = nt(picked_ref[h, 0], dparts[h])
            both = part if both is None else both + part
            dprobs = nn(expand, spreaded)
            probs = probs_ref[0, h * VARP : (h + 1) * VARP, :]
            ds = probs * (dprobs - jnp.sum(probs * dprobs, axis=0, keepdims=True))
            ds_s[h * VARP : (h + 1) * VARP, :] = jnp.where(keep, ds, 0.0).astype(BF16)
            spreaded = later
        mix[:, j * 128 : (j + 1) * 128] += both
    dscore[...] += nt(ds_s[...], fields)

    @pl.when(item == pl.num_programs(0) - 1)
    def _():
        lines = iota((128, OUT), 0)
        owned = spread()
        drows = jnp.zeros((128, OUT), F32)
        for h in range(HEADS):
            mine = dscore[h * VARP : (h + 1) * VARP, :]
            line = jnp.sum(jnp.where(owned, mine, 0.0), axis=0, keepdims=True) * SCALE
            drows = drows + jnp.where(lines == h, line, 0.0)
        drows = drows.astype(BF16)
        mixed = mix[...].astype(BF16)
        embed = embed_ref[:, :OUT]
        acc[:, 2 * D : 2 * D + OUT] = nt(agg_ref[:, D:], mixed) + nn(probe_ref[...], drows)
        acc[:, D : 2 * D] = nn(embed, mixed)
        dprobe = nt(embed, drows)
        heads = jnp.where(iota((128, D), 1) // HEAD == iota((128, D), 0), 1.0, 0.0).astype(BF16)
        coarse = dprobe.astype(BF16)
        fine = (dprobe - coarse.astype(F32)).astype(BF16)
        by_column = nn(coarse, heads) + nn(fine, heads)
        eye = iota((D, D), 0) == iota((D, D), 1)
        query = embed_ref[:, OUT : OUT + 1].astype(F32)
        query_row = jnp.sum(jnp.where(eye, query, 0.0), axis=0, keepdims=True)
        acc[:, :D] = by_column * query_row
        dquery = jnp.sum(agg_ref[:, :D].astype(F32) * by_column, axis=0, keepdims=True)
        column = jnp.sum(jnp.where(eye, dquery, 0.0), axis=1, keepdims=True)
        acc[:, 2 * D + OUT :] = jnp.where(iota((D, OUTP - OUT), 1) == 0, column, 0.0)
        split_rows(acc, grp, keep_ref, send_ref)


def mod_tiles(rows):
    return -(-4 * (6 * D // 128) // rows)


def shares_of():
    shares = lax.axis_size("seq") // CUTS
    _, seq = place()
    return shares, seq // shares, lax.rem(seq, shares)


def added(refs, at=None):
    total = None
    for ref in refs:
        value = (ref[...] if at is None else ref[at]).astype(F32)
        total = value if total is None else total + value
    return total


def sum_cores(pairs, sources, *refs):
    ins, outs, table = refs[: 2 * sources], refs[2 * sources : -1], refs[-1]
    shares, _, share = shares_of()
    first, second = outs[:pairs], outs[pairs:]
    half = table.shape[1] // 2
    size = half // shares
    per = ins[0].shape[1] // 16
    count = sum(ref.shape[2] for ref in ins[::2]) // 128 * per
    for j in range(pairs):
        at = 0
        for keep_ref, got_ref in zip(ins[::2], ins[1::2]):
            total = (keep_ref[j].astype(F32) + got_ref[j].astype(F32)).astype(BF16)
            for t in range(total.shape[1] // 128):
                for g in range(per):
                    table[j, at] = total[g * 16 : (g + 1) * 16, t * 128 : (t + 1) * 128]
                    at += 1
        for spare in range(count, 2 * half):
            table[j, spare] = jnp.zeros(table.shape[2:], BF16)
        first[j][...] = table[j, :half]
        for n in range(shares):
            at = half + jnp.bitwise_xor(share, n) * size
            second[n][j * size : (j + 1) * size] = table[j, pl.ds(at, size)]


def sum_cores_once(pairs, *refs):
    (keep_ref, got_ref), outs = refs[:2], refs[2:]
    per = keep_ref.shape[1] // 16
    count = keep_ref.shape[2] // 128 * per
    for j in range(pairs):
        total = (keep_ref[j].astype(F32) + got_ref[j].astype(F32)).astype(BF16)
        for t in range(keep_ref.shape[2] // 128):
            for g in range(per):
                outs[j][t * per + g] = total[g * 16 : (g + 1) * 16, t * 128 : (t + 1) * 128]
        for spare in range(count, outs[j].shape[0]):
            outs[j][spare] = jnp.zeros(outs[j].shape[1:], BF16)


def sum_and_deal(over_cuts, *refs):
    outs, table = refs[-1 - (CUTS if over_cuts else shares_of()[0]) : -1], refs[-1]
    _, cut, share = shares_of()
    table[...] = added(refs[: -1 - len(outs)]).astype(BF16)
    size = outs[0].shape[0]
    for n, ref in enumerate(outs):
        ref[...] = table[pl.ds(jnp.bitwise_xor(cut if over_cuts else share, n) * size, size)]


def sum_both(pairs, shares, *refs):
    by_grp, by_share = refs[:pairs], refs[pairs : pairs + shares]
    outs, (table,) = refs[pairs + shares : -1], refs[-1:]
    _, _, share = shares_of()
    table[...] = added(by_grp).astype(BF16)
    size = outs[0].shape[0]
    for n in range(shares):
        outs[n][...] = table[pl.ds(jnp.bitwise_xor(share, n) * size, size)]
    for j in range(pairs):
        at = slice(j * size, (j + 1) * size)
        outs[shares + j][...] = added(by_share, at).astype(BF16)


def sum_both_again(pairs, shares, *refs):
    by_share, by_grp = refs[:shares], refs[shares : shares + pairs]
    outs, (table,) = refs[pairs + shares : -1], refs[-1:]
    _, cut, _ = shares_of()
    size = outs[0].shape[0] // 2
    table[0] = added(by_share).astype(BF16)
    table[1] = added(by_grp).astype(BF16)
    for m in range(CUTS):
        at = pl.ds(jnp.bitwise_xor(cut, m) * size, size)
        outs[m][:size] = table[0, at]
        outs[m][size:] = table[1, at]


def sum_pieces(*refs):
    sources, (out_ref, square_ref) = refs[:-2], refs[-2:]
    total = added(sources)
    out_ref[...] = total.astype(BF16)
    square_ref[...] = jnp.sum(total * total, axis=0)


def sum_late(start, stop, *refs):
    early_ref, loss_ref, lead_ref = refs[:3]
    sources, out_ref = refs[3:-1], refs[-1]
    grp, _ = place()
    shares, cut, share = shares_of()
    rows = lead_ref.shape[0] // lax.axis_size("grp")
    lead = lead_ref[pl.ds(pl.multiple_of(grp * rows, 16), rows), :].astype(F32)
    cols = [lead[:, g : g + 1] for g in range(3)]

    def gram(f, g):
        return jnp.sum(cols[f] * cols[g], axis=0, keepdims=True)

    row = lax.rem(iota((16, 1), 0), 4)

    def pick(*values):
        out = jnp.zeros((16, 1), F32)
        for r, value in values:
            out = jnp.where(row == r, value, out)
        return out

    same = pick(*[(g, gram(g, g)) for g in range(3)])
    next_one = pick((1, 2 * gram(0, 1)), (2, 2 * gram(1, 2)))
    next_two = pick((2, 2 * gram(0, 2)))
    size = (out_ref.shape[0] - 1) // 2
    plain = jnp.zeros((16, 128), F32)
    for half in range(2):
        for k in range(size):
            total = added(sources, half * size + k)
            out_ref[half * size + k] = total.astype(BF16)
            index = ((half * shares + share) * CUTS + cut) * size + k
            special = jnp.logical_and(index >= start, index < stop)
            square = total * total
            mixed = (
                square * same
                + total * pltpu.roll(total, 1, 0) * next_one
                + total * pltpu.roll(total, 2, 0) * next_two
            )
            plain = plain + jnp.where(special, mixed, square)
    squares = jnp.sum(jnp.sum(plain + early_ref[...], axis=0, keepdims=True), axis=1, keepdims=True)
    rider = jnp.zeros((16, 128), F32)
    for at, value in ((0, loss_ref[0:1, :]), (3, jnp.broadcast_to(squares, (1, 128)))):
        for part in range(3):
            piece = value.astype(BF16).astype(F32)
            rider = jnp.where(iota((16, 128), 0) == at + part, piece, rider)
            value = value - piece
    out_ref[2 * size] = rider.astype(BF16)


def stack_late(*refs):
    pieces, (column_ref, reduced_ref) = refs[:-2], refs[-2:]
    count = column_ref.shape[1]
    rider = jnp.zeros((16, 128), F32)
    for m, ref in enumerate(pieces):
        column_ref[m] = ref[:count]
        rider = rider + ref[count].astype(F32)
    reduced_ref[...] = jnp.concatenate(
        [rider[0:1] + rider[1:2] + rider[2:3], rider[3:4] + rider[4:5] + rider[5:6]]
        + [jnp.zeros((6, 128), F32)],
        axis=0,
    )


def stack(*refs):
    for m, ref in enumerate(refs[:-1]):
        refs[-1][m] = ref[...]


def step_values(param, first, second, grad):
    first = beta_first * first + (1.0 - beta_first) * grad
    second = beta_second * second + (1.0 - beta_second) * grad * grad
    mean_hat = first * (1.0 / (1.0 - beta_first**STEP))
    var_hat = second * (1.0 / (1.0 - beta_second**STEP))
    param = param - learn_rate * (
        mean_hat / (jnp.sqrt(var_hat) + adam_epsilon) + decay_rate * param
    )
    return param, first, second, param.astype(BF16)


def optimize(shares, *refs):
    reduced_ref, sum_ref, lead_ref = refs[:3]
    early = refs[3 : 3 + shares]
    late = refs[3 + shares : 3 + 2 * shares]
    wide = refs[3 + 2 * shares : 6 + 2 * shares]
    tall = refs[6 + 2 * shares : 9 + 2 * shares]
    query = refs[9 + 2 * shares : 12 + 2 * shares]
    outs = refs[12 + 2 * shares :]
    scalars, wide_hbm, tall_hbm, query_out = outs[:3], outs[3:7], outs[7:11], outs[11:15]
    early_s, late_s, wide_out, tall_out, sems = outs[15], outs[16], outs[17:21], outs[21:25], outs[25]
    grp, _ = place()
    _, cut, share = shares_of()
    for table, stacks, halves in ((early_s, early, 1), (late_s, late, 2)):
        size = stacks[0].shape[1] // halves
        for n, ref in enumerate(stacks):
            for m in range(CUTS):
                for half in range(halves):
                    at = (half * shares + jnp.bitwise_xor(share, n)) * CUTS
                    at = (at + jnp.bitwise_xor(cut, m)) * size
                    table[pl.ds(at, size)] = ref[m, half * size : (half + 1) * size]
    norm = jnp.sqrt(reduced_ref[1:2, 0:1])
    for ref, value in zip(scalars, (reduced_ref[0:1, 0:1], sum_ref[0:1, 0:1], norm)):
        ref[...] = value
    factor = jnp.minimum(1.0, clip_limit / (norm + 1e-06))
    rows = wide[0].shape[0]
    per = rows // 16

    def tile(table, t):
        return jnp.concatenate([table[t * per + g] for g in range(per)], axis=0).astype(F32)

    def put(ins, targets, at, grad):
        new = step_values(*[r[at] for r in ins], grad * factor)
        for ref, value in zip(targets, new):
            ref[at] = value

    def at(t, width=128):
        return (slice(None), slice(t * 128, t * 128 + width))

    copies = []

    def flush(sources, targets, lo, hi):
        for source, target in zip(sources, targets):
            copy = pltpu.make_async_copy(
                source.at[:, lo:hi], target.at[:, lo:hi], sems.at[len(copies)]
            )
            copy.start()
            copies.append(copy)

    low = half_low((rows, 128))
    for t in range(6):
        put(wide, wide_out, at(t), tile(late_s, t))
    for t in range(3):
        put(wide, wide_out, at(6 + t), tile(late_s, 15 + t))
    flush(wide_out, wide_hbm, 0, 3 * D)
    lead = lead_ref[pl.ds(pl.multiple_of(grp * rows, 16), rows), :].astype(F32)
    lines = jnp.concatenate([tile(late_s, 27 + t) for t in range(mod_tiles(rows))], axis=0)
    for t in range(18):
        grad = lead[:, 0:1] * lines[4 * t : 4 * t + 1]
        for g in (1, 2):
            grad = grad + lead[:, g : g + 1] * lines[4 * t + g : 4 * t + g + 1]
        put(wide, wide_out, at(9 + t), grad)
    flush(wide_out, wide_hbm, 3 * D, 9 * D)
    qkv = 18
    for j in range(3):
        put(wide, wide_out, at(27 + j), tile(late_s, qkv + 6 + j))
        one, two = tile(late_s, qkv + 2 * j), tile(late_s, qkv + 2 * j + 1)
        put(wide, wide_out, at(30 + j), jnp.where(low, one, swap_halves(two)))
        put(wide, wide_out, at(33 + j), jnp.where(low, swap_halves(one), two))
    flush(wide_out, wide_hbm, 9 * D, 12 * D)
    for t in range(15 + 8):
        put(wide, wide_out, at(36 + t), tile(early_s, t))
    rest = OUT - 8 * 128
    put(wide, wide_out, at(59, rest), tile(early_s, 23)[:, :rest])
    flush(wide_out, wide_hbm, 12 * D, wide[0].shape[1])
    for t in range(8):
        put(tall, tall_out, at(t), tile(late_s, 6 + t))
    flush(tall_out, tall_hbm, 0, 8 * 128)
    last = tile(late_s, 14)
    lane = iota((rows, 128), 1)
    for t in range(FF // 128):
        turned = pltpu.roll(tile(early_s, 24 + t), rest, 1)
        put(tall, tall_out, at(8 + t), jnp.where(lane < rest, last, turned))
        if t == 0:
            eye = iota((rows, rows), 0) == iota((rows, rows), 1)
            grad = jnp.sum(jnp.where(eye, last[:, rest : rest + 1], 0.0), axis=0, keepdims=True)
            put(query, query_out, (slice(None), slice(None)), grad)
        last = turned
    put(tall, tall_out, at(8 + FF // 128, rest), last[:, :rest])
    flush(tall_out, tall_hbm, 8 * 128, tall[0].shape[1])
    for copy in copies:
        copy.wait()


def shift(value, axis, bit):
    size = lax.axis_size(axis)
    return lax.ppermute(value, axis, [(i, i ^ bit) for i in range(size)])


def gather_blocks(own, group, behind=None):
    blocks = {0: own}
    for j in range(2, group, 2):
        blocks[j] = shift(own, "grp", j)
    if behind is not None:
        blocks = behind(blocks)
    for j in range(0, group, 2):
        blocks[j + 1] = shift(blocks[j], "grp", 1)
    return [blocks[j] for j in range(group)]


def granules(rows, cols, shares):
    unit = 2 * shares * CUTS
    return -(-(rows // 16) * (cols // 128) // unit) * unit


def piece_shape(count):
    return sds((count, 16, 128), BF16)


def reduce_cores(*sources, after=()):
    pairs, rows, _ = sources[0][0].shape
    shares = lax.axis_size("seq") // CUTS
    count = granules(rows, sum(keep.shape[2] for keep, _ in sources), shares)
    results = call(
        functools.partial(sum_cores, pairs, len(sources)),
        [piece_shape(count // 2)] * pairs + [piece_shape(count // 2 // shares * pairs)] * shares,
        scratch=[pltpu.VMEM((pairs, count, 16, 128), BF16)],
        after=after,
    )(*[x for source in sources for x in source])
    return results[:pairs], results[pairs:]


def reduce_cores_once(keep, got, after=()):
    pairs, rows, cols = keep.shape
    parts = lax.axis_size("seq")
    count = -(-(rows // 16) * (cols // 128) // parts) * parts
    halves = call(
        functools.partial(sum_cores_once, pairs), [piece_shape(count)] * pairs, after=after
    )(keep, got)
    return [halves[0]] + [shift(halves[j], "grp", 2 * j) for j in range(1, pairs)]


def reduce_and_deal(pieces, over, after=()):
    count = pieces[0].shape[0]
    number = CUTS if over else lax.axis_size("seq") // CUTS
    outs = call(
        functools.partial(sum_and_deal, over),
        [piece_shape(count // number)] * number,
        scratch=[pltpu.VMEM((count, 16, 128), BF16)],
        after=after,
    )(*pieces)
    if over:
        return over_cuts(outs[0], outs[1:])
    return [outs[0]] + [shift(outs[n], "seq", n) for n in range(1, number)]


def exchange_once(by_grp, by_share):
    return [by_grp[0]] + [shift(by_grp[j], "grp", 2 * j) for j in range(1, len(by_grp))], [
        by_share[0]
    ] + [shift(by_share[n], "seq", n) for n in range(1, len(by_share))]


def reduce_once(by_grp, by_share, after=()):
    pairs, shares = len(by_grp), len(by_share)
    size = by_grp[0].shape[0] // shares
    results = call(
        functools.partial(sum_both, pairs, shares),
        [piece_shape(size)] * (pairs + shares),
        scratch=[pltpu.VMEM(by_grp[0].shape, BF16)],
        after=after,
    )(*by_grp, *by_share)
    return results[:shares], results[shares:]


def exchange_again(by_share, by_grp):
    pairs, shares = len(by_grp), len(by_share)
    return [by_share[0]] + [shift(by_share[n], "seq", n) for n in range(1, shares)], [
        by_grp[0]
    ] + [shift(by_grp[j], "grp", 2 * j) for j in range(1, pairs)]


def reduce_twice(by_share, by_grp, after=()):
    pairs, shares = len(by_grp), len(by_share)
    size = by_grp[0].shape[0]
    return call(
        functools.partial(sum_both_again, pairs, shares),
        [piece_shape(2 * size // CUTS)] * CUTS,
        scratch=[pltpu.VMEM((2, size, 16, 128), BF16)],
        after=after,
    )(*by_share, *by_grp)


def over_cuts(first, others=None):
    shares = lax.axis_size("seq") // CUTS
    sent = [first] * (CUTS - 1) if others is None else others
    return [first] + [shift(sent[m - 1], "seq", m * shares) for m in range(1, CUTS)]


def stacked(pieces):
    return call(stack, sds((CUTS,) + pieces[0].shape, BF16))(*pieces)


def over_shares(column):
    shares = lax.axis_size("seq") // CUTS
    return [column] + [shift(column, "seq", n) for n in range(1, shares)]


def butterfly(value, axis, bit, stop):
    while bit < stop:
        value = value + shift(value, axis, bit)
        bit *= 2
    return value


def lead_table():
    half = D // 2
    hours = 6.0 * np.exp2(np.arange(3, dtype=np.float32))
    freqs = np.exp(-np.log(np.float32(1000.0)) * np.arange(half, dtype=np.float32) / half)
    angles = hours[None, :] * freqs.astype(np.float32)[:, None]
    waves = np.concatenate([np.sin(angles), np.cos(angles)], axis=0)
    table = np.zeros((D, 128), np.float32)
    table[:, :3] = waves / (1.0 + np.exp(-waves))
    return jnp.asarray(table).astype(BF16)


def cosine_table(count):
    line = np.arange(count, dtype=np.float32)
    return jnp.asarray(np.cos(np.pi * ((line + 0.5) / count - 0.5)).astype(np.float32))


def per_device(
    fields,
    targets,
    land_mask,
    interval,
    samples,
    wide_weights,
    wide_firsts,
    wide_seconds,
    tall_weights,
    tall_firsts,
    tall_seconds,
    query_vector,
    query_firsts,
    query_seconds,
):
    group = lax.axis_size("grp")
    parts = lax.axis_size("seq")
    shares = parts // CUTS
    rows, columns = wide_weights.shape
    items, tokens = fields.shape[:2]
    units = items * HEADS // CUTS
    every = items * tokens
    late_cols = D + FF + OUTP + FF

    query_row = query_vector.reshape(1, rows)
    tall = [x.T for x in (tall_weights, tall_firsts, tall_seconds)]
    lead = lead_table()
    cosines = cosine_table(tokens // COLS * parts)
    fields = fields.transpose(0, 2, 1)
    targets = targets.transpose(0, 2, 1)
    mask = jnp.pad(
        land_mask.transpose(0, 2, 1), ((0, 0), (0, VARP - VARS), (0, 0)), constant_values=-1
    )

    def columns_of(index):
        return pl.BlockSpec((rows, 3 * D), lambda i: (0, index))

    first_own = call(
        pack_first,
        sds((rows, 2 * D + OUTP), BF16),
        grid=(1,),
        in_specs=[columns_of(0), columns_of(0), pl.BlockSpec((1, rows), lambda i: (0, 0))],
        out_specs=whole(),
        us=2,
        limit=62,
    )(wide_weights, tall[0], query_row)
    second_own = call(
        pack_second,
        sds((rows + RIDERS, 4 * D), BF16),
        grid=(1,),
        in_specs=[smem(), smem()] + [columns_of(i) for i in range(4)] + [whole(), whole()],
        out_specs=whole(),
        scratch=[pltpu.VMEM((RIDERS, 4 * D), F32)],
        us=3,
        limit=62,
        after=(first_own,),
    )(samples, cosines, *[wide_weights] * 4, lead, mask)
    first = gather_blocks(
        first_own,
        group,
        lambda blocks: {j: once_ready(block, (second_own,)) for j, block in blocks.items()},
    )

    by_item = pl.BlockSpec((tokens, D), lambda i: (i, 0))

    def lane_block(height):
        return pl.BlockSpec((1, height, tokens), lambda i: (i, 0, 0))

    heads_spec = pl.BlockSpec((HEADS, 1, OUT, tokens), lambda i: (0, i, 0, 0))
    packed = units * (tokens + tokens // 2) + 16

    probs, picked, gathered, agg_weights, embed, fused_w, probe = call(
        functools.partial(aggregate, group),
        [
            in_hbm((items, HEADS * VARP, tokens), F32),
            in_hbm((HEADS, items, OUT, tokens), BF16),
            sds((every, D), BF16),
            in_hbm((D, 2 * D), BF16),
            in_hbm((D, OUTP), BF16),
            in_hbm((OUT, D), BF16),
            in_hbm((D, 128), BF16),
        ],
        grid=(items,),
        in_specs=[lane_block(OUT), lane_block(VARP)] + [whole()] * group,
        out_specs=[lane_block(HEADS * VARP), heads_spec, by_item] + [whole()] * 4,
        scratch=[
            pltpu.VMEM((HEADS * VARP, OUT), BF16),
            pltpu.VMEM((D, OUT), BF16),
            pltpu.VMEM((D, tokens), F32),
        ],
        us=10,
        limit=34,
    )(fields, mask, *first)
    second = gather_blocks(
        second_own,
        group,
        lambda blocks: {j: once_ready(block, (gathered,)) for j, block in blocks.items()},
    )
    late_own = call(
        pack_late,
        sds((rows, late_cols), BF16),
        grid=(1,),
        in_specs=[columns_of(4), columns_of(5), columns_of(6), whole()],
        out_specs=whole(),
        us=2,
        limit=62,
        after=(gathered,),
    )(wide_weights, wide_weights, wide_weights, tall[0])
    late_blocks = gather_blocks(late_own, group)

    results = call(
        functools.partial(project, group),
        [
            in_hbm((every, D), F32),
            in_hbm((every, D), BF16),
            in_hbm((D, 4 * D), BF16),
            in_hbm((8, 6 * D), F32),
        ]
        + [sds((packed, 128), BF16)] * CUTS,
        grid=(items,),
        in_specs=[smem(), by_item] + [whole()] * group,
        out_specs=[by_item, by_item] + [whole()] * (2 + CUTS),
        scratch=[pltpu.VMEM((items * HEADS, tokens + tokens // 2, 128), BF16)],
        us=4,
        limit=34,
        after=(late_own,),
    )(interval, gathered, *second)
    x0, n1, second_weights, mods = results[:4]
    dealt = results[4:]

    own = over_cuts(dealt[0], dealt[1:])
    keys_only = [x[: units * tokens + 16] for x in own]
    others = [shift(keys_only[m], "seq", n) for n in range(1, shares) for m in range(CUTS)]
    keys_total = parts * tokens

    half_in = pl.BlockSpec((1, tokens // 2, 128), lambda u: (u, 0, 0))
    kept_spec = pl.BlockSpec((1, CUTS, tokens, 128), lambda u: (u, 0, 0, 0))
    lse_spec = pl.BlockSpec((1, CUTS, 8, tokens), lambda u: (u, 0, 0, 0))
    pack_spec = pl.BlockSpec((1, CUTS, tokens // 2, 128), lambda u: (u, 0, 0, 0))
    half_out = sds((units, tokens // 2, 128), BF16)
    results = call(
        functools.partial(attend, shares),
        [half_out] * CUTS
        + [
            in_hbm((units, CUTS, tokens, 128), F32),
            in_hbm((units, CUTS, 8, tokens), F32),
            in_hbm((8, 128), F32),
        ],
        grid=(units,),
        in_specs=[whole()] * (CUTS * shares),
        out_specs=[half_in] * CUTS + [kept_spec, lse_spec, whole()],
        scratch=[pltpu.VMEM((keys_total, 128), BF16)],
        us=9,
        limit=60 if shares > 2 else 34,
    )(*own, *others)
    backs, (kept, lse, weight_sum) = results[:CUTS], results[CUTS:]
    heads_in = over_cuts(backs[0], backs[1:])

    saved = [D, D, D, FF, D, OUT, D, FF]
    results = call(
        functools.partial(middle, group),
        [in_hbm((every, D), F32), in_hbm((items, 8, D), F32), in_hbm((8, 128), F32)]
        + [half_out] * CUTS
        + [sds((every, width), BF16) for width in saved],
        grid=(items,),
        in_specs=[smem(), smem(), smem(), whole(), by_item, lane_block(OUT), lane_block(VARP)]
        + [whole()] * (CUTS + group + 1),
        out_specs=[by_item, pl.BlockSpec((1, 8, D), lambda i: (i, 0, 0))]
        + [whole()] * (1 + CUTS)
        + [pl.BlockSpec((tokens, width), lambda i: (i, 0)) for width in saved],
        scratch=[
            pltpu.VMEM((D, late_cols), BF16),
            pltpu.VMEM((items * HEADS, tokens // 2, 128), BF16),
            pltpu.VMEM((items * HEADS, tokens // 2, 128), BF16),
        ],
        us=11,
        limit=34,
    )(
        interval,
        samples,
        cosines,
        weight_sum,
        x0,
        targets,
        mask,
        *heads_in,
        *late_blocks,
        mods,
    )
    dx1, mod_rows, loss = results[:3]
    sends, operands = results[3 : 3 + CUTS], results[3 + CUTS :]
    early_keep, early_send = call(
        middle_weights,
        [sds((group // 2, rows, late_cols), BF16)] * 2,
        scratch=[pltpu.VMEM((D, late_cols), F32)],
        us=6,
        limit=34,
    )(*operands)
    grads_in = over_cuts(sends[0], sends[1:])

    def of_unit(u, *shape):
        return pl.BlockSpec((1,) + shape, lambda i: (u,) + (0,) * len(shape))

    def back_of(u, after):
        results = call(
            functools.partial(attend_back, shares, u),
            [sds((1, CUTS, tokens // 2, 128), BF16)]
            + [sds((1, CUTS, tokens, 128), BF16)] * shares,
            grid=(1,),
            in_specs=[whole()] * (CUTS * shares)
            + [of_unit(u, tokens // 2, 128)] * CUTS
            + [of_unit(u, CUTS, tokens, 128), of_unit(u, CUTS, 8, tokens)],
            out_specs=[whole()] * (1 + shares),
            scratch=[
                pltpu.VMEM((keys_total, 128), BF16),
                pltpu.VMEM((128, keys_total), BF16),
                pltpu.VMEM((keys_total, 128), F32),
            ],
            us=6,
            limit=60 if shares > 2 else 34,
            after=after,
        )(*own, *others, *grads_in, kept, lse)
        far = results[2:]
        if u == 2:
            far = [once_ready(far[0], units_in[0][1:]), *far[1:]]
        return results[:2], [shift(far[n], "seq", n + 1) for n in range(shares - 1)]

    def joined(near, far):
        dealt = call(
            functools.partial(join_back, shares),
            [sds((tokens + tokens // 2, 128), BF16)] * CUTS,
        )(*near, *far)
        return over_cuts(dealt[0], dealt[1:])

    early_once = reduce_cores_once(early_keep, shift(early_send, "grp", 1))
    partial_sums, units_in = [], []
    for u in range(units):
        after = (early_once[0],) if u == 0 else (partial_sums[u - 1][0][0],)
        if u >= 2:
            units_in.append(joined(*partial_sums[u - 2]))
        partial_sums.append(back_of(u, after))
    units_in.append(joined(*partial_sums[-2]))
    units_in.append(joined(*partial_sums[-1]))
    early_twice = reduce_and_deal(early_once, False, after=(units_in[1][1],))

    second_cols = 4 * D + mod_tiles(rows) * 128
    dagg, second_keep, second_send = call(
        functools.partial(project_back, units),
        [
            sds((items, D, tokens), BF16),
            sds((group // 2, rows, second_cols), BF16),
            sds((group // 2, rows, second_cols), BF16),
        ],
        grid=(items,),
        in_specs=[
            smem(),
            by_item,
            by_item,
            by_item,
            pl.BlockSpec((1, 8, D), lambda i: (i, 0, 0)),
            by_item,
        ]
        + [whole()] * (2 + CUTS * units),
        out_specs=[pl.BlockSpec((1, D, tokens), lambda i: (i, 0, 0))] + [whole()] * 2,
        scratch=[
            pltpu.VMEM((items * HEADS, tokens + tokens // 2, 128), BF16),
            pltpu.VMEM((tokens, 3 * D), BF16),
            pltpu.VMEM((D, 4 * D), F32),
            pltpu.VMEM((8, 6 * D), F32),
            pltpu.VMEM((mod_tiles(rows) * rows, 128), F32),
        ],
        us=4,
        limit=34,
    )(
        interval,
        x0,
        n1,
        dx1,
        mod_rows,
        gathered,
        second_weights,
        mods,
        *[x for unit in units_in for x in unit],
    )
    second_got = shift(second_send, "grp", 1)
    early_pieces = reduce_and_deal(early_twice, True, after=(dagg,))
    late_keep, late_send = call(
        aggregate_back,
        [sds((group // 2, rows, 2 * D + OUTP), BF16)] * 2,
        grid=(items,),
        in_specs=[
            pl.BlockSpec((1, D, tokens), lambda i: (i, 0, 0)),
            lane_block(HEADS * VARP),
            heads_spec,
            lane_block(OUT),
            lane_block(VARP),
        ]
        + [whole()] * 4,
        out_specs=[whole()] * 2,
        scratch=[
            pltpu.VMEM((HEADS * VARP, tokens), BF16),
            pltpu.VMEM((D, 2 * D + OUTP), F32),
            pltpu.VMEM((OUT, D), F32),
            pltpu.VMEM((HEADS * VARP, OUT), F32),
        ],
        us=13,
        limit=34,
        after=(early_pieces[0],),
    )(dagg, probs, picked, fields, mask, fused_w, agg_weights, embed, probe)
    early_piece, early_squares = call(
        sum_pieces,
        [piece_shape(early_pieces[0].shape[0]), sds((16, 128), F32)],
        after=(late_keep,),
    )(*early_pieces)
    early_column = over_cuts(early_piece)
    late_first = reduce_cores(
        (late_keep, shift(once_ready(late_send, (early_piece,)), "grp", 1)),
        (second_keep, second_got),
    )
    late_second = reduce_once(*exchange_once(*late_first))
    early_column = stacked(early_column)
    late_second = [[once_ready(x, (early_column,)) for x in side] for side in late_second]
    late_twice = exchange_again(*late_second)
    early_all = over_shares(once_ready(early_column, (late_twice[0][1], late_twice[1][1])))
    late_third = reduce_twice(*late_twice)
    late_pieces = over_cuts(late_third[0], late_third[1:])
    start = (rows // 16) * 27
    stop = (rows // 16) * (27 + mod_tiles(rows))
    count = late_pieces[0].shape[0]
    late_piece = call(
        functools.partial(sum_late, start, stop), piece_shape(count + 1), after=early_all[1:]
    )(early_squares, loss, lead, *late_pieces)
    late_column, reduced = call(
        stack_late, [sds((CUTS, count, 16, 128), BF16), sds((8, 128), F32)]
    )(*over_cuts(late_piece))
    late_all = over_shares(late_column)
    reduced = butterfly(reduced, "grp", 1, group)
    reduced = butterfly(reduced, "seq", 1, shares)

    def like(x, dtype=F32):
        return sds(x.shape, dtype)

    results = call(
        functools.partial(optimize, shares),
        [sds((1, 1), F32)] * 3
        + [like(wide_weights)] * 3
        + [like(wide_weights, BF16)]
        + [like(tall[0])] * 3
        + [like(tall[0], BF16)]
        + [like(query_row)] * 3
        + [like(query_row, BF16)],
        out_specs=[whole()] * 3 + [pl.BlockSpec(memory_space=pl.ANY)] * 8 + [whole()] * 4,
        scratch=[
            pltpu.VMEM((parts * early_piece.shape[0], 16, 128), BF16),
            pltpu.VMEM((parts * count, 16, 128), BF16),
        ]
        + [pltpu.VMEM(wide_weights.shape, dtype) for dtype in (F32, F32, F32, BF16)]
        + [pltpu.VMEM(tall[0].shape, dtype) for dtype in (F32, F32, F32, BF16)]
        + [pltpu.SemaphoreType.DMA((24,))],
        us=10,
        limit=34,
    )(
        reduced,
        weight_sum,
        lead,
        *early_all,
        *late_all,
        wide_weights,
        wide_firsts,
        wide_seconds,
        *tall,
        query_row,
        query_firsts.reshape(1, rows),
        query_seconds.reshape(1, rows),
    )
    tall_out = tuple(r.T for r in results[7:11])
    query_out = tuple(r.reshape(rows) for r in results[11:15])
    return tuple(r.reshape(()) for r in results[:3]) + tuple(results[3:7]) + tall_out + query_out


def solution(mesh):
    placed = (
        P("grp", "seq", None),
        P("grp", "seq", None),
        P("grp", "seq", None),
        P("grp"),
        P("grp"),
        P("grp", None),
        P("grp", None),
        P("grp", None),
        P(None, "grp"),
        P(None, "grp"),
        P(None, "grp"),
        P("grp"),
        P("grp"),
        P("grp"),
    )
    return jax.shard_map(
        per_device,
        mesh=mesh,
        in_specs=placed,
        out_specs=(
            P(),
            P(),
            P(),
            P("grp", None),
            P("grp", None),
            P("grp", None),
            P("grp", None),
            P(None, "grp"),
            P(None, "grp"),
            P(None, "grp"),
            P(None, "grp"),
            P("grp"),
            P("grp"),
            P("grp"),
            P("grp"),
        ),
        check_vma=False,
    )
```

```python
import functools

import jax
import numpy as np
import jax.numpy as jnp
from jax import lax
from jax.experimental import pallas as pl
from jax.experimental.pallas import tpu as pltpu
from jax.sharding import PartitionSpec as P

D = 384
HEADS = 6
HEAD = 64
FF = 1536
VARS = 69
PIX = 16
OUT = VARS * PIX
OUTP = 1152
VARP = 80
COLS = 128
STEP = 5
CUTS = 4
SCALE = HEAD**-0.5
LOG2E = 1.4426950408889634

beta_first = 0.5
beta_second = 0.5
learn_rate = 0.1
decay_rate = 0.01
adam_epsilon = 1e-08
clip_limit = 0.05
norm_epsilon = 1e-06
masked_score = -1e30

F32 = jnp.float32
BF16 = jnp.bfloat16
MIB = 1024 * 1024
RIDERS = 32


def dot(left, right, a, b):
    return lax.dot_general(left, right, (((a,), (b,)), ((), ())), preferred_element_type=F32)


def nn(left, right):
    return dot(left, right, 1, 0)


def nt(left, right):
    return dot(left, right, 1, 1)


def tn(left, right):
    return dot(left, right, 0, 0)


def iota(shape, dim):
    return lax.broadcasted_iota(jnp.int32, shape, dim)


def half_low(shape):
    return iota(shape, len(shape) - 1) < HEAD


def swap_halves(tile):
    return pltpu.roll(tile, HEAD, 1)


def spread():
    return iota((VARP, OUT), 1) // PIX == iota((VARP, OUT), 0)


def ones_where(mask):
    return jnp.where(mask, 1.0, 0.0).astype(BF16)


def place():
    grp = lax.axis_index("grp")
    seq = lax.axis_index("seq")
    return grp, seq


def call(
    kernel, outs, grid=(), in_specs=None, out_specs=None, scratch=(), us=1, limit=34, after=()
):
    def run(*args):
        if after:
            args = (once_ready(args[0], after), *args[1:])
        kw = {} if out_specs is None else {"out_specs": out_specs}
        return pl.pallas_call(
            kernel,
            out_shape=outs,
            grid=grid,
            in_specs=list(in_specs) if in_specs else [whole()] * len(args),
            scratch_shapes=list(scratch),
            cost_estimate=pl.CostEstimate(
                flops=int(us * 1.15e9), transcendentals=0, bytes_accessed=1024
            ),
            compiler_params=pltpu.CompilerParams(vmem_limit_bytes=limit * MIB),
            **kw,
        )(*args)

    return run


def once_ready(value, after):
    return lax.optimization_barrier((value, *after))[0]


def whole():
    return pl.BlockSpec(memory_space=pltpu.VMEM)


def smem():
    return pl.BlockSpec(memory_space=pltpu.SMEM)


def sds(shape, dtype):
    return jax.ShapeDtypeStruct(shape, dtype)


def in_hbm(shape, dtype):
    return pltpu.HBM(shape, dtype)


def standardize(x):
    centered = x - jnp.mean(x, axis=-1, keepdims=True)
    rstd = lax.rsqrt(jnp.mean(centered * centered, axis=-1, keepdims=True) + norm_epsilon)
    return centered * rstd, rstd


def standardize_back(grad, normed, rstd):
    return rstd * (
        grad
        - jnp.mean(grad, axis=-1, keepdims=True)
        - normed * jnp.mean(grad * normed, axis=-1, keepdims=True)
    )


def gelu_parts(x):
    k = 0.7978845608028654
    inner = k * (x + 0.044715 * x * x * x)
    t = jnp.tanh(inner)
    value = 0.5 * x * (1.0 + t)
    slope = 0.5 * (1.0 + t) + 0.5 * x * (1.0 - t * t) * k * (1.0 + 3 * 0.044715 * x * x)
    return value, slope


def pack_first(agg_ref, tall_ref, query_ref, first_ref):
    rows = agg_ref.shape[0]
    first_ref[:, : 2 * D] = agg_ref[:, : 2 * D].astype(BF16)
    eye = iota((rows, rows), 0) == iota((rows, rows), 1)
    column = jnp.sum(jnp.where(eye, query_ref[...], 0.0), axis=1, keepdims=True)
    lane = iota((rows, OUTP), 1)
    embed = jnp.where(lane < OUT, tall_ref[...], jnp.where(lane == OUT, column, 0.0))
    first_ref[:, 2 * D :] = embed.astype(BF16)


def pack_second(*refs):
    samples, cosines, agg_ref, mod_a, mod_b, wide_ref, lead_ref, mask_ref = refs[:8]
    second_ref, rider_s = refs[8:]
    rows = wide_ref.shape[0]
    grp, seq = place()
    second_ref[:rows, :D] = agg_ref[:, 2 * D :].astype(BF16)
    low = half_low((rows, 128))
    for j in range(HEADS // 2):
        k = wide_ref[:, D + j * 128 : D + (j + 1) * 128]
        v = wide_ref[:, 2 * D + j * 128 : 2 * D + (j + 1) * 128]
        at = D + 2 * j * 128
        second_ref[:rows, at : at + 128] = jnp.where(low, k, swap_halves(v)).astype(BF16)
        second_ref[:rows, at + 128 : at + 256] = jnp.where(low, swap_halves(k), v).astype(BF16)
    second_ref[:rows, 3 * D :] = wide_ref[:, :D].astype(BF16)
    rider_s[...] = jnp.zeros_like(rider_s)

    def ride(row, value):
        for part in range(3):
            piece = value.astype(BF16).astype(F32)
            at = part * 8 + row
            rider_s[at : at + 1, : 3 * D] = piece
            value = value - piece

    lead = lead_ref[pl.ds(pl.multiple_of(grp * rows, 16), rows), :].astype(F32)
    for half, ref in ((0, mod_a), (1, mod_b)):
        mod = ref[...].astype(BF16).astype(F32)
        for g in range(3):
            ride(2 * g + half, jnp.sum(lead[:, g : g + 1] * mod, axis=0, keepdims=True))
    items, _, tokens = mask_ref.shape
    total = jnp.zeros((1, 1), F32)
    for i in range(items):
        present = jnp.maximum(mask_ref[i], 0).astype(F32)
        weighed = jnp.sum(present, axis=0, keepdims=True) * line_weights(
            samples[i], cosines, seq, iota((1, tokens), 1)
        )
        total = total + jnp.sum(weighed, axis=1, keepdims=True)
    ride(6, jnp.broadcast_to(total, (1, 3 * D)))
    second_ref[rows:, :] = rider_s[...].astype(BF16)


def line_weights(count, cosines, seq, position):
    lines = position.size // COLS
    value = jnp.zeros(position.shape, F32)
    for r in range(lines):
        value = jnp.where(position // COLS == r, cosines[seq * lines + r], value)
    return value * count.astype(F32)


def pack_late(wide_a, wide_b, wide_c, tall_ref, late_ref):
    rows = wide_a.shape[0]
    late_ref[:, : 3 * D] = wide_a[...].astype(BF16)
    late_ref[:, 3 * D : 6 * D] = wide_b[...].astype(BF16)
    rest = D + FF + OUT - 6 * D
    late_ref[:, 6 * D : D + FF + OUT] = wide_c[:, :rest].astype(BF16)
    late_ref[:, D + FF + OUT : D + FF + OUTP] = jnp.zeros((rows, OUTP - OUT), BF16)
    late_ref[:, D + FF + OUTP :] = tall_ref[:, OUT:].astype(BF16)


def assemble(target, blocks, grp, lo, hi):
    rows = target.shape[0] // len(blocks)
    for j, ref in enumerate(blocks):
        at = pl.multiple_of(jnp.bitwise_xor(grp, j) * rows, 16)
        target[pl.ds(at, rows), :] = ref[:rows, lo:hi]


def unride(target, blocks):
    target[...] = jnp.zeros_like(target)
    for g in range(4):
        for half in range(2):
            total = jnp.zeros((1, 3 * D), F32)
            for ref in blocks:
                for part in range(3):
                    at = ref.shape[0] - RIDERS + part * 8 + min(2 * g + half, 6)
                    total = total + ref[at : at + 1, : 3 * D].astype(F32)
            target[g : g + 1, half * 3 * D : (half + 1) * 3 * D] = total


def prepare(blocks, grp, outs, score_s, fused_s):
    (agg_ref, embed_ref, fused_ref, probe_ref) = outs
    assemble(agg_ref, blocks, grp, 0, 2 * D)
    assemble(embed_ref, blocks, grp, 2 * D, 2 * D + OUTP)
    query = embed_ref[:, OUT : OUT + 1].astype(F32)
    picked = jnp.where(iota((D, 128), 1) == iota((D, 128), 0) // HEAD, query, 0.0).astype(BF16)
    probe = nn(agg_ref[:, :D], picked).astype(BF16)
    probe_ref[...] = probe
    embed = embed_ref[:, :OUT]
    rows = tn(probe, embed) * SCALE
    mine = spread()
    for h in range(HEADS):
        score_s[h * VARP : (h + 1) * VARP, :] = jnp.where(mine, rows[h : h + 1, :], 0.0).astype(
            BF16
        )
    fused = tn(agg_ref[:, D:], embed)
    fused_s[...] = fused.astype(BF16)
    fused_ref[...] = fused.T.astype(BF16)


def aggregate(group, *refs):
    (fields_ref, mask_ref) = refs[:2]
    blocks, outs = refs[2 : 2 + group], refs[2 + group :]
    (probs_ref, picked_ref, gathered_ref), kept = outs[:3], outs[3:7]
    score_s, fused_s, turned_s = outs[7:]
    grp, _ = place()

    @pl.when(pl.program_id(0) == 0)
    def _():
        prepare(blocks, grp, kept, score_s, fused_s)

    fields = fields_ref[0]
    wide_fields = fields.astype(F32)
    mask = mask_ref[0]
    scores = nn(score_s[...], fields)
    expand = ones_where(iota((OUT, VARP), 0) // PIX == iota((OUT, VARP), 1))
    rounded = []
    for h in range(HEADS):
        s = jnp.where(
            mask > 0,
            scores[h * VARP : (h + 1) * VARP],
            jnp.where(mask < 0, -3e38, masked_score),
        )
        e = jnp.exp(s - jnp.max(s, axis=0, keepdims=True))
        a = e / jnp.sum(e, axis=0, keepdims=True)
        probs_ref[0, h * VARP : (h + 1) * VARP, :] = a
        rounded.append(a.astype(BF16))
    expanded = nn(expand, rounded[0])
    for h in range(HEADS):
        later = nn(expand, rounded[h + 1]) if h + 1 < HEADS else None
        picked = (expanded * wide_fields).astype(BF16)
        picked_ref[h, 0] = picked
        turned_s[h * HEAD : (h + 1) * HEAD, :] = nn(fused_s[h * HEAD : (h + 1) * HEAD, :], picked)
        expanded = later
    gathered_ref[...] = turned_s[...].T.astype(BF16)


def project(group, *refs):
    (interval, gathered_ref), blocks, outs = refs[:2], refs[2 : 2 + group], refs[2 + group :]
    (x0_ref, n1_ref, weights, mod_s), units, (unit_s,) = outs[:4], outs[4:-1], outs[-1:]
    item = pl.program_id(0)
    grp, seq = place()
    tokens = gathered_ref.shape[0]

    @pl.when(item == 0)
    def _():
        assemble(weights, blocks, grp, 0, 4 * D)
        unride(mod_s, blocks)

    x0 = nn(gathered_ref[...], weights[:, :D])
    x0_ref[...] = x0
    mod = mod_s[pl.ds(interval[item], 1), :]
    normed, _ = standardize(x0)
    n1 = (normed * (1.0 + mod[:, D : 2 * D]) + mod[:, :D]).astype(BF16)
    n1_ref[...] = n1
    qkv = nn(n1, weights[:, D:])
    half = tokens // 2
    low = half_low((half, 128))
    packed = tokens + half
    for h in range(HEADS):
        unit_s[HEADS * item + h, :tokens, :] = qkv[:, h * 128 : (h + 1) * 128].astype(BF16)
    for j in range(HEADS // 2):
        pair = qkv[:, 2 * D + j * 128 : 2 * D + (j + 1) * 128] * (SCALE * LOG2E)
        top, bottom = pair[:half], pair[half:]
        unit_s[HEADS * item + 2 * j, tokens:packed, :] = jnp.where(
            low, top, swap_halves(bottom)
        ).astype(BF16)
        unit_s[HEADS * item + 2 * j + 1, tokens:packed, :] = jnp.where(
            low, swap_halves(top), bottom
        ).astype(BF16)

    @pl.when(item == pl.num_programs(0) - 1)
    def _():
        value = jnp.broadcast_to(mod_s[3:4, :128], (16, 128))
        high = value.astype(BF16)
        value = value - high.astype(F32)
        middle_part = value.astype(BF16)
        low_part = (value - middle_part.astype(F32)).astype(BF16)
        lane = iota((16, 128), 1)
        rides = jnp.where(
            lane < 32,
            high.astype(F32),
            jnp.where(
                lane < 64,
                middle_part.astype(F32),
                jnp.where(lane < 96, low_part.astype(F32), 0.0),
            ),
        ).astype(BF16)
        a = seq // (lax.axis_size("seq") // CUTS)
        rounds = unit_s.shape[0] // CUTS
        queries = rounds * tokens + 16
        for m in range(CUTS):
            units[m][rounds * tokens : queries, :] = rides
            for r in range(rounds):
                unit = CUTS * r + jnp.bitwise_xor(a, m)
                units[m][r * tokens : (r + 1) * tokens, :] = unit_s[unit, :tokens, :]
                at = queries + r * half
                units[m][at : at + half, :] = unit_s[unit, tokens:packed, :]


def deal(targets, source, seq):
    a = seq // (lax.axis_size("seq") // CUTS)
    for m in range(CUTS):
        for r in range(targets[m].shape[0]):
            targets[m][r] = source[CUTS * r + jnp.bitwise_xor(a, m)]


def collect(target, sources, seq):
    a = seq // (lax.axis_size("seq") // CUTS)
    for m in range(CUTS):
        for r in range(sources[m].shape[0]):
            target[CUTS * r + jnp.bitwise_xor(a, m)] = sources[m][r]


def unpack(pack, at_low):
    wide = pack.astype(F32)
    low = half_low(wide.shape)
    if at_low:
        both = [jnp.where(low, wide, 0.0), jnp.where(low, swap_halves(wide), 0.0)]
    else:
        both = [jnp.where(low, 0.0, swap_halves(wide)), jnp.where(low, 0.0, wide)]
    return jnp.concatenate(both, axis=0).astype(BF16)


def pack_rows(tile, at_low):
    half = tile.shape[0] // 2
    top, bottom = tile[:half], tile[half:]
    low = half_low(top.shape)
    if at_low:
        return jnp.where(low, top, swap_halves(bottom))
    return jnp.where(low, swap_halves(top), bottom)


def attend(shares, *refs):
    own = refs[:CUTS]
    others = refs[CUTS : CUTS * shares]
    backs = refs[CUTS * shares : CUTS * shares + CUTS]
    kept_ref, lse_ref, weight_ref, keys_s = refs[CUTS * shares + CUTS :]
    tokens = kept_ref.shape[2]
    half = tokens // 2
    unit = pl.program_id(0)
    rows = own[0].shape[0] - 16
    rider = rows * tokens // (tokens + half)

    @pl.when(unit == 0)
    def _():
        total = jnp.zeros((16, 128), F32)
        for ref in own + others:
            total = total + ref[rider : rider + 16, :].astype(F32)
        total = jnp.sum(total[0:8], axis=1, keepdims=True) / 32.0
        weight_ref[...] = jnp.broadcast_to(total, (8, 128))

    for n, ref in enumerate(own + others):
        at = pl.ds(pl.multiple_of(unit * tokens, tokens), tokens)
        keys_s[n * tokens : (n + 1) * tokens, :] = ref[at, :]
    keys = keys_s[...]
    values = jnp.where(half_low(keys.shape), jnp.ones_like(keys), keys)

    def scores_of(m):
        at = pl.ds(pl.multiple_of(rider + 16 + unit * half, 16), half)
        return nt(unpack(own[m][at, :], True), keys)

    scores = scores_of(0)
    for m in range(CUTS):
        later = scores_of(m + 1) if m + 1 < CUTS else None
        top = jnp.max(scores, axis=1, keepdims=True)
        out = nn(jnp.exp2(scores - top).astype(BF16), values)
        total = out[:, 0:1]
        out = out / total
        lse = jnp.broadcast_to(top + jnp.log2(total), (tokens, 128)).T
        lse_ref[0, m] = lse[:8]
        kept_ref[0, m] = out
        backs[m][0] = pack_rows(out, False).astype(BF16)
        scores = later


def middle(group, *refs):
    (interval, samples, cosines, sum_ref, x0_ref, fields_ref, mask_ref) = refs[:7]
    heads_in = refs[7 : 7 + CUTS]
    blocks = refs[7 + CUTS : 7 + CUTS + group]
    mod_s = refs[7 + CUTS + group]
    outs = refs[7 + CUTS + group + 1 :]
    (dx1_ref, rows_ref, loss_ref) = outs[:3]
    sends = outs[3 : 3 + CUTS]
    attended_s, db1_ref, n2_ref, dh_ref, nf_ref, dpred_ref, db2_ref, active_ref = outs[
        3 + CUTS : 11 + CUTS
    ]
    weights, head_s, grad_s = outs[11 + CUTS :]
    item = pl.program_id(0)
    grp, seq = place()
    tokens = x0_ref.shape[0]
    half = tokens // 2

    @pl.when(item == 0)
    def _():
        assemble(weights, blocks, grp, 0, D + FF + OUTP + FF)
        collect(head_s, heads_in, seq)
        loss_ref[...] = jnp.zeros_like(loss_ref)

    low = half_low((half, 128))
    for j in range(HEADS // 2):
        one = head_s[HEADS * item + 2 * j].astype(F32)
        two = head_s[HEADS * item + 2 * j + 1].astype(F32)
        attended_s[:half, j * 128 : (j + 1) * 128] = jnp.where(low, one, swap_halves(two)).astype(
            BF16
        )
        attended_s[half:, j * 128 : (j + 1) * 128] = jnp.where(low, swap_halves(one), two).astype(
            BF16
        )
    out_w = slice(0, D)
    up_w = slice(D, D + FF)
    head_w = slice(D + FF, D + FF + OUT)
    down_w = slice(D + FF + OUTP, D + FF + OUTP + FF)
    mod = mod_s[pl.ds(interval[item], 1), :]
    gate_a, shift_b, scale_b, gate_b = [mod[:, k * D : (k + 1) * D] for k in range(2, 6)]
    attended = attended_s[...]
    branch_a = nn(attended, weights[:, out_w])
    x1 = x0_ref[...] + gate_a * branch_a
    normed_b, rstd_b = standardize(x1)
    n2 = (normed_b * (1.0 + scale_b) + shift_b).astype(BF16)
    n2_ref[...] = n2
    value, slope = gelu_parts(nn(n2, weights[:, up_w]))
    active = value.astype(BF16)
    active_ref[...] = active
    branch_b = nt(active, weights[:, down_w])
    x2 = x1 + gate_b * branch_b
    final, rstd_f = standardize(x2)
    nf = final.astype(BF16)
    nf_ref[...] = nf
    diff = nn(nf, weights[:, head_w]) - fields_ref[0].astype(F32).T
    present = tn(ones_where(mask_ref[0] > 0), ones_where(spread()))
    weight = line_weights(samples[item], cosines, seq, iota((tokens, 1), 0))
    weight_grad = weight * (2.0 / PIX) / sum_ref[0:1, 0:1]
    masked = present * diff
    each = jnp.sum(masked * diff, axis=1, keepdims=True) * weight
    loss_ref[...] += jnp.broadcast_to(jnp.sum(each, axis=0, keepdims=True) / PIX, (8, 128))
    dpred = (masked * weight_grad).astype(BF16)
    dpred_ref[...] = dpred

    dx2 = standardize_back(nt(dpred, weights[:, head_w]), final, rstd_f)
    db2 = (gate_b * dx2).astype(BF16)
    db2_ref[...] = db2
    d_gate_b = jnp.sum(dx2 * branch_b, axis=0, keepdims=True)
    dh = (nn(db2, weights[:, down_w]) * slope).astype(BF16)
    dh_ref[...] = dh
    dn2 = nt(dh, weights[:, up_w])
    d_shift_b = jnp.sum(dn2, axis=0, keepdims=True)
    d_scale_b = jnp.sum(dn2 * normed_b, axis=0, keepdims=True)
    dx1 = dx2 + standardize_back(dn2 * (1.0 + scale_b), normed_b, rstd_b)
    dx1_ref[...] = dx1
    d_gate_a = jnp.sum(dx1 * branch_a, axis=0, keepdims=True)
    db1 = (gate_a * dx1).astype(BF16)
    db1_ref[...] = db1
    dout = nt(db1, weights[:, out_w])
    rows_ref[0] = jnp.concatenate(
        [d_gate_a, d_shift_b, d_scale_b, d_gate_b, jnp.zeros((4, D), F32)], axis=0
    )
    for j in range(HEADS // 2):
        pair = dout[:, j * 128 : (j + 1) * 128]
        top, bottom = pair[:half], pair[half:]
        grad_s[HEADS * item + 2 * j] = jnp.where(low, top, swap_halves(bottom)).astype(BF16)
        grad_s[HEADS * item + 2 * j + 1] = jnp.where(low, swap_halves(top), bottom).astype(BF16)

    @pl.when(item == pl.num_programs(0) - 1)
    def _():
        deal(sends, grad_s, seq)


def middle_weights(*refs):
    attended, db1, n2, dh, nf, dpred, db2, active = refs[:8]
    keep_ref, send_ref, acc = refs[8:]
    grp, _ = place()
    acc[:, :D] = tn(attended[...], db1[...])
    acc[:, D : D + FF] = tn(n2[...], dh[...])
    acc[:, D + FF : D + FF + OUT] = tn(nf[...], dpred[...])
    acc[:, D + FF + OUT : D + FF + OUTP] = jnp.zeros((D, OUTP - OUT), F32)
    acc[:, D + FF + OUTP :] = tn(db2[...], active[...])
    split_rows(acc, grp, keep_ref, send_ref)


def split_rows(acc, grp, keep_ref, send_ref):
    rows = keep_ref.shape[1]
    for j in range(keep_ref.shape[0]):
        for odd, ref in ((0, keep_ref), (1, send_ref)):
            at = pl.multiple_of(jnp.bitwise_xor(grp, 2 * j + odd) * rows, 16)
            ref[j, :, : acc.shape[1]] = acc[pl.ds(at, rows), :].astype(BF16)


def attend_back(shares, unit, *refs):
    own = refs[:CUTS]
    others = refs[CUTS : CUTS * shares]
    grads = refs[CUTS * shares : CUTS * shares + CUTS]
    kept_ref, lse_ref = refs[CUTS * shares + CUTS : CUTS * shares + CUTS + 2]
    outs = refs[CUTS * shares + CUTS + 2 :]
    dq_ref, own_ref = outs[:2]
    far_refs = outs[2 : 2 + shares - 1]
    keys_s, turned_s, acc = outs[2 + shares - 1 :]
    tokens = kept_ref.shape[2]
    for n, ref in enumerate(own + others):
        keys_s[n * tokens : (n + 1) * tokens, :] = ref[unit * tokens : (unit + 1) * tokens, :]
    turned_s[...] = keys_s[...].T
    every = range(CUTS)
    half = tokens // 2
    at = (own[0].shape[0] - 16) * tokens // (tokens + half) + 16 + unit * half
    queries = jnp.concatenate(
        [unpack(own[m][at : at + half, :], True) for m in every], axis=0
    )
    grads = [unpack(grads[m][0], False) for m in every]
    delta = jnp.concatenate(
        [
            jnp.sum((grads[m].astype(F32) * kept_ref[0, m]).T, axis=0, keepdims=True)
            for m in every
        ],
        axis=1,
    )
    grads = jnp.concatenate(grads, axis=0)
    lse = jnp.concatenate([lse_ref[0, m, 0:1, :] for m in every], axis=1)
    chunk = 2 * tokens
    count = keys_s.shape[0] // chunk

    def products_of(c):
        keys = keys_s[c * chunk : (c + 1) * chunk, :]
        return nt(keys, queries), nt(keys, grads)

    products, dq = products_of(0), None
    for c in range(count):
        scores, dprobs = products
        if c + 1 < count:
            products = products_of(c + 1)
        probs = jnp.exp2(scores - lse)
        dscores = (probs * (dprobs - delta)).astype(BF16)
        acc[c * chunk : (c + 1) * chunk, :] = nn(probs.astype(BF16), grads) + nn(dscores, queries)
        part = nn(turned_s[:, c * chunk : (c + 1) * chunk], dscores)
        dq = part if dq is None else dq + part
    for m in every:
        turned = dq[:, m * tokens : (m + 1) * tokens].T * SCALE
        dq_ref[0, m] = pack_rows(turned, True).astype(BF16)
    factor = jnp.where(half_low((1, 128)), 1.0 / LOG2E, 1.0)
    for m in range(CUTS):
        own_ref[0, m] = (acc[m * tokens : (m + 1) * tokens, :] * factor).astype(BF16)
        for n, ref in enumerate(far_refs):
            at = ((n + 1) * CUTS + m) * tokens
            ref[0, m] = (acc[at : at + tokens, :] * factor).astype(BF16)


def join_back(shares, *refs):
    dq_ref, own_ref = refs[:2]
    far = refs[2 : 2 + shares - 1]
    outs = refs[2 + shares - 1 :]
    tokens = own_ref.shape[2]
    for m in range(CUTS):
        total = own_ref[0, m].astype(F32)
        for ref in far:
            total = total + ref[0, m].astype(F32)
        outs[m][:tokens, :] = total.astype(BF16)
        outs[m][tokens:, :] = dq_ref[0, m]


def project_back(rounds, *refs):
    (interval, x0_ref, n1_ref, dx1_ref, rows_ref, gathered_ref, weights, mod_s) = refs[:8]
    units, outs = refs[8 : 8 + CUTS * rounds], refs[8 + CUTS * rounds :]
    (dagg_ref, keep_ref, send_ref) = outs[:3]
    unit_s, dqkv_s, acc, dmod_ref, lines_s = outs[3:]
    item = pl.program_id(0)
    grp, seq = place()
    tokens = x0_ref.shape[0]
    half = tokens // 2

    @pl.when(item == 0)
    def _():
        a = seq // (lax.axis_size("seq") // CUTS)
        for r in range(rounds):
            for m in range(CUTS):
                unit_s[CUTS * r + jnp.bitwise_xor(a, m)] = units[CUTS * r + m][...]
        acc[...] = jnp.zeros_like(acc)
        dmod_ref[...] = jnp.zeros_like(dmod_ref)

    low = half_low((half, 128))
    for h in range(HEADS):
        dqkv_s[:, h * 128 : (h + 1) * 128] = unit_s[HEADS * item + h, :tokens, :]
    for j in range(HEADS // 2):
        one = unit_s[HEADS * item + 2 * j, tokens:, :].astype(F32)
        two = unit_s[HEADS * item + 2 * j + 1, tokens:, :].astype(F32)
        lanes = slice(2 * D + j * 128, 2 * D + (j + 1) * 128)
        dqkv_s[:half, lanes] = jnp.where(low, one, swap_halves(two)).astype(BF16)
        dqkv_s[half:, lanes] = jnp.where(low, swap_halves(one), two).astype(BF16)
    dqkv = dqkv_s[...]
    which = interval[item]
    mod = mod_s[pl.ds(which, 1), :]
    acc[:, D:] += tn(n1_ref[...], dqkv)
    dn1 = nt(dqkv, weights[:, D:])
    normed, rstd = standardize(x0_ref[...])
    d_shift = jnp.sum(dn1, axis=0, keepdims=True)
    d_scale = jnp.sum(dn1 * normed, axis=0, keepdims=True)
    dx0 = (
        dx1_ref[...] + standardize_back(dn1 * (1.0 + mod[:, D : 2 * D]), normed, rstd)
    ).astype(BF16)
    rows = rows_ref[0]
    for k, row in enumerate([d_shift, d_scale] + [rows[r : r + 1] for r in range(4)]):
        dmod_ref[pl.ds(which, 1), k * D : (k + 1) * D] += row

    acc[:, :D] += tn(gathered_ref[...], dx0)
    dagg_ref[0] = nt(weights[:, :D], dx0).astype(BF16)

    @pl.when(item == pl.num_programs(0) - 1)
    def _():
        split_rows(acc, grp, keep_ref, send_ref)
        lines_s[...] = jnp.zeros_like(lines_s)
        for t in range(6 * D // 128):
            lines_s[4 * t : 4 * t + 3, :] = dmod_ref[0:3, t * 128 : (t + 1) * 128]
        rows = keep_ref.shape[1]
        for t in range(mod_tiles(rows)):
            tile = lines_s[t * rows : (t + 1) * rows, :].astype(BF16)
            at = acc.shape[1] + t * 128
            for j in range(keep_ref.shape[0]):
                keep_ref[j, :, at : at + 128] = tile
                send_ref[j, :, at : at + 128] = tile


def aggregate_back(*refs):
    (dagg_ref, probs_ref, picked_ref, fields_ref, mask_ref) = refs[:5]
    (fused_ref, agg_ref, embed_ref, probe_ref) = refs[5:9]
    keep_ref, send_ref, ds_s, acc, mix, dscore = refs[9:]
    item = pl.program_id(0)
    grp, _ = place()
    tokens = dagg_ref.shape[2]

    @pl.when(item == 0)
    def _():
        mix[...] = jnp.zeros_like(mix)
        dscore[...] = jnp.zeros_like(dscore)

    dagg = dagg_ref[0].astype(F32)
    fields = fields_ref[0]
    wide_fields = fields.astype(F32)
    keep = mask_ref[0] > 0
    expand = ones_where(spread())
    upper = iota((128, tokens), 0) < HEAD
    dparts = []
    for h in range(HEADS):
        mine = upper if h % 2 == 0 else jnp.logical_not(upper)
        pair = slice(h // 2 * 128, (h // 2 + 1) * 128)
        dparts.append(jnp.where(mine, dagg[pair], 0.0).astype(BF16))

    def spread_out(h):
        return nn(fused_ref[:, h // 2 * 128 : (h // 2 + 1) * 128], dparts[h])

    spreaded = spread_out(0)
    for j in range(HEADS // 2):
        both = None
        for h in (2 * j, 2 * j + 1):
            later = spread_out(h + 1) if h + 1 < HEADS else None
            spreaded = (spreaded * wide_fields).astype(BF16)
            part = nt(picked_ref[h, 0], dparts[h])
            both = part if both is None else both + part
            dprobs = nn(expand, spreaded)
            probs = probs_ref[0, h * VARP : (h + 1) * VARP, :]
            ds = probs * (dprobs - jnp.sum(probs * dprobs, axis=0, keepdims=True))
            ds_s[h * VARP : (h + 1) * VARP, :] = jnp.where(keep, ds, 0.0).astype(BF16)
            spreaded = later
        mix[:, j * 128 : (j + 1) * 128] += both
    dscore[...] += nt(ds_s[...], fields)

    @pl.when(item == pl.num_programs(0) - 1)
    def _():
        lines = iota((128, OUT), 0)
        owned = spread()
        drows = jnp.zeros((128, OUT), F32)
        for h in range(HEADS):
            mine = dscore[h * VARP : (h + 1) * VARP, :]
            line = jnp.sum(jnp.where(owned, mine, 0.0), axis=0, keepdims=True) * SCALE
            drows = drows + jnp.where(lines == h, line, 0.0)
        drows = drows.astype(BF16)
        mixed = mix[...].astype(BF16)
        embed = embed_ref[:, :OUT]
        acc[:, 2 * D : 2 * D + OUT] = nt(agg_ref[:, D:], mixed) + nn(probe_ref[...], drows)
        acc[:, D : 2 * D] = nn(embed, mixed)
        dprobe = nt(embed, drows)
        heads = jnp.where(iota((128, D), 1) // HEAD == iota((128, D), 0), 1.0, 0.0).astype(BF16)
        coarse = dprobe.astype(BF16)
        fine = (dprobe - coarse.astype(F32)).astype(BF16)
        by_column = nn(coarse, heads) + nn(fine, heads)
        eye = iota((D, D), 0) == iota((D, D), 1)
        query = embed_ref[:, OUT : OUT + 1].astype(F32)
        query_row = jnp.sum(jnp.where(eye, query, 0.0), axis=0, keepdims=True)
        acc[:, :D] = by_column * query_row
        dquery = jnp.sum(agg_ref[:, :D].astype(F32) * by_column, axis=0, keepdims=True)
        column = jnp.sum(jnp.where(eye, dquery, 0.0), axis=1, keepdims=True)
        acc[:, 2 * D + OUT :] = jnp.where(iota((D, OUTP - OUT), 1) == 0, column, 0.0)
        split_rows(acc, grp, keep_ref, send_ref)


def mod_tiles(rows):
    return -(-4 * (6 * D // 128) // rows)


def shares_of():
    shares = lax.axis_size("seq") // CUTS
    _, seq = place()
    return shares, seq // shares, lax.rem(seq, shares)


def added(refs, at=None):
    total = None
    for ref in refs:
        value = (ref[...] if at is None else ref[at]).astype(F32)
        total = value if total is None else total + value
    return total


def sum_cores(pairs, sources, *refs):
    ins, outs, table = refs[: 2 * sources], refs[2 * sources : -1], refs[-1]
    shares, _, share = shares_of()
    first, second = outs[:pairs], outs[pairs:]
    half = table.shape[1] // 2
    size = half // shares
    per = ins[0].shape[1] // 16
    count = sum(ref.shape[2] for ref in ins[::2]) // 128 * per
    for j in range(pairs):
        at = 0
        for keep_ref, got_ref in zip(ins[::2], ins[1::2]):
            total = (keep_ref[j].astype(F32) + got_ref[j].astype(F32)).astype(BF16)
            for t in range(total.shape[1] // 128):
                for g in range(per):
                    table[j, at] = total[g * 16 : (g + 1) * 16, t * 128 : (t + 1) * 128]
                    at += 1
        for spare in range(count, 2 * half):
            table[j, spare] = jnp.zeros(table.shape[2:], BF16)
        first[j][...] = table[j, :half]
        for n in range(shares):
            at = half + jnp.bitwise_xor(share, n) * size
            second[n][j * size : (j + 1) * size] = table[j, pl.ds(at, size)]


def sum_cores_once(pairs, *refs):
    (keep_ref, got_ref), outs = refs[:2], refs[2:]
    per = keep_ref.shape[1] // 16
    count = keep_ref.shape[2] // 128 * per
    for j in range(pairs):
        total = (keep_ref[j].astype(F32) + got_ref[j].astype(F32)).astype(BF16)
        for t in range(keep_ref.shape[2] // 128):
            for g in range(per):
                outs[j][t * per + g] = total[g * 16 : (g + 1) * 16, t * 128 : (t + 1) * 128]
        for spare in range(count, outs[j].shape[0]):
            outs[j][spare] = jnp.zeros(outs[j].shape[1:], BF16)


def sum_and_deal(over_cuts, *refs):
    outs, table = refs[-1 - (CUTS if over_cuts else shares_of()[0]) : -1], refs[-1]
    _, cut, share = shares_of()
    table[...] = added(refs[: -1 - len(outs)]).astype(BF16)
    size = outs[0].shape[0]
    for n, ref in enumerate(outs):
        ref[...] = table[pl.ds(jnp.bitwise_xor(cut if over_cuts else share, n) * size, size)]


def sum_both(pairs, shares, *refs):
    by_grp, by_share = refs[:pairs], refs[pairs : pairs + shares]
    outs, (table,) = refs[pairs + shares : -1], refs[-1:]
    _, _, share = shares_of()
    table[...] = added(by_grp).astype(BF16)
    size = outs[0].shape[0]
    for n in range(shares):
        outs[n][...] = table[pl.ds(jnp.bitwise_xor(share, n) * size, size)]
    for j in range(pairs):
        at = slice(j * size, (j + 1) * size)
        outs[shares + j][...] = added(by_share, at).astype(BF16)


def sum_both_again(pairs, shares, *refs):
    by_share, by_grp = refs[:shares], refs[shares : shares + pairs]
    outs, (table,) = refs[pairs + shares : -1], refs[-1:]
    _, cut, _ = shares_of()
    size = outs[0].shape[0] // 2
    table[0] = added(by_share).astype(BF16)
    table[1] = added(by_grp).astype(BF16)
    for m in range(CUTS):
        at = pl.ds(jnp.bitwise_xor(cut, m) * size, size)
        outs[m][:size] = table[0, at]
        outs[m][size:] = table[1, at]


def sum_pieces(*refs):
    sources, (out_ref, square_ref) = refs[:-2], refs[-2:]
    total = added(sources)
    out_ref[...] = total.astype(BF16)
    square_ref[...] = jnp.sum(total * total, axis=0)


def sum_late(start, stop, *refs):
    early_ref, loss_ref, lead_ref = refs[:3]
    sources, out_ref = refs[3:-1], refs[-1]
    grp, _ = place()
    shares, cut, share = shares_of()
    rows = lead_ref.shape[0] // lax.axis_size("grp")
    lead = lead_ref[pl.ds(pl.multiple_of(grp * rows, 16), rows), :].astype(F32)
    cols = [lead[:, g : g + 1] for g in range(3)]

    def gram(f, g):
        return jnp.sum(cols[f] * cols[g], axis=0, keepdims=True)

    row = lax.rem(iota((16, 1), 0), 4)

    def pick(*values):
        out = jnp.zeros((16, 1), F32)
        for r, value in values:
            out = jnp.where(row == r, value, out)
        return out

    same = pick(*[(g, gram(g, g)) for g in range(3)])
    next_one = pick((1, 2 * gram(0, 1)), (2, 2 * gram(1, 2)))
    next_two = pick((2, 2 * gram(0, 2)))
    size = (out_ref.shape[0] - 1) // 2
    plain = jnp.zeros((16, 128), F32)
    for half in range(2):
        for k in range(size):
            total = added(sources, half * size + k)
            out_ref[half * size + k] = total.astype(BF16)
            index = ((half * shares + share) * CUTS + cut) * size + k
            special = jnp.logical_and(index >= start, index < stop)
            square = total * total
            mixed = (
                square * same
                + total * pltpu.roll(total, 1, 0) * next_one
                + total * pltpu.roll(total, 2, 0) * next_two
            )
            plain = plain + jnp.where(special, mixed, square)
    squares = jnp.sum(jnp.sum(plain + early_ref[...], axis=0, keepdims=True), axis=1, keepdims=True)
    rider = jnp.zeros((16, 128), F32)
    for at, value in ((0, loss_ref[0:1, :]), (3, jnp.broadcast_to(squares, (1, 128)))):
        for part in range(3):
            piece = value.astype(BF16).astype(F32)
            rider = jnp.where(iota((16, 128), 0) == at + part, piece, rider)
            value = value - piece
    out_ref[2 * size] = rider.astype(BF16)


def stack_late(*refs):
    pieces, (column_ref, reduced_ref) = refs[:-2], refs[-2:]
    count = column_ref.shape[1]
    rider = jnp.zeros((16, 128), F32)
    for m, ref in enumerate(pieces):
        column_ref[m] = ref[:count]
        rider = rider + ref[count].astype(F32)
    reduced_ref[...] = jnp.concatenate(
        [rider[0:1] + rider[1:2] + rider[2:3], rider[3:4] + rider[4:5] + rider[5:6]]
        + [jnp.zeros((6, 128), F32)],
        axis=0,
    )


def stack(*refs):
    for m, ref in enumerate(refs[:-1]):
        refs[-1][m] = ref[...]


def step_values(param, first, second, grad):
    first = beta_first * first + (1.0 - beta_first) * grad
    second = beta_second * second + (1.0 - beta_second) * grad * grad
    mean_hat = first * (1.0 / (1.0 - beta_first**STEP))
    var_hat = second * (1.0 / (1.0 - beta_second**STEP))
    param = param - learn_rate * (
        mean_hat / (jnp.sqrt(var_hat) + adam_epsilon) + decay_rate * param
    )
    return param, first, second, param.astype(BF16)


def optimize(shares, *refs):
    reduced_ref, sum_ref, lead_ref = refs[:3]
    early = refs[3 : 3 + shares]
    late = refs[3 + shares : 3 + 2 * shares]
    wide = refs[3 + 2 * shares : 6 + 2 * shares]
    tall = refs[6 + 2 * shares : 9 + 2 * shares]
    query = refs[9 + 2 * shares : 12 + 2 * shares]
    outs = refs[12 + 2 * shares :]
    scalars, wide_hbm, tall_hbm, query_out = outs[:3], outs[3:7], outs[7:11], outs[11:15]
    early_s, late_s, wide_out, tall_out, sems = outs[15], outs[16], outs[17:21], outs[21:25], outs[25]
    grp, _ = place()
    _, cut, share = shares_of()
    for table, stacks, halves in ((early_s, early, 1), (late_s, late, 2)):
        size = stacks[0].shape[1] // halves
        for n, ref in enumerate(stacks):
            for m in range(CUTS):
                for half in range(halves):
                    at = (half * shares + jnp.bitwise_xor(share, n)) * CUTS
                    at = (at + jnp.bitwise_xor(cut, m)) * size
                    table[pl.ds(at, size)] = ref[m, half * size : (half + 1) * size]
    norm = jnp.sqrt(reduced_ref[1:2, 0:1])
    for ref, value in zip(scalars, (reduced_ref[0:1, 0:1], sum_ref[0:1, 0:1], norm)):
        ref[...] = value
    factor = jnp.minimum(1.0, clip_limit / (norm + 1e-06))
    rows = wide[0].shape[0]
    per = rows // 16

    def tile(table, t):
        return jnp.concatenate([table[t * per + g] for g in range(per)], axis=0).astype(F32)

    def put(ins, targets, at, grad):
        new = step_values(*[r[at] for r in ins], grad * factor)
        for ref, value in zip(targets, new):
            ref[at] = value

    def at(t, width=128):
        return (slice(None), slice(t * 128, t * 128 + width))

    copies = []

    def flush(sources, targets, lo, hi):
        for source, target in zip(sources, targets):
            copy = pltpu.make_async_copy(
                source.at[:, lo:hi], target.at[:, lo:hi], sems.at[len(copies)]
            )
            copy.start()
            copies.append(copy)

    low = half_low((rows, 128))
    for t in range(6):
        put(wide, wide_out, at(t), tile(late_s, t))
    for t in range(3):
        put(wide, wide_out, at(6 + t), tile(late_s, 15 + t))
    flush(wide_out, wide_hbm, 0, 3 * D)
    lead = lead_ref[pl.ds(pl.multiple_of(grp * rows, 16), rows), :].astype(F32)
    lines = jnp.concatenate([tile(late_s, 27 + t) for t in range(mod_tiles(rows))], axis=0)
    for t in range(18):
        grad = lead[:, 0:1] * lines[4 * t : 4 * t + 1]
        for g in (1, 2):
            grad = grad + lead[:, g : g + 1] * lines[4 * t + g : 4 * t + g + 1]
        put(wide, wide_out, at(9 + t), grad)
    flush(wide_out, wide_hbm, 3 * D, 9 * D)
    qkv = 18
    for j in range(3):
        put(wide, wide_out, at(27 + j), tile(late_s, qkv + 6 + j))
        one, two = tile(late_s, qkv + 2 * j), tile(late_s, qkv + 2 * j + 1)
        put(wide, wide_out, at(30 + j), jnp.where(low, one, swap_halves(two)))
        put(wide, wide_out, at(33 + j), jnp.where(low, swap_halves(one), two))
    flush(wide_out, wide_hbm, 9 * D, 12 * D)
    for t in range(15 + 8):
        put(wide, wide_out, at(36 + t), tile(early_s, t))
    rest = OUT - 8 * 128
    put(wide, wide_out, at(59, rest), tile(early_s, 23)[:, :rest])
    flush(wide_out, wide_hbm, 12 * D, wide[0].shape[1])
    for t in range(8):
        put(tall, tall_out, at(t), tile(late_s, 6 + t))
    flush(tall_out, tall_hbm, 0, 8 * 128)
    last = tile(late_s, 14)
    lane = iota((rows, 128), 1)
    for t in range(FF // 128):
        turned = pltpu.roll(tile(early_s, 24 + t), rest, 1)
        put(tall, tall_out, at(8 + t), jnp.where(lane < rest, last, turned))
        if t == 0:
            eye = iota((rows, rows), 0) == iota((rows, rows), 1)
            grad = jnp.sum(jnp.where(eye, last[:, rest : rest + 1], 0.0), axis=0, keepdims=True)
            put(query, query_out, (slice(None), slice(None)), grad)
        last = turned
    put(tall, tall_out, at(8 + FF // 128, rest), last[:, :rest])
    flush(tall_out, tall_hbm, 8 * 128, tall[0].shape[1])
    for copy in copies:
        copy.wait()


def shift(value, axis, bit):
    size = lax.axis_size(axis)
    return lax.ppermute(value, axis, [(i, i ^ bit) for i in range(size)])


def gather_blocks(own, group, behind=None):
    blocks = {0: own}
    for j in range(2, group, 2):
        blocks[j] = shift(own, "grp", j)
    if behind is not None:
        blocks = behind(blocks)
    for j in range(0, group, 2):
        blocks[j + 1] = shift(blocks[j], "grp", 1)
    return [blocks[j] for j in range(group)]


def granules(rows, cols, shares):
    unit = 2 * shares * CUTS
    return -(-(rows // 16) * (cols // 128) // unit) * unit


def piece_shape(count):
    return sds((count, 16, 128), BF16)


def reduce_cores(*sources, after=()):
    pairs, rows, _ = sources[0][0].shape
    shares = lax.axis_size("seq") // CUTS
    count = granules(rows, sum(keep.shape[2] for keep, _ in sources), shares)
    results = call(
        functools.partial(sum_cores, pairs, len(sources)),
        [piece_shape(count // 2)] * pairs + [piece_shape(count // 2 // shares * pairs)] * shares,
        scratch=[pltpu.VMEM((pairs, count, 16, 128), BF16)],
        after=after,
    )(*[x for source in sources for x in source])
    return results[:pairs], results[pairs:]


def reduce_cores_once(keep, got, after=()):
    pairs, rows, cols = keep.shape
    parts = lax.axis_size("seq")
    count = -(-(rows // 16) * (cols // 128) // parts) * parts
    halves = call(
        functools.partial(sum_cores_once, pairs), [piece_shape(count)] * pairs, after=after
    )(keep, got)
    return [halves[0]] + [shift(halves[j], "grp", 2 * j) for j in range(1, pairs)]


def reduce_and_deal(pieces, over, after=()):
    count = pieces[0].shape[0]
    number = CUTS if over else lax.axis_size("seq") // CUTS
    outs = call(
        functools.partial(sum_and_deal, over),
        [piece_shape(count // number)] * number,
        scratch=[pltpu.VMEM((count, 16, 128), BF16)],
        after=after,
    )(*pieces)
    if over:
        return over_cuts(outs[0], outs[1:])
    return [outs[0]] + [shift(outs[n], "seq", n) for n in range(1, number)]


def exchange_once(by_grp, by_share):
    return [by_grp[0]] + [shift(by_grp[j], "grp", 2 * j) for j in range(1, len(by_grp))], [
        by_share[0]
    ] + [shift(by_share[n], "seq", n) for n in range(1, len(by_share))]


def reduce_once(by_grp, by_share, after=()):
    pairs, shares = len(by_grp), len(by_share)
    size = by_grp[0].shape[0] // shares
    results = call(
        functools.partial(sum_both, pairs, shares),
        [piece_shape(size)] * (pairs + shares),
        scratch=[pltpu.VMEM(by_grp[0].shape, BF16)],
        after=after,
    )(*by_grp, *by_share)
    return results[:shares], results[shares:]


def exchange_again(by_share, by_grp):
    pairs, shares = len(by_grp), len(by_share)
    return [by_share[0]] + [shift(by_share[n], "seq", n) for n in range(1, shares)], [
        by_grp[0]
    ] + [shift(by_grp[j], "grp", 2 * j) for j in range(1, pairs)]


def reduce_twice(by_share, by_grp, after=()):
    pairs, shares = len(by_grp), len(by_share)
    size = by_grp[0].shape[0]
    return call(
        functools.partial(sum_both_again, pairs, shares),
        [piece_shape(2 * size // CUTS)] * CUTS,
        scratch=[pltpu.VMEM((2, size, 16, 128), BF16)],
        after=after,
    )(*by_share, *by_grp)


def over_cuts(first, others=None):
    shares = lax.axis_size("seq") // CUTS
    sent = [first] * (CUTS - 1) if others is None else others
    return [first] + [shift(sent[m - 1], "seq", m * shares) for m in range(1, CUTS)]


def stacked(pieces):
    return call(stack, sds((CUTS,) + pieces[0].shape, BF16))(*pieces)


def over_shares(column):
    shares = lax.axis_size("seq") // CUTS
    return [column] + [shift(column, "seq", n) for n in range(1, shares)]


def butterfly(value, axis, bit, stop):
    while bit < stop:
        value = value + shift(value, axis, bit)
        bit *= 2
    return value


def lead_table():
    half = D // 2
    hours = 6.0 * np.exp2(np.arange(3, dtype=np.float32))
    freqs = np.exp(-np.log(np.float32(1000.0)) * np.arange(half, dtype=np.float32) / half)
    angles = hours[None, :] * freqs.astype(np.float32)[:, None]
    waves = np.concatenate([np.sin(angles), np.cos(angles)], axis=0)
    table = np.zeros((D, 128), np.float32)
    table[:, :3] = waves / (1.0 + np.exp(-waves))
    return jnp.asarray(table).astype(BF16)


def cosine_table(count):
    line = np.arange(count, dtype=np.float32)
    return jnp.asarray(np.cos(np.pi * ((line + 0.5) / count - 0.5)).astype(np.float32))


def per_device(
    fields,
    targets,
    land_mask,
    interval,
    samples,
    wide_weights,
    wide_firsts,
    wide_seconds,
    tall_weights,
    tall_firsts,
    tall_seconds,
    query_vector,
    query_firsts,
    query_seconds,
):
    group = lax.axis_size("grp")
    parts = lax.axis_size("seq")
    shares = parts // CUTS
    rows, columns = wide_weights.shape
    items, tokens = fields.shape[:2]
    units = items * HEADS // CUTS
    every = items * tokens
    late_cols = D + FF + OUTP + FF

    query_row = query_vector.reshape(1, rows)
    tall = [x.T for x in (tall_weights, tall_firsts, tall_seconds)]
    lead = lead_table()
    cosines = cosine_table(tokens // COLS * parts)
    fields = fields.transpose(0, 2, 1)
    targets = targets.transpose(0, 2, 1)
    mask = jnp.pad(
        land_mask.transpose(0, 2, 1), ((0, 0), (0, VARP - VARS), (0, 0)), constant_values=-1
    )

    def columns_of(index):
        return pl.BlockSpec((rows, 3 * D), lambda i: (0, index))

    first_own = call(
        pack_first,
        sds((rows, 2 * D + OUTP), BF16),
        grid=(1,),
        in_specs=[columns_of(0), columns_of(0), pl.BlockSpec((1, rows), lambda i: (0, 0))],
        out_specs=whole(),
        us=2,
        limit=62,
    )(wide_weights, tall[0], query_row)
    second_own = call(
        pack_second,
        sds((rows + RIDERS, 4 * D), BF16),
        grid=(1,),
        in_specs=[smem(), smem()] + [columns_of(i) for i in range(4)] + [whole(), whole()],
        out_specs=whole(),
        scratch=[pltpu.VMEM((RIDERS, 4 * D), F32)],
        us=3,
        limit=62,
        after=(first_own,),
    )(samples, cosines, *[wide_weights] * 4, lead, mask)
    first = gather_blocks(
        first_own,
        group,
        lambda blocks: {j: once_ready(block, (second_own,)) for j, block in blocks.items()},
    )

    by_item = pl.BlockSpec((tokens, D), lambda i: (i, 0))

    def lane_block(height):
        return pl.BlockSpec((1, height, tokens), lambda i: (i, 0, 0))

    heads_spec = pl.BlockSpec((HEADS, 1, OUT, tokens), lambda i: (0, i, 0, 0))
    packed = units * (tokens + tokens // 2) + 16

    probs, picked, gathered, agg_weights, embed, fused_w, probe = call(
        functools.partial(aggregate, group),
        [
            in_hbm((items, HEADS * VARP, tokens), F32),
            in_hbm((HEADS, items, OUT, tokens), BF16),
            sds((every, D), BF16),
            in_hbm((D, 2 * D), BF16),
            in_hbm((D, OUTP), BF16),
            in_hbm((OUT, D), BF16),
            in_hbm((D, 128), BF16),
        ],
        grid=(items,),
        in_specs=[lane_block(OUT), lane_block(VARP)] + [whole()] * group,
        out_specs=[lane_block(HEADS * VARP), heads_spec, by_item] + [whole()] * 4,
        scratch=[
            pltpu.VMEM((HEADS * VARP, OUT), BF16),
            pltpu.VMEM((D, OUT), BF16),
            pltpu.VMEM((D, tokens), F32),
        ],
        us=10,
        limit=62,
    )(fields, mask, *first)
    second = gather_blocks(
        second_own,
        group,
        lambda blocks: {j: once_ready(block, (gathered,)) for j, block in blocks.items()},
    )
    late_own = call(
        pack_late,
        sds((rows, late_cols), BF16),
        grid=(1,),
        in_specs=[columns_of(4), columns_of(5), columns_of(6), whole()],
        out_specs=whole(),
        us=2,
        limit=62,
        after=(gathered,),
    )(wide_weights, wide_weights, wide_weights, tall[0])
    late_blocks = gather_blocks(late_own, group)

    results = call(
        functools.partial(project, group),
        [
            in_hbm((every, D), F32),
            in_hbm((every, D), BF16),
            in_hbm((D, 4 * D), BF16),
            in_hbm((8, 6 * D), F32),
        ]
        + [sds((packed, 128), BF16)] * CUTS,
        grid=(items,),
        in_specs=[smem(), by_item] + [whole()] * group,
        out_specs=[by_item, by_item] + [whole()] * (2 + CUTS),
        scratch=[pltpu.VMEM((items * HEADS, tokens + tokens // 2, 128), BF16)],
        us=4,
        limit=34,
        after=(late_own,),
    )(interval, gathered, *second)
    x0, n1, second_weights, mods = results[:4]
    dealt = results[4:]

    own = over_cuts(dealt[0], dealt[1:])
    keys_only = [x[: units * tokens + 16] for x in own]
    others = [shift(keys_only[m], "seq", n) for n in range(1, shares) for m in range(CUTS)]
    keys_total = parts * tokens

    half_in = pl.BlockSpec((1, tokens // 2, 128), lambda u: (u, 0, 0))
    kept_spec = pl.BlockSpec((1, CUTS, tokens, 128), lambda u: (u, 0, 0, 0))
    lse_spec = pl.BlockSpec((1, CUTS, 8, tokens), lambda u: (u, 0, 0, 0))
    pack_spec = pl.BlockSpec((1, CUTS, tokens // 2, 128), lambda u: (u, 0, 0, 0))
    half_out = sds((units, tokens // 2, 128), BF16)
    results = call(
        functools.partial(attend, shares),
        [half_out] * CUTS
        + [
            in_hbm((units, CUTS, tokens, 128), F32),
            in_hbm((units, CUTS, 8, tokens), F32),
            in_hbm((8, 128), F32),
        ],
        grid=(units,),
        in_specs=[whole()] * (CUTS * shares),
        out_specs=[half_in] * CUTS + [kept_spec, lse_spec, whole()],
        scratch=[pltpu.VMEM((keys_total, 128), BF16)],
        us=9,
        limit=60 if shares > 2 else 34,
    )(*own, *others)
    backs, (kept, lse, weight_sum) = results[:CUTS], results[CUTS:]
    heads_in = over_cuts(backs[0], backs[1:])

    saved = [D, D, D, FF, D, OUT, D, FF]
    results = call(
        functools.partial(middle, group),
        [in_hbm((every, D), F32), in_hbm((items, 8, D), F32), in_hbm((8, 128), F32)]
        + [half_out] * CUTS
        + [sds((every, width), BF16) for width in saved],
        grid=(items,),
        in_specs=[smem(), smem(), smem(), whole(), by_item, lane_block(OUT), lane_block(VARP)]
        + [whole()] * (CUTS + group + 1),
        out_specs=[by_item, pl.BlockSpec((1, 8, D), lambda i: (i, 0, 0))]
        + [whole()] * (1 + CUTS)
        + [pl.BlockSpec((tokens, width), lambda i: (i, 0)) for width in saved],
        scratch=[
            pltpu.VMEM((D, late_cols), BF16),
            pltpu.VMEM((items * HEADS, tokens // 2, 128), BF16),
            pltpu.VMEM((items * HEADS, tokens // 2, 128), BF16),
        ],
        us=11,
        limit=34,
    )(
        interval,
        samples,
        cosines,
        weight_sum,
        x0,
        targets,
        mask,
        *heads_in,
        *late_blocks,
        mods,
    )
    dx1, mod_rows, loss = results[:3]
    sends, operands = results[3 : 3 + CUTS], results[3 + CUTS :]
    early_keep, early_send = call(
        middle_weights,
        [sds((group // 2, rows, late_cols), BF16)] * 2,
        scratch=[pltpu.VMEM((D, late_cols), F32)],
        us=6,
        limit=34,
    )(*operands)
    grads_in = over_cuts(sends[0], sends[1:])

    def of_unit(u, *shape):
        return pl.BlockSpec((1,) + shape, lambda i: (u,) + (0,) * len(shape))

    def back_of(u, after):
        results = call(
            functools.partial(attend_back, shares, u),
            [sds((1, CUTS, tokens // 2, 128), BF16)]
            + [sds((1, CUTS, tokens, 128), BF16)] * shares,
            grid=(1,),
            in_specs=[whole()] * (CUTS * shares)
            + [of_unit(u, tokens // 2, 128)] * CUTS
            + [of_unit(u, CUTS, tokens, 128), of_unit(u, CUTS, 8, tokens)],
            out_specs=[whole()] * (1 + shares),
            scratch=[
                pltpu.VMEM((keys_total, 128), BF16),
                pltpu.VMEM((128, keys_total), BF16),
                pltpu.VMEM((keys_total, 128), F32),
            ],
            us=6,
            limit=60 if shares > 2 else 34,
            after=after,
        )(*own, *others, *grads_in, kept, lse)
        far = results[2:]
        if u == 2:
            far = [once_ready(far[0], units_in[0][1:]), *far[1:]]
        return results[:2], [shift(far[n], "seq", n + 1) for n in range(shares - 1)]

    def joined(near, far):
        dealt = call(
            functools.partial(join_back, shares),
            [sds((tokens + tokens // 2, 128), BF16)] * CUTS,
        )(*near, *far)
        return over_cuts(dealt[0], dealt[1:])

    early_once = reduce_cores_once(early_keep, shift(early_send, "grp", 1))
    partial_sums, units_in = [], []
    for u in range(units):
        after = (early_once[0],) if u == 0 else (partial_sums[u - 1][0][0],)
        if u >= 2:
            units_in.append(joined(*partial_sums[u - 2]))
        partial_sums.append(back_of(u, after))
    units_in.append(joined(*partial_sums[-2]))
    units_in.append(joined(*partial_sums[-1]))
    early_twice = reduce_and_deal(early_once, False, after=(units_in[1][1],))

    second_cols = 4 * D + mod_tiles(rows) * 128
    dagg, second_keep, second_send = call(
        functools.partial(project_back, units),
        [
            sds((items, D, tokens), BF16),
            sds((group // 2, rows, second_cols), BF16),
            sds((group // 2, rows, second_cols), BF16),
        ],
        grid=(items,),
        in_specs=[
            smem(),
            by_item,
            by_item,
            by_item,
            pl.BlockSpec((1, 8, D), lambda i: (i, 0, 0)),
            by_item,
        ]
        + [whole()] * (2 + CUTS * units),
        out_specs=[pl.BlockSpec((1, D, tokens), lambda i: (i, 0, 0))] + [whole()] * 2,
        scratch=[
            pltpu.VMEM((items * HEADS, tokens + tokens // 2, 128), BF16),
            pltpu.VMEM((tokens, 3 * D), BF16),
            pltpu.VMEM((D, 4 * D), F32),
            pltpu.VMEM((8, 6 * D), F32),
            pltpu.VMEM((mod_tiles(rows) * rows, 128), F32),
        ],
        us=4,
        limit=34,
    )(
        interval,
        x0,
        n1,
        dx1,
        mod_rows,
        gathered,
        second_weights,
        mods,
        *[x for unit in units_in for x in unit],
    )
    second_got = shift(second_send, "grp", 1)
    early_pieces = reduce_and_deal(early_twice, True, after=(dagg,))
    late_keep, late_send = call(
        aggregate_back,
        [sds((group // 2, rows, 2 * D + OUTP), BF16)] * 2,
        grid=(items,),
        in_specs=[
            pl.BlockSpec((1, D, tokens), lambda i: (i, 0, 0)),
            lane_block(HEADS * VARP),
            heads_spec,
            lane_block(OUT),
            lane_block(VARP),
        ]
        + [whole()] * 4,
        out_specs=[whole()] * 2,
        scratch=[
            pltpu.VMEM((HEADS * VARP, tokens), BF16),
            pltpu.VMEM((D, 2 * D + OUTP), F32),
            pltpu.VMEM((OUT, D), F32),
            pltpu.VMEM((HEADS * VARP, OUT), F32),
        ],
        us=13,
        limit=34,
        after=(early_pieces[0],),
    )(dagg, probs, picked, fields, mask, fused_w, agg_weights, embed, probe)
    early_piece, early_squares = call(
        sum_pieces,
        [piece_shape(early_pieces[0].shape[0]), sds((16, 128), F32)],
        after=(late_keep,),
    )(*early_pieces)
    early_column = over_cuts(early_piece)
    late_first = reduce_cores(
        (late_keep, shift(once_ready(late_send, (early_piece,)), "grp", 1)),
        (second_keep, second_got),
    )
    late_second = reduce_once(*exchange_once(*late_first))
    early_column = stacked(early_column)
    late_second = [[once_ready(x, (early_column,)) for x in side] for side in late_second]
    late_twice = exchange_again(*late_second)
    early_all = over_shares(once_ready(early_column, (late_twice[0][1], late_twice[1][1])))
    late_third = reduce_twice(*late_twice)
    late_pieces = over_cuts(late_third[0], late_third[1:])
    start = (rows // 16) * 27
    stop = (rows // 16) * (27 + mod_tiles(rows))
    count = late_pieces[0].shape[0]
    late_piece = call(
        functools.partial(sum_late, start, stop), piece_shape(count + 1), after=early_all[1:]
    )(early_squares, loss, lead, *late_pieces)
    late_column, reduced = call(
        stack_late, [sds((CUTS, count, 16, 128), BF16), sds((8, 128), F32)]
    )(*over_cuts(late_piece))
    late_all = over_shares(late_column)
    reduced = butterfly(reduced, "grp", 1, group)
    reduced = butterfly(reduced, "seq", 1, shares)

    def like(x, dtype=F32):
        return sds(x.shape, dtype)

    results = call(
        functools.partial(optimize, shares),
        [sds((1, 1), F32)] * 3
        + [like(wide_weights)] * 3
        + [like(wide_weights, BF16)]
        + [like(tall[0])] * 3
        + [like(tall[0], BF16)]
        + [like(query_row)] * 3
        + [like(query_row, BF16)],
        out_specs=[whole()] * 3 + [pl.BlockSpec(memory_space=pl.ANY)] * 8 + [whole()] * 4,
        scratch=[
            pltpu.VMEM((parts * early_piece.shape[0], 16, 128), BF16),
            pltpu.VMEM((parts * count, 16, 128), BF16),
        ]
        + [pltpu.VMEM(wide_weights.shape, dtype) for dtype in (F32, F32, F32, BF16)]
        + [pltpu.VMEM(tall[0].shape, dtype) for dtype in (F32, F32, F32, BF16)]
        + [pltpu.SemaphoreType.DMA((24,))],
        us=10,
        limit=34,
    )(
        reduced,
        weight_sum,
        lead,
        *early_all,
        *late_all,
        wide_weights,
        wide_firsts,
        wide_seconds,
        *tall,
        query_row,
        query_firsts.reshape(1, rows),
        query_seconds.reshape(1, rows),
    )
    tall_out = tuple(r.T for r in results[7:11])
    query_out = tuple(r.reshape(rows) for r in results[11:15])
    return tuple(r.reshape(()) for r in results[:3]) + tuple(results[3:7]) + tall_out + query_out


def solution(mesh):
    placed = (
        P("grp", "seq", None),
        P("grp", "seq", None),
        P("grp", "seq", None),
        P("grp"),
        P("grp"),
        P("grp", None),
        P("grp", None),
        P("grp", None),
        P(None, "grp"),
        P(None, "grp"),
        P(None, "grp"),
        P("grp"),
        P("grp"),
        P("grp"),
    )
    return jax.shard_map(
        per_device,
        mesh=mesh,
        in_specs=placed,
        out_specs=(
            P(),
            P(),
            P(),
            P("grp", None),
            P("grp", None),
            P("grp", None),
            P("grp", None),
            P(None, "grp"),
            P(None, "grp"),
            P(None, "grp"),
            P(None, "grp"),
            P("grp"),
            P("grp"),
            P("grp"),
            P("grp"),
        ),
        check_vma=False,
    )
```

```python
import functools

import jax
import numpy as np
import jax.numpy as jnp
from jax import lax
from jax.experimental import pallas as pl
from jax.experimental.pallas import tpu as pltpu
from jax.sharding import PartitionSpec as P

D = 384
HEADS = 6
HEAD = 64
FF = 1536
VARS = 69
PIX = 16
OUT = VARS * PIX
OUTP = 1152
VARP = 80
COLS = 128
STEP = 5
CUTS = 4
SCALE = HEAD**-0.5
LOG2E = 1.4426950408889634

beta_first = 0.5
beta_second = 0.5
learn_rate = 0.1
decay_rate = 0.01
adam_epsilon = 1e-08
clip_limit = 0.05
norm_epsilon = 1e-06
masked_score = -1e30

F32 = jnp.float32
BF16 = jnp.bfloat16
MIB = 1024 * 1024
RIDERS = 32


def dot(left, right, a, b):
    return lax.dot_general(left, right, (((a,), (b,)), ((), ())), preferred_element_type=F32)


def nn(left, right):
    return dot(left, right, 1, 0)


def nt(left, right):
    return dot(left, right, 1, 1)


def tn(left, right):
    return dot(left, right, 0, 0)


def iota(shape, dim):
    return lax.broadcasted_iota(jnp.int32, shape, dim)


def half_low(shape):
    return iota(shape, len(shape) - 1) < HEAD


def swap_halves(tile):
    return pltpu.roll(tile, HEAD, 1)


def spread():
    return iota((VARP, OUT), 1) // PIX == iota((VARP, OUT), 0)


def ones_where(mask):
    return jnp.where(mask, 1.0, 0.0).astype(BF16)


def place():
    grp = lax.axis_index("grp")
    seq = lax.axis_index("seq")
    return grp, seq


def call(
    kernel, outs, grid=(), in_specs=None, out_specs=None, scratch=(), us=1, limit=16, after=()
):
    def run(*args):
        if after:
            args = (once_ready(args[0], after), *args[1:])
        kw = {} if out_specs is None else {"out_specs": out_specs}
        return pl.pallas_call(
            kernel,
            out_shape=outs,
            grid=grid,
            in_specs=list(in_specs) if in_specs else [whole()] * len(args),
            scratch_shapes=list(scratch),
            cost_estimate=pl.CostEstimate(
                flops=int(us * 1.15e9), transcendentals=0, bytes_accessed=1024
            ),
            compiler_params=pltpu.CompilerParams(vmem_limit_bytes=limit * MIB),
            **kw,
        )(*args)

    return run


def once_ready(value, after):
    return lax.optimization_barrier((value, *after))[0]


def whole():
    return pl.BlockSpec(memory_space=pltpu.VMEM)


def smem():
    return pl.BlockSpec(memory_space=pltpu.SMEM)


def sds(shape, dtype):
    return jax.ShapeDtypeStruct(shape, dtype)


def in_hbm(shape, dtype):
    return pltpu.HBM(shape, dtype)


def standardize(x):
    centered = x - jnp.mean(x, axis=-1, keepdims=True)
    rstd = lax.rsqrt(jnp.mean(centered * centered, axis=-1, keepdims=True) + norm_epsilon)
    return centered * rstd, rstd


def standardize_back(grad, normed, rstd):
    return rstd * (
        grad
        - jnp.mean(grad, axis=-1, keepdims=True)
        - normed * jnp.mean(grad * normed, axis=-1, keepdims=True)
    )


def gelu_parts(x):
    k = 0.7978845608028654
    inner = k * (x + 0.044715 * x * x * x)
    t = jnp.tanh(inner)
    value = 0.5 * x * (1.0 + t)
    slope = 0.5 * (1.0 + t) + 0.5 * x * (1.0 - t * t) * k * (1.0 + 3 * 0.044715 * x * x)
    return value, slope


def pack_first(agg_ref, tall_ref, query_ref, first_ref):
    rows = agg_ref.shape[0]
    first_ref[:, : 2 * D] = agg_ref[:, : 2 * D].astype(BF16)
    eye = iota((rows, rows), 0) == iota((rows, rows), 1)
    column = jnp.sum(jnp.where(eye, query_ref[...], 0.0), axis=1, keepdims=True)
    lane = iota((rows, OUTP), 1)
    embed = jnp.where(lane < OUT, tall_ref[...], jnp.where(lane == OUT, column, 0.0))
    first_ref[:, 2 * D :] = embed.astype(BF16)


def pack_second(*refs):
    samples, cosines, agg_ref, mod_a, mod_b, wide_ref, lead_ref, mask_ref = refs[:8]
    second_ref, rider_s = refs[8:]
    rows = wide_ref.shape[0]
    grp, seq = place()
    second_ref[:rows, :D] = agg_ref[:, 2 * D :].astype(BF16)
    low = half_low((rows, 128))
    for j in range(HEADS // 2):
        k = wide_ref[:, D + j * 128 : D + (j + 1) * 128]
        v = wide_ref[:, 2 * D + j * 128 : 2 * D + (j + 1) * 128]
        at = D + 2 * j * 128
        second_ref[:rows, at : at + 128] = jnp.where(low, k, swap_halves(v)).astype(BF16)
        second_ref[:rows, at + 128 : at + 256] = jnp.where(low, swap_halves(k), v).astype(BF16)
    second_ref[:rows, 3 * D :] = wide_ref[:, :D].astype(BF16)
    rider_s[...] = jnp.zeros_like(rider_s)

    def ride(row, value):
        for part in range(3):
            piece = value.astype(BF16).astype(F32)
            at = part * 8 + row
            rider_s[at : at + 1, : 3 * D] = piece
            value = value - piece

    lead = lead_ref[pl.ds(pl.multiple_of(grp * rows, 16), rows), :].astype(F32)
    for half, ref in ((0, mod_a), (1, mod_b)):
        mod = ref[...].astype(BF16).astype(F32)
        for g in range(3):
            ride(2 * g + half, jnp.sum(lead[:, g : g + 1] * mod, axis=0, keepdims=True))
    items, _, tokens = mask_ref.shape
    total = jnp.zeros((1, 1), F32)
    for i in range(items):
        present = jnp.maximum(mask_ref[i], 0).astype(F32)
        weighed = jnp.sum(present, axis=0, keepdims=True) * line_weights(
            samples[i], cosines, seq, iota((1, tokens), 1)
        )
        total = total + jnp.sum(weighed, axis=1, keepdims=True)
    ride(6, jnp.broadcast_to(total, (1, 3 * D)))
    second_ref[rows:, :] = rider_s[...].astype(BF16)


def line_weights(count, cosines, seq, position):
    lines = position.size // COLS
    value = jnp.zeros(position.shape, F32)
    for r in range(lines):
        value = jnp.where(position // COLS == r, cosines[seq * lines + r], value)
    return value * count.astype(F32)


def pack_late(wide_a, wide_b, wide_c, tall_ref, late_ref):
    rows = wide_a.shape[0]
    late_ref[:, : 3 * D] = wide_a[...].astype(BF16)
    late_ref[:, 3 * D : 6 * D] = wide_b[...].astype(BF16)
    rest = D + FF + OUT - 6 * D
    late_ref[:, 6 * D : D + FF + OUT] = wide_c[:, :rest].astype(BF16)
    late_ref[:, D + FF + OUT : D + FF + OUTP] = jnp.zeros((rows, OUTP - OUT), BF16)
    late_ref[:, D + FF + OUTP :] = tall_ref[:, OUT:].astype(BF16)


def assemble(target, blocks, grp, lo, hi):
    rows = target.shape[0] // len(blocks)
    for j, ref in enumerate(blocks):
        at = pl.multiple_of(jnp.bitwise_xor(grp, j) * rows, 16)
        target[pl.ds(at, rows), :] = ref[:rows, lo:hi]


def unride(target, blocks):
    target[...] = jnp.zeros_like(target)
    for g in range(4):
        for half in range(2):
            total = jnp.zeros((1, 3 * D), F32)
            for ref in blocks:
                for part in range(3):
                    at = ref.shape[0] - RIDERS + part * 8 + min(2 * g + half, 6)
                    total = total + ref[at : at + 1, : 3 * D].astype(F32)
            target[g : g + 1, half * 3 * D : (half + 1) * 3 * D] = total


def prepare(blocks, grp, outs, score_s, fused_s):
    (agg_ref, embed_ref, fused_ref, probe_ref) = outs
    assemble(agg_ref, blocks, grp, 0, 2 * D)
    assemble(embed_ref, blocks, grp, 2 * D, 2 * D + OUTP)
    query = embed_ref[:, OUT : OUT + 1].astype(F32)
    picked = jnp.where(iota((D, 128), 1) == iota((D, 128), 0) // HEAD, query, 0.0).astype(BF16)
    probe = nn(agg_ref[:, :D], picked).astype(BF16)
    probe_ref[...] = probe
    embed = embed_ref[:, :OUT]
    rows = tn(probe, embed) * SCALE
    mine = spread()
    for h in range(HEADS):
        score_s[h * VARP : (h + 1) * VARP, :] = jnp.where(mine, rows[h : h + 1, :], 0.0).astype(
            BF16
        )
    fused = tn(agg_ref[:, D:], embed)
    fused_s[...] = fused.astype(BF16)
    fused_ref[...] = fused.T.astype(BF16)


def aggregate(group, *refs):
    (fields_ref, mask_ref) = refs[:2]
    blocks, outs = refs[2 : 2 + group], refs[2 + group :]
    (probs_ref, picked_ref, gathered_ref), kept = outs[:3], outs[3:7]
    score_s, fused_s, turned_s = outs[7:]
    grp, _ = place()

    @pl.when(pl.program_id(0) == 0)
    def _():
        prepare(blocks, grp, kept, score_s, fused_s)

    fields = fields_ref[0]
    wide_fields = fields.astype(F32)
    mask = mask_ref[0]
    scores = nn(score_s[...], fields)
    expand = ones_where(iota((OUT, VARP), 0) // PIX == iota((OUT, VARP), 1))
    rounded = []
    for h in range(HEADS):
        s = jnp.where(
            mask > 0,
            scores[h * VARP : (h + 1) * VARP],
            jnp.where(mask < 0, -3e38, masked_score),
        )
        e = jnp.exp(s - jnp.max(s, axis=0, keepdims=True))
        a = e / jnp.sum(e, axis=0, keepdims=True)
        probs_ref[0, h * VARP : (h + 1) * VARP, :] = a
        rounded.append(a.astype(BF16))
    expanded = nn(expand, rounded[0])
    for h in range(HEADS):
        later = nn(expand, rounded[h + 1]) if h + 1 < HEADS else None
        picked = (expanded * wide_fields).astype(BF16)
        picked_ref[h, 0] = picked
        turned_s[h * HEAD : (h + 1) * HEAD, :] = nn(fused_s[h * HEAD : (h + 1) * HEAD, :], picked)
        expanded = later
    gathered_ref[...] = turned_s[...].T.astype(BF16)


def project(group, *refs):
    (interval, gathered_ref), blocks, outs = refs[:2], refs[2 : 2 + group], refs[2 + group :]
    (x0_ref, n1_ref, weights, mod_s), units, (unit_s,) = outs[:4], outs[4:-1], outs[-1:]
    item = pl.program_id(0)
    grp, seq = place()
    tokens = gathered_ref.shape[0]

    @pl.when(item == 0)
    def _():
        assemble(weights, blocks, grp, 0, 4 * D)
        unride(mod_s, blocks)

    x0 = nn(gathered_ref[...], weights[:, :D])
    x0_ref[...] = x0
    mod = mod_s[pl.ds(interval[item], 1), :]
    normed, _ = standardize(x0)
    n1 = (normed * (1.0 + mod[:, D : 2 * D]) + mod[:, :D]).astype(BF16)
    n1_ref[...] = n1
    qkv = nn(n1, weights[:, D:])
    half = tokens // 2
    low = half_low((half, 128))
    packed = tokens + half
    for h in range(HEADS):
        unit_s[HEADS * item + h, :tokens, :] = qkv[:, h * 128 : (h + 1) * 128].astype(BF16)
    for j in range(HEADS // 2):
        pair = qkv[:, 2 * D + j * 128 : 2 * D + (j + 1) * 128] * (SCALE * LOG2E)
        top, bottom = pair[:half], pair[half:]
        unit_s[HEADS * item + 2 * j, tokens:packed, :] = jnp.where(
            low, top, swap_halves(bottom)
        ).astype(BF16)
        unit_s[HEADS * item + 2 * j + 1, tokens:packed, :] = jnp.where(
            low, swap_halves(top), bottom
        ).astype(BF16)

    @pl.when(item == pl.num_programs(0) - 1)
    def _():
        value = jnp.broadcast_to(mod_s[3:4, :128], (16, 128))
        high = value.astype(BF16)
        value = value - high.astype(F32)
        middle_part = value.astype(BF16)
        low_part = (value - middle_part.astype(F32)).astype(BF16)
        lane = iota((16, 128), 1)
        rides = jnp.where(
            lane < 32,
            high.astype(F32),
            jnp.where(
                lane < 64,
                middle_part.astype(F32),
                jnp.where(lane < 96, low_part.astype(F32), 0.0),
            ),
        ).astype(BF16)
        a = seq // (lax.axis_size("seq") // CUTS)
        rounds = unit_s.shape[0] // CUTS
        queries = rounds * tokens + 16
        for m in range(CUTS):
            units[m][rounds * tokens : queries, :] = rides
            for r in range(rounds):
                unit = CUTS * r + jnp.bitwise_xor(a, m)
                units[m][r * tokens : (r + 1) * tokens, :] = unit_s[unit, :tokens, :]
                at = queries + r * half
                units[m][at : at + half, :] = unit_s[unit, tokens:packed, :]


def deal(targets, source, seq):
    a = seq // (lax.axis_size("seq") // CUTS)
    for m in range(CUTS):
        for r in range(targets[m].shape[0]):
            targets[m][r] = source[CUTS * r + jnp.bitwise_xor(a, m)]


def collect(target, sources, seq):
    a = seq // (lax.axis_size("seq") // CUTS)
    for m in range(CUTS):
        for r in range(sources[m].shape[0]):
            target[CUTS * r + jnp.bitwise_xor(a, m)] = sources[m][r]


def unpack(pack, at_low):
    wide = pack.astype(F32)
    low = half_low(wide.shape)
    if at_low:
        both = [jnp.where(low, wide, 0.0), jnp.where(low, swap_halves(wide), 0.0)]
    else:
        both = [jnp.where(low, 0.0, swap_halves(wide)), jnp.where(low, 0.0, wide)]
    return jnp.concatenate(both, axis=0).astype(BF16)


def pack_rows(tile, at_low):
    half = tile.shape[0] // 2
    top, bottom = tile[:half], tile[half:]
    low = half_low(top.shape)
    if at_low:
        return jnp.where(low, top, swap_halves(bottom))
    return jnp.where(low, swap_halves(top), bottom)


def attend(shares, *refs):
    own = refs[:CUTS]
    others = refs[CUTS : CUTS * shares]
    backs = refs[CUTS * shares : CUTS * shares + CUTS]
    kept_ref, lse_ref, weight_ref, keys_s = refs[CUTS * shares + CUTS :]
    tokens = kept_ref.shape[2]
    half = tokens // 2
    unit = pl.program_id(0)
    rows = own[0].shape[0] - 16
    rider = rows * tokens // (tokens + half)

    @pl.when(unit == 0)
    def _():
        total = jnp.zeros((16, 128), F32)
        for ref in own + others:
            total = total + ref[rider : rider + 16, :].astype(F32)
        total = jnp.sum(total[0:8], axis=1, keepdims=True) / 32.0
        weight_ref[...] = jnp.broadcast_to(total, (8, 128))

    for n, ref in enumerate(own + others):
        at = pl.ds(pl.multiple_of(unit * tokens, tokens), tokens)
        keys_s[n * tokens : (n + 1) * tokens, :] = ref[at, :]
    keys = keys_s[...]
    values = jnp.where(half_low(keys.shape), jnp.ones_like(keys), keys)

    def scores_of(m):
        at = pl.ds(pl.multiple_of(rider + 16 + unit * half, 16), half)
        return nt(unpack(own[m][at, :], True), keys)

    scores = scores_of(0)
    for m in range(CUTS):
        later = scores_of(m + 1) if m + 1 < CUTS else None
        top = jnp.max(scores, axis=1, keepdims=True)
        out = nn(jnp.exp2(scores - top).astype(BF16), values)
        total = out[:, 0:1]
        out = out / total
        lse = jnp.broadcast_to(top + jnp.log2(total), (tokens, 128)).T
        lse_ref[0, m] = lse[:8]
        kept_ref[0, m] = out
        backs[m][0] = pack_rows(out, False).astype(BF16)
        scores = later


def middle(group, *refs):
    (interval, samples, cosines, sum_ref, x0_ref, fields_ref, mask_ref) = refs[:7]
    heads_in = refs[7 : 7 + CUTS]
    blocks = refs[7 + CUTS : 7 + CUTS + group]
    mod_s = refs[7 + CUTS + group]
    outs = refs[7 + CUTS + group + 1 :]
    (dx1_ref, rows_ref, loss_ref) = outs[:3]
    sends = outs[3 : 3 + CUTS]
    attended_s, db1_ref, n2_ref, dh_ref, nf_ref, dpred_ref, db2_ref, active_ref = outs[
        3 + CUTS : 11 + CUTS
    ]
    weights, head_s, grad_s = outs[11 + CUTS :]
    item = pl.program_id(0)
    grp, seq = place()
    tokens = x0_ref.shape[0]
    half = tokens // 2

    @pl.when(item == 0)
    def _():
        assemble(weights, blocks, grp, 0, D + FF + OUTP + FF)
        collect(head_s, heads_in, seq)
        loss_ref[...] = jnp.zeros_like(loss_ref)

    low = half_low((half, 128))
    for j in range(HEADS // 2):
        one = head_s[HEADS * item + 2 * j].astype(F32)
        two = head_s[HEADS * item + 2 * j + 1].astype(F32)
        attended_s[:half, j * 128 : (j + 1) * 128] = jnp.where(low, one, swap_halves(two)).astype(
            BF16
        )
        attended_s[half:, j * 128 : (j + 1) * 128] = jnp.where(low, swap_halves(one), two).astype(
            BF16
        )
    out_w = slice(0, D)
    up_w = slice(D, D + FF)
    head_w = slice(D + FF, D + FF + OUT)
    down_w = slice(D + FF + OUTP, D + FF + OUTP + FF)
    mod = mod_s[pl.ds(interval[item], 1), :]
    gate_a, shift_b, scale_b, gate_b = [mod[:, k * D : (k + 1) * D] for k in range(2, 6)]
    attended = attended_s[...]
    branch_a = nn(attended, weights[:, out_w])
    x1 = x0_ref[...] + gate_a * branch_a
    normed_b, rstd_b = standardize(x1)
    n2 = (normed_b * (1.0 + scale_b) + shift_b).astype(BF16)
    n2_ref[...] = n2
    value, slope = gelu_parts(nn(n2, weights[:, up_w]))
    active = value.astype(BF16)
    active_ref[...] = active
    branch_b = nt(active, weights[:, down_w])
    x2 = x1 + gate_b * branch_b
    final, rstd_f = standardize(x2)
    nf = final.astype(BF16)
    nf_ref[...] = nf
    diff = nn(nf, weights[:, head_w]) - fields_ref[0].astype(F32).T
    present = tn(ones_where(mask_ref[0] > 0), ones_where(spread()))
    weight = line_weights(samples[item], cosines, seq, iota((tokens, 1), 0))
    weight_grad = weight * (2.0 / PIX) / sum_ref[0:1, 0:1]
    masked = present * diff
    each = jnp.sum(masked * diff, axis=1, keepdims=True) * weight
    loss_ref[...] += jnp.broadcast_to(jnp.sum(each, axis=0, keepdims=True) / PIX, (8, 128))
    dpred = (masked * weight_grad).astype(BF16)
    dpred_ref[...] = dpred

    dx2 = standardize_back(nt(dpred, weights[:, head_w]), final, rstd_f)
    db2 = (gate_b * dx2).astype(BF16)
    db2_ref[...] = db2
    d_gate_b = jnp.sum(dx2 * branch_b, axis=0, keepdims=True)
    dh = (nn(db2, weights[:, down_w]) * slope).astype(BF16)
    dh_ref[...] = dh
    dn2 = nt(dh, weights[:, up_w])
    d_shift_b = jnp.sum(dn2, axis=0, keepdims=True)
    d_scale_b = jnp.sum(dn2 * normed_b, axis=0, keepdims=True)
    dx1 = dx2 + standardize_back(dn2 * (1.0 + scale_b), normed_b, rstd_b)
    dx1_ref[...] = dx1
    d_gate_a = jnp.sum(dx1 * branch_a, axis=0, keepdims=True)
    db1 = (gate_a * dx1).astype(BF16)
    db1_ref[...] = db1
    dout = nt(db1, weights[:, out_w])
    rows_ref[0] = jnp.concatenate(
        [d_gate_a, d_shift_b, d_scale_b, d_gate_b, jnp.zeros((4, D), F32)], axis=0
    )
    for j in range(HEADS // 2):
        pair = dout[:, j * 128 : (j + 1) * 128]
        top, bottom = pair[:half], pair[half:]
        grad_s[HEADS * item + 2 * j] = jnp.where(low, top, swap_halves(bottom)).astype(BF16)
        grad_s[HEADS * item + 2 * j + 1] = jnp.where(low, swap_halves(top), bottom).astype(BF16)

    @pl.when(item == pl.num_programs(0) - 1)
    def _():
        deal(sends, grad_s, seq)


def middle_weights(*refs):
    attended, db1, n2, dh, nf, dpred, db2, active = refs[:8]
    keep_ref, send_ref, acc = refs[8:]
    grp, _ = place()
    acc[:, :D] = tn(attended[...], db1[...])
    acc[:, D : D + FF] = tn(n2[...], dh[...])
    acc[:, D + FF : D + FF + OUT] = tn(nf[...], dpred[...])
    acc[:, D + FF + OUT : D + FF + OUTP] = jnp.zeros((D, OUTP - OUT), F32)
    acc[:, D + FF + OUTP :] = tn(db2[...], active[...])
    split_rows(acc, grp, keep_ref, send_ref)


def split_rows(acc, grp, keep_ref, send_ref):
    rows = keep_ref.shape[1]
    for j in range(keep_ref.shape[0]):
        for odd, ref in ((0, keep_ref), (1, send_ref)):
            at = pl.multiple_of(jnp.bitwise_xor(grp, 2 * j + odd) * rows, 16)
            ref[j, :, : acc.shape[1]] = acc[pl.ds(at, rows), :].astype(BF16)


def attend_back(shares, unit, *refs):
    own = refs[:CUTS]
    others = refs[CUTS : CUTS * shares]
    grads = refs[CUTS * shares : CUTS * shares + CUTS]
    kept_ref, lse_ref = refs[CUTS * shares + CUTS : CUTS * shares + CUTS + 2]
    outs = refs[CUTS * shares + CUTS + 2 :]
    dq_ref, own_ref = outs[:2]
    far_refs = outs[2 : 2 + shares - 1]
    keys_s, turned_s, acc = outs[2 + shares - 1 :]
    tokens = kept_ref.shape[2]
    for n, ref in enumerate(own + others):
        keys_s[n * tokens : (n + 1) * tokens, :] = ref[unit * tokens : (unit + 1) * tokens, :]
    turned_s[...] = keys_s[...].T
    every = range(CUTS)
    half = tokens // 2
    at = (own[0].shape[0] - 16) * tokens // (tokens + half) + 16 + unit * half
    queries = jnp.concatenate(
        [unpack(own[m][at : at + half, :], True) for m in every], axis=0
    )
    grads = [unpack(grads[m][0], False) for m in every]
    delta = jnp.concatenate(
        [
            jnp.sum((grads[m].astype(F32) * kept_ref[0, m]).T, axis=0, keepdims=True)
            for m in every
        ],
        axis=1,
    )
    grads = jnp.concatenate(grads, axis=0)
    lse = jnp.concatenate([lse_ref[0, m, 0:1, :] for m in every], axis=1)
    chunk = 2 * tokens
    count = keys_s.shape[0] // chunk

    def products_of(c):
        keys = keys_s[c * chunk : (c + 1) * chunk, :]
        return nt(keys, queries), nt(keys, grads)

    products, dq = products_of(0), None
    for c in range(count):
        scores, dprobs = products
        if c + 1 < count:
            products = products_of(c + 1)
        probs = jnp.exp2(scores - lse)
        dscores = (probs * (dprobs - delta)).astype(BF16)
        acc[c * chunk : (c + 1) * chunk, :] = nn(probs.astype(BF16), grads) + nn(dscores, queries)
        part = nn(turned_s[:, c * chunk : (c + 1) * chunk], dscores)
        dq = part if dq is None else dq + part
    for m in every:
        turned = dq[:, m * tokens : (m + 1) * tokens].T * SCALE
        dq_ref[0, m] = pack_rows(turned, True).astype(BF16)
    factor = jnp.where(half_low((1, 128)), 1.0 / LOG2E, 1.0)
    for m in range(CUTS):
        own_ref[0, m] = (acc[m * tokens : (m + 1) * tokens, :] * factor).astype(BF16)
        for n, ref in enumerate(far_refs):
            at = ((n + 1) * CUTS + m) * tokens
            ref[0, m] = (acc[at : at + tokens, :] * factor).astype(BF16)


def join_back(shares, *refs):
    dq_ref, own_ref = refs[:2]
    far = refs[2 : 2 + shares - 1]
    outs = refs[2 + shares - 1 :]
    tokens = own_ref.shape[2]
    for m in range(CUTS):
        total = own_ref[0, m].astype(F32)
        for ref in far:
            total = total + ref[0, m].astype(F32)
        outs[m][:tokens, :] = total.astype(BF16)
        outs[m][tokens:, :] = dq_ref[0, m]


def project_back(rounds, *refs):
    (interval, x0_ref, n1_ref, dx1_ref, rows_ref, gathered_ref, weights, mod_s) = refs[:8]
    units, outs = refs[8 : 8 + CUTS * rounds], refs[8 + CUTS * rounds :]
    (dagg_ref, keep_ref, send_ref) = outs[:3]
    unit_s, dqkv_s, acc, dmod_ref, lines_s = outs[3:]
    item = pl.program_id(0)
    grp, seq = place()
    tokens = x0_ref.shape[0]
    half = tokens // 2

    @pl.when(item == 0)
    def _():
        a = seq // (lax.axis_size("seq") // CUTS)
        for r in range(rounds):
            for m in range(CUTS):
                unit_s[CUTS * r + jnp.bitwise_xor(a, m)] = units[CUTS * r + m][...]
        acc[...] = jnp.zeros_like(acc)
        dmod_ref[...] = jnp.zeros_like(dmod_ref)

    low = half_low((half, 128))
    for h in range(HEADS):
        dqkv_s[:, h * 128 : (h + 1) * 128] = unit_s[HEADS * item + h, :tokens, :]
    for j in range(HEADS // 2):
        one = unit_s[HEADS * item + 2 * j, tokens:, :].astype(F32)
        two = unit_s[HEADS * item + 2 * j + 1, tokens:, :].astype(F32)
        lanes = slice(2 * D + j * 128, 2 * D + (j + 1) * 128)
        dqkv_s[:half, lanes] = jnp.where(low, one, swap_halves(two)).astype(BF16)
        dqkv_s[half:, lanes] = jnp.where(low, swap_halves(one), two).astype(BF16)
    dqkv = dqkv_s[...]
    which = interval[item]
    mod = mod_s[pl.ds(which, 1), :]
    acc[:, D:] += tn(n1_ref[...], dqkv)
    dn1 = nt(dqkv, weights[:, D:])
    normed, rstd = standardize(x0_ref[...])
    d_shift = jnp.sum(dn1, axis=0, keepdims=True)
    d_scale = jnp.sum(dn1 * normed, axis=0, keepdims=True)
    dx0 = (
        dx1_ref[...] + standardize_back(dn1 * (1.0 + mod[:, D : 2 * D]), normed, rstd)
    ).astype(BF16)
    rows = rows_ref[0]
    for k, row in enumerate([d_shift, d_scale] + [rows[r : r + 1] for r in range(4)]):
        dmod_ref[pl.ds(which, 1), k * D : (k + 1) * D] += row

    acc[:, :D] += tn(gathered_ref[...], dx0)
    dagg_ref[0] = nt(weights[:, :D], dx0).astype(BF16)

    @pl.when(item == pl.num_programs(0) - 1)
    def _():
        split_rows(acc, grp, keep_ref, send_ref)
        lines_s[...] = jnp.zeros_like(lines_s)
        for t in range(6 * D // 128):
            lines_s[4 * t : 4 * t + 3, :] = dmod_ref[0:3, t * 128 : (t + 1) * 128]
        rows = keep_ref.shape[1]
        for t in range(mod_tiles(rows)):
            tile = lines_s[t * rows : (t + 1) * rows, :].astype(BF16)
            at = acc.shape[1] + t * 128
            for j in range(keep_ref.shape[0]):
                keep_ref[j, :, at : at + 128] = tile
                send_ref[j, :, at : at + 128] = tile


def aggregate_back(*refs):
    (dagg_ref, probs_ref, picked_ref, fields_ref, mask_ref) = refs[:5]
    (fused_ref, agg_ref, embed_ref, probe_ref) = refs[5:9]
    keep_ref, send_ref, ds_s, acc, mix, dscore = refs[9:]
    item = pl.program_id(0)
    grp, _ = place()
    tokens = dagg_ref.shape[2]

    @pl.when(item == 0)
    def _():
        mix[...] = jnp.zeros_like(mix)
        dscore[...] = jnp.zeros_like(dscore)

    dagg = dagg_ref[0].astype(F32)
    fields = fields_ref[0]
    wide_fields = fields.astype(F32)
    keep = mask_ref[0] > 0
    expand = ones_where(spread())
    upper = iota((128, tokens), 0) < HEAD
    dparts = []
    for h in range(HEADS):
        mine = upper if h % 2 == 0 else jnp.logical_not(upper)
        pair = slice(h // 2 * 128, (h // 2 + 1) * 128)
        dparts.append(jnp.where(mine, dagg[pair], 0.0).astype(BF16))

    def spread_out(h):
        return nn(fused_ref[:, h // 2 * 128 : (h // 2 + 1) * 128], dparts[h])

    spreaded = spread_out(0)
    for j in range(HEADS // 2):
        both = None
        for h in (2 * j, 2 * j + 1):
            later = spread_out(h + 1) if h + 1 < HEADS else None
            spreaded = (spreaded * wide_fields).astype(BF16)
            part = nt(picked_ref[h, 0], dparts[h])
            both = part if both is None else both + part
            dprobs = nn(expand, spreaded)
            probs = probs_ref[0, h * VARP : (h + 1) * VARP, :]
            ds = probs * (dprobs - jnp.sum(probs * dprobs, axis=0, keepdims=True))
            ds_s[h * VARP : (h + 1) * VARP, :] = jnp.where(keep, ds, 0.0).astype(BF16)
            spreaded = later
        mix[:, j * 128 : (j + 1) * 128] += both
    dscore[...] += nt(ds_s[...], fields)

    @pl.when(item == pl.num_programs(0) - 1)
    def _():
        lines = iota((128, OUT), 0)
        owned = spread()
        drows = jnp.zeros((128, OUT), F32)
        for h in range(HEADS):
            mine = dscore[h * VARP : (h + 1) * VARP, :]
            line = jnp.sum(jnp.where(owned, mine, 0.0), axis=0, keepdims=True) * SCALE
            drows = drows + jnp.where(lines == h, line, 0.0)
        drows = drows.astype(BF16)
        mixed = mix[...].astype(BF16)
        embed = embed_ref[:, :OUT]
        acc[:, 2 * D : 2 * D + OUT] = nt(agg_ref[:, D:], mixed) + nn(probe_ref[...], drows)
        acc[:, D : 2 * D] = nn(embed, mixed)
        dprobe = nt(embed, drows)
        heads = jnp.where(iota((128, D), 1) // HEAD == iota((128, D), 0), 1.0, 0.0).astype(BF16)
        coarse = dprobe.astype(BF16)
        fine = (dprobe - coarse.astype(F32)).astype(BF16)
        by_column = nn(coarse, heads) + nn(fine, heads)
        eye = iota((D, D), 0) == iota((D, D), 1)
        query = embed_ref[:, OUT : OUT + 1].astype(F32)
        query_row = jnp.sum(jnp.where(eye, query, 0.0), axis=0, keepdims=True)
        acc[:, :D] = by_column * query_row
        dquery = jnp.sum(agg_ref[:, :D].astype(F32) * by_column, axis=0, keepdims=True)
        column = jnp.sum(jnp.where(eye, dquery, 0.0), axis=1, keepdims=True)
        acc[:, 2 * D + OUT :] = jnp.where(iota((D, OUTP - OUT), 1) == 0, column, 0.0)
        split_rows(acc, grp, keep_ref, send_ref)


def mod_tiles(rows):
    return -(-4 * (6 * D // 128) // rows)


def shares_of():
    shares = lax.axis_size("seq") // CUTS
    _, seq = place()
    return shares, seq // shares, lax.rem(seq, shares)


def added(refs, at=None):
    total = None
    for ref in refs:
        value = (ref[...] if at is None else ref[at]).astype(F32)
        total = value if total is None else total + value
    return total


def sum_cores(pairs, sources, *refs):
    ins, outs, table = refs[: 2 * sources], refs[2 * sources : -1], refs[-1]
    shares, _, share = shares_of()
    first, second = outs[:pairs], outs[pairs:]
    half = table.shape[1] // 2
    size = half // shares
    per = ins[0].shape[1] // 16
    count = sum(ref.shape[2] for ref in ins[::2]) // 128 * per
    for j in range(pairs):
        at = 0
        for keep_ref, got_ref in zip(ins[::2], ins[1::2]):
            total = (keep_ref[j].astype(F32) + got_ref[j].astype(F32)).astype(BF16)
            for t in range(total.shape[1] // 128):
                for g in range(per):
                    table[j, at] = total[g * 16 : (g + 1) * 16, t * 128 : (t + 1) * 128]
                    at += 1
        for spare in range(count, 2 * half):
            table[j, spare] = jnp.zeros(table.shape[2:], BF16)
        first[j][...] = table[j, :half]
        for n in range(shares):
            at = half + jnp.bitwise_xor(share, n) * size
            second[n][j * size : (j + 1) * size] = table[j, pl.ds(at, size)]


def sum_cores_once(pairs, *refs):
    (keep_ref, got_ref), outs = refs[:2], refs[2:]
    per = keep_ref.shape[1] // 16
    count = keep_ref.shape[2] // 128 * per
    for j in range(pairs):
        total = (keep_ref[j].astype(F32) + got_ref[j].astype(F32)).astype(BF16)
        for t in range(keep_ref.shape[2] // 128):
            for g in range(per):
                outs[j][t * per + g] = total[g * 16 : (g + 1) * 16, t * 128 : (t + 1) * 128]
        for spare in range(count, outs[j].shape[0]):
            outs[j][spare] = jnp.zeros(outs[j].shape[1:], BF16)


def sum_and_deal(over_cuts, *refs):
    outs, table = refs[-1 - (CUTS if over_cuts else shares_of()[0]) : -1], refs[-1]
    _, cut, share = shares_of()
    table[...] = added(refs[: -1 - len(outs)]).astype(BF16)
    size = outs[0].shape[0]
    for n, ref in enumerate(outs):
        ref[...] = table[pl.ds(jnp.bitwise_xor(cut if over_cuts else share, n) * size, size)]


def sum_both(pairs, shares, *refs):
    by_grp, by_share = refs[:pairs], refs[pairs : pairs + shares]
    outs, (table,) = refs[pairs + shares : -1], refs[-1:]
    _, _, share = shares_of()
    table[...] = added(by_grp).astype(BF16)
    size = outs[0].shape[0]
    for n in range(shares):
        outs[n][...] = table[pl.ds(jnp.bitwise_xor(share, n) * size, size)]
    for j in range(pairs):
        at = slice(j * size, (j + 1) * size)
        outs[shares + j][...] = added(by_share, at).astype(BF16)


def sum_both_again(pairs, shares, *refs):
    by_share, by_grp = refs[:shares], refs[shares : shares + pairs]
    outs, (table,) = refs[pairs + shares : -1], refs[-1:]
    _, cut, _ = shares_of()
    size = outs[0].shape[0] // 2
    table[0] = added(by_share).astype(BF16)
    table[1] = added(by_grp).astype(BF16)
    for m in range(CUTS):
        at = pl.ds(jnp.bitwise_xor(cut, m) * size, size)
        outs[m][:size] = table[0, at]
        outs[m][size:] = table[1, at]


def sum_pieces(*refs):
    sources, (out_ref, square_ref) = refs[:-2], refs[-2:]
    total = added(sources)
    out_ref[...] = total.astype(BF16)
    square_ref[...] = jnp.sum(total * total, axis=0)


def sum_late(start, stop, *refs):
    early_ref, loss_ref, lead_ref = refs[:3]
    sources, out_ref = refs[3:-1], refs[-1]
    grp, _ = place()
    shares, cut, share = shares_of()
    rows = lead_ref.shape[0] // lax.axis_size("grp")
    lead = lead_ref[pl.ds(pl.multiple_of(grp * rows, 16), rows), :].astype(F32)
    cols = [lead[:, g : g + 1] for g in range(3)]

    def gram(f, g):
        return jnp.sum(cols[f] * cols[g], axis=0, keepdims=True)

    row = lax.rem(iota((16, 1), 0), 4)

    def pick(*values):
        out = jnp.zeros((16, 1), F32)
        for r, value in values:
            out = jnp.where(row == r, value, out)
        return out

    same = pick(*[(g, gram(g, g)) for g in range(3)])
    next_one = pick((1, 2 * gram(0, 1)), (2, 2 * gram(1, 2)))
    next_two = pick((2, 2 * gram(0, 2)))
    size = (out_ref.shape[0] - 1) // 2
    plain = jnp.zeros((16, 128), F32)
    for half in range(2):
        for k in range(size):
            total = added(sources, half * size + k)
            out_ref[half * size + k] = total.astype(BF16)
            index = ((half * shares + share) * CUTS + cut) * size + k
            special = jnp.logical_and(index >= start, index < stop)
            square = total * total
            mixed = (
                square * same
                + total * pltpu.roll(total, 1, 0) * next_one
                + total * pltpu.roll(total, 2, 0) * next_two
            )
            plain = plain + jnp.where(special, mixed, square)
    squares = jnp.sum(jnp.sum(plain + early_ref[...], axis=0, keepdims=True), axis=1, keepdims=True)
    rider = jnp.zeros((16, 128), F32)
    for at, value in ((0, loss_ref[0:1, :]), (3, jnp.broadcast_to(squares, (1, 128)))):
        for part in range(3):
            piece = value.astype(BF16).astype(F32)
            rider = jnp.where(iota((16, 128), 0) == at + part, piece, rider)
            value = value - piece
    out_ref[2 * size] = rider.astype(BF16)


def stack_late(*refs):
    pieces, (column_ref, reduced_ref) = refs[:-2], refs[-2:]
    count = column_ref.shape[1]
    rider = jnp.zeros((16, 128), F32)
    for m, ref in enumerate(pieces):
        column_ref[m] = ref[:count]
        rider = rider + ref[count].astype(F32)
    reduced_ref[...] = jnp.concatenate(
        [rider[0:1] + rider[1:2] + rider[2:3], rider[3:4] + rider[4:5] + rider[5:6]]
        + [jnp.zeros((6, 128), F32)],
        axis=0,
    )


def stack(*refs):
    for m, ref in enumerate(refs[:-1]):
        refs[-1][m] = ref[...]


def step_values(param, first, second, grad):
    first = beta_first * first + (1.0 - beta_first) * grad
    second = beta_second * second + (1.0 - beta_second) * grad * grad
    mean_hat = first * (1.0 / (1.0 - beta_first**STEP))
    var_hat = second * (1.0 / (1.0 - beta_second**STEP))
    param = param - learn_rate * (
        mean_hat / (jnp.sqrt(var_hat) + adam_epsilon) + decay_rate * param
    )
    return param, first, second, param.astype(BF16)


def optimize(shares, *refs):
    reduced_ref, sum_ref, lead_ref = refs[:3]
    early = refs[3 : 3 + shares]
    late = refs[3 + shares : 3 + 2 * shares]
    wide = refs[3 + 2 * shares : 6 + 2 * shares]
    tall = refs[6 + 2 * shares : 9 + 2 * shares]
    query = refs[9 + 2 * shares : 12 + 2 * shares]
    outs = refs[12 + 2 * shares :]
    scalars, wide_hbm, tall_hbm, query_out = outs[:3], outs[3:7], outs[7:11], outs[11:15]
    early_s, late_s, wide_out, tall_out, sems = outs[15], outs[16], outs[17:21], outs[21:25], outs[25]
    grp, _ = place()
    _, cut, share = shares_of()
    for table, stacks, halves in ((early_s, early, 1), (late_s, late, 2)):
        size = stacks[0].shape[1] // halves
        for n, ref in enumerate(stacks):
            for m in range(CUTS):
                for half in range(halves):
                    at = (half * shares + jnp.bitwise_xor(share, n)) * CUTS
                    at = (at + jnp.bitwise_xor(cut, m)) * size
                    table[pl.ds(at, size)] = ref[m, half * size : (half + 1) * size]
    norm = jnp.sqrt(reduced_ref[1:2, 0:1])
    for ref, value in zip(scalars, (reduced_ref[0:1, 0:1], sum_ref[0:1, 0:1], norm)):
        ref[...] = value
    factor = jnp.minimum(1.0, clip_limit / (norm + 1e-06))
    rows = wide[0].shape[0]
    per = rows // 16

    def tile(table, t):
        return jnp.concatenate([table[t * per + g] for g in range(per)], axis=0).astype(F32)

    def put(ins, targets, at, grad):
        new = step_values(*[r[at] for r in ins], grad * factor)
        for ref, value in zip(targets, new):
            ref[at] = value

    def at(t, width=128):
        return (slice(None), slice(t * 128, t * 128 + width))

    copies = []

    def flush(sources, targets, lo, hi):
        for source, target in zip(sources, targets):
            copy = pltpu.make_async_copy(
                source.at[:, lo:hi], target.at[:, lo:hi], sems.at[len(copies)]
            )
            copy.start()
            copies.append(copy)

    low = half_low((rows, 128))
    for t in range(6):
        put(wide, wide_out, at(t), tile(late_s, t))
    for t in range(3):
        put(wide, wide_out, at(6 + t), tile(late_s, 15 + t))
    flush(wide_out, wide_hbm, 0, 3 * D)
    lead = lead_ref[pl.ds(pl.multiple_of(grp * rows, 16), rows), :].astype(F32)
    lines = jnp.concatenate([tile(late_s, 27 + t) for t in range(mod_tiles(rows))], axis=0)
    for t in range(18):
        grad = lead[:, 0:1] * lines[4 * t : 4 * t + 1]
        for g in (1, 2):
            grad = grad + lead[:, g : g + 1] * lines[4 * t + g : 4 * t + g + 1]
        put(wide, wide_out, at(9 + t), grad)
    flush(wide_out, wide_hbm, 3 * D, 9 * D)
    qkv = 18
    for j in range(3):
        put(wide, wide_out, at(27 + j), tile(late_s, qkv + 6 + j))
        one, two = tile(late_s, qkv + 2 * j), tile(late_s, qkv + 2 * j + 1)
        put(wide, wide_out, at(30 + j), jnp.where(low, one, swap_halves(two)))
        put(wide, wide_out, at(33 + j), jnp.where(low, swap_halves(one), two))
    flush(wide_out, wide_hbm, 9 * D, 12 * D)
    for t in range(15 + 8):
        put(wide, wide_out, at(36 + t), tile(early_s, t))
    rest = OUT - 8 * 128
    put(wide, wide_out, at(59, rest), tile(early_s, 23)[:, :rest])
    flush(wide_out, wide_hbm, 12 * D, wide[0].shape[1])
    for t in range(8):
        put(tall, tall_out, at(t), tile(late_s, 6 + t))
    flush(tall_out, tall_hbm, 0, 8 * 128)
    last = tile(late_s, 14)
    lane = iota((rows, 128), 1)
    for t in range(FF // 128):
        turned = pltpu.roll(tile(early_s, 24 + t), rest, 1)
        put(tall, tall_out, at(8 + t), jnp.where(lane < rest, last, turned))
        if t == 0:
            eye = iota((rows, rows), 0) == iota((rows, rows), 1)
            grad = jnp.sum(jnp.where(eye, last[:, rest : rest + 1], 0.0), axis=0, keepdims=True)
            put(query, query_out, (slice(None), slice(None)), grad)
        last = turned
    put(tall, tall_out, at(8 + FF // 128, rest), last[:, :rest])
    flush(tall_out, tall_hbm, 8 * 128, tall[0].shape[1])
    for copy in copies:
        copy.wait()


def shift(value, axis, bit):
    size = lax.axis_size(axis)
    return lax.ppermute(value, axis, [(i, i ^ bit) for i in range(size)])


def gather_blocks(own, group, behind=None):
    blocks = {0: own}
    for j in range(2, group, 2):
        blocks[j] = shift(own, "grp", j)
    if behind is not None:
        blocks = behind(blocks)
    for j in range(0, group, 2):
        blocks[j + 1] = shift(blocks[j], "grp", 1)
    return [blocks[j] for j in range(group)]


def granules(rows, cols, shares):
    unit = 2 * shares * CUTS
    return -(-(rows // 16) * (cols // 128) // unit) * unit


def piece_shape(count):
    return sds((count, 16, 128), BF16)


def reduce_cores(*sources, after=()):
    pairs, rows, _ = sources[0][0].shape
    shares = lax.axis_size("seq") // CUTS
    count = granules(rows, sum(keep.shape[2] for keep, _ in sources), shares)
    results = call(
        functools.partial(sum_cores, pairs, len(sources)),
        [piece_shape(count // 2)] * pairs + [piece_shape(count // 2 // shares * pairs)] * shares,
        scratch=[pltpu.VMEM((pairs, count, 16, 128), BF16)],
        after=after,
    )(*[x for source in sources for x in source])
    return results[:pairs], results[pairs:]


def reduce_cores_once(keep, got, after=()):
    pairs, rows, cols = keep.shape
    parts = lax.axis_size("seq")
    count = -(-(rows // 16) * (cols // 128) // parts) * parts
    halves = call(
        functools.partial(sum_cores_once, pairs), [piece_shape(count)] * pairs, after=after
    )(keep, got)
    return [halves[0]] + [shift(halves[j], "grp", 2 * j) for j in range(1, pairs)]


def reduce_and_deal(pieces, over, after=()):
    count = pieces[0].shape[0]
    number = CUTS if over else lax.axis_size("seq") // CUTS
    outs = call(
        functools.partial(sum_and_deal, over),
        [piece_shape(count // number)] * number,
        scratch=[pltpu.VMEM((count, 16, 128), BF16)],
        after=after,
    )(*pieces)
    if over:
        return over_cuts(outs[0], outs[1:])
    return [outs[0]] + [shift(outs[n], "seq", n) for n in range(1, number)]


def exchange_once(by_grp, by_share):
    return [by_grp[0]] + [shift(by_grp[j], "grp", 2 * j) for j in range(1, len(by_grp))], [
        by_share[0]
    ] + [shift(by_share[n], "seq", n) for n in range(1, len(by_share))]


def reduce_once(by_grp, by_share, after=()):
    pairs, shares = len(by_grp), len(by_share)
    size = by_grp[0].shape[0] // shares
    results = call(
        functools.partial(sum_both, pairs, shares),
        [piece_shape(size)] * (pairs + shares),
        scratch=[pltpu.VMEM(by_grp[0].shape, BF16)],
        after=after,
    )(*by_grp, *by_share)
    return results[:shares], results[shares:]


def exchange_again(by_share, by_grp):
    pairs, shares = len(by_grp), len(by_share)
    return [by_share[0]] + [shift(by_share[n], "seq", n) for n in range(1, shares)], [
        by_grp[0]
    ] + [shift(by_grp[j], "grp", 2 * j) for j in range(1, pairs)]


def reduce_twice(by_share, by_grp, after=()):
    pairs, shares = len(by_grp), len(by_share)
    size = by_grp[0].shape[0]
    return call(
        functools.partial(sum_both_again, pairs, shares),
        [piece_shape(2 * size // CUTS)] * CUTS,
        scratch=[pltpu.VMEM((2, size, 16, 128), BF16)],
        after=after,
    )(*by_share, *by_grp)


def over_cuts(first, others=None):
    shares = lax.axis_size("seq") // CUTS
    sent = [first] * (CUTS - 1) if others is None else others
    return [first] + [shift(sent[m - 1], "seq", m * shares) for m in range(1, CUTS)]


def stacked(pieces):
    return call(stack, sds((CUTS,) + pieces[0].shape, BF16))(*pieces)


def over_shares(column):
    shares = lax.axis_size("seq") // CUTS
    return [column] + [shift(column, "seq", n) for n in range(1, shares)]


def butterfly(value, axis, bit, stop):
    while bit < stop:
        value = value + shift(value, axis, bit)
        bit *= 2
    return value


def lead_table():
    half = D // 2
    hours = 6.0 * np.exp2(np.arange(3, dtype=np.float32))
    freqs = np.exp(-np.log(np.float32(1000.0)) * np.arange(half, dtype=np.float32) / half)
    angles = hours[None, :] * freqs.astype(np.float32)[:, None]
    waves = np.concatenate([np.sin(angles), np.cos(angles)], axis=0)
    table = np.zeros((D, 128), np.float32)
    table[:, :3] = waves / (1.0 + np.exp(-waves))
    return jnp.asarray(table).astype(BF16)


def cosine_table(count):
    line = np.arange(count, dtype=np.float32)
    return jnp.asarray(np.cos(np.pi * ((line + 0.5) / count - 0.5)).astype(np.float32))


def per_device(
    fields,
    targets,
    land_mask,
    interval,
    samples,
    wide_weights,
    wide_firsts,
    wide_seconds,
    tall_weights,
    tall_firsts,
    tall_seconds,
    query_vector,
    query_firsts,
    query_seconds,
):
    group = lax.axis_size("grp")
    parts = lax.axis_size("seq")
    shares = parts // CUTS
    rows, columns = wide_weights.shape
    items, tokens = fields.shape[:2]
    units = items * HEADS // CUTS
    every = items * tokens
    late_cols = D + FF + OUTP + FF

    query_row = query_vector.reshape(1, rows)
    tall = [x.T for x in (tall_weights, tall_firsts, tall_seconds)]
    lead = lead_table()
    cosines = cosine_table(tokens // COLS * parts)
    fields = fields.transpose(0, 2, 1)
    targets = targets.transpose(0, 2, 1)
    mask = jnp.pad(
        land_mask.transpose(0, 2, 1), ((0, 0), (0, VARP - VARS), (0, 0)), constant_values=-1
    )

    def columns_of(index):
        return pl.BlockSpec((rows, 3 * D), lambda i: (0, index))

    first_own = call(
        pack_first,
        sds((rows, 2 * D + OUTP), BF16),
        grid=(1,),
        in_specs=[columns_of(0), columns_of(0), pl.BlockSpec((1, rows), lambda i: (0, 0))],
        out_specs=whole(),
        us=2,
        limit=62,
    )(wide_weights, tall[0], query_row)
    second_own = call(
        pack_second,
        sds((rows + RIDERS, 4 * D), BF16),
        grid=(1,),
        in_specs=[smem(), smem()] + [columns_of(i) for i in range(4)] + [whole(), whole()],
        out_specs=whole(),
        scratch=[pltpu.VMEM((RIDERS, 4 * D), F32)],
        us=3,
        limit=62,
        after=(first_own,),
    )(samples, cosines, *[wide_weights] * 4, lead, mask)
    first = gather_blocks(
        first_own,
        group,
        lambda blocks: {j: once_ready(block, (second_own,)) for j, block in blocks.items()},
    )

    by_item = pl.BlockSpec((tokens, D), lambda i: (i, 0))

    def lane_block(height):
        return pl.BlockSpec((1, height, tokens), lambda i: (i, 0, 0))

    heads_spec = pl.BlockSpec((HEADS, 1, OUT, tokens), lambda i: (0, i, 0, 0))
    packed = units * (tokens + tokens // 2) + 16

    probs, picked, gathered, agg_weights, embed, fused_w, probe = call(
        functools.partial(aggregate, group),
        [
            in_hbm((items, HEADS * VARP, tokens), F32),
            in_hbm((HEADS, items, OUT, tokens), BF16),
            sds((every, D), BF16),
            in_hbm((D, 2 * D), BF16),
            in_hbm((D, OUTP), BF16),
            in_hbm((OUT, D), BF16),
            in_hbm((D, 128), BF16),
        ],
        grid=(items,),
        in_specs=[lane_block(OUT), lane_block(VARP)] + [whole()] * group,
        out_specs=[lane_block(HEADS * VARP), heads_spec, by_item] + [whole()] * 4,
        scratch=[
            pltpu.VMEM((HEADS * VARP, OUT), BF16),
            pltpu.VMEM((D, OUT), BF16),
            pltpu.VMEM((D, tokens), F32),
        ],
        us=10,
        limit=62,
    )(fields, mask, *first)
    second = gather_blocks(
        second_own,
        group,
        lambda blocks: {j: once_ready(block, (gathered,)) for j, block in blocks.items()},
    )
    late_own = call(
        pack_late,
        sds((rows, late_cols), BF16),
        grid=(1,),
        in_specs=[columns_of(4), columns_of(5), columns_of(6), whole()],
        out_specs=whole(),
        us=2,
        limit=62,
        after=(gathered,),
    )(wide_weights, wide_weights, wide_weights, tall[0])
    late_blocks = gather_blocks(late_own, group)

    results = call(
        functools.partial(project, group),
        [
            in_hbm((every, D), F32),
            in_hbm((every, D), BF16),
            in_hbm((D, 4 * D), BF16),
            in_hbm((8, 6 * D), F32),
        ]
        + [sds((packed, 128), BF16)] * CUTS,
        grid=(items,),
        in_specs=[smem(), by_item] + [whole()] * group,
        out_specs=[by_item, by_item] + [whole()] * (2 + CUTS),
        scratch=[pltpu.VMEM((items * HEADS, tokens + tokens // 2, 128), BF16)],
        us=4,
        limit=34,
        after=(late_own,),
    )(interval, gathered, *second)
    x0, n1, second_weights, mods = results[:4]
    dealt = results[4:]

    own = over_cuts(dealt[0], dealt[1:])
    keys_only = [x[: units * tokens + 16] for x in own]
    others = [shift(keys_only[m], "seq", n) for n in range(1, shares) for m in range(CUTS)]
    keys_total = parts * tokens

    half_in = pl.BlockSpec((1, tokens // 2, 128), lambda u: (u, 0, 0))
    kept_spec = pl.BlockSpec((1, CUTS, tokens, 128), lambda u: (u, 0, 0, 0))
    lse_spec = pl.BlockSpec((1, CUTS, 8, tokens), lambda u: (u, 0, 0, 0))
    pack_spec = pl.BlockSpec((1, CUTS, tokens // 2, 128), lambda u: (u, 0, 0, 0))
    half_out = sds((units, tokens // 2, 128), BF16)
    results = call(
        functools.partial(attend, shares),
        [half_out] * CUTS
        + [
            in_hbm((units, CUTS, tokens, 128), F32),
            in_hbm((units, CUTS, 8, tokens), F32),
            in_hbm((8, 128), F32),
        ],
        grid=(units,),
        in_specs=[whole()] * (CUTS * shares),
        out_specs=[half_in] * CUTS + [kept_spec, lse_spec, whole()],
        scratch=[pltpu.VMEM((keys_total, 128), BF16)],
        us=9,
        limit=60 if shares > 2 else 34,
    )(*own, *others)
    backs, (kept, lse, weight_sum) = results[:CUTS], results[CUTS:]
    heads_in = over_cuts(backs[0], backs[1:])

    saved = [D, D, D, FF, D, OUT, D, FF]
    results = call(
        functools.partial(middle, group),
        [in_hbm((every, D), F32), in_hbm((items, 8, D), F32), in_hbm((8, 128), F32)]
        + [half_out] * CUTS
        + [sds((every, width), BF16) for width in saved],
        grid=(items,),
        in_specs=[smem(), smem(), smem(), whole(), by_item, lane_block(OUT), lane_block(VARP)]
        + [whole()] * (CUTS + group + 1),
        out_specs=[by_item, pl.BlockSpec((1, 8, D), lambda i: (i, 0, 0))]
        + [whole()] * (1 + CUTS)
        + [pl.BlockSpec((tokens, width), lambda i: (i, 0)) for width in saved],
        scratch=[
            pltpu.VMEM((D, late_cols), BF16),
            pltpu.VMEM((items * HEADS, tokens // 2, 128), BF16),
            pltpu.VMEM((items * HEADS, tokens // 2, 128), BF16),
        ],
        us=11,
        limit=34,
    )(
        interval,
        samples,
        cosines,
        weight_sum,
        x0,
        targets,
        mask,
        *heads_in,
        *late_blocks,
        mods,
    )
    dx1, mod_rows, loss = results[:3]
    sends, operands = results[3 : 3 + CUTS], results[3 + CUTS :]
    early_keep, early_send = call(
        middle_weights,
        [sds((group // 2, rows, late_cols), BF16)] * 2,
        scratch=[pltpu.VMEM((D, late_cols), F32)],
        us=6,
        limit=34,
    )(*operands)
    grads_in = over_cuts(sends[0], sends[1:])

    def of_unit(u, *shape):
        return pl.BlockSpec((1,) + shape, lambda i: (u,) + (0,) * len(shape))

    def back_of(u, after):
        results = call(
            functools.partial(attend_back, shares, u),
            [sds((1, CUTS, tokens // 2, 128), BF16)]
            + [sds((1, CUTS, tokens, 128), BF16)] * shares,
            grid=(1,),
            in_specs=[whole()] * (CUTS * shares)
            + [of_unit(u, tokens // 2, 128)] * CUTS
            + [of_unit(u, CUTS, tokens, 128), of_unit(u, CUTS, 8, tokens)],
            out_specs=[whole()] * (1 + shares),
            scratch=[
                pltpu.VMEM((keys_total, 128), BF16),
                pltpu.VMEM((128, keys_total), BF16),
                pltpu.VMEM((keys_total, 128), F32),
            ],
            us=6,
            limit=60 if shares > 2 else 34,
            after=after,
        )(*own, *others, *grads_in, kept, lse)
        far = results[2:]
        if u == 2:
            far = [once_ready(far[0], units_in[0][1:]), *far[1:]]
        return results[:2], [shift(far[n], "seq", n + 1) for n in range(shares - 1)]

    def joined(near, far):
        dealt = call(
            functools.partial(join_back, shares),
            [sds((tokens + tokens // 2, 128), BF16)] * CUTS,
        )(*near, *far)
        return over_cuts(dealt[0], dealt[1:])

    early_once = reduce_cores_once(early_keep, shift(early_send, "grp", 1))
    partial_sums, units_in = [], []
    for u in range(units):
        after = (early_once[0],) if u == 0 else (partial_sums[u - 1][0][0],)
        if u >= 2:
            units_in.append(joined(*partial_sums[u - 2]))
        partial_sums.append(back_of(u, after))
    units_in.append(joined(*partial_sums[-2]))
    units_in.append(joined(*partial_sums[-1]))
    early_twice = reduce_and_deal(early_once, False, after=(units_in[1][1],))

    second_cols = 4 * D + mod_tiles(rows) * 128
    dagg, second_keep, second_send = call(
        functools.partial(project_back, units),
        [
            sds((items, D, tokens), BF16),
            sds((group // 2, rows, second_cols), BF16),
            sds((group // 2, rows, second_cols), BF16),
        ],
        grid=(items,),
        in_specs=[
            smem(),
            by_item,
            by_item,
            by_item,
            pl.BlockSpec((1, 8, D), lambda i: (i, 0, 0)),
            by_item,
        ]
        + [whole()] * (2 + CUTS * units),
        out_specs=[pl.BlockSpec((1, D, tokens), lambda i: (i, 0, 0))] + [whole()] * 2,
        scratch=[
            pltpu.VMEM((items * HEADS, tokens + tokens // 2, 128), BF16),
            pltpu.VMEM((tokens, 3 * D), BF16),
            pltpu.VMEM((D, 4 * D), F32),
            pltpu.VMEM((8, 6 * D), F32),
            pltpu.VMEM((mod_tiles(rows) * rows, 128), F32),
        ],
        us=4,
        limit=34,
    )(
        interval,
        x0,
        n1,
        dx1,
        mod_rows,
        gathered,
        second_weights,
        mods,
        *[x for unit in units_in for x in unit],
    )
    second_got = shift(second_send, "grp", 1)
    early_pieces = reduce_and_deal(early_twice, True, after=(dagg,))
    late_keep, late_send = call(
        aggregate_back,
        [sds((group // 2, rows, 2 * D + OUTP), BF16)] * 2,
        grid=(items,),
        in_specs=[
            pl.BlockSpec((1, D, tokens), lambda i: (i, 0, 0)),
            lane_block(HEADS * VARP),
            heads_spec,
            lane_block(OUT),
            lane_block(VARP),
        ]
        + [whole()] * 4,
        out_specs=[whole()] * 2,
        scratch=[
            pltpu.VMEM((HEADS * VARP, tokens), BF16),
            pltpu.VMEM((D, 2 * D + OUTP), F32),
            pltpu.VMEM((OUT, D), F32),
            pltpu.VMEM((HEADS * VARP, OUT), F32),
        ],
        us=13,
        limit=34,
        after=(early_pieces[0],),
    )(dagg, probs, picked, fields, mask, fused_w, agg_weights, embed, probe)
    early_piece, early_squares = call(
        sum_pieces,
        [piece_shape(early_pieces[0].shape[0]), sds((16, 128), F32)],
        after=(late_keep,),
    )(*early_pieces)
    early_column = over_cuts(early_piece)
    late_first = reduce_cores(
        (late_keep, shift(once_ready(late_send, (early_piece,)), "grp", 1)),
        (second_keep, second_got),
    )
    late_second = reduce_once(*exchange_once(*late_first))
    early_column = stacked(early_column)
    late_second = [[once_ready(x, (early_column,)) for x in side] for side in late_second]
    late_twice = exchange_again(*late_second)
    early_all = over_shares(once_ready(early_column, (late_twice[0][1], late_twice[1][1])))
    late_third = reduce_twice(*late_twice)
    late_pieces = over_cuts(late_third[0], late_third[1:])
    start = (rows // 16) * 27
    stop = (rows // 16) * (27 + mod_tiles(rows))
    count = late_pieces[0].shape[0]
    late_piece = call(
        functools.partial(sum_late, start, stop), piece_shape(count + 1), after=early_all[1:]
    )(early_squares, loss, lead, *late_pieces)
    late_column, reduced = call(
        stack_late, [sds((CUTS, count, 16, 128), BF16), sds((8, 128), F32)]
    )(*over_cuts(late_piece))
    late_all = over_shares(late_column)
    reduced = butterfly(reduced, "grp", 1, group)
    reduced = butterfly(reduced, "seq", 1, shares)

    def like(x, dtype=F32):
        return sds(x.shape, dtype)

    results = call(
        functools.partial(optimize, shares),
        [sds((1, 1), F32)] * 3
        + [like(wide_weights)] * 3
        + [like(wide_weights, BF16)]
        + [like(tall[0])] * 3
        + [like(tall[0], BF16)]
        + [like(query_row)] * 3
        + [like(query_row, BF16)],
        out_specs=[whole()] * 3 + [pl.BlockSpec(memory_space=pl.ANY)] * 8 + [whole()] * 4,
        scratch=[
            pltpu.VMEM((parts * early_piece.shape[0], 16, 128), BF16),
            pltpu.VMEM((parts * count, 16, 128), BF16),
        ]
        + [pltpu.VMEM(wide_weights.shape, dtype) for dtype in (F32, F32, F32, BF16)]
        + [pltpu.VMEM(tall[0].shape, dtype) for dtype in (F32, F32, F32, BF16)]
        + [pltpu.SemaphoreType.DMA((24,))],
        us=10,
        limit=34,
    )(
        reduced,
        weight_sum,
        lead,
        *early_all,
        *late_all,
        wide_weights,
        wide_firsts,
        wide_seconds,
        *tall,
        query_row,
        query_firsts.reshape(1, rows),
        query_seconds.reshape(1, rows),
    )
    tall_out = tuple(r.T for r in results[7:11])
    query_out = tuple(r.reshape(rows) for r in results[11:15])
    return tuple(r.reshape(()) for r in results[:3]) + tuple(results[3:7]) + tall_out + query_out


def solution(mesh):
    placed = (
        P("grp", "seq", None),
        P("grp", "seq", None),
        P("grp", "seq", None),
        P("grp"),
        P("grp"),
        P("grp", None),
        P("grp", None),
        P("grp", None),
        P(None, "grp"),
        P(None, "grp"),
        P(None, "grp"),
        P("grp"),
        P("grp"),
        P("grp"),
    )
    return jax.shard_map(
        per_device,
        mesh=mesh,
        in_specs=placed,
        out_specs=(
            P(),
            P(),
            P(),
            P("grp", None),
            P("grp", None),
            P("grp", None),
            P("grp", None),
            P(None, "grp"),
            P(None, "grp"),
            P(None, "grp"),
            P(None, "grp"),
            P("grp"),
            P("grp"),
            P("grp"),
            P("grp"),
        ),
        check_vma=False,
    )
```
